32 devices in a mesh: leaf: 4 (over z), rows: 8 (over y, x, core).
Axes of the slice: x: 2, y: 2, z: 4, core: 2. Of those that a mesh axis runs over, the one named last changes fastest.
Arguments:
- rhs: bfloat16 [147456, 512], P(('leaf', 'rows')), may hold values from -6 to 6
- leaf_order: int32 [576, 256], P(('leaf', 'rows')), may hold values from 0 to 255, each once within a row
- leaf_inv: bfloat16 [576, 256, 256], P(('leaf', 'rows')), may hold values from -0.375 to 0.375
- right_basis: bfloat16 [3, 147456, 128], P(None, ('leaf', 'rows')), may hold values from -0.03125 to 0.03125
- left_basis: bfloat16 [3, 147456, 128], P(None, ('leaf', 'rows')), may hold values from -0.375 to 0.375
- rank_perm: int32 [3, 128], replicated, may hold values from 0 to 127, each once within a row
- joined: float32 [7, 256, 256], replicated, may hold values from -0.375 to 0.375
Outputs:
- solution: float32 [147456, 512], P(('leaf', 'rows'))
The draws below stay inside these ranges and needn't reach their ends.
Inputs may be any that keep to these rules, and one draw needn't show every extreme that they name: Each row of leaf_order names every number below 256 once. Each row of rank_perm names every number below 128 once.
All inputs are finite; a program needn't handle non-finite values.
Results may differ from the reference program's by a relative error of at most 0.0003.
Values sent between devices are 32-bit elements; how exact they have to be, the bound alone decides.
No kernel may reach another device: no remote copies, remote signals or barrier semaphores. Data moves between devices by JAX's collectives and lax.ppermute only.
A program may use at most 128 MiB of HBM per device.

```python
import jax
import jax.numpy as jnp
from jax import lax

BLOCK_ORDER = 256
RANK_WIDTH = 128
TARGETS = 512
ROWS_DEV = 4608
LEVELS = 3
ROW_BITS = 3
NODE_COUNT = 7
TOTAL_ROWS = 147456
BLOCK_COUNT = 576
N_ROWS = 8


def shard_levels(stream_key, dims, pieces, smallest, high):
    def one(position, shards_of):
        draws = jax.random.uniform(jax.random.fold_in(jax.random.fold_in(stream_key, 6), position), (shards_of,), jnp.float32, smallest / len(pieces), high / len(pieces))
        return jnp.repeat(jnp.exp(draws), dims[position] // shards_of).reshape((-1,) + (1,) * (len(dims) - position - 1))

    level = one(*pieces[0])
    for cut in pieces[1:]:
        level = level * one(*cut)
    return level


def gaussian(stream_key, extent, spread, most, split=(), kind=jnp.bfloat16):
    entries = jax.random.normal(stream_key, extent, jnp.float32) * spread
    if len(split) > 0:
        entries = shard_levels(stream_key, extent, split, -0.22, 0.18) * entries
    return jnp.clip(entries, min=-most, max=most).astype(kind)


def setup_inputs(seed: int = 0) -> dict:
    splits = jax.random.split(jax.random.key(seed), 8)
    rhs = gaussian(splits[0], (TOTAL_ROWS, TARGETS), 1.0, 6.0, ((0, 32),))
    leaf_order = jax.vmap(lambda own: jax.random.permutation(own, BLOCK_ORDER))(jax.random.split(splits[1], BLOCK_COUNT)).reshape((BLOCK_COUNT, BLOCK_ORDER)).astype(jnp.int32)
    leaf_inv = gaussian(splits[2], (BLOCK_COUNT, BLOCK_ORDER, BLOCK_ORDER), BLOCK_ORDER ** -0.5, 0.375, ((0, 32),))
    right_basis = gaussian(splits[3], (LEVELS, TOTAL_ROWS, RANK_WIDTH), (ROWS_DEV * N_ROWS) ** -0.5, 0.03125, ((1, 32),))
    left_basis = gaussian(splits[4], (LEVELS, TOTAL_ROWS, RANK_WIDTH), (2 * RANK_WIDTH) ** -0.5, 0.375, ((1, 32),))
    rank_perm = jax.vmap(lambda own: jax.random.permutation(own, RANK_WIDTH))(jax.random.split(splits[5], LEVELS)).reshape((LEVELS, RANK_WIDTH)).astype(jnp.int32)
    joined = gaussian(splits[6], (NODE_COUNT, 2 * RANK_WIDTH, 2 * RANK_WIDTH), (2 * RANK_WIDTH) ** -0.5, 0.375, (), jnp.float32)
    return dict(rhs=rhs, leaf_order=leaf_order, leaf_inv=leaf_inv, right_basis=right_basis, left_basis=left_basis, rank_perm=rank_perm, joined=joined)


HIGHEST = lax.Precision.HIGHEST


def reference(rhs, leaf_order, leaf_inv, right_basis, left_basis, rank_perm, joined):
    block_count = leaf_inv.shape[0]
    blocks = rhs.reshape(block_count, BLOCK_ORDER, TARGETS)
    ordered = jnp.take_along_axis(blocks, leaf_order[:, :, None], axis=1)
    current = jnp.einsum("bij,bjr->bir", leaf_inv.astype(jnp.float32), ordered.astype(jnp.float32),
                         precision=HIGHEST).reshape(TOTAL_ROWS, TARGETS)
    for tree_level in range(LEVELS):
        child_rows = ROWS_DEV * 2 ** (ROW_BITS - 1 + tree_level)
        children = TOTAL_ROWS // child_rows
        right_rows = right_basis[tree_level].astype(jnp.float32).reshape(children, child_rows, RANK_WIDTH)
        projection = jnp.einsum("cmk,cmr->ckr", right_rows, current.reshape(children, child_rows, TARGETS),
                                precision=HIGHEST)
        picked = projection[:, rank_perm[tree_level], :]
        offset = NODE_COUNT + 1 - (NODE_COUNT + 1) // 2 ** tree_level
        node_inverse = joined[offset:offset + children // 2]
        stacked = picked.reshape(children // 2, 2 * RANK_WIDTH, TARGETS)
        coefficient = jnp.einsum("nij,njr->nir", node_inverse, stacked,
                                 precision=HIGHEST).reshape(children, RANK_WIDTH, TARGETS)
        left_rows = left_basis[tree_level].astype(jnp.float32).reshape(children, child_rows, RANK_WIDTH)
        update = jnp.einsum("cmk,ckr->cmr", left_rows, coefficient, precision=HIGHEST)
        current = current - update.reshape(TOTAL_ROWS, TARGETS)
    return current
```

```python
import functools

import jax
import jax.numpy as jnp
from jax import lax
from jax.experimental import pallas as pl
from jax.experimental.pallas import tpu as pltpu
from jax.sharding import PartitionSpec as P

HIGHEST = lax.Precision.HIGHEST
MIB = 1 << 20


def dot(a, b, contract, exact=False):
    return lax.dot_general(
        a, b, ((contract[:1], contract[1:]), ((), ())),
        precision=HIGHEST if exact else None, preferred_element_type=jnp.float32,
    )


def halves(value):
    high_part = value.astype(jnp.bfloat16)
    low_part = (value - high_part.astype(jnp.float32)).astype(jnp.bfloat16)
    return high_part, low_part


def blocks_per_step(nblocks, most):
    return max(size for size in range(1, most + 1) if nblocks % size == 0)


def gram_kernel(levels, right_ref, left_ref, gram_ref):
    @pl.when(pl.program_id(0) == 0)
    def _():
        gram_ref[...] = jnp.zeros_like(gram_ref)

    right = jnp.concatenate([right_ref[l] for l in range(1, levels)], axis=1)
    left = jnp.concatenate([left_ref[l] for l in range(levels - 1)], axis=1)
    gram_ref[...] += dot(right, left, (0, 0))


def project_kernel(levels, per_step, width, order_ref, inv_ref, right_ref, rhs_ref,
                   moved_ref, out_ref, factor_ref, total_ref):
    step = pl.program_id(0)
    rank = right_ref.shape[2]
    kinds = levels * rank
    place = lax.broadcasted_iota(jnp.int32, (width, width), 0)
    for b in range(per_step):
        order = order_ref[pl.ds(step * per_step + b, 1), :]
        chosen = (place == order).astype(jnp.float32).astype(jnp.bfloat16)
        moved = dot(inv_ref[b], chosen, (1, 1)).astype(jnp.bfloat16)
        moved_ref[b] = moved
        rows = pl.ds(b * width, width)
        right = jnp.concatenate([right_ref[l, rows, :] for l in range(levels)], axis=1)
        high_part, low_part = halves(dot(right, moved, (0, 0)))
        factor_ref[:kinds, rows] = high_part
        factor_ref[kinds:, rows] = low_part
    term = dot(factor_ref[...], rhs_ref[...], (1, 0))

    @pl.when(step == 0)
    def _():
        total_ref[...] = term

    @pl.when(step > 0)
    def _():
        total_ref[...] += term

    @pl.when(step == pl.num_programs(0) - 1)
    def _():
        out_ref[...] = (total_ref[:kinds] + total_ref[kinds:]).T


def picker(perm_ref, level, rank):
    spot = lax.broadcasted_iota(jnp.int32, (rank, rank), 0)
    return (spot == perm_ref[level:level + 1, :]).astype(jnp.float32)


def node_kernel(levels, parts_ref, gram_ref, joined_ref, perm_ref, coef_ref, rest_ref):
    count, share, _ = parts_ref.shape
    rank = perm_ref.shape[1]
    half = count // 2
    low_sum = sum(parts_ref[s] for s in range(half))
    high_sum = sum(parts_ref[s] for s in range(half, count))
    own = jnp.concatenate([low_sum[:, :rank], high_sum[:, :rank]], axis=0)
    picked = dot(own, picker(perm_ref, 0, rank), (1, 0), True)
    picked = jnp.concatenate([picked[:share], picked[share:]], axis=1)
    coef = dot(picked, joined_ref[...], (1, 1), True)
    rest = low_sum[:, rank:] + high_sum[:, rank:]
    size = (levels - 1) * rank
    for side in range(2):
        part = coef[:, side * rank:(side + 1) * rank]
        coef_ref[side] = part
        gram = gram_ref[:, side, :, :rank].reshape(size, rank)
        rest = rest - dot(part, gram, (1, 1), True)
    rest_ref[...] = rest


def tree_kernel(levels, rest_ref, gram_ref, coef_ref, joined_ref, perm_ref, leaf_ref, out_ref):
    leaves, share, _ = rest_ref.shape
    count = out_ref.shape[0]
    rank = perm_ref.shape[1]
    leaf = leaf_ref[0]
    own = []
    found = {}
    for level in range(1, levels):
        span = 2 ** (level - 1)
        children = leaves // span
        totals = []
        for child in range(children):
            total = 0.0
            for member in range(child * span, (child + 1) * span):
                total = total + rest_ref[member, :, (level - 1) * rank:level * rank]
                for below in range(1, level):
                    gram = gram_ref[member, (level - 2) * rank:(level - 1) * rank,
                                    (below - 1) * rank:below * rank]
                    total = total - dot(found[below, member // 2 ** (below - 1)], gram, (1, 1), True)
            totals.append(total)
        picked = dot(jnp.concatenate(totals, axis=0), picker(perm_ref, level, rank), (1, 0), True)
        offset = 2 * leaves - 2 * leaves // 2 ** level
        chosen = jnp.zeros((share, rank), jnp.float32)
        for node in range(children // 2):
            pair = jnp.concatenate(
                [picked[(2 * node + side) * share:(2 * node + side + 1) * share] for side in range(2)],
                axis=1)
            coef = dot(pair, joined_ref[offset + node], (1, 1), True)
            for side in range(2):
                part = coef[:, side * rank:(side + 1) * rank]
                found[level, 2 * node + side] = part
                chosen = jnp.where(leaf // span == 2 * node + side, part, chosen)
        own.append(chosen)
    for target in range(count):
        out_ref[target] = jnp.concatenate([coef_ref[target // (count // 2)]] + own, axis=1)


def expand_kernel(levels, per_step, width, coef_ref, moved_ref, rhs_ref, left_ref, out_ref, factor_ref):
    kinds = coef_ref.shape[1]

    @pl.when(pl.program_id(0) == 0)
    def _():
        high_part, low_part = halves(coef_ref[...].T)
        factor_ref[:kinds, :] = high_part
        factor_ref[kinds:, :] = low_part

    for b in range(per_step):
        rows = pl.ds(b * width, width)
        left = jnp.concatenate([left_ref[l, rows, :] for l in range(levels)] * 2, axis=1)
        out_ref[rows, :] = dot(moved_ref[b], rhs_ref[rows, :], (1, 0)) - dot(left, factor_ref[...], (1, 0))


def whole(shape):
    return pl.BlockSpec(shape, lambda *_: (0,) * len(shape))


def params(mib):
    return pltpu.CompilerParams(vmem_limit_bytes=mib * MIB)


def per_device(rhs, leaf_order, leaf_inv, right_basis, left_basis, rank_perm, joined):
    levels, rows, rank = right_basis.shape
    nblocks, width, _ = leaf_inv.shape
    columns = rhs.shape[1]
    leaves = lax.axis_size("leaf")
    count = lax.axis_size("rows")
    leaf = lax.axis_index("leaf")
    kinds = levels * rank
    size = kinds - rank
    share = columns // count

    per_step = blocks_per_step(nblocks, 6)
    steps = nblocks // per_step
    tile = per_step * width
    gram = pl.pallas_call(
        functools.partial(gram_kernel, levels),
        grid=(steps,),
        in_specs=[pl.BlockSpec((levels, tile, rank), lambda i: (0, i, 0))] * 2,
        out_specs=whole((size, size)),
        out_shape=jax.ShapeDtypeStruct((size, size), jnp.float32),
        compiler_params=params(32),
        name="gram",
    )(right_basis, left_basis)

    per_step = blocks_per_step(nblocks, 3)
    steps = nblocks // per_step
    tile = per_step * width
    moved, partial_value = pl.pallas_call(
        functools.partial(project_kernel, levels, per_step, width),
        grid=(steps,),
        in_specs=[
            whole((nblocks, width)),
            pl.BlockSpec((per_step, width, width), lambda i: (i, 0, 0)),
            pl.BlockSpec((levels, tile, rank), lambda i: (0, i, 0)),
            pl.BlockSpec((tile, columns), lambda i: (i, 0)),
        ],
        out_specs=[
            pl.BlockSpec((per_step, width, width), lambda i: (i, 0, 0)),
            whole((columns, kinds)),
        ],
        out_shape=[
            jax.ShapeDtypeStruct((nblocks, width, width), jnp.bfloat16),
            jax.ShapeDtypeStruct((columns, kinds), jnp.float32),
        ],
        scratch_shapes=[
            pltpu.VMEM((2 * kinds, tile), jnp.bfloat16),
            pltpu.VMEM((2 * kinds, columns), jnp.float32),
        ],
        compiler_params=params(32),
        name="project",
    )(leaf_order, leaf_inv, right_basis, rhs)

    gram_rows = size // count
    gram_parts = lax.all_to_all(gram, "rows", 0, 0, tiled=True).reshape(2, count // 2, gram_rows, size)
    gram_all = lax.all_gather(gram_parts.sum(1), "rows", axis=0)
    deeper = size - rank
    gram_leaf = (gram_all[:, 0] + gram_all[:, 1]).reshape(size, size)[rank:, rank:]
    gram_leaves = lax.all_gather(gram_leaf, "leaf", axis=0)

    parts = lax.all_to_all(partial_value, "rows", 0, 0, tiled=True).reshape(count, share, kinds)
    coef, rest = pl.pallas_call(
        functools.partial(node_kernel, levels),
        out_shape=[
            jax.ShapeDtypeStruct((2, share, rank), jnp.float32),
            jax.ShapeDtypeStruct((share, size), jnp.float32),
        ],
        compiler_params=params(16),
        name="node",
    )(parts, gram_all, lax.dynamic_index_in_dim(joined, leaf, 0, keepdims=False), rank_perm)

    rest_all = lax.all_gather(rest, "leaf", axis=0)
    coef_out = pl.pallas_call(
        functools.partial(tree_kernel, levels),
        in_specs=[pl.BlockSpec()] * 5 + [pl.BlockSpec(memory_space=pltpu.SMEM)],
        out_shape=jax.ShapeDtypeStruct((count, share, kinds), jnp.float32),
        compiler_params=params(24),
        name="tree",
    )(rest_all, gram_leaves, coef, joined, rank_perm, leaf.reshape(1).astype(jnp.int32))
    coef_all = lax.all_to_all(coef_out, "rows", 0, 0, tiled=True).reshape(columns, kinds)

    return pl.pallas_call(
        functools.partial(expand_kernel, levels, per_step, width),
        grid=(steps,),
        in_specs=[
            whole((columns, kinds)),
            pl.BlockSpec((per_step, width, width), lambda i: (i, 0, 0)),
            pl.BlockSpec((tile, columns), lambda i: (i, 0)),
            pl.BlockSpec((levels, tile, rank), lambda i: (0, i, 0)),
        ],
        out_specs=pl.BlockSpec((tile, columns), lambda i: (i, 0)),
        out_shape=jax.ShapeDtypeStruct((rows, columns), jnp.float32),
        scratch_shapes=[pltpu.VMEM((2 * kinds, columns), jnp.bfloat16)],
        compiler_params=params(32),
        name="expand",
    )(coef_all, moved, rhs, left_basis)


def solution(mesh):
    return jax.shard_map(
        per_device,
        mesh=mesh,
        in_specs=(
            P(("leaf", "rows"), None),
            P(("leaf", "rows"), None),
            P(("leaf", "rows"), None, None),
            P(None, ("leaf", "rows"), None),
            P(None, ("leaf", "rows"), None),
            P(),
            P(),
        ),
        out_specs=P(("leaf", "rows"), None),
        check_vma=False,
    )
```

```python
import functools

import jax
import jax.numpy as jnp
from jax import lax
from jax.experimental import pallas as pl
from jax.experimental.pallas import tpu as pltpu
from jax.sharding import PartitionSpec as P

HIGHEST = lax.Precision.HIGHEST
MIB = 1 << 20
BOTH = ("leaf", "rows")


def dot(a, b, contract, exact=False):
    return lax.dot_general(
        a, b, ((contract[:1], contract[1:]), ((), ())),
        precision=HIGHEST if exact else None, preferred_element_type=jnp.float32,
    )


def halves(value):
    high_part = value.astype(jnp.bfloat16)
    low_part = (value - high_part.astype(jnp.float32)).astype(jnp.bfloat16)
    return high_part, low_part


def swap(value, axis, mask):
    count = lax.axis_size(axis)
    return lax.ppermute(value, axis, [(i, i ^ mask) for i in range(count)])


def blocks_per_step(nblocks, most):
    return max(size for size in range(1, most + 1) if nblocks % size == 0)


def below_pairs(levels, first=0):
    return [(level, below) for level in range(levels) for below in range(first, level)]


def gram_kernel(levels, right_ref, left_ref, keep_ref, send_ref, gram_ref):
    step = pl.program_id(0)
    rank = right_ref.shape[2]
    half = rank // 2

    @pl.when(step == 0)
    def _():
        gram_ref[...] = jnp.zeros_like(gram_ref)

    right = jnp.concatenate([right_ref[l] for l in range(1, levels)], axis=1)
    left = jnp.concatenate([left_ref[l] for l in range(levels - 1)], axis=1)
    gram_ref[...] += dot(right, left, (0, 0))

    @pl.when(step == pl.num_programs(0) - 1)
    def _():
        core = lax.axis_index("rows") % 2
        for spot, (level, below) in enumerate(below_pairs(levels)):
            lanes = pl.ds(spot * rank, rank)
            for ref, side in ((keep_ref, core), (send_ref, 1 - core)):
                rows = pl.ds(pl.multiple_of((level - 1) * rank + side * half, half), half)
                ref[:, lanes] = gram_ref[rows, pl.ds(below * rank, rank)]


def project_kernel(levels, per_step, width, order_ref, inv_ref, right_ref, rhs_ref,
                   moved_ref, keep_ref, send_ref, factor_ref, total_ref, flip_ref):
    step = pl.program_id(0)
    rank = right_ref.shape[2]
    kinds = levels * rank
    place = lax.broadcasted_iota(jnp.int32, (width, width), 0)
    for b in range(per_step):
        order = order_ref[pl.ds(step * per_step + b, 1), :]
        chosen = (place == order).astype(jnp.float32).astype(jnp.bfloat16)
        moved = dot(inv_ref[b], chosen, (1, 1)).astype(jnp.bfloat16)
        moved_ref[b] = moved
        rows = pl.ds(b * width, width)
        right = jnp.concatenate([right_ref[l, rows, :] for l in range(levels)], axis=1)
        high_part, low_part = halves(dot(right, moved, (0, 0)))
        factor_ref[:kinds, rows] = high_part
        factor_ref[kinds:, rows] = low_part
    term = dot(factor_ref[...], rhs_ref[...], (1, 0))

    @pl.when(step == 0)
    def _():
        total_ref[...] = term

    @pl.when(step > 0)
    def _():
        total_ref[...] += term

    @pl.when(step == pl.num_programs(0) - 1)
    def _():
        flip_ref[...] = (total_ref[:kinds] + total_ref[kinds:]).T
        me = lax.axis_index("rows")
        slots, share, _ = keep_ref.shape
        for slot in range(slots):
            for ref, owner in ((keep_ref, me ^ (2 * slot)), (send_ref, me ^ (2 * slot + 1))):
                ref[slot] = flip_ref[pl.ds(pl.multiple_of(owner * share, share), share), :]


def merge_kernel(keep_ref, got_ref, *out_refs):
    for slot, out_ref in enumerate(out_refs):
        out_ref[...] = keep_ref[slot] + got_ref[slot]


def prepare_kernel(index_ref, joined_ref, perm_ref, out_ref):
    rank = perm_ref.shape[1]
    spot = lax.broadcasted_iota(jnp.int32, (rank, rank), 0)
    chosen = (spot == perm_ref[pl.ds(pl.program_id(0), 1), :]).astype(jnp.float32)
    for side in range(2):
        lanes = pl.ds(side * rank, rank)
        out_ref[0, :, lanes] = dot(joined_ref[0, :, lanes], chosen, (1, 1), True)


def by_side(side, own, other):
    return jnp.where(side == 0, own, other), jnp.where(side == 0, other, own)


def pack_message(message_ref, pieces):
    row = 0
    for piece in pieces:
        message_ref[pl.ds(row, piece.shape[0]), :] = piece
        row += piece.shape[0]


def node_kernel(levels, rank, slots, *refs):
    part_refs = refs[:slots]
    gram_refs = refs[slots:slots + 4]
    joined_ref, own_ref, other_ref, message_ref = refs[slots + 4:]
    me = lax.axis_index("rows")
    core, side = me % 2, me // slots
    half = slots // 2
    sums = [sum(ref[...] for ref in part_refs[:half]), sum(ref[...] for ref in part_refs[half:])]
    picked = jnp.concatenate(by_side(side, sums[0][:, :rank], sums[1][:, :rank]), axis=1)
    coef = dot(picked, joined_ref[0], (1, 1), True)
    sides = by_side(side, coef[:, :rank], coef[:, rank:])
    own_ref[...] = sides[0]
    other_ref[...] = sides[1]
    mine, theirs, pair_mine, pair_theirs = (ref[...] for ref in gram_refs)
    grams = [jnp.concatenate(by_side(core, mine, pair_mine), axis=0),
             jnp.concatenate(by_side(core, theirs, pair_theirs), axis=0)]
    rest = sums[0] + sums[1]
    pairs = below_pairs(levels)
    spots = [spot for spot, (_, below) in enumerate(pairs) if below == 0]
    pieces = []
    for level in range(1, levels):
        value = rest[:, level * rank:(level + 1) * rank]
        lanes = slice(spots[level - 1] * rank, (spots[level - 1] + 1) * rank)
        for part, gram in zip(sides, grams):
            value = value - dot(part, gram[:, lanes], (1, 1), True)
        pieces.append(value)
    for spot, (_, below) in enumerate(pairs):
        if below > 0:
            lanes = slice(spot * rank, (spot + 1) * rank)
            pieces.append(grams[0][:, lanes] + grams[1][:, lanes])
    pack_message(message_ref, pieces)


def level_kernel(levels, level, share, sent_ref, got_ref, joined_ref, coef_ref, *message_ref):
    rank = sent_ref.shape[1]
    side = lax.axis_index("leaf") // 2 ** (level - 1) % 2
    more = levels - level
    values = []
    for ref in (sent_ref, got_ref):
        values.append([ref[pl.ds(i * share, share), :] for i in range(more)])
    picked = jnp.concatenate(by_side(side, values[0][0], values[1][0]), axis=1)
    coef = dot(picked, joined_ref[level], (1, 1), True)
    sides = by_side(side, coef[:, :rank], coef[:, rank:])
    coef_ref[...] = sides[0]
    if not message_ref:
        return
    pairs = below_pairs(levels, level)
    grams = []
    for ref in (sent_ref, got_ref):
        grams.append({pair: ref[pl.ds(more * share + spot * rank, rank), :] for spot, pair in enumerate(pairs)})
    pieces = []
    for upper in range(level + 1, levels):
        value = values[0][upper - level] + values[1][upper - level]
        for part, gram in zip(sides, grams):
            value = value - dot(part, gram[upper, level], (1, 1), True)
        pieces.append(value)
    for pair in pairs:
        if pair[1] > level:
            pieces.append(grams[0][pair] + grams[1][pair])
    pack_message(message_ref[0], pieces)


def pack_kernel(*refs):
    levels = len(refs) - 3
    other_ref, own_refs, own_out, other_out = refs[0], refs[1:-2], refs[-2], refs[-1]
    own = [ref[...] for ref in own_refs]
    own_out[...] = jnp.concatenate(own, axis=1)
    other_out[...] = jnp.concatenate([other_ref[...]] + own[1:], axis=1)


def expand_kernel(levels, per_step, width, slots, *refs):
    piece_refs = refs[:2 * slots]
    moved_ref, rhs_ref, left_ref, out_ref, flip_ref, factor_ref = refs[2 * slots:]
    share, kinds = piece_refs[0].shape

    @pl.when(pl.program_id(0) == 0)
    def _():
        me = lax.axis_index("rows")
        for slot in range(2 * slots):
            owner = me ^ slot
            flip_ref[pl.ds(pl.multiple_of(owner * share, share), share), :] = piece_refs[slot][...]
        high_part, low_part = halves(flip_ref[...].T)
        factor_ref[:kinds, :] = high_part
        factor_ref[kinds:, :] = low_part

    for b in range(per_step):
        rows = pl.ds(b * width, width)
        left = jnp.concatenate([left_ref[l, rows, :] for l in range(levels)] * 2, axis=1)
        out_ref[rows, :] = dot(moved_ref[b], rhs_ref[rows, :], (1, 0)) - dot(left, factor_ref[...], (1, 0))


def whole(shape):
    return pl.BlockSpec(shape, lambda *_: (0,) * len(shape))


def params(mib):
    return pltpu.CompilerParams(vmem_limit_bytes=mib * MIB)


def floats(*shape):
    return jax.ShapeDtypeStruct(shape, jnp.float32)


def per_device(rhs, leaf_order, leaf_inv, right_basis, left_basis, rank_perm, joined):
    levels, rows, rank = right_basis.shape
    nblocks, width, _ = leaf_inv.shape
    columns = rhs.shape[1]
    leaves = lax.axis_size("leaf")
    count = lax.axis_size("rows")
    leaf = lax.axis_index("leaf")
    slots = count // 2
    kinds = levels * rank
    size = kinds - rank
    share = columns // count
    gram_lanes = len(below_pairs(levels)) * rank

    per_step = blocks_per_step(nblocks, 6)
    steps = nblocks // per_step
    tile = per_step * width
    gram_keep, gram_send = pl.pallas_call(
        functools.partial(gram_kernel, levels),
        grid=(steps,),
        in_specs=[pl.BlockSpec((levels, tile, rank), lambda i: (0, i, 0))] * 2,
        out_specs=[whole((rank // 2, gram_lanes))] * 2,
        out_shape=[floats(rank // 2, gram_lanes)] * 2,
        scratch_shapes=[pltpu.VMEM((size, size), jnp.float32)],
        compiler_params=params(56),
        name="gram",
    )(right_basis, left_basis)

    gram_got = swap(gram_send, "rows", 1)

    per_step = blocks_per_step(nblocks, 3)
    steps = nblocks // per_step
    tile = per_step * width
    moved, keep, send = pl.pallas_call(
        functools.partial(project_kernel, levels, per_step, width),
        grid=(steps,),
        in_specs=[
            whole((nblocks, width)),
            pl.BlockSpec((per_step, width, width), lambda i: (i, 0, 0)),
            pl.BlockSpec((levels, tile, rank), lambda i: (0, i, 0)),
            pl.BlockSpec((tile, columns), lambda i: (i, 0)),
        ],
        out_specs=[pl.BlockSpec((per_step, width, width), lambda i: (i, 0, 0))]
        + [whole((slots, share, kinds))] * 2,
        out_shape=[jax.ShapeDtypeStruct((nblocks, width, width), jnp.bfloat16)]
        + [floats(slots, share, kinds)] * 2,
        scratch_shapes=[
            pltpu.VMEM((2 * kinds, tile), jnp.bfloat16),
            pltpu.VMEM((2 * kinds, columns), jnp.float32),
            pltpu.VMEM((columns, kinds), jnp.float32),
        ],
        compiler_params=params(56),
        name="project",
    )(leaf_order, leaf_inv, right_basis, rhs)

    got = swap(send, "rows", 1)
    merged = pl.pallas_call(
        merge_kernel, out_shape=[floats(share, kinds)] * slots, compiler_params=params(8), name="merge",
    )(keep, got)
    parts = [merged[0]] + [swap(merged[s], "rows", 2 * s) for s in range(1, slots)]

    gram = gram_keep + gram_got
    mask = 2
    while mask < slots:
        gram = gram + swap(gram, "rows", mask)
        mask *= 2
    gram_other = swap(gram, "rows", slots)
    grams = [gram, gram_other, swap(gram, "rows", 1), swap(gram_other, "rows", 1)]

    index = jnp.stack([2 * leaves - 2 * leaves // 2 ** l + leaf // 2 ** l for l in range(levels)])
    prepared = pl.pallas_call(
        prepare_kernel,
        grid_spec=pltpu.PrefetchScalarGridSpec(
            num_scalar_prefetch=1,
            grid=(levels,),
            in_specs=[
                pl.BlockSpec((1, 2 * rank, 2 * rank), lambda i, index: (index[i], 0, 0)),
                pl.BlockSpec((levels, rank), lambda i, index: (0, 0)),
            ],
            out_specs=pl.BlockSpec((1, 2 * rank, 2 * rank), lambda i, index: (i, 0, 0)),
        ),
        out_shape=floats(levels, 2 * rank, 2 * rank),
        compiler_params=params(8),
        name="prepare",
    )(index.astype(jnp.int32), joined, rank_perm)

    def message_shape(level):
        return floats((levels - level) * share + len(below_pairs(levels, level)) * rank, rank)

    own, other, message = pl.pallas_call(
        functools.partial(node_kernel, levels, rank, slots),
        out_shape=[floats(share, rank)] * 2 + [message_shape(1)],
        compiler_params=params(8),
        name="node",
    )(*parts, *grams, prepared)
    coefs = [own]
    for level in range(1, levels):
        last = level + 1 == levels
        arrived = swap(message, "leaf", 2 ** (level - 1))
        outs = pl.pallas_call(
            functools.partial(level_kernel, levels, level, share),
            out_shape=[floats(share, rank)] + ([] if last else [message_shape(level + 1)]),
            compiler_params=params(8),
            name=f"level{level}",
        )(message, arrived, prepared)
        coefs.append(outs[0])
        message = outs[-1]
    own_pack, other_pack = pl.pallas_call(
        pack_kernel, out_shape=[floats(share, kinds)] * 2, compiler_params=params(8), name="pack",
    )(other, *coefs)

    pieces = []
    for slot in range(slots):
        piece = own_pack if slot < slots // 2 else other_pack
        piece = swap(piece, "rows", 2 * slot) if slot > 0 else piece
        pieces += [piece, swap(piece, "rows", 1)]

    return pl.pallas_call(
        functools.partial(expand_kernel, levels, per_step, width, slots),
        grid=(steps,),
        in_specs=[whole((share, kinds))] * count + [
            pl.BlockSpec((per_step, width, width), lambda i: (i, 0, 0)),
            pl.BlockSpec((tile, columns), lambda i: (i, 0)),
            pl.BlockSpec((levels, tile, rank), lambda i: (0, i, 0)),
        ],
        out_specs=pl.BlockSpec((tile, columns), lambda i: (i, 0)),
        out_shape=floats(rows, columns),
        scratch_shapes=[
            pltpu.VMEM((columns, kinds), jnp.float32),
            pltpu.VMEM((2 * kinds, columns), jnp.bfloat16),
        ],
        compiler_params=params(24),
        name="expand",
    )(*pieces, moved, rhs, left_basis)


def solution(mesh):
    return jax.shard_map(
        per_device,
        mesh=mesh,
        in_specs=(
            P(("leaf", "rows"), None),
            P(("leaf", "rows"), None),
            P(("leaf", "rows"), None, None),
            P(None, ("leaf", "rows"), None),
            P(None, ("leaf", "rows"), None),
            P(),
            P(),
        ),
        out_specs=P(("leaf", "rows"), None),
        check_vma=False,
    )
```

```python
import functools

import jax
import jax.numpy as jnp
from jax import lax
from jax.experimental import pallas as pl
from jax.experimental.pallas import tpu as pltpu
from jax.sharding import PartitionSpec as P

HIGHEST = lax.Precision.HIGHEST
MIB = 1 << 20
BOTH = ("leaf", "rows")


def dot(a, b, contract, exact=False):
    return lax.dot_general(
        a, b, ((contract[:1], contract[1:]), ((), ())),
        precision=HIGHEST if exact else None, preferred_element_type=jnp.float32,
    )


def halves(value):
    high_part = value.astype(jnp.bfloat16)
    low_part = (value - high_part.astype(jnp.float32)).astype(jnp.bfloat16)
    return high_part, low_part


def swap(value, axis, mask):
    count = lax.axis_size(axis)
    return lax.ppermute(value, axis, [(i, i ^ mask) for i in range(count)])


def blocks_per_step(nblocks, most):
    return max(size for size in range(1, most + 1) if nblocks % size == 0)


def below_pairs(levels, first=0):
    return [(level, below) for level in range(levels) for below in range(first, level)]


def factor_kernel(levels, per_step, width, order_ref, inv_ref, right_ref, left_ref,
                  factor_ref, moved_ref, keep_ref, send_ref,
                  inv_buf, right_buf, left_buf, gram_ref, sems):
    rank = right_ref.shape[2]
    kinds = levels * rank
    half = rank // 2
    tile = per_step * width
    steps = inv_ref.shape[0] // per_step

    def copies(step):
        rows = pl.ds(pl.multiple_of(step * tile, tile), tile)
        blocks = pl.ds(step * per_step, per_step)
        return (
            pltpu.make_async_copy(right_ref.at[:, rows], right_buf.at[:, rows], sems.at[0, step]),
            pltpu.make_async_copy(inv_ref.at[blocks], inv_buf.at[blocks], sems.at[1, step]),
            pltpu.make_async_copy(left_ref.at[:levels - 1, rows], left_buf.at[:, rows], sems.at[2, step]),
        )

    for step in range(steps):
        for copy in copies(step):
            copy.start()
    gram_ref[...] = jnp.zeros_like(gram_ref)
    place = lax.broadcasted_iota(jnp.int32, (width, width), 0)

    def body(step, _):
        for copy in copies(step):
            copy.wait()
        rows = pl.ds(pl.multiple_of(step * tile, tile), tile)
        right = jnp.concatenate([right_buf[l, rows, :] for l in range(levels)], axis=1).T
        left = jnp.concatenate([left_buf[l, rows, :] for l in range(levels - 1)], axis=1)
        gram_ref[...] += dot(right[rank:], left, (1, 0))
        for b in range(per_step):
            block = step * per_step + b
            chosen = (place == order_ref[pl.ds(block, 1), :]).astype(jnp.float32).astype(jnp.bfloat16)
            moved = dot(inv_buf[block], chosen, (1, 1)).astype(jnp.bfloat16)
            moved_ref[block] = moved
            lanes = pl.ds(pl.multiple_of(block * width, width), width)
            high_part, low_part = halves(dot(right[:, b * width:(b + 1) * width], moved, (1, 0)))
            factor_ref[:kinds, lanes] = high_part
            factor_ref[kinds:, lanes] = low_part
        return 0

    lax.fori_loop(0, steps, body, 0)
    core = lax.axis_index("rows") % 2
    for spot, (level, below) in enumerate(below_pairs(levels)):
        lanes = pl.ds(spot * rank, rank)
        for ref, side in ((keep_ref, core), (send_ref, 1 - core)):
            rows = pl.ds(pl.multiple_of((level - 1) * rank + side * half, half), half)
            ref[:, lanes] = gram_ref[rows, pl.ds(below * rank, rank)]


def project_kernel(factor_ref, rhs_ref, keep_ref, send_ref, flip_ref):
    kinds = factor_ref.shape[0] // 2
    columns = rhs_ref.shape[1]
    part = min(256, columns)
    for begin in range(0, columns, part):
        total = dot(factor_ref[...], rhs_ref[:, begin:begin + part], (1, 0))
        flip_ref[begin:begin + part, :] = (total[:kinds] + total[kinds:]).T
    me = lax.axis_index("rows")
    slots, share, _ = keep_ref.shape
    for slot in range(slots):
        for ref, owner in ((keep_ref, me ^ (2 * slot)), (send_ref, me ^ (2 * slot + 1))):
            ref[slot] = flip_ref[pl.ds(pl.multiple_of(owner * share, share), share), :]


def merge_kernel(keep_ref, got_ref, *out_refs):
    for slot, out_ref in enumerate(out_refs):
        out_ref[...] = keep_ref[slot] + got_ref[slot]


def prepare_kernel(index_ref, joined_ref, perm_ref, out_ref):
    rank = perm_ref.shape[1]
    spot = lax.broadcasted_iota(jnp.int32, (rank, rank), 0)
    chosen = (spot == perm_ref[pl.ds(pl.program_id(0), 1), :]).astype(jnp.float32)
    for side in range(2):
        lanes = pl.ds(side * rank, rank)
        out_ref[0, :, lanes] = dot(joined_ref[0, :, lanes], chosen, (1, 1), True)


def by_side(side, own, other):
    return jnp.where(side == 0, own, other), jnp.where(side == 0, other, own)


def pack_message(message_ref, pieces):
    row = 0
    for piece in pieces:
        message_ref[pl.ds(row, piece.shape[0]), :] = piece
        row += piece.shape[0]


def node_kernel(levels, rank, slots, *refs):
    part_refs = refs[:slots]
    gram_refs = refs[slots:slots + 4]
    joined_ref, own_ref, other_ref, message_ref = refs[slots + 4:]
    me = lax.axis_index("rows")
    core, side = me % 2, me // slots
    half = slots // 2
    sums = [sum(ref[...] for ref in part_refs[:half]), sum(ref[...] for ref in part_refs[half:])]
    picked = jnp.concatenate(by_side(side, sums[0][:, :rank], sums[1][:, :rank]), axis=1)
    coef = dot(picked, joined_ref[0], (1, 1), True)
    sides = by_side(side, coef[:, :rank], coef[:, rank:])
    own_ref[...] = sides[0]
    other_ref[...] = sides[1]
    mine, theirs, pair_mine, pair_theirs = (ref[...] for ref in gram_refs)
    grams = [jnp.concatenate(by_side(core, mine, pair_mine), axis=0),
             jnp.concatenate(by_side(core, theirs, pair_theirs), axis=0)]
    rest = sums[0] + sums[1]
    pairs = below_pairs(levels)
    spots = [spot for spot, (_, below) in enumerate(pairs) if below == 0]
    pieces = []
    for level in range(1, levels):
        value = rest[:, level * rank:(level + 1) * rank]
        lanes = slice(spots[level - 1] * rank, (spots[level - 1] + 1) * rank)
        for part, gram in zip(sides, grams):
            value = value - dot(part, gram[:, lanes], (1, 1), True)
        pieces.append(value)
    for spot, (_, below) in enumerate(pairs):
        if below > 0:
            lanes = slice(spot * rank, (spot + 1) * rank)
            pieces.append(grams[0][:, lanes] + grams[1][:, lanes])
    pack_message(message_ref, pieces)


def level_kernel(levels, level, share, sent_ref, got_ref, joined_ref, coef_ref, *message_ref):
    rank = sent_ref.shape[1]
    side = lax.axis_index("leaf") // 2 ** (level - 1) % 2
    more = levels - level
    values = []
    for ref in (sent_ref, got_ref):
        values.append([ref[pl.ds(i * share, share), :] for i in range(more)])
    picked = jnp.concatenate(by_side(side, values[0][0], values[1][0]), axis=1)
    coef = dot(picked, joined_ref[level], (1, 1), True)
    sides = by_side(side, coef[:, :rank], coef[:, rank:])
    coef_ref[...] = sides[0]
    if not message_ref:
        return
    pairs = below_pairs(levels, level)
    grams = []
    for ref in (sent_ref, got_ref):
        grams.append({pair: ref[pl.ds(more * share + spot * rank, rank), :] for spot, pair in enumerate(pairs)})
    pieces = []
    for upper in range(level + 1, levels):
        value = values[0][upper - level] + values[1][upper - level]
        for part, gram in zip(sides, grams):
            value = value - dot(part, gram[upper, level], (1, 1), True)
        pieces.append(value)
    for pair in pairs:
        if pair[1] > level:
            pieces.append(grams[0][pair] + grams[1][pair])
    pack_message(message_ref[0], pieces)


def pack_kernel(*refs):
    levels = len(refs) - 3
    other_ref, own_refs, own_out, other_out = refs[0], refs[1:-2], refs[-2], refs[-1]
    own = [ref[...] for ref in own_refs]
    own_out[...] = jnp.concatenate(own, axis=1)
    other_out[...] = jnp.concatenate([other_ref[...]] + own[1:], axis=1)


def expand_kernel(levels, per_step, width, slots, *refs):
    piece_refs = refs[:2 * slots]
    moved_ref, rhs_ref, left_ref, out_ref, flip_ref, factor_ref, out_buf, sems = refs[2 * slots:]
    share, kinds = piece_refs[0].shape
    tile = per_step * width
    steps = moved_ref.shape[0] // per_step
    me = lax.axis_index("rows")
    for slot in range(2 * slots):
        owner = me ^ slot
        flip_ref[pl.ds(pl.multiple_of(owner * share, share), share), :] = piece_refs[slot][...]
    high_part, low_part = halves(flip_ref[...].T)
    factor_ref[:kinds, :] = high_part
    factor_ref[kinds:, :] = low_part

    def copy(step):
        rows = pl.ds(pl.multiple_of(step * tile, tile), tile)
        return pltpu.make_async_copy(out_buf.at[rows], out_ref.at[rows], sems.at[step])

    def body(step, _):
        rows = pl.ds(pl.multiple_of(step * tile, tile), tile)
        left = jnp.concatenate([left_ref[l, rows, :] for l in range(levels)] * 2, axis=1)
        update = dot(left, factor_ref[...], (1, 0))
        for b in range(per_step):
            block = step * per_step + b
            rows = pl.ds(pl.multiple_of(block * width, width), width)
            first = dot(moved_ref[block], rhs_ref[rows, :], (1, 0))
            out_buf[rows, :] = first - update[b * width:(b + 1) * width]
        copy(step).start()
        return 0

    lax.fori_loop(0, steps, body, 0)
    for step in range(steps):
        copy(step).wait()


def whole(shape):
    return pl.BlockSpec(shape, lambda *_: (0,) * len(shape))


def params(mib):
    return pltpu.CompilerParams(vmem_limit_bytes=mib * MIB)


def floats(*shape):
    return jax.ShapeDtypeStruct(shape, jnp.float32)


def per_device(rhs, leaf_order, leaf_inv, right_basis, left_basis, rank_perm, joined):
    levels, rows, rank = right_basis.shape
    nblocks, width, _ = leaf_inv.shape
    columns = rhs.shape[1]
    leaves = lax.axis_size("leaf")
    count = lax.axis_size("rows")
    leaf = lax.axis_index("leaf")
    slots = count // 2
    kinds = levels * rank
    size = kinds - rank
    share = columns // count
    gram_lanes = len(below_pairs(levels)) * rank

    per_step = blocks_per_step(nblocks, 3)
    factors, moved, gram_keep, gram_send = pl.pallas_call(
        functools.partial(factor_kernel, levels, per_step, width),
        in_specs=[pl.BlockSpec()] + [pl.BlockSpec(memory_space=pl.ANY)] * 3,
        out_shape=[
            jax.ShapeDtypeStruct((2 * kinds, rows), jnp.bfloat16),
            jax.ShapeDtypeStruct((nblocks, width, width), jnp.bfloat16),
        ] + [floats(rank // 2, gram_lanes)] * 2,
        scratch_shapes=[
            pltpu.VMEM((nblocks, width, width), jnp.bfloat16),
            pltpu.VMEM((levels, rows, rank), jnp.bfloat16),
            pltpu.VMEM((levels - 1, rows, rank), jnp.bfloat16),
            pltpu.VMEM((size, size), jnp.float32),
            pltpu.SemaphoreType.DMA((3, nblocks // per_step)),
        ],
        compiler_params=params(32),
        name="factor",
    )(leaf_order, leaf_inv, right_basis, left_basis)

    gram_got = swap(gram_send, "rows", 1)

    keep, send = pl.pallas_call(
        project_kernel,
        out_shape=[floats(slots, share, kinds)] * 2,
        scratch_shapes=[pltpu.VMEM((columns, kinds), jnp.float32)],
        compiler_params=params(24),
        name="project",
    )(factors, rhs)

    got = swap(send, "rows", 1)
    merged = pl.pallas_call(
        merge_kernel, out_shape=[floats(share, kinds)] * slots, compiler_params=params(8), name="merge",
    )(keep, got)
    parts = [merged[0]] + [swap(merged[s], "rows", 2 * s) for s in range(1, slots)]

    gram = gram_keep + gram_got
    mask = 2
    while mask < slots:
        gram = gram + swap(gram, "rows", mask)
        mask *= 2
    gram_other = swap(gram, "rows", slots)
    grams = [gram, gram_other, swap(gram, "rows", 1), swap(gram_other, "rows", 1)]

    index = jnp.stack([2 * leaves - 2 * leaves // 2 ** l + leaf // 2 ** l for l in range(levels)])
    prepared = pl.pallas_call(
        prepare_kernel,
        grid_spec=pltpu.PrefetchScalarGridSpec(
            num_scalar_prefetch=1,
            grid=(levels,),
            in_specs=[
                pl.BlockSpec((1, 2 * rank, 2 * rank), lambda i, index: (index[i], 0, 0)),
                pl.BlockSpec((levels, rank), lambda i, index: (0, 0)),
            ],
            out_specs=pl.BlockSpec((1, 2 * rank, 2 * rank), lambda i, index: (i, 0, 0)),
        ),
        out_shape=floats(levels, 2 * rank, 2 * rank),
        compiler_params=params(8),
        name="prepare",
    )(index.astype(jnp.int32), joined, rank_perm)

    def message_shape(level):
        return floats((levels - level) * share + len(below_pairs(levels, level)) * rank, rank)

    own, other, message = pl.pallas_call(
        functools.partial(node_kernel, levels, rank, slots),
        out_shape=[floats(share, rank)] * 2 + [message_shape(1)],
        compiler_params=params(8),
        name="node",
    )(*parts, *grams, prepared)
    coefs = [own]
    for level in range(1, levels):
        last = level + 1 == levels
        arrived = swap(message, "leaf", 2 ** (level - 1))
        outs = pl.pallas_call(
            functools.partial(level_kernel, levels, level, share),
            out_shape=[floats(share, rank)] + ([] if last else [message_shape(level + 1)]),
            compiler_params=params(8),
            name=f"level{level}",
        )(message, arrived, prepared)
        coefs.append(outs[0])
        message = outs[-1]
    own_pack, other_pack = pl.pallas_call(
        pack_kernel, out_shape=[floats(share, kinds)] * 2, compiler_params=params(8), name="pack",
    )(other, *coefs)

    pieces = []
    for slot in range(slots):
        piece = own_pack if slot < slots // 2 else other_pack
        piece = swap(piece, "rows", 2 * slot) if slot > 0 else piece
        pieces += [piece, swap(piece, "rows", 1)]

    per_step = blocks_per_step(nblocks, 2)
    return pl.pallas_call(
        functools.partial(expand_kernel, levels, per_step, width, slots),
        out_specs=pl.BlockSpec(memory_space=pl.ANY),
        out_shape=floats(rows, columns),
        scratch_shapes=[
            pltpu.VMEM((columns, kinds), jnp.float32),
            pltpu.VMEM((2 * kinds, columns), jnp.bfloat16),
            pltpu.VMEM((rows, columns), jnp.float32),
            pltpu.SemaphoreType.DMA((nblocks // per_step,)),
        ],
        compiler_params=params(32),
        name="expand",
    )(*pieces, moved, rhs, left_basis)


def solution(mesh):
    return jax.shard_map(
        per_device,
        mesh=mesh,
        in_specs=(
            P(("leaf", "rows"), None),
            P(("leaf", "rows"), None),
            P(("leaf", "rows"), None, None),
            P(None, ("leaf", "rows"), None),
            P(None, ("leaf", "rows"), None),
            P(),
            P(),
        ),
        out_specs=P(("leaf", "rows"), None),
        check_vma=False,
    )
```

```python
import functools

import jax
import jax.numpy as jnp
from jax import lax
from jax.experimental import pallas as pl
from jax.experimental.pallas import tpu as pltpu
from jax.sharding import PartitionSpec as P

HIGHEST = lax.Precision.HIGHEST
MIB = 1 << 20


def dot(a, b, contract, exact=False):
    return lax.dot_general(
        a, b, ((contract[:1], contract[1:]), ((), ())),
        precision=HIGHEST if exact else None, preferred_element_type=jnp.float32,
    )


def halves(value):
    high_part = value.astype(jnp.bfloat16)
    low_part = (value - high_part.astype(jnp.float32)).astype(jnp.bfloat16)
    return high_part, low_part


def swap(value, axis, mask):
    count = lax.axis_size(axis)
    return lax.ppermute(value, axis, [(i, i ^ mask) for i in range(count)])


def blocks_per_step(nblocks, most):
    return max(size for size in range(1, most + 1) if nblocks % size == 0)


def below_pairs(levels, first=0):
    return [(level, below) for level in range(levels) for below in range(first, level)]


def gram_kernel(levels, per_step, width, right_ref, left_ref, flip_ref, keep_ref, send_ref,
                right_buf, left_buf, gram_ref, sems):
    rank = right_ref.shape[2]
    half = rank // 2
    tile = per_step * width
    steps = right_ref.shape[1] // tile

    def copies(step):
        rows = pl.ds(pl.multiple_of(step * tile, tile), tile)
        return (
            pltpu.make_async_copy(right_ref.at[:, rows], right_buf.at[:, rows], sems.at[0, step]),
            pltpu.make_async_copy(left_ref.at[:levels - 1, rows], left_buf.at[:, rows], sems.at[1, step]),
        )

    for step in range(steps):
        for copy in copies(step):
            copy.start()
    gram_ref[...] = jnp.zeros_like(gram_ref)

    def body(step, _):
        for copy in copies(step):
            copy.wait()
        rows = pl.ds(pl.multiple_of(step * tile, tile), tile)
        right = jnp.concatenate([right_buf[l, rows, :] for l in range(levels)], axis=1).T
        flip_ref[:, rows] = right
        left = jnp.concatenate([left_buf[l, rows, :] for l in range(levels - 1)], axis=1)
        gram_ref[...] += dot(right[rank:], left, (1, 0))
        return 0

    lax.fori_loop(0, steps, body, 0)
    core = lax.axis_index("rows") % 2
    for spot, (level, below) in enumerate(below_pairs(levels)):
        lanes = pl.ds(spot * rank, rank)
        for ref, side in ((keep_ref, core), (send_ref, 1 - core)):
            rows = pl.ds(pl.multiple_of((level - 1) * rank + side * half, half), half)
            ref[:, lanes] = gram_ref[rows, pl.ds(below * rank, rank)]


def factor_kernel(per_step, width, order_ref, inv_ref, flip_ref, factor_ref, moved_ref):
    kinds = flip_ref.shape[0]
    place = lax.broadcasted_iota(jnp.int32, (width, width), 0)

    def body(step, _):
        blocks = [step * per_step + b for b in range(per_step)]
        chosen = [(place == order_ref[pl.ds(block, 1), :]).astype(jnp.float32).astype(jnp.bfloat16)
                  for block in blocks]
        moved = [dot(inv_ref[block], pick, (1, 1)).astype(jnp.bfloat16) for block, pick in zip(blocks, chosen)]
        for block, inverse in zip(blocks, moved):
            moved_ref[block] = inverse
            lanes = pl.ds(pl.multiple_of(block * width, width), width)
            high_part, low_part = halves(dot(flip_ref[:, lanes], inverse, (1, 0)))
            factor_ref[:kinds, lanes] = high_part
            factor_ref[kinds:, lanes] = low_part
        return 0

    lax.fori_loop(0, inv_ref.shape[0] // per_step, body, 0)


def project_kernel(half, factor_ref, rhs_ref, *refs):
    kinds = factor_ref.shape[0] // 2
    keep_ref, send_ref, total_ref = refs[-3:]
    spots, share, _ = keep_ref.shape
    part = total_ref.shape[0]
    total = dot(factor_ref[...], rhs_ref[:, half * part:(half + 1) * part], (1, 0))
    total_ref[...] = (total[:kinds] + total[kinds:]).T
    core = lax.axis_index("rows") % 2
    for spot in range(spots):
        for ref, owner in ((keep_ref, 2 * spot + core), (send_ref, 2 * spot + 1 - core)):
            ref[spot] = total_ref[pl.ds(pl.multiple_of(owner * share, share), share), :]
    if len(refs) > 3:
        mine_ref, got_ref, gram_ref = refs[:-3][0], refs[:-3][1], refs[:-3][2]
        gram_ref[...] = mine_ref[...] + got_ref[...]


def merge_kernel(keep_a, got_a, keep_b, got_b, mine_ref, got_ref, gram_ref, *out_refs):
    chip = lax.axis_index("rows") // 2
    slots = len(out_refs)
    for slot, out_ref in enumerate(out_refs):
        owner = chip ^ slot
        spot = owner % (slots // 2)
        first = keep_a[spot] + got_a[spot]
        second = keep_b[spot] + got_b[spot]
        out_ref[...] = jnp.where(owner < slots // 2, first, second)
    gram_ref[...] = mine_ref[...] + got_ref[...]


def prepare_kernel(levels, joined_ref, perm_ref, out_ref, joined_buf, sems):
    rank = perm_ref.shape[1]
    leaves = lax.axis_size("leaf")
    leaf = lax.axis_index("leaf")
    copies = []
    for level in range(levels):
        node = 2 * leaves - 2 * leaves // 2 ** level + leaf // 2 ** level
        copies.append(pltpu.make_async_copy(joined_ref.at[node], joined_buf.at[level], sems.at[level]))
        copies[-1].start()
    spot = lax.broadcasted_iota(jnp.int32, (rank, rank), 0)
    for level in range(levels):
        copies[level].wait()
        chosen = (spot == perm_ref[level:level + 1, :]).astype(jnp.float32)
        for side in range(2):
            lanes = pl.ds(side * rank, rank)
            out_ref[level, :, lanes] = dot(joined_buf[level, :, lanes], chosen, (1, 1), True)


def by_side(side, own, other):
    return jnp.where(side == 0, own, other), jnp.where(side == 0, other, own)


def pack_message(message_ref, pieces):
    row = 0
    for piece in pieces:
        message_ref[pl.ds(row, piece.shape[0]), :] = piece
        row += piece.shape[0]


def node_kernel(rank, slots, *refs):
    part_refs = refs[:slots]
    joined_ref, own_ref, other_ref, rest_ref = refs[slots:]
    side = lax.axis_index("rows") // slots
    half = slots // 2
    sums = [sum(ref[...] for ref in part_refs[:half]), sum(ref[...] for ref in part_refs[half:])]
    picked = jnp.concatenate(by_side(side, sums[0][:, :rank], sums[1][:, :rank]), axis=1)
    coef = dot(picked, joined_ref[0], (1, 1), True)
    own_ref[...], other_ref[...] = by_side(side, coef[:, :rank], coef[:, rank:])
    rest_ref[...] = (sums[0] + sums[1])[:, rank:]


def correct_kernel(levels, rank, own_ref, other_ref, rest_ref, mine_ref, theirs_ref, pair_mine_ref,
                   pair_theirs_ref, message_ref):
    core = lax.axis_index("rows") % 2
    grams = [jnp.concatenate(by_side(core, mine_ref[...], pair_mine_ref[...]), axis=0),
             jnp.concatenate(by_side(core, theirs_ref[...], pair_theirs_ref[...]), axis=0)]
    sides = [own_ref[...], other_ref[...]]
    pairs = below_pairs(levels)
    spots = [spot for spot, (_, below) in enumerate(pairs) if below == 0]
    pieces = []
    for level in range(1, levels):
        value = rest_ref[:, (level - 1) * rank:level * rank]
        lanes = slice(spots[level - 1] * rank, (spots[level - 1] + 1) * rank)
        for part, gram in zip(sides, grams):
            value = value - dot(part, gram[:, lanes], (1, 1), True)
        pieces.append(value)
    for spot, (_, below) in enumerate(pairs):
        if below > 0:
            lanes = slice(spot * rank, (spot + 1) * rank)
            pieces.append(grams[0][:, lanes] + grams[1][:, lanes])
    pack_message(message_ref, pieces)


def level_kernel(levels, level, share, sent_ref, got_ref, joined_ref, coef_ref, *message_ref):
    rank = sent_ref.shape[1]
    side = lax.axis_index("leaf") // 2 ** (level - 1) % 2
    more = levels - level
    values = []
    for ref in (sent_ref, got_ref):
        values.append([ref[pl.ds(i * share, share), :] for i in range(more)])
    picked = jnp.concatenate(by_side(side, values[0][0], values[1][0]), axis=1)
    coef = dot(picked, joined_ref[level], (1, 1), True)
    sides = by_side(side, coef[:, :rank], coef[:, rank:])
    coef_ref[...] = sides[0]
    if not message_ref:
        return
    pairs = below_pairs(levels, level)
    grams = []
    for ref in (sent_ref, got_ref):
        grams.append({pair: ref[pl.ds(more * share + spot * rank, rank), :] for spot, pair in enumerate(pairs)})
    pieces = []
    for upper in range(level + 1, levels):
        value = values[0][upper - level] + values[1][upper - level]
        for part, gram in zip(sides, grams):
            value = value - dot(part, gram[upper, level], (1, 1), True)
        pieces.append(value)
    for pair in pairs:
        if pair[1] > level:
            pieces.append(grams[0][pair] + grams[1][pair])
    pack_message(message_ref[0], pieces)


def pack_kernel(*refs):
    levels = len(refs) - 3
    other_ref, own_refs, own_out, other_out = refs[0], refs[1:-2], refs[-2], refs[-1]
    own = [ref[...] for ref in own_refs]
    own_out[...] = jnp.concatenate(own, axis=1)
    other_out[...] = jnp.concatenate([other_ref[...]] + own[1:], axis=1)


def expand_kernel(levels, per_step, width, slots, *refs):
    piece_refs = refs[:2 * slots]
    moved_ref, rhs_ref, left_ref, out_ref, flip_ref, factor_ref, out_buf, sems = refs[2 * slots:]
    share, kinds = piece_refs[0].shape
    tile = per_step * width
    steps = moved_ref.shape[0] // per_step
    me = lax.axis_index("rows")
    for slot in range(2 * slots):
        owner = me ^ slot
        flip_ref[pl.ds(pl.multiple_of(owner * share, share), share), :] = piece_refs[slot][...]
    high_part, low_part = halves(flip_ref[...].T)
    factor_ref[:kinds, :] = high_part
    factor_ref[kinds:, :] = low_part

    def copy(step):
        rows = pl.ds(pl.multiple_of(step * tile, tile), tile)
        return pltpu.make_async_copy(out_buf.at[rows], out_ref.at[rows], sems.at[step])

    def body(step, _):
        rows = pl.ds(pl.multiple_of(step * tile, tile), tile)
        left = jnp.concatenate([left_ref[l, rows, :] for l in range(levels)] * 2, axis=1)
        update = dot(left, factor_ref[...], (1, 0))
        for b in range(per_step):
            block = step * per_step + b
            rows = pl.ds(pl.multiple_of(block * width, width), width)
            first = dot(moved_ref[block], rhs_ref[rows, :], (1, 0))
            out_buf[rows, :] = first - update[b * width:(b + 1) * width]
        copy(step).start()
        return 0

    lax.fori_loop(0, steps, body, 0)
    for step in range(steps):
        copy(step).wait()


def settings(mib, micros):
    return dict(
        compiler_params=pltpu.CompilerParams(vmem_limit_bytes=mib * MIB),
        cost_estimate=pl.CostEstimate(flops=int(micros * 1.1e9), bytes_accessed=0, transcendentals=0),
    )


def floats(*shape):
    return jax.ShapeDtypeStruct(shape, jnp.float32)


def per_device(rhs, leaf_order, leaf_inv, right_basis, left_basis, rank_perm, joined):
    levels, rows, rank = right_basis.shape
    nblocks, width, _ = leaf_inv.shape
    columns = rhs.shape[1]
    leaves = lax.axis_size("leaf")
    count = lax.axis_size("rows")
    slots = count // 2
    kinds = levels * rank
    size = kinds - rank
    share = columns // count
    gram_lanes = len(below_pairs(levels)) * rank

    per_step = blocks_per_step(nblocks, 3)
    flipped, gram_keep, gram_send = pl.pallas_call(
        functools.partial(gram_kernel, levels, per_step, width),
        in_specs=[pl.BlockSpec(memory_space=pltpu.HBM)] * 2,
        out_shape=[jax.ShapeDtypeStruct((kinds, rows), jnp.bfloat16)] + [floats(rank // 2, gram_lanes)] * 2,
        scratch_shapes=[
            pltpu.VMEM((levels, rows, rank), jnp.bfloat16),
            pltpu.VMEM((levels - 1, rows, rank), jnp.bfloat16),
            pltpu.VMEM((size, size), jnp.float32),
            pltpu.SemaphoreType.DMA((2, nblocks // per_step)),
        ],
        name="gram",
        **settings(24, 3),
    )(pltpu.with_memory_space_constraint(right_basis, pltpu.HBM),
      pltpu.with_memory_space_constraint(left_basis, pltpu.HBM))
    gram_got = swap(gram_send, "rows", 1)

    factors, moved = pl.pallas_call(
        functools.partial(factor_kernel, per_step, width),
        out_shape=[
            jax.ShapeDtypeStruct((2 * kinds, rows), jnp.bfloat16),
            jax.ShapeDtypeStruct((nblocks, width, width), jnp.bfloat16),
        ],
        name="factor",
        **settings(24, 4),
    )(leaf_order, leaf_inv, flipped)

    def project(half, *grams):
        return pl.pallas_call(
            functools.partial(project_kernel, half),
            out_shape=[floats(rank // 2, gram_lanes)] * (len(grams) // 2) + [floats(slots // 2, share, kinds)] * 2,
            scratch_shapes=[pltpu.VMEM((columns // 2, kinds), jnp.float32)],
            name="project",
            **settings(24, 2.4),
        )(factors, rhs, *grams)

    gram, keep_a, send_a = project(0, gram_keep, gram_got)
    got_a = swap(send_a, "rows", 1)
    mask = 2
    while 2 * mask < slots:
        gram = gram + swap(gram, "rows", mask)
        mask *= 2
    gram_got = swap(gram, "rows", mask)
    keep_b, send_b = project(1)
    got_b = swap(send_b, "rows", 1)
    gram, *merged = pl.pallas_call(
        merge_kernel,
        out_shape=[floats(rank // 2, gram_lanes)] + [floats(share, kinds)] * slots,
        name="merge",
        **settings(8, 1),
    )(keep_a, got_a, keep_b, got_b, gram, gram_got)
    parts = [merged[0]] + [swap(merged[s], "rows", 2 * s) for s in range(1, slots)]
    gram_other = swap(gram, "rows", slots)
    grams = [gram, gram_other, swap(gram, "rows", 1), swap(gram_other, "rows", 1)]

    prepared = pl.pallas_call(
        functools.partial(prepare_kernel, levels),
        in_specs=[pl.BlockSpec(memory_space=pltpu.HBM), pl.BlockSpec()],
        out_shape=floats(levels, 2 * rank, 2 * rank),
        scratch_shapes=[pltpu.VMEM((levels, 2 * rank, 2 * rank), jnp.float32), pltpu.SemaphoreType.DMA((levels,))],
        name="prepare",
        **settings(8, 2),
    )(pltpu.with_memory_space_constraint(joined, pltpu.HBM), rank_perm)

    def message_shape(level):
        return floats((levels - level) * share + len(below_pairs(levels, level)) * rank, rank)

    own, other, rest = pl.pallas_call(
        functools.partial(node_kernel, rank, slots),
        out_shape=[floats(share, rank)] * 2 + [floats(share, size)],
        name="node",
        **settings(8, 1),
    )(*parts, prepared)
    message = pl.pallas_call(
        functools.partial(correct_kernel, levels, rank),
        out_shape=message_shape(1),
        name="correct",
        **settings(8, 1),
    )(own, other, rest, *grams)
    coefs = [own]
    for level in range(1, levels):
        last = level + 1 == levels
        arrived = swap(message, "leaf", 2 ** (level - 1))
        outs = pl.pallas_call(
            functools.partial(level_kernel, levels, level, share),
            out_shape=[floats(share, rank)] + ([] if last else [message_shape(level + 1)]),
            name=f"level{level}",
            **settings(8, 0.7),
        )(message, arrived, prepared)
        coefs.append(outs[0])
        message = outs[-1]
    own_pack, other_pack = pl.pallas_call(
        pack_kernel, out_shape=[floats(share, kinds)] * 2, name="pack", **settings(8, 0.2),
    )(other, *coefs)

    pieces = []
    for slot in range(slots):
        piece = own_pack if slot < slots // 2 else other_pack
        piece = swap(piece, "rows", 2 * slot) if slot > 0 else piece
        pieces += [piece, swap(piece, "rows", 1)]

    per_step = blocks_per_step(nblocks, 2)
    return pl.pallas_call(
        functools.partial(expand_kernel, levels, per_step, width, slots),
        out_specs=pl.BlockSpec(memory_space=pl.ANY),
        out_shape=floats(rows, columns),
        scratch_shapes=[
            pltpu.VMEM((columns, kinds), jnp.float32),
            pltpu.VMEM((2 * kinds, columns), jnp.bfloat16),
            pltpu.VMEM((rows, columns), jnp.float32),
            pltpu.SemaphoreType.DMA((nblocks // per_step,)),
        ],
        name="expand",
        **settings(32, 7),
    )(*pieces, moved, rhs, left_basis)


def solution(mesh):
    return jax.shard_map(
        per_device,
        mesh=mesh,
        in_specs=(
            P(("leaf", "rows"), None),
            P(("leaf", "rows"), None),
            P(("leaf", "rows"), None, None),
            P(None, ("leaf", "rows"), None),
            P(None, ("leaf", "rows"), None),
            P(),
            P(),
        ),
        out_specs=P(("leaf", "rows"), None),
        check_vma=False,
    )
```

```python
import functools

import jax
import jax.numpy as jnp
from jax import lax
from jax.experimental import pallas as pl
from jax.experimental.pallas import tpu as pltpu
from jax.sharding import PartitionSpec as P

HIGHEST = lax.Precision.HIGHEST
MIB = 1 << 20


def dot(a, b, contract, exact=False):
    return lax.dot_general(
        a, b, ((contract[:1], contract[1:]), ((), ())),
        precision=HIGHEST if exact else None, preferred_element_type=jnp.float32,
    )


def halves(value):
    high_part = value.astype(jnp.bfloat16)
    low_part = (value - high_part.astype(jnp.float32)).astype(jnp.bfloat16)
    return high_part, low_part


def swap(value, axis, mask):
    count = lax.axis_size(axis)
    return lax.ppermute(value, axis, [(i, i ^ mask) for i in range(count)])


def blocks_per_step(nblocks, most):
    return max(size for size in range(1, most + 1) if nblocks % size == 0)


def below_pairs(levels, first=0):
    return [(level, below) for level in range(levels) for below in range(first, level)]


def gram_kernel(levels, per_step, width, right_ref, left_ref, flip_ref, keep_ref, send_ref,
                right_buf, left_buf, gram_ref, sems):
    rank = right_ref.shape[2]
    half = rank // 2
    tile = per_step * width
    steps = right_ref.shape[1] // tile

    def copies(step):
        rows = pl.ds(pl.multiple_of(step * tile, tile), tile)
        return (
            pltpu.make_async_copy(right_ref.at[:, rows], right_buf.at[:, rows], sems.at[0, step]),
            pltpu.make_async_copy(left_ref.at[:levels - 1, rows], left_buf.at[:, rows], sems.at[1, step]),
        )

    for step in range(steps):
        for copy in copies(step):
            copy.start()
    gram_ref[...] = jnp.zeros_like(gram_ref)

    def body(step, _):
        for copy in copies(step):
            copy.wait()
        rows = pl.ds(pl.multiple_of(step * tile, tile), tile)
        right = jnp.concatenate([right_buf[l, rows, :] for l in range(levels)], axis=1).T
        flip_ref[:, rows] = right
        left = jnp.concatenate([left_buf[l, rows, :] for l in range(levels - 1)], axis=1)
        gram_ref[...] += dot(right[rank:], left, (1, 0))
        return 0

    lax.fori_loop(0, steps, body, 0)
    core = lax.axis_index("rows") % 2
    for spot, (level, below) in enumerate(below_pairs(levels)):
        lanes = pl.ds(spot * rank, rank)
        for ref, side in ((keep_ref, core), (send_ref, 1 - core)):
            rows = pl.ds(pl.multiple_of((level - 1) * rank + side * half, half), half)
            ref[:, lanes] = gram_ref[rows, pl.ds(below * rank, rank)]


def permute_kernel(per_step, width, order_ref, inv_ref, moved_ref):
    place = lax.broadcasted_iota(jnp.int32, (width, width), 0)

    def body(step, _):
        for b in range(per_step):
            block = step * per_step + b
            chosen = (place == order_ref[pl.ds(block, 1), :]).astype(jnp.float32).astype(jnp.bfloat16)
            moved_ref[block] = dot(inv_ref[block], chosen, (1, 1)).astype(jnp.bfloat16)
        return 0

    lax.fori_loop(0, inv_ref.shape[0] // per_step, body, 0)


def weigh_kernel(per_step, width, moved_ref, flip_ref, after_ref, factor_ref):
    kinds = flip_ref.shape[0]

    def body(step, _):
        for b in range(per_step):
            block = step * per_step + b
            lanes = pl.ds(pl.multiple_of(block * width, width), width)
            high_part, low_part = halves(dot(flip_ref[:, lanes], moved_ref[block], (1, 0)))
            factor_ref[:kinds, lanes] = high_part
            factor_ref[kinds:, lanes] = low_part
        return 0

    lax.fori_loop(0, moved_ref.shape[0] // per_step, body, 0)


def solve_kernel(per_step, width, moved_ref, rhs_ref, after_ref, out_ref):
    def body(step, _):
        for b in range(per_step):
            block = step * per_step + b
            rows = pl.ds(pl.multiple_of(block * width, width), width)
            out_ref[rows, :] = dot(moved_ref[block], rhs_ref[rows, :], (1, 0))
        return 0

    lax.fori_loop(0, moved_ref.shape[0] // per_step, body, 0)


def half_lanes(far, me, count, part):
    side = me // (count // 2)
    return pl.ds(pl.multiple_of((1 - side if far else side) * part, part), part)


def project_kernel(far, factor_ref, rhs_ref, after_ref, keep_ref, send_ref, total_ref):
    kinds = factor_ref.shape[0] // 2
    slots, share, _ = keep_ref.shape
    part = total_ref.shape[0]
    me = lax.axis_index("rows")
    total = dot(factor_ref[...], rhs_ref[:, half_lanes(far, me, 4 * slots, part)], (1, 0))
    total_ref[...] = (total[:kinds] + total[kinds:]).T
    for slot in range(slots):
        for ref, mask in ((keep_ref, 2 * slot), (send_ref, 2 * slot + 1)):
            owner = (me ^ mask) % (2 * slots)
            ref[slot] = total_ref[pl.ds(pl.multiple_of(owner * share, share), share), :]


def merge_kernel(keep_ref, got_ref, *out_refs):
    for slot, out_ref in enumerate(out_refs):
        out_ref[...] = keep_ref[slot] + got_ref[slot]


def add_kernel(mine_ref, got_ref, out_ref):
    out_ref[...] = mine_ref[...] + got_ref[...]


def prepare_kernel(levels, joined_ref, perm_ref, out_ref, joined_buf, sems):
    rank = perm_ref.shape[1]
    leaves = lax.axis_size("leaf")
    leaf = lax.axis_index("leaf")
    copies = []
    for level in range(levels):
        node = 2 * leaves - 2 * leaves // 2 ** level + leaf // 2 ** level
        copies.append(pltpu.make_async_copy(joined_ref.at[node], joined_buf.at[level], sems.at[level]))
        copies[-1].start()
    spot = lax.broadcasted_iota(jnp.int32, (rank, rank), 0)
    for level in range(levels):
        copies[level].wait()
        chosen = (spot == perm_ref[level:level + 1, :]).astype(jnp.float32)
        for side in range(2):
            lanes = pl.ds(side * rank, rank)
            out_ref[level, :, lanes] = dot(joined_buf[level, :, lanes], chosen, (1, 1), True)


def by_side(side, own, other):
    return jnp.where(side == 0, own, other), jnp.where(side == 0, other, own)


def pack_message(message_ref, pieces):
    row = 0
    for piece in pieces:
        message_ref[pl.ds(row, piece.shape[0]), :] = piece
        row += piece.shape[0]


def node_kernel(rank, slots, *refs):
    part_refs = refs[:slots]
    joined_ref, own_ref, other_ref, rest_ref = refs[slots:]
    side = lax.axis_index("rows") // slots
    half = slots // 2
    sums = [sum(ref[...] for ref in part_refs[:half]), sum(ref[...] for ref in part_refs[half:])]
    picked = jnp.concatenate(by_side(side, sums[0][:, :rank], sums[1][:, :rank]), axis=1)
    coef = dot(picked, joined_ref[0], (1, 1), True)
    own_ref[...], other_ref[...] = by_side(side, coef[:, :rank], coef[:, rank:])
    rest_ref[...] = (sums[0] + sums[1])[:, rank:]


def correct_kernel(levels, rank, own_ref, other_ref, rest_ref, mine_ref, theirs_ref, pair_mine_ref,
                   pair_theirs_ref, message_ref):
    core = lax.axis_index("rows") % 2
    grams = [jnp.concatenate(by_side(core, mine_ref[...], pair_mine_ref[...]), axis=0),
             jnp.concatenate(by_side(core, theirs_ref[...], pair_theirs_ref[...]), axis=0)]
    pairs = below_pairs(levels)
    lanes = {pair: slice(spot * rank, (spot + 1) * rank) for spot, pair in enumerate(pairs)}
    joint = jnp.concatenate(
        [jnp.concatenate([gram[:, lanes[level, 0]] for gram in grams], axis=1) for level in range(1, levels)], axis=0)
    rest = rest_ref[...] - dot(jnp.concatenate([own_ref[...], other_ref[...]], axis=1), joint, (1, 1), True)
    pieces = [rest[:, level * rank:(level + 1) * rank] for level in range(levels - 1)]
    for pair in pairs:
        if pair[1] > 0:
            pieces.append(grams[0][:, lanes[pair]] + grams[1][:, lanes[pair]])
    pack_message(message_ref, pieces)


def level_kernel(levels, level, share, sent_ref, got_ref, joined_ref, coef_ref, *message_ref):
    rank = sent_ref.shape[1]
    side = lax.axis_index("leaf") // 2 ** (level - 1) % 2
    more = levels - level
    values = []
    for ref in (sent_ref, got_ref):
        values.append([ref[pl.ds(i * share, share), :] for i in range(more)])
    picked = jnp.concatenate(by_side(side, values[0][0], values[1][0]), axis=1)
    coef = dot(picked, joined_ref[level], (1, 1), True)
    sides = by_side(side, coef[:, :rank], coef[:, rank:])
    coef_ref[...] = sides[0]
    if not message_ref:
        return
    pairs = below_pairs(levels, level)
    grams = []
    for ref in (sent_ref, got_ref):
        grams.append({pair: ref[pl.ds(more * share + spot * rank, rank), :] for spot, pair in enumerate(pairs)})
    uppers = list(range(level + 1, levels))
    joint = jnp.concatenate(
        [jnp.concatenate([gram[upper, level] for gram in grams], axis=1) for upper in uppers], axis=0)
    change = dot(jnp.concatenate(sides, axis=1), joint, (1, 1), True)
    pieces = [values[0][upper - level] + values[1][upper - level] - change[:, i * rank:(i + 1) * rank]
              for i, upper in enumerate(uppers)]
    for pair in pairs:
        if pair[1] > level:
            pieces.append(grams[0][pair] + grams[1][pair])
    pack_message(message_ref[0], pieces)


def pack_kernel(*refs):
    levels = len(refs) - 3
    other_ref, own_refs, own_out, other_out = refs[0], refs[1:-2], refs[-2], refs[-1]
    own = [ref[...] for ref in own_refs]
    own_out[...] = jnp.concatenate(own, axis=1)
    other_out[...] = jnp.concatenate([other_ref[...]] + own[1:], axis=1)


def expand_kernel(far, levels, per_step, width, slots, *refs):
    piece_refs = refs[:2 * slots]
    first_ref, left_ref = refs[2 * slots:2 * slots + 2]
    out_ref, flip_ref, factor_ref, out_buf, sems = refs[-5:]
    share, kinds = piece_refs[0].shape
    tile = per_step * width
    steps = out_buf.shape[0] // tile
    me = lax.axis_index("rows")
    lanes = half_lanes(far, me, 4 * slots, out_buf.shape[1])
    for slot in range(2 * slots):
        owner = (me ^ slot) % (2 * slots)
        flip_ref[pl.ds(pl.multiple_of(owner * share, share), share), :] = piece_refs[slot][...]
    high_part, low_part = halves(flip_ref[...].T)
    factor_ref[:kinds, :] = high_part
    factor_ref[kinds:, :] = low_part

    def copy(step):
        rows = pl.ds(pl.multiple_of(step * tile, tile), tile)
        return pltpu.make_async_copy(out_buf.at[rows], out_ref.at[rows, lanes], sems.at[step])

    def body(step, _):
        rows = pl.ds(pl.multiple_of(step * tile, tile), tile)
        left = jnp.concatenate([left_ref[l, rows, :] for l in range(levels)] * 2, axis=1)
        out_buf[rows, :] = first_ref[rows, lanes] - dot(left, factor_ref[...], (1, 0))
        copy(step).start()
        return 0

    lax.fori_loop(0, steps, body, 0)
    for step in range(steps):
        copy(step).wait()


def settings(mib, micros):
    return dict(
        compiler_params=pltpu.CompilerParams(vmem_limit_bytes=mib * MIB),
        cost_estimate=pl.CostEstimate(flops=int(micros * 1.1e9), bytes_accessed=0, transcendentals=0),
    )


def floats(*shape):
    return jax.ShapeDtypeStruct(shape, jnp.float32)


def per_device(rhs, leaf_order, leaf_inv, right_basis, left_basis, rank_perm, joined):
    levels, rows, rank = right_basis.shape
    nblocks, width, _ = leaf_inv.shape
    columns = rhs.shape[1]
    leaves = lax.axis_size("leaf")
    count = lax.axis_size("rows")
    slots = count // 2
    kinds = levels * rank
    size = kinds - rank
    share = columns // count
    gram_lanes = len(below_pairs(levels)) * rank

    per_step = blocks_per_step(nblocks, 3)
    flipped, gram_keep, gram_send = pl.pallas_call(
        functools.partial(gram_kernel, levels, per_step, width),
        in_specs=[pl.BlockSpec(memory_space=pltpu.HBM)] * 2,
        out_shape=[jax.ShapeDtypeStruct((kinds, rows), jnp.bfloat16)] + [floats(rank // 2, gram_lanes)] * 2,
        scratch_shapes=[
            pltpu.VMEM((levels, rows, rank), jnp.bfloat16),
            pltpu.VMEM((levels - 1, rows, rank), jnp.bfloat16),
            pltpu.VMEM((size, size), jnp.float32),
            pltpu.SemaphoreType.DMA((2, nblocks // per_step)),
        ],
        name="gram",
        **settings(24, 3),
    )(pltpu.with_memory_space_constraint(right_basis, pltpu.HBM),
      pltpu.with_memory_space_constraint(left_basis, pltpu.HBM))
    gram_got = swap(gram_send, "rows", 1)

    moved = pl.pallas_call(
        functools.partial(permute_kernel, per_step, width),
        out_shape=jax.ShapeDtypeStruct((nblocks, width, width), jnp.bfloat16),
        name="permute",
        **settings(8, 1.5),
    )(leaf_order, leaf_inv)

    def add(mine, got):
        return pl.pallas_call(
            add_kernel, out_shape=floats(*mine.shape), name="add", **settings(8, 0.1),
        )(mine, got)

    gram = add(gram_keep, gram_got)
    factors = pl.pallas_call(
        functools.partial(weigh_kernel, per_step, width),
        out_shape=jax.ShapeDtypeStruct((2 * kinds, rows), jnp.bfloat16),
        name="weigh",
        **settings(8, 2.4),
    )(moved, flipped, gram)

    def project(far, after):
        return pl.pallas_call(
            functools.partial(project_kernel, far),
            out_shape=[floats(slots // 2, share, kinds)] * 2,
            scratch_shapes=[pltpu.VMEM((columns // 2, kinds), jnp.float32)],
            name="project_far" if far else "project_near",
            **settings(12, 2.1),
        )(factors, rhs, after)

    def merge(keep, got):
        return pl.pallas_call(
            merge_kernel, out_shape=[floats(share, kinds)] * (slots // 2), name="merge", **settings(8, 0.1),
        )(keep, got)

    keep_far, send_far = project(True, gram)
    got_far = swap(send_far, "rows", 1)
    mask = 2
    while mask < slots:
        gram = add(gram, swap(gram, "rows", mask))
        mask *= 2
    keep_near, send_near = project(False, gram)
    got_near = swap(send_near, "rows", 1)
    merged = [None] * (slots // 2) + list(merge(keep_far, got_far))
    merged[:slots // 2] = merge(keep_near, got_near)
    parts = [merged[0]] + [swap(merged[s], "rows", 2 * s) for s in range(1, slots)]
    gram_other = swap(gram, "rows", slots)
    grams = [gram, gram_other, swap(gram, "rows", 1), swap(gram_other, "rows", 1)]
    first = pl.pallas_call(
        functools.partial(solve_kernel, per_step, width),
        out_shape=floats(rows, columns),
        name="solve",
        **settings(8, 1.7),
    )(moved, rhs, merged[0])

    prepared = pl.pallas_call(
        functools.partial(prepare_kernel, levels),
        in_specs=[pl.BlockSpec(memory_space=pltpu.HBM), pl.BlockSpec()],
        out_shape=floats(levels, 2 * rank, 2 * rank),
        scratch_shapes=[pltpu.VMEM((levels, 2 * rank, 2 * rank), jnp.float32), pltpu.SemaphoreType.DMA((levels,))],
        name="prepare",
        **settings(8, 2),
    )(pltpu.with_memory_space_constraint(joined, pltpu.HBM), rank_perm)

    def message_shape(level):
        return floats((levels - level) * share + len(below_pairs(levels, level)) * rank, rank)

    own, other, rest = pl.pallas_call(
        functools.partial(node_kernel, rank, slots),
        out_shape=[floats(share, rank)] * 2 + [floats(share, size)],
        name="node",
        **settings(8, 1),
    )(*parts, prepared)
    message = pl.pallas_call(
        functools.partial(correct_kernel, levels, rank),
        out_shape=message_shape(1),
        name="correct",
        **settings(8, 1),
    )(own, other, rest, *grams)
    coefs = [own]
    for level in range(1, levels):
        last = level + 1 == levels
        arrived = swap(message, "leaf", 2 ** (level - 1))
        outs = pl.pallas_call(
            functools.partial(level_kernel, levels, level, share),
            out_shape=[floats(share, rank)] + ([] if last else [message_shape(level + 1)]),
            name=f"level{level}",
            **settings(8, 0.7),
        )(message, arrived, prepared)
        coefs.append(outs[0])
        message = outs[-1]
    own_pack, other_pack = pl.pallas_call(
        pack_kernel, out_shape=[floats(share, kinds)] * 2, name="pack", **settings(8, 0.2),
    )(other, *coefs)

    pieces = []
    for slot in range(slots):
        piece = own_pack if slot < slots // 2 else other_pack
        piece = swap(piece, "rows", 2 * slot) if slot > 0 else piece
        pieces += [piece, swap(piece, "rows", 1)]

    def expand(far, *extra):
        begin = count // 2 if far else 0
        operands = (*pieces[begin:begin + count // 2], first, left_basis, *extra)
        inner = [pl.BlockSpec()] * (count // 2 + 2) + [pl.BlockSpec(memory_space=pl.ANY)] * len(extra)
        return pl.pallas_call(
            functools.partial(expand_kernel, far, levels, per_step, width, slots // 2),
            in_specs=inner,
            out_specs=pl.BlockSpec(memory_space=pl.ANY),
            out_shape=floats(rows, columns),
            scratch_shapes=[
                pltpu.VMEM((columns // 2, kinds), jnp.float32),
                pltpu.VMEM((2 * kinds, columns // 2), jnp.bfloat16),
                pltpu.VMEM((rows, columns // 2), jnp.float32),
                pltpu.SemaphoreType.DMA((nblocks // per_step,)),
            ],
            input_output_aliases={len(operands) - 1: 0} if extra else {},
            name="expand_far" if far else "expand_near",
            **settings(14, 2.6),
        )(*operands)

    return expand(True, expand(False))


def solution(mesh):
    return jax.shard_map(
        per_device,
        mesh=mesh,
        in_specs=(
            P(("leaf", "rows"), None),
            P(("leaf", "rows"), None),
            P(("leaf", "rows"), None, None),
            P(None, ("leaf", "rows"), None),
            P(None, ("leaf", "rows"), None),
            P(),
            P(),
        ),
        out_specs=P(("leaf", "rows"), None),
        check_vma=False,
    )
```

```python
import functools

import jax
import jax.numpy as jnp
from jax import lax
from jax.experimental import pallas as pl
from jax.experimental.pallas import tpu as pltpu
from jax.sharding import PartitionSpec as P

HIGHEST = lax.Precision.HIGHEST
MIB = 1 << 20


def dot(a, b, contract, exact=False):
    return lax.dot_general(
        a, b, ((contract[:1], contract[1:]), ((), ())),
        precision=HIGHEST if exact else None, preferred_element_type=jnp.float32,
    )


def halves(value):
    high_part = value.astype(jnp.bfloat16)
    low_part = (value - high_part.astype(jnp.float32)).astype(jnp.bfloat16)
    return high_part, low_part


def swap(value, axis, mask):
    count = lax.axis_size(axis)
    return lax.ppermute(value, axis, [(i, i ^ mask) for i in range(count)])


def blocks_per_step(nblocks, most):
    return max(size for size in range(1, most + 1) if nblocks % size == 0)


def below_pairs(levels, first=0):
    return [(level, below) for level in range(levels) for below in range(first, level)]


def gram_kernel(levels, per_step, width, right_ref, left_ref, flip_ref, keep_ref, send_ref,
                right_buf, left_buf, gram_ref, sems):
    rank = right_ref.shape[2]
    half = rank // 2
    tile = per_step * width
    steps = right_ref.shape[1] // tile

    def copies(step):
        rows = pl.ds(pl.multiple_of(step * tile, tile), tile)
        return (
            pltpu.make_async_copy(right_ref.at[:, rows], right_buf.at[:, rows], sems.at[0, step]),
            pltpu.make_async_copy(left_ref.at[:levels - 1, rows], left_buf.at[:, rows], sems.at[1, step]),
        )

    for step in range(steps):
        for priority, copy in enumerate(copies(step)):
            copy.start(priority=priority)
    gram_ref[...] = jnp.zeros_like(gram_ref)

    def body(step, _):
        for copy in copies(step):
            copy.wait()
        rows = pl.ds(pl.multiple_of(step * tile, tile), tile)
        right = jnp.concatenate([right_buf[l, rows, :] for l in range(levels)], axis=1).T
        flip_ref[:, rows] = right
        left = jnp.concatenate([left_buf[l, rows, :] for l in range(levels - 1)], axis=1)
        gram_ref[...] += dot(right[rank:], left, (1, 0))
        return 0

    lax.fori_loop(0, steps, body, 0)
    core = lax.axis_index("rows") % 2
    for spot, (level, below) in enumerate(below_pairs(levels)):
        lanes = pl.ds(spot * rank, rank)
        for ref, side in ((keep_ref, core), (send_ref, 1 - core)):
            rows = pl.ds(pl.multiple_of((level - 1) * rank + side * half, half), half)
            ref[:, lanes] = gram_ref[rows, pl.ds(below * rank, rank)]


def permute_kernel(per_step, width, order_ref, inv_ref, moved_ref):
    place = lax.broadcasted_iota(jnp.int32, (width, width), 0)

    def body(step, _):
        for b in range(per_step):
            block = step * per_step + b
            chosen = (place == order_ref[pl.ds(block, 1), :]).astype(jnp.float32).astype(jnp.bfloat16)
            moved_ref[block] = dot(inv_ref[block], chosen, (1, 1)).astype(jnp.bfloat16)
        return 0

    lax.fori_loop(0, inv_ref.shape[0] // per_step, body, 0)


def weigh_kernel(per_step, width, moved_ref, flip_ref, after_ref, factor_ref):
    kinds = flip_ref.shape[0]

    def body(step, _):
        for b in range(per_step):
            block = step * per_step + b
            lanes = pl.ds(pl.multiple_of(block * width, width), width)
            high_part, low_part = halves(dot(flip_ref[:, lanes], moved_ref[block], (1, 0)))
            factor_ref[:kinds, lanes] = high_part
            factor_ref[kinds:, lanes] = low_part
        return 0

    lax.fori_loop(0, moved_ref.shape[0] // per_step, body, 0)


def solve_kernel(per_step, width, moved_ref, rhs_ref, after_ref, out_ref):
    def body(step, _):
        for b in range(per_step):
            block = step * per_step + b
            rows = pl.ds(pl.multiple_of(block * width, width), width)
            out_ref[rows, :] = dot(moved_ref[block], rhs_ref[rows, :], (1, 0))
        return 0

    lax.fori_loop(0, moved_ref.shape[0] // per_step, body, 0)


def half_lanes(far, me, count, part):
    side = me // (count // 2)
    return pl.ds(pl.multiple_of((1 - side if far else side) * part, part), part)


def project_kernel(far, factor_ref, rhs_ref, after_ref, keep_ref, send_ref, total_ref):
    kinds = factor_ref.shape[0] // 2
    slots, share, _ = keep_ref.shape
    part = total_ref.shape[0]
    me = lax.axis_index("rows")
    total = dot(factor_ref[...], rhs_ref[:, half_lanes(far, me, 4 * slots, part)], (1, 0))
    total_ref[...] = (total[:kinds] + total[kinds:]).T
    for slot in range(slots):
        for ref, mask in ((keep_ref, 2 * slot), (send_ref, 2 * slot + 1)):
            owner = (me ^ mask) % (2 * slots)
            ref[slot] = total_ref[pl.ds(pl.multiple_of(owner * share, share), share), :]


def merge_kernel(keep_ref, got_ref, *out_refs):
    for slot, out_ref in enumerate(out_refs):
        out_ref[...] = keep_ref[slot] + got_ref[slot]


def add_kernel(mine_ref, got_ref, out_ref):
    out_ref[...] = mine_ref[...] + got_ref[...]


def prepare_kernel(levels, joined_ref, perm_ref, out_ref, joined_buf, sems):
    rank = perm_ref.shape[1]
    leaves = lax.axis_size("leaf")
    leaf = lax.axis_index("leaf")
    copies = []
    for level in range(levels):
        node = 2 * leaves - 2 * leaves // 2 ** level + leaf // 2 ** level
        copies.append(pltpu.make_async_copy(joined_ref.at[node], joined_buf.at[level], sems.at[level]))
        copies[-1].start()
    spot = lax.broadcasted_iota(jnp.int32, (rank, rank), 0)
    for level in range(levels):
        copies[level].wait()
        chosen = (spot == perm_ref[level:level + 1, :]).astype(jnp.float32)
        for side in range(2):
            lanes = pl.ds(side * rank, rank)
            out_ref[level, :, lanes] = dot(joined_buf[level, :, lanes], chosen, (1, 1), True)


def by_side(side, own, other):
    return jnp.where(side == 0, own, other), jnp.where(side == 0, other, own)


def pack_message(message_ref, pieces):
    row = 0
    for piece in pieces:
        message_ref[pl.ds(row, piece.shape[0]), :] = piece
        row += piece.shape[0]


def node_kernel(rank, slots, *refs):
    part_refs = refs[:slots]
    joined_ref, own_ref, other_ref, rest_ref = refs[slots:]
    side = lax.axis_index("rows") // slots
    half = slots // 2
    sums = [sum(ref[...] for ref in part_refs[:half]), sum(ref[...] for ref in part_refs[half:])]
    picked = jnp.concatenate(by_side(side, sums[0][:, :rank], sums[1][:, :rank]), axis=1)
    coef = dot(picked, joined_ref[0], (1, 1), True)
    own_ref[...], other_ref[...] = by_side(side, coef[:, :rank], coef[:, rank:])
    rest_ref[...] = (sums[0] + sums[1])[:, rank:]


def correct_kernel(levels, rank, own_ref, other_ref, rest_ref, mine_ref, theirs_ref, pair_mine_ref,
                   pair_theirs_ref, message_ref):
    core = lax.axis_index("rows") % 2
    grams = [jnp.concatenate(by_side(core, mine_ref[...], pair_mine_ref[...]), axis=0),
             jnp.concatenate(by_side(core, theirs_ref[...], pair_theirs_ref[...]), axis=0)]
    pairs = below_pairs(levels)
    lanes = {pair: slice(spot * rank, (spot + 1) * rank) for spot, pair in enumerate(pairs)}
    joint = jnp.concatenate(
        [jnp.concatenate([gram[:, lanes[level, 0]] for gram in grams], axis=1) for level in range(1, levels)], axis=0)
    rest = rest_ref[...] - dot(jnp.concatenate([own_ref[...], other_ref[...]], axis=1), joint, (1, 1), True)
    pieces = [rest[:, level * rank:(level + 1) * rank] for level in range(levels - 1)]
    for pair in pairs:
        if pair[1] > 0:
            pieces.append(grams[0][:, lanes[pair]] + grams[1][:, lanes[pair]])
    pack_message(message_ref, pieces)


def level_kernel(levels, level, share, sent_ref, got_ref, joined_ref, after_ref, coef_ref, *message_ref):
    rank = sent_ref.shape[1]
    side = lax.axis_index("leaf") // 2 ** (level - 1) % 2
    more = levels - level
    values = []
    for ref in (sent_ref, got_ref):
        values.append([ref[pl.ds(i * share, share), :] for i in range(more)])
    picked = jnp.concatenate(by_side(side, values[0][0], values[1][0]), axis=1)
    coef = dot(picked, joined_ref[level], (1, 1), True)
    sides = by_side(side, coef[:, :rank], coef[:, rank:])
    coef_ref[...] = sides[0]
    if not message_ref:
        return
    pairs = below_pairs(levels, level)
    grams = []
    for ref in (sent_ref, got_ref):
        grams.append({pair: ref[pl.ds(more * share + spot * rank, rank), :] for spot, pair in enumerate(pairs)})
    uppers = list(range(level + 1, levels))
    joint = jnp.concatenate(
        [jnp.concatenate([gram[upper, level] for gram in grams], axis=1) for upper in uppers], axis=0)
    change = dot(jnp.concatenate(sides, axis=1), joint, (1, 1), True)
    pieces = [values[0][upper - level] + values[1][upper - level] - change[:, i * rank:(i + 1) * rank]
              for i, upper in enumerate(uppers)]
    for pair in pairs:
        if pair[1] > level:
            pieces.append(grams[0][pair] + grams[1][pair])
    pack_message(message_ref[0], pieces)


def pack_kernel(*refs):
    levels = len(refs) - 3
    other_ref, own_refs, own_out, other_out = refs[0], refs[1:-2], refs[-2], refs[-1]
    own = [ref[...] for ref in own_refs]
    own_out[...] = jnp.concatenate(own, axis=1)
    other_out[...] = jnp.concatenate([other_ref[...]] + own[1:], axis=1)


def expand_kernel(far, levels, per_step, width, slots, *refs):
    piece_refs = refs[:2 * slots]
    first_ref, left_ref = refs[2 * slots:2 * slots + 2]
    out_ref, flip_ref, factor_ref, out_buf, sems = refs[-5:]
    share, kinds = piece_refs[0].shape
    tile = per_step * width
    steps = out_buf.shape[0] // tile
    me = lax.axis_index("rows")
    lanes = half_lanes(far, me, 4 * slots, out_buf.shape[1])
    for slot in range(2 * slots):
        owner = (me ^ slot) % (2 * slots)
        flip_ref[pl.ds(pl.multiple_of(owner * share, share), share), :] = piece_refs[slot][...]
    high_part, low_part = halves(flip_ref[...].T)
    factor_ref[:kinds, :] = high_part
    factor_ref[kinds:, :] = low_part

    def copy(step):
        rows = pl.ds(step * tile, tile)
        return pltpu.make_async_copy(out_buf.at[rows], out_ref.at[rows, lanes], sems.at[step])

    for step in range(steps):
        rows = pl.ds(step * tile, tile)
        left = jnp.concatenate([left_ref[l, rows, :] for l in range(levels)] * 2, axis=1)
        out_buf[rows, :] = first_ref[rows, lanes] - dot(left, factor_ref[...], (1, 0))
        copy(step).start(priority=step % 2)
    for step in range(steps):
        copy(step).wait()


def settings(mib, micros):
    return dict(
        compiler_params=pltpu.CompilerParams(vmem_limit_bytes=mib * MIB),
        cost_estimate=pl.CostEstimate(flops=int(micros * 1.1e9), bytes_accessed=0, transcendentals=0),
    )


def floats(*shape):
    return jax.ShapeDtypeStruct(shape, jnp.float32)


def per_device(rhs, leaf_order, leaf_inv, right_basis, left_basis, rank_perm, joined):
    levels, rows, rank = right_basis.shape
    nblocks, width, _ = leaf_inv.shape
    columns = rhs.shape[1]
    leaves = lax.axis_size("leaf")
    count = lax.axis_size("rows")
    slots = count // 2
    kinds = levels * rank
    size = kinds - rank
    share = columns // count
    gram_lanes = len(below_pairs(levels)) * rank

    per_step = blocks_per_step(nblocks, 3)
    flipped, gram_keep, gram_send = pl.pallas_call(
        functools.partial(gram_kernel, levels, per_step, width),
        in_specs=[pl.BlockSpec(memory_space=pltpu.HBM)] * 2,
        out_shape=[jax.ShapeDtypeStruct((kinds, rows), jnp.bfloat16)] + [floats(rank // 2, gram_lanes)] * 2,
        scratch_shapes=[
            pltpu.VMEM((levels, rows, rank), jnp.bfloat16),
            pltpu.VMEM((levels - 1, rows, rank), jnp.bfloat16),
            pltpu.VMEM((size, size), jnp.float32),
            pltpu.SemaphoreType.DMA((2, nblocks // per_step)),
        ],
        name="gram",
        **settings(24, 3),
    )(pltpu.with_memory_space_constraint(right_basis, pltpu.HBM),
      pltpu.with_memory_space_constraint(left_basis, pltpu.HBM))
    gram_got = swap(gram_send, "rows", 1)

    moved = pl.pallas_call(
        functools.partial(permute_kernel, blocks_per_step(nblocks, 6), width),
        out_shape=jax.ShapeDtypeStruct((nblocks, width, width), jnp.bfloat16),
        name="permute",
        **settings(8, 1.5),
    )(leaf_order, leaf_inv)

    def add(mine, got):
        return pl.pallas_call(
            add_kernel, out_shape=floats(*mine.shape), name="add", **settings(8, 0.1),
        )(mine, got)

    gram = add(gram_keep, gram_got)
    factors = pl.pallas_call(
        functools.partial(weigh_kernel, per_step, width),
        out_shape=jax.ShapeDtypeStruct((2 * kinds, rows), jnp.bfloat16),
        name="weigh",
        **settings(8, 2.4),
    )(moved, flipped, gram)

    def project(far, after):
        return pl.pallas_call(
            functools.partial(project_kernel, far),
            out_shape=[floats(slots // 2, share, kinds)] * 2,
            scratch_shapes=[pltpu.VMEM((columns // 2, kinds), jnp.float32)],
            name="project_far" if far else "project_near",
            **settings(12, 2.1),
        )(factors, rhs, after)

    def merge(keep, got):
        return pl.pallas_call(
            merge_kernel, out_shape=[floats(share, kinds)] * (slots // 2), name="merge", **settings(8, 0.1),
        )(keep, got)

    keep_far, send_far = project(True, gram)
    got_far = swap(send_far, "rows", 1)
    mask = 2
    while mask < slots:
        gram = add(gram, swap(gram, "rows", mask))
        mask *= 2
    keep_near, send_near = project(False, gram)
    got_near = swap(send_near, "rows", 1)
    merged = [None] * (slots // 2) + list(merge(keep_far, got_far))
    merged[:slots // 2] = merge(keep_near, got_near)
    parts = [merged[0]] + [swap(merged[s], "rows", 2 * s) for s in range(1, slots)]
    gram_other = swap(gram, "rows", slots)
    grams = [gram, gram_other, swap(gram, "rows", 1), swap(gram_other, "rows", 1)]
    first = pl.pallas_call(
        functools.partial(solve_kernel, per_step, width),
        out_shape=floats(rows, columns),
        name="solve",
        **settings(8, 1.7),
    )(moved, rhs, merged[0])

    prepared = pl.pallas_call(
        functools.partial(prepare_kernel, levels),
        in_specs=[pl.BlockSpec(memory_space=pltpu.HBM), pl.BlockSpec()],
        out_shape=floats(levels, 2 * rank, 2 * rank),
        scratch_shapes=[pltpu.VMEM((levels, 2 * rank, 2 * rank), jnp.float32), pltpu.SemaphoreType.DMA((levels,))],
        name="prepare",
        **settings(8, 2),
    )(pltpu.with_memory_space_constraint(joined, pltpu.HBM), rank_perm)

    def message_shape(level):
        return floats((levels - level) * share + len(below_pairs(levels, level)) * rank, rank)

    own, other, rest = pl.pallas_call(
        functools.partial(node_kernel, rank, slots),
        out_shape=[floats(share, rank)] * 2 + [floats(share, size)],
        name="node",
        **settings(8, 1),
    )(*parts, prepared)
    message = pl.pallas_call(
        functools.partial(correct_kernel, levels, rank),
        out_shape=message_shape(1),
        name="correct",
        **settings(8, 1),
    )(own, other, rest, *grams)
    coefs = [own]
    for level in range(1, levels):
        last = level + 1 == levels
        arrived = swap(message, "leaf", 2 ** level - 1)
        outs = pl.pallas_call(
            functools.partial(level_kernel, levels, level, share),
            out_shape=[floats(share, rank)] + ([] if last else [message_shape(level + 1)]),
            name=f"level{level}",
            **settings(8, 0.7),
        )(message, arrived, prepared, first)
        coefs.append(outs[0])
        message = outs[-1]
    own_pack, other_pack = pl.pallas_call(
        pack_kernel, out_shape=[floats(share, kinds)] * 2, name="pack", **settings(8, 0.2),
    )(other, *coefs)

    steps = nblocks // per_step

    def expand(far, *extra):
        begin = count // 2 if far else 0
        operands = (*pieces[begin:begin + count // 2], first, left_basis, *extra)
        inner = [pl.BlockSpec()] * (count // 2 + 2) + [pl.BlockSpec(memory_space=pl.ANY)] * len(extra)
        return pl.pallas_call(
            functools.partial(expand_kernel, far, levels, per_step, width, slots // 2),
            in_specs=inner,
            out_specs=pl.BlockSpec(memory_space=pl.ANY),
            out_shape=floats(rows, columns),
            scratch_shapes=[
                pltpu.VMEM((columns // 2, kinds), jnp.float32),
                pltpu.VMEM((2 * kinds, columns // 2), jnp.bfloat16),
                pltpu.VMEM((rows, columns // 2), jnp.float32),
                pltpu.SemaphoreType.DMA((steps,)),
            ],
            input_output_aliases={len(operands) - 1: 0} if extra else {},
            name="expand_far" if far else "expand_near",
            **settings(14, 2.6),
        )(*operands)

    pieces = []
    for slot in range(slots):
        piece = own_pack if slot < slots // 2 else other_pack
        piece = swap(piece, "rows", 2 * slot) if slot > 0 else piece
        pieces += [piece, swap(piece, "rows", 1)]
    return expand(True, expand(False))


def solution(mesh):
    return jax.shard_map(
        per_device,
        mesh=mesh,
        in_specs=(
            P(("leaf", "rows"), None),
            P(("leaf", "rows"), None),
            P(("leaf", "rows"), None, None),
            P(None, ("leaf", "rows"), None),
            P(None, ("leaf", "rows"), None),
            P(),
            P(),
        ),
        out_specs=P(("leaf", "rows"), None),
        check_vma=False,
    )
```

```python
import functools

import jax
import jax.numpy as jnp
from jax import lax
from jax.experimental import pallas as pl
from jax.experimental.pallas import tpu as pltpu
from jax.sharding import PartitionSpec as P

HIGHEST = lax.Precision.HIGHEST
MIB = 1 << 20


def dot(a, b, contract, exact=False):
    return lax.dot_general(
        a, b, ((contract[:1], contract[1:]), ((), ())),
        precision=HIGHEST if exact else None, preferred_element_type=jnp.float32,
    )


def halves(value):
    high_part = value.astype(jnp.bfloat16)
    low_part = (value - high_part.astype(jnp.float32)).astype(jnp.bfloat16)
    return high_part, low_part


def swap(value, axis, mask):
    count = lax.axis_size(axis)
    return lax.ppermute(value, axis, [(i, i ^ mask) for i in range(count)])


def blocks_per_step(nblocks, most):
    return max(size for size in range(1, most + 1) if nblocks % size == 0)


def below_pairs(levels, first=0):
    return [(level, below) for level in range(levels) for below in range(first, level)]


def gram_kernel(levels, per_step, width, right_ref, left_ref, flip_ref, keep_ref, send_ref,
                right_buf, left_buf, gram_ref, sems):
    rank = right_ref.shape[2]
    half = rank // 2
    tile = per_step * width
    steps = right_ref.shape[1] // tile

    def copies(step):
        rows = pl.ds(pl.multiple_of(step * tile, tile), tile)
        return (
            pltpu.make_async_copy(right_ref.at[:, rows], right_buf.at[:, rows], sems.at[0, step]),
            pltpu.make_async_copy(left_ref.at[:levels - 1, rows], left_buf.at[:, rows], sems.at[1, step]),
        )

    for step in range(steps):
        for copy in copies(step):
            copy.start()
    gram_ref[...] = jnp.zeros_like(gram_ref)

    def body(step, _):
        for copy in copies(step):
            copy.wait()
        rows = pl.ds(pl.multiple_of(step * tile, tile), tile)
        right = jnp.concatenate([right_buf[l, rows, :] for l in range(levels)], axis=1).T
        flip_ref[:, rows] = right
        left = jnp.concatenate([left_buf[l, rows, :] for l in range(levels - 1)], axis=1)
        gram_ref[...] += dot(right[rank:], left, (1, 0))
        return 0

    lax.fori_loop(0, steps, body, 0)
    core = lax.axis_index("rows") % 2
    for spot, (level, below) in enumerate(below_pairs(levels)):
        lanes = pl.ds(spot * rank, rank)
        for ref, side in ((keep_ref, core), (send_ref, 1 - core)):
            rows = pl.ds(pl.multiple_of((level - 1) * rank + side * half, half), half)
            ref[:, lanes] = gram_ref[rows, pl.ds(below * rank, rank)]


def permute_kernel(per_step, width, order_ref, inv_ref, moved_ref):
    place = lax.broadcasted_iota(jnp.int32, (width, width), 0)

    def body(step, _):
        for b in range(per_step):
            block = step * per_step + b
            chosen = (place == order_ref[pl.ds(block, 1), :]).astype(jnp.float32).astype(jnp.bfloat16)
            moved_ref[block] = dot(inv_ref[block], chosen, (1, 1)).astype(jnp.bfloat16)
        return 0

    lax.fori_loop(0, inv_ref.shape[0] // per_step, body, 0)


def weigh_kernel(per_step, width, moved_ref, flip_ref, after_ref, factor_ref):
    kinds = flip_ref.shape[0]

    def body(step, _):
        for b in range(per_step):
            block = step * per_step + b
            lanes = pl.ds(pl.multiple_of(block * width, width), width)
            high_part, low_part = halves(dot(flip_ref[:, lanes], moved_ref[block], (1, 0)))
            factor_ref[:kinds, lanes] = high_part
            factor_ref[kinds:, lanes] = low_part
        return 0

    lax.fori_loop(0, moved_ref.shape[0] // per_step, body, 0)


def solve_kernel(per_step, width, moved_ref, rhs_ref, after_ref, out_ref):
    def body(step, _):
        for b in range(per_step):
            block = step * per_step + b
            rows = pl.ds(pl.multiple_of(block * width, width), width)
            out_ref[rows, :] = dot(moved_ref[block], rhs_ref[rows, :], (1, 0))
        return 0

    lax.fori_loop(0, moved_ref.shape[0] // per_step, body, 0)


def project_kernel(other, factor_ref, rhs_ref, after_ref, out_ref):
    kinds, part = out_ref.shape
    core = lax.axis_index("rows") % 2
    lanes = pl.ds(pl.multiple_of((1 - core if other else core) * part, part), part)
    total = dot(factor_ref[...], rhs_ref[:, lanes], (1, 0))
    out_ref[...] = total[:kinds] + total[kinds:]


def merge_kernel(keep_ref, got_ref, *refs):
    out_refs, flip_ref = refs[:-1], refs[-1]
    share = out_refs[0].shape[0]
    chip = lax.axis_index("rows") // 2
    flip_ref[...] = (keep_ref[...] + got_ref[...]).T
    for slot, out_ref in enumerate(out_refs):
        out_ref[...] = flip_ref[pl.ds(pl.multiple_of((chip ^ slot) * share, share), share), :]


def add_kernel(mine_ref, got_ref, out_ref):
    out_ref[...] = mine_ref[...] + got_ref[...]


def prepare_kernel(levels, joined_ref, perm_ref, out_ref, joined_buf, sems):
    rank = perm_ref.shape[1]
    leaves = lax.axis_size("leaf")
    leaf = lax.axis_index("leaf")
    copies = []
    for level in range(levels):
        node = 2 * leaves - 2 * leaves // 2 ** level + leaf // 2 ** level
        copies.append(pltpu.make_async_copy(joined_ref.at[node], joined_buf.at[level], sems.at[level]))
        copies[-1].start()
    spot = lax.broadcasted_iota(jnp.int32, (rank, rank), 0)
    for level in range(levels):
        copies[level].wait()
        chosen = (spot == perm_ref[level:level + 1, :]).astype(jnp.float32)
        for side in range(2):
            lanes = pl.ds(side * rank, rank)
            out_ref[level, :, lanes] = dot(joined_buf[level, :, lanes], chosen, (1, 1), True)


def by_side(side, own, other):
    return jnp.where(side == 0, own, other), jnp.where(side == 0, other, own)


def pack_message(message_ref, pieces):
    row = 0
    for piece in pieces:
        message_ref[pl.ds(row, piece.shape[0]), :] = piece
        row += piece.shape[0]


def node_kernel(rank, slots, *refs):
    part_refs = refs[:slots]
    joined_ref, own_ref, other_ref, rest_ref = refs[slots:]
    side = lax.axis_index("rows") // slots
    half = slots // 2
    sums = [sum(ref[...] for ref in part_refs[:half]), sum(ref[...] for ref in part_refs[half:])]
    picked = jnp.concatenate(by_side(side, sums[0][:, :rank], sums[1][:, :rank]), axis=1)
    coef = dot(picked, joined_ref[0], (1, 1), True)
    own_ref[...], other_ref[...] = by_side(side, coef[:, :rank], coef[:, rank:])
    rest_ref[...] = (sums[0] + sums[1])[:, rank:]


def correct_kernel(levels, rank, own_ref, other_ref, rest_ref, mine_ref, theirs_ref, pair_mine_ref,
                   pair_theirs_ref, message_ref):
    core = lax.axis_index("rows") % 2
    grams = [jnp.concatenate(by_side(core, mine_ref[...], pair_mine_ref[...]), axis=0),
             jnp.concatenate(by_side(core, theirs_ref[...], pair_theirs_ref[...]), axis=0)]
    pairs = below_pairs(levels)
    lanes = {pair: slice(spot * rank, (spot + 1) * rank) for spot, pair in enumerate(pairs)}
    joint = jnp.concatenate(
        [jnp.concatenate([gram[:, lanes[level, 0]] for gram in grams], axis=1) for level in range(1, levels)], axis=0)
    rest = rest_ref[...] - dot(jnp.concatenate([own_ref[...], other_ref[...]], axis=1), joint, (1, 1), True)
    pieces = [rest[:, level * rank:(level + 1) * rank] for level in range(levels - 1)]
    for pair in pairs:
        if pair[1] > 0:
            pieces.append(grams[0][:, lanes[pair]] + grams[1][:, lanes[pair]])
    pack_message(message_ref, pieces)


def level_kernel(levels, level, share, sent_ref, got_ref, joined_ref, after_ref, coef_ref, *message_ref):
    rank = sent_ref.shape[1]
    side = lax.axis_index("leaf") // 2 ** (level - 1) % 2
    more = levels - level
    values = []
    for ref in (sent_ref, got_ref):
        values.append([ref[pl.ds(i * share, share), :] for i in range(more)])
    picked = jnp.concatenate(by_side(side, values[0][0], values[1][0]), axis=1)
    coef = dot(picked, joined_ref[level], (1, 1), True)
    sides = by_side(side, coef[:, :rank], coef[:, rank:])
    coef_ref[...] = sides[0]
    if not message_ref:
        return
    pairs = below_pairs(levels, level)
    grams = []
    for ref in (sent_ref, got_ref):
        grams.append({pair: ref[pl.ds(more * share + spot * rank, rank), :] for spot, pair in enumerate(pairs)})
    uppers = list(range(level + 1, levels))
    joint = jnp.concatenate(
        [jnp.concatenate([gram[upper, level] for gram in grams], axis=1) for upper in uppers], axis=0)
    change = dot(jnp.concatenate(sides, axis=1), joint, (1, 1), True)
    pieces = [values[0][upper - level] + values[1][upper - level] - change[:, i * rank:(i + 1) * rank]
              for i, upper in enumerate(uppers)]
    for pair in pairs:
        if pair[1] > level:
            pieces.append(grams[0][pair] + grams[1][pair])
    pack_message(message_ref[0], pieces)


def pack_kernel(*refs):
    other_ref, own_refs, own_out, other_out = refs[0], refs[1:-2], refs[-2], refs[-1]
    own = [ref[...] for ref in own_refs]
    own_out[...] = jnp.concatenate(own, axis=1)
    other_out[...] = jnp.concatenate([other_ref[...]] + own[1:], axis=1)


def expand_kernel(levels, tile, count, *refs):
    piece_refs = refs[:count]
    first_ref, left_ref, out_ref, flip_ref, factor_ref, out_buf, sems = refs[count:]
    share, kinds = piece_refs[0].shape
    me = lax.axis_index("rows")
    for slot, ref in enumerate(piece_refs):
        owner = me ^ slot
        row = (owner % 2 * (count // 2) + owner // 2) * share
        flip_ref[pl.ds(pl.multiple_of(row, share), share), :] = ref[...]
    high_part, low_part = halves(flip_ref[...].T)
    factor_ref[:kinds, :] = high_part
    factor_ref[kinds:, :] = low_part
    copies = []
    for step in range(out_buf.shape[0] // tile):
        rows = pl.ds(step * tile, tile)
        left = jnp.concatenate([left_ref[l, rows, :] for l in range(levels)] * 2, axis=1)
        out_buf[rows, :] = first_ref[rows, :] - dot(left, factor_ref[...], (1, 0))
        copies.append(pltpu.make_async_copy(out_buf.at[rows], out_ref.at[rows], sems.at[step]))
        copies[-1].start(priority=step % 2)
    for copy in copies:
        copy.wait()


def settings(mib, micros):
    return dict(
        compiler_params=pltpu.CompilerParams(vmem_limit_bytes=mib * MIB),
        cost_estimate=pl.CostEstimate(flops=int(micros * 1.1e9), bytes_accessed=0, transcendentals=0),
    )


def floats(*shape):
    return jax.ShapeDtypeStruct(shape, jnp.float32)


def per_device(rhs, leaf_order, leaf_inv, right_basis, left_basis, rank_perm, joined):
    levels, rows, rank = right_basis.shape
    nblocks, width, _ = leaf_inv.shape
    columns = rhs.shape[1]
    leaves = lax.axis_size("leaf")
    count = lax.axis_size("rows")
    slots = count // 2
    kinds = levels * rank
    size = kinds - rank
    share = columns // count
    gram_lanes = len(below_pairs(levels)) * rank

    per_step = blocks_per_step(nblocks, 3)
    flipped, gram_keep, gram_send = pl.pallas_call(
        functools.partial(gram_kernel, levels, per_step, width),
        in_specs=[pl.BlockSpec(memory_space=pltpu.HBM)] * 2,
        out_shape=[jax.ShapeDtypeStruct((kinds, rows), jnp.bfloat16)] + [floats(rank // 2, gram_lanes)] * 2,
        scratch_shapes=[
            pltpu.VMEM((levels, rows, rank), jnp.bfloat16),
            pltpu.VMEM((levels - 1, rows, rank), jnp.bfloat16),
            pltpu.VMEM((size, size), jnp.float32),
            pltpu.SemaphoreType.DMA((2, nblocks // per_step)),
        ],
        name="gram",
        **settings(24, 3),
    )(pltpu.with_memory_space_constraint(right_basis, pltpu.HBM),
      pltpu.with_memory_space_constraint(left_basis, pltpu.HBM))
    gram_got = swap(gram_send, "rows", 1)

    moved = pl.pallas_call(
        functools.partial(permute_kernel, blocks_per_step(nblocks, 6), width),
        out_shape=jax.ShapeDtypeStruct((nblocks, width, width), jnp.bfloat16),
        name="permute",
        **settings(8, 1.5),
    )(leaf_order, leaf_inv)

    def add(mine, got):
        return pl.pallas_call(
            add_kernel, out_shape=floats(*mine.shape), name="add", **settings(8, 0.1),
        )(mine, got)

    gram = add(gram_keep, gram_got)
    factors = pl.pallas_call(
        functools.partial(weigh_kernel, per_step, width),
        out_shape=jax.ShapeDtypeStruct((2 * kinds, rows), jnp.bfloat16),
        name="weigh",
        **settings(8, 2.4),
    )(moved, flipped, gram)

    def project(other, after):
        return pl.pallas_call(
            functools.partial(project_kernel, other),
            out_shape=floats(kinds, columns // 2),
            name="project_other" if other else "project_own",
            **settings(12, 1 if other else 8),
        )(factors, rhs, after)

    send = project(True, gram)
    got = swap(send, "rows", 1)
    mask = 2
    while mask < slots:
        gram = add(gram, swap(gram, "rows", mask))
        mask *= 2
    keep = project(False, gram)
    merged = pl.pallas_call(
        merge_kernel,
        out_shape=[floats(share, kinds)] * slots,
        scratch_shapes=[pltpu.VMEM((columns // 2, kinds), jnp.float32)],
        name="merge",
        **settings(8, 0.4),
    )(keep, got)
    parts = [merged[0]] + [swap(merged[s], "rows", 2 * s) for s in range(1, slots)]
    gram_other = swap(gram, "rows", slots)
    grams = [gram, gram_other, swap(gram, "rows", 1), swap(gram_other, "rows", 1)]
    first = pl.pallas_call(
        functools.partial(solve_kernel, per_step, width),
        out_shape=floats(rows, columns),
        name="solve",
        **settings(8, 1.7),
    )(moved, rhs, merged[0])

    prepared = pl.pallas_call(
        functools.partial(prepare_kernel, levels),
        in_specs=[pl.BlockSpec(memory_space=pltpu.HBM), pl.BlockSpec()],
        out_shape=floats(levels, 2 * rank, 2 * rank),
        scratch_shapes=[pltpu.VMEM((levels, 2 * rank, 2 * rank), jnp.float32), pltpu.SemaphoreType.DMA((levels,))],
        name="prepare",
        **settings(8, 2),
    )(pltpu.with_memory_space_constraint(joined, pltpu.HBM), rank_perm)

    def message_shape(level):
        return floats((levels - level) * share + len(below_pairs(levels, level)) * rank, rank)

    own, other, rest = pl.pallas_call(
        functools.partial(node_kernel, rank, slots),
        out_shape=[floats(share, rank)] * 2 + [floats(share, size)],
        name="node",
        **settings(8, 1),
    )(*parts, prepared)
    message = pl.pallas_call(
        functools.partial(correct_kernel, levels, rank),
        out_shape=message_shape(1),
        name="correct",
        **settings(8, 1),
    )(own, other, rest, *grams)
    coefs = [own]
    for level in range(1, levels):
        last = level + 1 == levels
        arrived = swap(message, "leaf", 2 ** (level - 1))
        outs = pl.pallas_call(
            functools.partial(level_kernel, levels, level, share),
            out_shape=[floats(share, rank)] + ([] if last else [message_shape(level + 1)]),
            name=f"level{level}",
            **settings(8, 0.7),
        )(message, arrived, prepared, first)
        coefs.append(outs[0])
        message = outs[-1]

    packs = pl.pallas_call(
        pack_kernel, out_shape=[floats(share, kinds)] * 2, name="pack", **settings(8, 0.1),
    )(other, *coefs)
    pieces = []
    for slot in range(slots):
        piece = packs[0 if slot < slots // 2 else 1]
        piece = swap(piece, "rows", 2 * slot) if slot > 0 else piece
        pieces += [piece, swap(piece, "rows", 1)]
    return pl.pallas_call(
        functools.partial(expand_kernel, levels, per_step * width, count),
        out_specs=pl.BlockSpec(memory_space=pl.ANY),
        out_shape=floats(rows, columns),
        scratch_shapes=[
            pltpu.VMEM((columns, kinds), jnp.float32),
            pltpu.VMEM((2 * kinds, columns), jnp.bfloat16),
            pltpu.VMEM((rows, columns), jnp.float32),
            pltpu.SemaphoreType.DMA((nblocks // per_step,)),
        ],
        name="expand",
        **settings(16, 5),
    )(*pieces, first, left_basis)


def solution(mesh):
    return jax.shard_map(
        per_device,
        mesh=mesh,
        in_specs=(
            P(("leaf", "rows"), None),
            P(("leaf", "rows"), None),
            P(("leaf", "rows"), None, None),
            P(None, ("leaf", "rows"), None),
            P(None, ("leaf", "rows"), None),
            P(),
            P(),
        ),
        out_specs=P(("leaf", "rows"), None),
        check_vma=False,
    )
```

```python
import functools

import jax
import jax.numpy as jnp
from jax import lax
from jax.experimental import pallas as pl
from jax.experimental.pallas import tpu as pltpu
from jax.sharding import PartitionSpec as P

HIGHEST = lax.Precision.HIGHEST
MIB = 1 << 20


def dot(a, b, contract, exact=False):
    return lax.dot_general(
        a, b, ((contract[:1], contract[1:]), ((), ())),
        precision=HIGHEST if exact else None, preferred_element_type=jnp.float32,
    )


def halves(value):
    high_part = value.astype(jnp.bfloat16)
    low_part = (value - high_part.astype(jnp.float32)).astype(jnp.bfloat16)
    return high_part, low_part


def swap(value, axis, mask):
    count = lax.axis_size(axis)
    return lax.ppermute(value, axis, [(i, i ^ mask) for i in range(count)])


def blocks_per_step(nblocks, most):
    return max(size for size in range(1, most + 1) if nblocks % size == 0)


def below_pairs(levels, first=0):
    return [(level, below) for level in range(levels) for below in range(first, level)]


def gram_kernel(levels, per_step, width, right_ref, left_ref, flip_ref, out_ref,
                right_buf, left_buf, gram_ref, sems):
    rank = right_ref.shape[2]
    tile = per_step * width
    steps = right_ref.shape[1] // tile

    def copies(step):
        rows = pl.ds(pl.multiple_of(step * tile, tile), tile)
        return (
            pltpu.make_async_copy(right_ref.at[:, rows], right_buf.at[:, rows], sems.at[0, step]),
            pltpu.make_async_copy(left_ref.at[:levels - 1, rows], left_buf.at[:, rows], sems.at[1, step]),
        )

    for step in range(steps):
        for copy in copies(step):
            copy.start()
    gram_ref[...] = jnp.zeros_like(gram_ref)

    def body(step, _):
        for copy in copies(step):
            copy.wait()
        rows = pl.ds(pl.multiple_of(step * tile, tile), tile)
        right = jnp.concatenate([right_buf[l, rows, :] for l in range(levels)], axis=1).T
        flip_ref[:, rows] = right
        left = jnp.concatenate([left_buf[l, rows, :] for l in range(levels - 1)], axis=1)
        gram_ref[...] += dot(right[rank:], left, (1, 0))
        return 0

    lax.fori_loop(0, steps, body, 0)
    for spot, (level, below) in enumerate(below_pairs(levels)):
        rows = pl.ds((level - 1) * rank, rank)
        out_ref[:, pl.ds(spot * rank, rank)] = gram_ref[rows, pl.ds(below * rank, rank)]


def permute_kernel(per_step, width, order_ref, inv_ref, moved_ref):
    place = lax.broadcasted_iota(jnp.int32, (width, width), 0)

    def body(step, _):
        for b in range(per_step):
            block = step * per_step + b
            chosen = (place == order_ref[pl.ds(block, 1), :]).astype(jnp.float32).astype(jnp.bfloat16)
            moved_ref[block] = dot(inv_ref[block], chosen, (1, 1)).astype(jnp.bfloat16)
        return 0

    lax.fori_loop(0, inv_ref.shape[0] // per_step, body, 0)


def weigh_kernel(per_step, width, moved_ref, flip_ref, after_ref, factor_ref):
    kinds = flip_ref.shape[0]

    def body(step, _):
        for b in range(per_step):
            block = step * per_step + b
            lanes = pl.ds(pl.multiple_of(block * width, width), width)
            high_part, low_part = halves(dot(flip_ref[:, lanes], moved_ref[block], (1, 0)))
            factor_ref[:kinds, lanes] = high_part
            factor_ref[kinds:, lanes] = low_part
        return 0

    lax.fori_loop(0, moved_ref.shape[0] // per_step, body, 0)


def solve_kernel(per_step, width, moved_ref, rhs_ref, *refs):
    out_ref = refs[-1]

    def body(step, _):
        for b in range(per_step):
            block = step * per_step + b
            rows = pl.ds(pl.multiple_of(block * width, width), width)
            out_ref[rows, :] = dot(moved_ref[block], rhs_ref[rows, :], (1, 0))
        return 0

    lax.fori_loop(0, moved_ref.shape[0] // per_step, body, 0)


def project_kernel(other, factor_ref, rhs_ref, after_ref, out_ref):
    kinds, part = out_ref.shape
    core = lax.axis_index("rows") % 2
    lanes = pl.ds(pl.multiple_of((1 - core if other else core) * part, part), part)
    total = dot(factor_ref[...], rhs_ref[:, lanes], (1, 0))
    out_ref[...] = total[:kinds] + total[kinds:]


def merge_kernel(keep_ref, got_ref, *refs):
    out_refs, flip_ref = refs[:-1], refs[-1]
    share = out_refs[0].shape[0]
    chip = lax.axis_index("rows") // 2
    flip_ref[...] = (keep_ref[...] + got_ref[...]).T
    for slot, out_ref in enumerate(out_refs):
        out_ref[...] = flip_ref[pl.ds(pl.multiple_of((chip ^ slot) * share, share), share), :]


def add_kernel(mine_ref, got_ref, out_ref):
    out_ref[...] = mine_ref[...] + got_ref[...]


def prepare_kernel(levels, joined_ref, perm_ref, out_ref, joined_buf, sems):
    rank = perm_ref.shape[1]
    leaves = lax.axis_size("leaf")
    leaf = lax.axis_index("leaf")
    copies = []
    for level in range(levels):
        node = 2 * leaves - 2 * leaves // 2 ** level + leaf // 2 ** level
        copies.append(pltpu.make_async_copy(joined_ref.at[node], joined_buf.at[level], sems.at[level]))
        copies[-1].start()
    spot = lax.broadcasted_iota(jnp.int32, (rank, rank), 0)
    for level in range(levels):
        copies[level].wait()
        chosen = (spot == perm_ref[level:level + 1, :]).astype(jnp.float32)
        for side in range(2):
            lanes = pl.ds(side * rank, rank)
            out_ref[level, :, lanes] = dot(joined_buf[level, :, lanes], chosen, (1, 1), True)


def by_side(side, own, other):
    return jnp.where(side == 0, own, other), jnp.where(side == 0, other, own)


def pack_message(message_ref, pieces):
    row = 0
    for piece in pieces:
        message_ref[pl.ds(row, piece.shape[0]), :] = piece
        row += piece.shape[0]


def node_kernel(rank, slots, *refs):
    part_refs = refs[:slots]
    joined_ref, own_ref, other_ref, rest_ref = refs[slots:]
    side = lax.axis_index("rows") // slots
    half = slots // 2
    sums = [sum(ref[...] for ref in part_refs[:half]), sum(ref[...] for ref in part_refs[half:])]
    picked = jnp.concatenate(by_side(side, sums[0][:, :rank], sums[1][:, :rank]), axis=1)
    coef = dot(picked, joined_ref[0], (1, 1), True)
    own_ref[...], other_ref[...] = by_side(side, coef[:, :rank], coef[:, rank:])
    rest_ref[...] = (sums[0] + sums[1])[:, rank:]


def correct_kernel(levels, rank, own_ref, other_ref, rest_ref, mine_ref, theirs_ref, pair_mine_ref,
                   pair_theirs_ref, message_ref):
    grams = [mine_ref[...] + pair_mine_ref[...], theirs_ref[...] + pair_theirs_ref[...]]
    pairs = below_pairs(levels)
    lanes = {pair: slice(spot * rank, (spot + 1) * rank) for spot, pair in enumerate(pairs)}
    joint = jnp.concatenate(
        [jnp.concatenate([gram[:, lanes[level, 0]] for gram in grams], axis=1) for level in range(1, levels)], axis=0)
    rest = rest_ref[...] - dot(jnp.concatenate([own_ref[...], other_ref[...]], axis=1), joint, (1, 1), True)
    pieces = [rest[:, level * rank:(level + 1) * rank] for level in range(levels - 1)]
    for pair in pairs:
        if pair[1] > 0:
            pieces.append(grams[0][:, lanes[pair]] + grams[1][:, lanes[pair]])
    pack_message(message_ref, pieces)


def level_kernel(levels, level, share, sent_ref, got_ref, joined_ref, after_ref, coef_ref, *message_ref):
    rank = sent_ref.shape[1]
    side = lax.axis_index("leaf") // 2 ** (level - 1) % 2
    more = levels - level
    values = []
    for ref in (sent_ref, got_ref):
        values.append([ref[pl.ds(i * share, share), :] for i in range(more)])
    picked = jnp.concatenate(by_side(side, values[0][0], values[1][0]), axis=1)
    coef = dot(picked, joined_ref[level], (1, 1), True)
    sides = by_side(side, coef[:, :rank], coef[:, rank:])
    coef_ref[...] = sides[0]
    if not message_ref:
        return
    pairs = below_pairs(levels, level)
    grams = []
    for ref in (sent_ref, got_ref):
        grams.append({pair: ref[pl.ds(more * share + spot * rank, rank), :] for spot, pair in enumerate(pairs)})
    uppers = list(range(level + 1, levels))
    joint = jnp.concatenate(
        [jnp.concatenate([gram[upper, level] for gram in grams], axis=1) for upper in uppers], axis=0)
    change = dot(jnp.concatenate(sides, axis=1), joint, (1, 1), True)
    pieces = [values[0][upper - level] + values[1][upper - level] - change[:, i * rank:(i + 1) * rank]
              for i, upper in enumerate(uppers)]
    for pair in pairs:
        if pair[1] > level:
            pieces.append(grams[0][pair] + grams[1][pair])
    pack_message(message_ref[0], pieces)


def pack_kernel(*refs):
    refs[-1][...] = jnp.concatenate([ref[...] for ref in refs[:-1]], axis=1)


def stack_kernel(after_ref, *refs):
    for slot, ref in enumerate(refs[:-1]):
        refs[-1][slot] = ref[...]


def split_factor(pieces, flip_ref, factor_ref):
    share, kinds = pieces[0].shape
    slots = len(pieces) // 2
    me = lax.axis_index("rows")
    for mask, ref in enumerate(pieces):
        owner = me ^ mask
        row = (owner % 2 * slots + owner // 2) * share
        flip_ref[pl.ds(pl.multiple_of(row, share), share), :] = ref[...]
    high_part, low_part = halves(flip_ref[...].T)
    factor_ref[:kinds, :] = high_part
    factor_ref[kinds:, :] = low_part


def apply_kernel(tile, own_ref, pair_ref, first_ref, left_ref, out_ref, flip_ref, factor_ref):
    pieces = [ref.at[slot] for slot in range(own_ref.shape[0]) for ref in (own_ref, pair_ref)]
    split_factor(pieces, flip_ref, factor_ref)
    for row in range(0, out_ref.shape[0], tile):
        rows = pl.ds(row, tile)
        left = jnp.concatenate([left_ref[0, rows, :]] * 2, axis=1)
        out_ref[rows, :] = first_ref[rows, :] - dot(left, factor_ref[...], (1, 0))


def expand_kernel(levels, tile, count, *refs):
    piece_refs = refs[:count]
    first_ref, left_ref, out_ref, flip_ref, factor_ref, out_buf, sems = refs[count:]
    split_factor(piece_refs, flip_ref, factor_ref)
    copies = []
    for step in range(out_buf.shape[0] // tile):
        rows = pl.ds(step * tile, tile)
        left = jnp.concatenate([left_ref[l, rows, :] for l in range(1, levels)] * 2, axis=1)
        out_buf[rows, :] = first_ref[rows, :] - dot(left, factor_ref[...], (1, 0))
        copies.append(pltpu.make_async_copy(out_buf.at[rows], out_ref.at[rows], sems.at[step]))
        copies[-1].start(priority=step % 2)
    for copy in copies:
        copy.wait()


def settings(mib, micros):
    return dict(
        compiler_params=pltpu.CompilerParams(vmem_limit_bytes=mib * MIB),
        cost_estimate=pl.CostEstimate(flops=int(micros * 1.1e9), bytes_accessed=0, transcendentals=0),
    )


def floats(*shape):
    return jax.ShapeDtypeStruct(shape, jnp.float32)


def per_device(rhs, leaf_order, leaf_inv, right_basis, left_basis, rank_perm, joined):
    levels, rows, rank = right_basis.shape
    nblocks, width, _ = leaf_inv.shape
    columns = rhs.shape[1]
    leaves = lax.axis_size("leaf")
    count = lax.axis_size("rows")
    slots = count // 2
    kinds = levels * rank
    size = kinds - rank
    share = columns // count
    gram_lanes = len(below_pairs(levels)) * rank

    per_step = blocks_per_step(nblocks, 3)
    flipped, gram = pl.pallas_call(
        functools.partial(gram_kernel, levels, per_step, width),
        in_specs=[pl.BlockSpec(memory_space=pltpu.HBM)] * 2,
        out_shape=[jax.ShapeDtypeStruct((kinds, rows), jnp.bfloat16), floats(rank, gram_lanes)],
        scratch_shapes=[
            pltpu.VMEM((levels, rows, rank), jnp.bfloat16),
            pltpu.VMEM((levels - 1, rows, rank), jnp.bfloat16),
            pltpu.VMEM((size, size), jnp.float32),
            pltpu.SemaphoreType.DMA((2, nblocks // per_step)),
        ],
        name="gram",
        **settings(24, 3),
    )(pltpu.with_memory_space_constraint(right_basis, pltpu.HBM),
      pltpu.with_memory_space_constraint(left_basis, pltpu.HBM))

    moved = pl.pallas_call(
        functools.partial(permute_kernel, blocks_per_step(nblocks, 6), width),
        out_shape=jax.ShapeDtypeStruct((nblocks, width, width), jnp.bfloat16),
        name="permute",
        **settings(8, 1.5),
    )(leaf_order, leaf_inv)

    def add(mine, got):
        return pl.pallas_call(
            add_kernel, out_shape=floats(*mine.shape), name="add", **settings(8, 0.1),
        )(mine, got)

    factors = pl.pallas_call(
        functools.partial(weigh_kernel, per_step, width),
        out_shape=jax.ShapeDtypeStruct((2 * kinds, rows), jnp.bfloat16),
        name="weigh",
        **settings(8, 2.4),
    )(moved, flipped, gram)

    def project(other, after):
        return pl.pallas_call(
            functools.partial(project_kernel, other),
            out_shape=floats(kinds, columns // 2),
            name="project_other" if other else "project_own",
            **settings(12, 1 if other else 8),
        )(factors, rhs, after)

    send = project(True, gram)
    got = swap(send, "rows", 1)
    mask = 2
    while mask < slots:
        gram = add(gram, swap(gram, "rows", mask))
        mask *= 2
    keep = project(False, gram)
    merged = pl.pallas_call(
        merge_kernel,
        out_shape=[floats(share, kinds)] * slots,
        scratch_shapes=[pltpu.VMEM((columns // 2, kinds), jnp.float32)],
        name="merge",
        **settings(8, 0.4),
    )(keep, got)
    parts = [merged[0]] + [swap(merged[s], "rows", 2 * s) for s in range(1, slots)]
    gram_other = swap(gram, "rows", slots)
    grams = [gram, gram_other, swap(gram, "rows", 1), swap(gram_other, "rows", 1)]
    prepared = pl.pallas_call(
        functools.partial(prepare_kernel, levels),
        in_specs=[pl.BlockSpec(memory_space=pltpu.HBM), pl.BlockSpec()],
        out_shape=floats(levels, 2 * rank, 2 * rank),
        scratch_shapes=[pltpu.VMEM((levels, 2 * rank, 2 * rank), jnp.float32), pltpu.SemaphoreType.DMA((levels,))],
        name="prepare",
        **settings(8, 2),
    )(pltpu.with_memory_space_constraint(joined, pltpu.HBM), rank_perm)

    def message_shape(level):
        return floats((levels - level) * share + len(below_pairs(levels, level)) * rank, rank)

    own, other, rest = pl.pallas_call(
        functools.partial(node_kernel, rank, slots),
        out_shape=[floats(share, rank)] * 2 + [floats(share, size)],
        name="node",
        **settings(8, 1),
    )(*parts, prepared)
    message = pl.pallas_call(
        functools.partial(correct_kernel, levels, rank),
        out_shape=message_shape(1),
        name="correct",
        **settings(8, 1),
    )(own, other, rest, *grams)
    early = [own] + [swap(own if slot < slots // 2 else other, "rows", 2 * slot) for slot in range(1, slots)]
    first = pl.pallas_call(
        functools.partial(solve_kernel, per_step, width),
        out_shape=floats(rows, columns),
        name="solve",
        **settings(8, 8),
    )(moved, rhs, merged[0])

    coefs = []
    for level in range(1, levels):
        last = level + 1 == levels
        arrived = swap(message, "leaf", 2 ** (level - 1))
        outs = pl.pallas_call(
            functools.partial(level_kernel, levels, level, share),
            out_shape=[floats(share, rank)] + ([] if last else [message_shape(level + 1)]),
            name=f"level{level}",
            **settings(8, 1 if last else 6),
        )(message, arrived, prepared, first if last else arrived)
        coefs.append(outs[0])
        message = outs[-1]
    stack = pl.pallas_call(
        stack_kernel, out_shape=floats(slots, share, rank), name="stack", **settings(8, 0.1),
    )(first, *early)
    second = pl.pallas_call(
        functools.partial(apply_kernel, per_step * width),
        out_shape=floats(rows, columns),
        scratch_shapes=[
            pltpu.VMEM((columns, rank), jnp.float32),
            pltpu.VMEM((2 * rank, columns), jnp.bfloat16),
        ],
        name="apply",
        **settings(8, 1.8),
    )(stack, swap(stack, "rows", 1), first, left_basis)

    pack = pl.pallas_call(
        pack_kernel, out_shape=floats(share, size), name="pack", **settings(8, 0.1),
    )(*coefs)
    pieces = []
    for slot in range(slots):
        piece = swap(pack, "rows", 2 * slot) if slot > 0 else pack
        pieces += [piece, swap(piece, "rows", 1)]
    return pl.pallas_call(
        functools.partial(expand_kernel, levels, per_step * width, count),
        out_specs=pl.BlockSpec(memory_space=pl.ANY),
        out_shape=floats(rows, columns),
        scratch_shapes=[
            pltpu.VMEM((columns, size), jnp.float32),
            pltpu.VMEM((2 * size, columns), jnp.bfloat16),
            pltpu.VMEM((rows, columns), jnp.float32),
            pltpu.SemaphoreType.DMA((nblocks // per_step,)),
        ],
        name="expand",
        **settings(16, 5),
    )(*pieces, second, left_basis)


def solution(mesh):
    return jax.shard_map(
        per_device,
        mesh=mesh,
        in_specs=(
            P(("leaf", "rows"), None),
            P(("leaf", "rows"), None),
            P(("leaf", "rows"), None, None),
            P(None, ("leaf", "rows"), None),
            P(None, ("leaf", "rows"), None),
            P(),
            P(),
        ),
        out_specs=P(("leaf", "rows"), None),
        check_vma=False,
    )
```

```python
import functools

import jax
import jax.numpy as jnp
from jax import lax
from jax.experimental import pallas as pl
from jax.experimental.pallas import tpu as pltpu
from jax.sharding import PartitionSpec as P

HIGHEST = lax.Precision.HIGHEST
MIB = 1 << 20


def dot(a, b, contract, exact=False):
    return lax.dot_general(
        a, b, ((contract[:1], contract[1:]), ((), ())),
        precision=HIGHEST if exact else None, preferred_element_type=jnp.float32,
    )


def halves(value):
    high_part = value.astype(jnp.bfloat16)
    low_part = (value - high_part.astype(jnp.float32)).astype(jnp.bfloat16)
    return high_part, low_part


def swap(value, axis, mask):
    count = lax.axis_size(axis)
    return lax.ppermute(value, axis, [(i, i ^ mask) for i in range(count)])


def blocks_per_step(nblocks, most):
    return max(size for size in range(1, most + 1) if nblocks % size == 0)


def below_pairs(levels, first=0):
    return [(level, below) for level in range(levels) for below in range(first, level)]


def gram_kernel(levels, per_step, width, right_ref, left_ref, flip_ref, out_ref,
                right_buf, left_buf, gram_ref, sems):
    rank = right_ref.shape[2]
    tile = per_step * width
    steps = right_ref.shape[1] // tile

    def copies(step):
        rows = pl.ds(pl.multiple_of(step * tile, tile), tile)
        return (
            pltpu.make_async_copy(right_ref.at[:, rows], right_buf.at[:, rows], sems.at[0, step]),
            pltpu.make_async_copy(left_ref.at[:levels - 1, rows], left_buf.at[:, rows], sems.at[1, step]),
        )

    for step in range(steps):
        for copy in copies(step):
            copy.start()
    gram_ref[...] = jnp.zeros_like(gram_ref)

    def body(step, _):
        for copy in copies(step):
            copy.wait()
        rows = pl.ds(pl.multiple_of(step * tile, tile), tile)
        right = jnp.concatenate([right_buf[l, rows, :] for l in range(levels)], axis=1).T
        flip_ref[:, rows] = right
        left = jnp.concatenate([left_buf[l, rows, :] for l in range(levels - 1)], axis=1)
        gram_ref[...] += dot(right[rank:], left, (1, 0))
        return 0

    lax.fori_loop(0, steps, body, 0)
    for spot, (level, below) in enumerate(below_pairs(levels)):
        rows = pl.ds((level - 1) * rank, rank)
        out_ref[:, pl.ds(spot * rank, rank)] = gram_ref[rows, pl.ds(below * rank, rank)]


def permute_kernel(per_step, width, order_ref, inv_ref, moved_ref):
    place = lax.broadcasted_iota(jnp.int32, (width, width), 0)

    def body(step, _):
        for b in range(per_step):
            block = step * per_step + b
            chosen = (place == order_ref[pl.ds(block, 1), :]).astype(jnp.float32).astype(jnp.bfloat16)
            moved_ref[block] = dot(inv_ref[block], chosen, (1, 1)).astype(jnp.bfloat16)
        return 0

    lax.fori_loop(0, inv_ref.shape[0] // per_step, body, 0)


def weigh_kernel(per_step, width, moved_ref, flip_ref, after_ref, factor_ref):
    kinds = flip_ref.shape[0]

    def body(step, _):
        for b in range(per_step):
            block = step * per_step + b
            lanes = pl.ds(pl.multiple_of(block * width, width), width)
            high_part, low_part = halves(dot(flip_ref[:, lanes], moved_ref[block], (1, 0)))
            factor_ref[:kinds, lanes] = high_part
            factor_ref[kinds:, lanes] = low_part
        return 0

    lax.fori_loop(0, moved_ref.shape[0] // per_step, body, 0)


def solve_kernel(per_step, width, moved_ref, rhs_ref, *refs):
    out_ref = refs[-1]

    def body(step, _):
        for b in range(per_step):
            block = step * per_step + b
            rows = pl.ds(pl.multiple_of(block * width, width), width)
            out_ref[rows, :] = dot(moved_ref[block], rhs_ref[rows, :], (1, 0))
        return 0

    lax.fori_loop(0, moved_ref.shape[0] // per_step, body, 0)


def project_kernel(other, factor_ref, rhs_ref, after_ref, out_ref):
    kinds, part = out_ref.shape
    core = lax.axis_index("rows") % 2
    lanes = pl.ds(pl.multiple_of((1 - core if other else core) * part, part), part)
    total = dot(factor_ref[...], rhs_ref[:, lanes], (1, 0))
    out_ref[...] = total[:kinds] + total[kinds:]


def merge_kernel(keep_ref, got_ref, *refs):
    out_refs, flip_ref = refs[:-1], refs[-1]
    share = out_refs[0].shape[0]
    chip = lax.axis_index("rows") // 2
    flip_ref[...] = (keep_ref[...] + got_ref[...]).T
    for slot, out_ref in enumerate(out_refs):
        out_ref[...] = flip_ref[pl.ds(pl.multiple_of((chip ^ slot) * share, share), share), :]


def add_kernel(mine_ref, got_ref, out_ref):
    out_ref[...] = mine_ref[...] + got_ref[...]


def prepare_kernel(levels, joined_ref, perm_ref, out_ref, joined_buf, sems):
    rank = perm_ref.shape[1]
    leaves = lax.axis_size("leaf")
    leaf = lax.axis_index("leaf")
    copies = []
    for level in range(levels):
        node = 2 * leaves - 2 * leaves // 2 ** level + leaf // 2 ** level
        copies.append(pltpu.make_async_copy(joined_ref.at[node], joined_buf.at[level], sems.at[level]))
        copies[-1].start()
    spot = lax.broadcasted_iota(jnp.int32, (rank, rank), 0)
    for level in range(levels):
        copies[level].wait()
        chosen = (spot == perm_ref[level:level + 1, :]).astype(jnp.float32)
        for side in range(2):
            lanes = pl.ds(side * rank, rank)
            out_ref[level, :, lanes] = dot(joined_buf[level, :, lanes], chosen, (1, 1), True)


def by_side(side, own, other):
    return jnp.where(side == 0, own, other), jnp.where(side == 0, other, own)


def pack_message(message_ref, pieces):
    row = 0
    for piece in pieces:
        message_ref[pl.ds(row, piece.shape[0]), :] = piece
        row += piece.shape[0]


def node_kernel(rank, slots, *refs):
    part_refs = refs[:slots]
    joined_ref, own_ref, other_ref, rest_ref = refs[slots:]
    side = lax.axis_index("rows") // slots
    half = slots // 2
    sums = [sum(ref[...] for ref in part_refs[:half]), sum(ref[...] for ref in part_refs[half:])]
    picked = jnp.concatenate(by_side(side, sums[0][:, :rank], sums[1][:, :rank]), axis=1)
    coef = dot(picked, joined_ref[0], (1, 1), True)
    own_ref[...], other_ref[...] = by_side(side, coef[:, :rank], coef[:, rank:])
    rest_ref[...] = (sums[0] + sums[1])[:, rank:]


def correct_kernel(levels, rank, own_ref, other_ref, rest_ref, mine_ref, theirs_ref, pair_mine_ref,
                   pair_theirs_ref, message_ref, share_ref):
    grams = [mine_ref[...] + pair_mine_ref[...], theirs_ref[...] + pair_theirs_ref[...]]
    share_ref[...] = other_ref[...]
    pairs = below_pairs(levels)
    lanes = {pair: slice(spot * rank, (spot + 1) * rank) for spot, pair in enumerate(pairs)}
    joint = jnp.concatenate(
        [jnp.concatenate([gram[:, lanes[level, 0]] for gram in grams], axis=1) for level in range(1, levels)], axis=0)
    rest = rest_ref[...] - dot(jnp.concatenate([own_ref[...], other_ref[...]], axis=1), joint, (1, 1), True)
    pieces = [rest[:, level * rank:(level + 1) * rank] for level in range(levels - 1)]
    for pair in pairs:
        if pair[1] > 0:
            pieces.append(grams[0][:, lanes[pair]] + grams[1][:, lanes[pair]])
    pack_message(message_ref, pieces)


def level_kernel(levels, level, share, sent_ref, got_ref, joined_ref, after_ref, coef_ref, *message_ref):
    rank = sent_ref.shape[1]
    side = lax.axis_index("leaf") // 2 ** (level - 1) % 2
    more = levels - level
    values = []
    for ref in (sent_ref, got_ref):
        values.append([ref[pl.ds(i * share, share), :] for i in range(more)])
    picked = jnp.concatenate(by_side(side, values[0][0], values[1][0]), axis=1)
    coef = dot(picked, joined_ref[level], (1, 1), True)
    sides = by_side(side, coef[:, :rank], coef[:, rank:])
    coef_ref[...] = sides[0]
    if not message_ref:
        return
    pairs = below_pairs(levels, level)
    grams = []
    for ref in (sent_ref, got_ref):
        grams.append({pair: ref[pl.ds(more * share + spot * rank, rank), :] for spot, pair in enumerate(pairs)})
    uppers = list(range(level + 1, levels))
    joint = jnp.concatenate(
        [jnp.concatenate([gram[upper, level] for gram in grams], axis=1) for upper in uppers], axis=0)
    change = dot(jnp.concatenate(sides, axis=1), joint, (1, 1), True)
    pieces = [values[0][upper - level] + values[1][upper - level] - change[:, i * rank:(i + 1) * rank]
              for i, upper in enumerate(uppers)]
    for pair in pairs:
        if pair[1] > level:
            pieces.append(grams[0][pair] + grams[1][pair])
    pack_message(message_ref[0], pieces)


def stack_kernel(low_ref, high_ref, *refs):
    held = low_ref.shape[0]
    refs[-1][:held] = low_ref[...]
    refs[-1][held:] = high_ref[...]


def split_factor(masks, pairs, flip_ref, factor_ref):
    slots, share, rank = pairs[0].shape
    me = lax.axis_index("rows")
    core, chip = me % 2, me // 2
    for i, ref in enumerate(pairs):
        side = core if i % 2 == 0 else 1 - core
        for spot, mask in enumerate(masks):
            row = (side * slots + (chip ^ mask)) * share
            rows = pl.ds(pl.multiple_of(row, share), share)
            flip_ref[rows, pl.ds(i // 2 * rank, rank)] = ref[spot]
    high_part, low_part = halves(flip_ref[...].T)
    kinds = flip_ref.shape[1]
    factor_ref[:kinds, :] = high_part
    factor_ref[kinds:, :] = low_part


def apply_kernel(masks, tile, own_ref, pair_ref, first_ref, left_ref, out_ref, flip_ref, factor_ref):
    split_factor(masks, (own_ref, pair_ref), flip_ref, factor_ref)
    for row in range(0, out_ref.shape[0], tile):
        rows = pl.ds(row, tile)
        left = jnp.concatenate([left_ref[0, rows, :]] * 2, axis=1)
        out_ref[rows, :] = first_ref[rows, :] - dot(left, factor_ref[...], (1, 0))


def expand_kernel(masks, levels, tile, *refs):
    first_ref, left_ref, out_ref, flip_ref, factor_ref, out_buf, sems = refs[2 * levels - 2:]
    split_factor(masks, refs[:2 * levels - 2], flip_ref, factor_ref)
    copies = []
    for step in range(out_buf.shape[0] // tile):
        rows = pl.ds(step * tile, tile)
        left = jnp.concatenate([left_ref[l, rows, :] for l in range(1, levels)] * 2, axis=1)
        out_buf[rows, :] = first_ref[rows, :] - dot(left, factor_ref[...], (1, 0))
        copies.append(pltpu.make_async_copy(out_buf.at[rows], out_ref.at[rows], sems.at[step]))
        copies[-1].start(priority=step % 2)
    for copy in copies:
        copy.wait()


def settings(mib, micros):
    return dict(
        compiler_params=pltpu.CompilerParams(vmem_limit_bytes=mib * MIB),
        cost_estimate=pl.CostEstimate(flops=int(micros * 1.1e9), bytes_accessed=0, transcendentals=0),
    )


def floats(*shape):
    return jax.ShapeDtypeStruct(shape, jnp.float32)


def per_device(rhs, leaf_order, leaf_inv, right_basis, left_basis, rank_perm, joined):
    levels, rows, rank = right_basis.shape
    nblocks, width, _ = leaf_inv.shape
    columns = rhs.shape[1]
    leaves = lax.axis_size("leaf")
    count = lax.axis_size("rows")
    slots = count // 2
    kinds = levels * rank
    size = kinds - rank
    share = columns // count
    gram_lanes = len(below_pairs(levels)) * rank

    per_step = blocks_per_step(nblocks, 3)
    flipped, gram = pl.pallas_call(
        functools.partial(gram_kernel, levels, per_step, width),
        in_specs=[pl.BlockSpec(memory_space=pltpu.HBM)] * 2,
        out_shape=[jax.ShapeDtypeStruct((kinds, rows), jnp.bfloat16), floats(rank, gram_lanes)],
        scratch_shapes=[
            pltpu.VMEM((levels, rows, rank), jnp.bfloat16),
            pltpu.VMEM((levels - 1, rows, rank), jnp.bfloat16),
            pltpu.VMEM((size, size), jnp.float32),
            pltpu.SemaphoreType.DMA((2, nblocks // per_step)),
        ],
        name="gram",
        **settings(24, 3),
    )(pltpu.with_memory_space_constraint(right_basis, pltpu.HBM),
      pltpu.with_memory_space_constraint(left_basis, pltpu.HBM))

    moved = pl.pallas_call(
        functools.partial(permute_kernel, blocks_per_step(nblocks, 6), width),
        out_shape=jax.ShapeDtypeStruct((nblocks, width, width), jnp.bfloat16),
        name="permute",
        **settings(8, 1.5),
    )(leaf_order, leaf_inv)

    def add(mine, got):
        return pl.pallas_call(
            add_kernel, out_shape=floats(*mine.shape), name="add", **settings(8, 0.1),
        )(mine, got)

    factors = pl.pallas_call(
        functools.partial(weigh_kernel, per_step, width),
        out_shape=jax.ShapeDtypeStruct((2 * kinds, rows), jnp.bfloat16),
        name="weigh",
        **settings(8, 2.4),
    )(moved, flipped, gram)

    def project(other, after):
        return pl.pallas_call(
            functools.partial(project_kernel, other),
            out_shape=floats(kinds, columns // 2),
            name="project_other" if other else "project_own",
            **settings(12, 1 if other else 8),
        )(factors, rhs, after)

    send = project(True, gram)
    got = swap(send, "rows", 1)
    mask = 2
    while mask < slots:
        gram = add(gram, swap(gram, "rows", mask))
        mask *= 2
    keep = project(False, gram)
    merged = pl.pallas_call(
        merge_kernel,
        out_shape=[floats(share, kinds)] * slots,
        scratch_shapes=[pltpu.VMEM((columns // 2, kinds), jnp.float32)],
        name="merge",
        **settings(8, 0.4),
    )(keep, got)
    parts = [merged[0]] + [swap(merged[s], "rows", 2 * s) for s in range(1, slots)]
    gram_other = swap(gram, "rows", slots)
    grams = [gram, gram_other, swap(gram, "rows", 1), swap(gram_other, "rows", 1)]
    prepared = pl.pallas_call(
        functools.partial(prepare_kernel, levels),
        in_specs=[pl.BlockSpec(memory_space=pltpu.HBM), pl.BlockSpec()],
        out_shape=floats(levels, 2 * rank, 2 * rank),
        scratch_shapes=[pltpu.VMEM((levels, 2 * rank, 2 * rank), jnp.float32), pltpu.SemaphoreType.DMA((levels,))],
        name="prepare",
        **settings(8, 2),
    )(pltpu.with_memory_space_constraint(joined, pltpu.HBM), rank_perm)

    def message_shape(level):
        return floats((levels - level) * share + len(below_pairs(levels, level)) * rank, rank)

    own, other, rest = pl.pallas_call(
        functools.partial(node_kernel, rank, slots),
        out_shape=[floats(share, rank)] * 2 + [floats(share, size)],
        name="node",
        **settings(8, 1),
    )(*parts, prepared)
    message, other = pl.pallas_call(
        functools.partial(correct_kernel, levels, rank),
        out_shape=[message_shape(1), floats(share, rank)],
        name="correct",
        **settings(8, 1),
    )(own, other, rest, *grams)
    first = pl.pallas_call(
        functools.partial(solve_kernel, per_step, width),
        out_shape=floats(rows, columns),
        name="solve",
        **settings(8, 2),
    )(moved, rhs, merged[0])

    bits = [slots] + [2 ** bit for bit in range(1, slots.bit_length() - 1)]
    masks = [0]
    for bit in bits:
        masks += [mask ^ bit // 2 for mask in masks]

    def stack(low, high, *after):
        return pl.pallas_call(
            stack_kernel,
            out_shape=floats(low.shape[0] + high.shape[0], share, rank),
            name="stack",
            **settings(8, 0.1),
        )(low, high, *after)

    def gather(mine, sent, *after):
        mine, sent = mine[None], sent[None]
        for bit in bits:
            mine = stack(mine, swap(sent, "rows", bit), *(after if bit == bits[-1] else ()))
            sent = mine
        return mine, swap(mine, "rows", 1)

    early = gather(own, other)
    second = pl.pallas_call(
        functools.partial(apply_kernel, masks, per_step * width),
        out_shape=floats(rows, columns),
        scratch_shapes=[
            pltpu.VMEM((columns, rank), jnp.float32),
            pltpu.VMEM((2 * rank, columns), jnp.bfloat16),
        ],
        name="apply",
        **settings(8, 1.8),
    )(*early, first, left_basis)

    pieces = []
    for level in range(1, levels):
        last = level + 1 == levels
        arrived = swap(message, "leaf", 2 ** (level - 1))
        outs = pl.pallas_call(
            functools.partial(level_kernel, levels, level, share),
            out_shape=[floats(share, rank)] + ([] if last else [message_shape(level + 1)]),
            name=f"level{level}",
            **settings(8, 8 if last else 8),
        )(message, arrived, prepared, first)
        pieces += gather(outs[0], outs[0], *((second,) if last else ()))
        message = outs[-1]

    return pl.pallas_call(
        functools.partial(expand_kernel, masks, levels, per_step * width),
        out_specs=pl.BlockSpec(memory_space=pl.ANY),
        out_shape=floats(rows, columns),
        scratch_shapes=[
            pltpu.VMEM((columns, size), jnp.float32),
            pltpu.VMEM((2 * size, columns), jnp.bfloat16),
            pltpu.VMEM((rows, columns), jnp.float32),
            pltpu.SemaphoreType.DMA((nblocks // per_step,)),
        ],
        name="expand",
        **settings(16, 5),
    )(*pieces, second, left_basis)


def solution(mesh):
    return jax.shard_map(
        per_device,
        mesh=mesh,
        in_specs=(
            P(("leaf", "rows"), None),
            P(("leaf", "rows"), None),
            P(("leaf", "rows"), None, None),
            P(None, ("leaf", "rows"), None),
            P(None, ("leaf", "rows"), None),
            P(),
            P(),
        ),
        out_specs=P(("leaf", "rows"), None),
        check_vma=False,
    )
```

```python
import functools

import jax
import jax.numpy as jnp
from jax import lax
from jax.experimental import pallas as pl
from jax.experimental.pallas import tpu as pltpu
from jax.sharding import PartitionSpec as P

HIGHEST = lax.Precision.HIGHEST
MIB = 1 << 20


def dot(a, b, contract, exact=False):
    return lax.dot_general(
        a, b, ((contract[:1], contract[1:]), ((), ())),
        precision=HIGHEST if exact else None, preferred_element_type=jnp.float32,
    )


def halves(value):
    high_part = value.astype(jnp.bfloat16)
    low_part = (value - high_part.astype(jnp.float32)).astype(jnp.bfloat16)
    return high_part, low_part


def swap(value, axis, mask):
    count = lax.axis_size(axis)
    return lax.ppermute(value, axis, [(i, i ^ mask) for i in range(count)])


def blocks_per_step(nblocks, most):
    return max(size for size in range(1, most + 1) if nblocks % size == 0)


def below_pairs(levels, first=0):
    return [(level, below) for level in range(levels) for below in range(first, level)]


def gram_kernel(levels, per_step, width, order_ref, inv_ref, right_ref, left_ref,
                moved_ref, flip_ref, out_ref, order_buf, inv_buf, right_buf, left_buf, gram_ref, order_sem, sems):
    rank = right_ref.shape[2]
    tile = per_step * width
    steps = right_ref.shape[1] // tile
    place = lax.broadcasted_iota(jnp.int32, (width, width), 0)
    order_copy = pltpu.make_async_copy(order_ref, order_buf, order_sem)
    copies = []
    for step in range(steps):
        rows = pl.ds(step * tile, tile)
        blocks = pl.ds(step * per_step, per_step)
        copies.append((
            pltpu.make_async_copy(right_ref.at[:, rows], right_buf.at[:, rows], sems.at[0, step]),
            pltpu.make_async_copy(left_ref.at[:levels - 1, rows], left_buf.at[:, rows], sems.at[1, step]),
            pltpu.make_async_copy(inv_ref.at[blocks], inv_buf.at[blocks], sems.at[2, step]),
        ))
        for copy in copies[-1]:
            copy.start()
        if step == 0:
            order_copy.start()
    gram_ref[...] = jnp.zeros_like(gram_ref)
    for step in range(steps):
        rows = pl.ds(step * tile, tile)
        copies[step][0].wait()
        copies[step][1].wait()
        right = jnp.concatenate([right_buf[l, rows, :] for l in range(levels)], axis=1).T
        flip_ref[:, rows] = right
        left = jnp.concatenate([left_buf[l, rows, :] for l in range(levels - 1)], axis=1)
        gram_ref[...] += dot(right[rank:], left, (1, 0))
        copies[step][2].wait()
        if step == 0:
            order_copy.wait()
        for b in range(per_step):
            block = step * per_step + b
            chosen = (place == order_buf[block:block + 1, :]).astype(jnp.float32).astype(jnp.bfloat16)
            moved_ref[block] = dot(inv_buf[block], chosen, (1, 1)).astype(jnp.bfloat16)
    for spot, (level, below) in enumerate(below_pairs(levels)):
        rows = pl.ds((level - 1) * rank, rank)
        out_ref[:, pl.ds(spot * rank, rank)] = gram_ref[rows, pl.ds(below * rank, rank)]


def weigh_kernel(per_step, width, moved_ref, flip_ref, after_ref, factor_ref):
    kinds = flip_ref.shape[0]

    def body(step, _):
        for b in range(per_step):
            block = step * per_step + b
            lanes = pl.ds(pl.multiple_of(block * width, width), width)
            high_part, low_part = halves(dot(flip_ref[:, lanes], moved_ref[block], (1, 0)))
            factor_ref[:kinds, lanes] = high_part
            factor_ref[kinds:, lanes] = low_part
        return 0

    lax.fori_loop(0, moved_ref.shape[0] // per_step, body, 0)


def solve_kernel(per_step, width, moved_ref, rhs_ref, *refs):
    out_ref = refs[-1]

    def body(step, _):
        for b in range(per_step):
            block = step * per_step + b
            rows = pl.ds(pl.multiple_of(block * width, width), width)
            out_ref[rows, :] = dot(moved_ref[block], rhs_ref[rows, :], (1, 0))
        return 0

    lax.fori_loop(0, moved_ref.shape[0] // per_step, body, 0)


def project_kernel(other, factor_ref, rhs_ref, after_ref, out_ref):
    kinds, part = out_ref.shape
    core = lax.axis_index("rows") % 2
    lanes = pl.ds(pl.multiple_of((1 - core if other else core) * part, part), part)
    total = dot(factor_ref[...], rhs_ref[:, lanes], (1, 0))
    out_ref[...] = total[:kinds] + total[kinds:]


def merge_kernel(keep_ref, got_ref, *refs):
    out_refs, flip_ref = refs[:-1], refs[-1]
    share = out_refs[0].shape[0]
    chip = lax.axis_index("rows") // 2
    flip_ref[...] = (keep_ref[...] + got_ref[...]).T
    for slot, out_ref in enumerate(out_refs):
        out_ref[...] = flip_ref[pl.ds(pl.multiple_of((chip ^ slot) * share, share), share), :]


def add_kernel(mine_ref, got_ref, out_ref):
    out_ref[...] = mine_ref[...] + got_ref[...]


def prepare_kernel(levels, joined_ref, perm_ref, out_ref, joined_buf, sems):
    rank = perm_ref.shape[1]
    leaves = lax.axis_size("leaf")
    leaf = lax.axis_index("leaf")
    copies = []
    for level in range(levels):
        node = 2 * leaves - 2 * leaves // 2 ** level + leaf // 2 ** level
        copies.append(pltpu.make_async_copy(joined_ref.at[node], joined_buf.at[level], sems.at[level]))
        copies[-1].start()
    spot = lax.broadcasted_iota(jnp.int32, (rank, rank), 0)
    for level in range(levels):
        copies[level].wait()
        chosen = (spot == perm_ref[level:level + 1, :]).astype(jnp.float32)
        for side in range(2):
            lanes = pl.ds(side * rank, rank)
            out_ref[level, :, lanes] = dot(joined_buf[level, :, lanes], chosen, (1, 1), True)


def by_side(side, own, other):
    return jnp.where(side == 0, own, other), jnp.where(side == 0, other, own)


def pack_message(message_ref, pieces):
    row = 0
    for piece in pieces:
        message_ref[pl.ds(row, piece.shape[0]), :] = piece
        row += piece.shape[0]


def node_kernel(rank, slots, *refs):
    part_refs = refs[:slots]
    joined_ref, own_ref, other_ref, rest_ref = refs[slots:]
    side = lax.axis_index("rows") // slots
    half = slots // 2
    sums = [sum(ref[...] for ref in part_refs[:half]), sum(ref[...] for ref in part_refs[half:])]
    picked = jnp.concatenate(by_side(side, sums[0][:, :rank], sums[1][:, :rank]), axis=1)
    coef = dot(picked, joined_ref[0], (1, 1), True)
    own_ref[...], other_ref[...] = by_side(side, coef[:, :rank], coef[:, rank:])
    rest_ref[...] = (sums[0] + sums[1])[:, rank:]


def correct_kernel(levels, rank, own_ref, other_ref, rest_ref, mine_ref, theirs_ref, pair_mine_ref,
                   pair_theirs_ref, message_ref):
    grams = [mine_ref[...] + pair_mine_ref[...], theirs_ref[...] + pair_theirs_ref[...]]
    pairs = below_pairs(levels)
    lanes = {pair: slice(spot * rank, (spot + 1) * rank) for spot, pair in enumerate(pairs)}
    joint = jnp.concatenate(
        [jnp.concatenate([gram[:, lanes[level, 0]] for gram in grams], axis=1) for level in range(1, levels)], axis=0)
    rest = rest_ref[...] - dot(jnp.concatenate([own_ref[...], other_ref[...]], axis=1), joint, (1, 1), True)
    pieces = [rest[:, level * rank:(level + 1) * rank] for level in range(levels - 1)]
    for pair in pairs:
        if pair[1] > 0:
            pieces.append(grams[0][:, lanes[pair]] + grams[1][:, lanes[pair]])
    pack_message(message_ref, pieces)


def level_kernel(levels, level, share, sent_ref, got_ref, joined_ref, after_ref, coef_ref, *message_ref):
    rank = sent_ref.shape[1]
    side = lax.axis_index("leaf") // 2 ** (level - 1) % 2
    more = levels - level
    values = []
    for ref in (sent_ref, got_ref):
        values.append([ref[pl.ds(i * share, share), :] for i in range(more)])
    picked = jnp.concatenate(by_side(side, values[0][0], values[1][0]), axis=1)
    coef = dot(picked, joined_ref[level], (1, 1), True)
    sides = by_side(side, coef[:, :rank], coef[:, rank:])
    coef_ref[...] = sides[0]
    if not message_ref:
        return
    pairs = below_pairs(levels, level)
    grams = []
    for ref in (sent_ref, got_ref):
        grams.append({pair: ref[pl.ds(more * share + spot * rank, rank), :] for spot, pair in enumerate(pairs)})
    uppers = list(range(level + 1, levels))
    joint = jnp.concatenate(
        [jnp.concatenate([gram[upper, level] for gram in grams], axis=1) for upper in uppers], axis=0)
    change = dot(jnp.concatenate(sides, axis=1), joint, (1, 1), True)
    pieces = [values[0][upper - level] + values[1][upper - level] - change[:, i * rank:(i + 1) * rank]
              for i, upper in enumerate(uppers)]
    for pair in pairs:
        if pair[1] > level:
            pieces.append(grams[0][pair] + grams[1][pair])
    pack_message(message_ref[0], pieces)


def pack_kernel(*refs):
    refs[-1][...] = jnp.concatenate([ref[...] for ref in refs[:-1]], axis=1)


def stack_kernel(after_ref, *refs):
    for slot, ref in enumerate(refs[:-1]):
        refs[-1][slot] = ref[...]


def relay_kernel(after_ref, ref, out_ref):
    out_ref[...] = ref[...]


def split_factor(pieces, flip_ref, factor_ref):
    share, kinds = pieces[0].shape
    slots = len(pieces) // 2
    me = lax.axis_index("rows")
    for mask, ref in enumerate(pieces):
        owner = me ^ mask
        row = (owner % 2 * slots + owner // 2) * share
        flip_ref[pl.ds(pl.multiple_of(row, share), share), :] = ref[...]
    high_part, low_part = halves(flip_ref[...].T)
    factor_ref[:kinds, :] = high_part
    factor_ref[kinds:, :] = low_part


def apply_kernel(tile, own_ref, pair_ref, first_ref, left_ref, out_ref, flip_ref, factor_ref):
    pieces = [ref.at[slot] for slot in range(own_ref.shape[0]) for ref in (own_ref, pair_ref)]
    split_factor(pieces, flip_ref, factor_ref)
    for row in range(0, out_ref.shape[0], tile):
        rows = pl.ds(row, tile)
        left = jnp.concatenate([left_ref[0, rows, :]] * 2, axis=1)
        out_ref[rows, :] = first_ref[rows, :] - dot(left, factor_ref[...], (1, 0))


def expand_kernel(levels, tile, count, *refs):
    piece_refs = refs[:count]
    first_ref, left_ref, out_ref, flip_ref, factor_ref, out_buf, sems = refs[count:]
    split_factor(piece_refs, flip_ref, factor_ref)
    copies = []
    for step in range(out_buf.shape[0] // tile):
        rows = pl.ds(step * tile, tile)
        left = jnp.concatenate([left_ref[l, rows, :] for l in range(1, levels)] * 2, axis=1)
        out_buf[rows, :] = first_ref[rows, :] - dot(left, factor_ref[...], (1, 0))
        copies.append(pltpu.make_async_copy(out_buf.at[rows], out_ref.at[rows], sems.at[step]))
        copies[-1].start(priority=step % 2)
    for copy in copies:
        copy.wait()


def settings(mib, micros):
    return dict(
        compiler_params=pltpu.CompilerParams(vmem_limit_bytes=mib * MIB),
        cost_estimate=pl.CostEstimate(flops=int(micros * 1.1e9), bytes_accessed=0, transcendentals=0),
    )


def floats(*shape):
    return jax.ShapeDtypeStruct(shape, jnp.float32)


def per_device(rhs, leaf_order, leaf_inv, right_basis, left_basis, rank_perm, joined):
    levels, rows, rank = right_basis.shape
    nblocks, width, _ = leaf_inv.shape
    columns = rhs.shape[1]
    leaves = lax.axis_size("leaf")
    count = lax.axis_size("rows")
    slots = count // 2
    kinds = levels * rank
    size = kinds - rank
    share = columns // count
    gram_lanes = len(below_pairs(levels)) * rank

    per_step = blocks_per_step(nblocks, 3)
    moved, flipped, gram = pl.pallas_call(
        functools.partial(gram_kernel, levels, per_step, width),
        in_specs=[pl.BlockSpec(memory_space=pltpu.HBM)] * 4,
        out_shape=[
            jax.ShapeDtypeStruct((nblocks, width, width), jnp.bfloat16),
            jax.ShapeDtypeStruct((kinds, rows), jnp.bfloat16),
            floats(rank, gram_lanes),
        ],
        scratch_shapes=[
            pltpu.VMEM((nblocks, width), jnp.int32),
            pltpu.VMEM((nblocks, width, width), jnp.bfloat16),
            pltpu.VMEM((levels, rows, rank), jnp.bfloat16),
            pltpu.VMEM((levels - 1, rows, rank), jnp.bfloat16),
            pltpu.VMEM((size, size), jnp.float32),
            pltpu.SemaphoreType.DMA,
            pltpu.SemaphoreType.DMA((3, nblocks // per_step)),
        ],
        name="gram",
        **settings(24, 4),
    )(*(pltpu.with_memory_space_constraint(x, pltpu.HBM) for x in (leaf_order, leaf_inv, right_basis, left_basis)))

    def add(mine, got):
        return pl.pallas_call(
            add_kernel, out_shape=floats(*mine.shape), name="add", **settings(8, 0.1),
        )(mine, got)

    factors = pl.pallas_call(
        functools.partial(weigh_kernel, blocks_per_step(nblocks, 9), width),
        out_shape=jax.ShapeDtypeStruct((2 * kinds, rows), jnp.bfloat16),
        name="weigh",
        **settings(8, 2.4),
    )(moved, flipped, gram)

    def project(other, after):
        return pl.pallas_call(
            functools.partial(project_kernel, other),
            out_shape=floats(kinds, columns // 2),
            name="project_other" if other else "project_own",
            **settings(12, 1 if other else 8),
        )(factors, rhs, after)

    send = project(True, gram)
    got = swap(send, "rows", 1)
    mask = 2
    while mask < slots:
        gram = add(gram, swap(gram, "rows", mask))
        mask *= 2
    keep = project(False, gram)
    merged = pl.pallas_call(
        merge_kernel,
        out_shape=[floats(share, kinds)] * slots,
        scratch_shapes=[pltpu.VMEM((columns // 2, kinds), jnp.float32)],
        name="merge",
        **settings(8, 0.4),
    )(keep, got)
    parts = [merged[0]] + [swap(merged[s], "rows", 2 * s) for s in range(1, slots)]
    gram_other = swap(gram, "rows", slots)
    grams = [gram, gram_other, swap(gram, "rows", 1), swap(gram_other, "rows", 1)]
    prepared = pl.pallas_call(
        functools.partial(prepare_kernel, levels),
        in_specs=[pl.BlockSpec(memory_space=pltpu.HBM), pl.BlockSpec()],
        out_shape=floats(levels, 2 * rank, 2 * rank),
        scratch_shapes=[pltpu.VMEM((levels, 2 * rank, 2 * rank), jnp.float32), pltpu.SemaphoreType.DMA((levels,))],
        name="prepare",
        **settings(8, 2),
    )(pltpu.with_memory_space_constraint(joined, pltpu.HBM), rank_perm)

    def message_shape(level):
        return floats((levels - level) * share + len(below_pairs(levels, level)) * rank, rank)

    own, other, rest = pl.pallas_call(
        functools.partial(node_kernel, rank, slots),
        out_shape=[floats(share, rank)] * 2 + [floats(share, size)],
        name="node",
        **settings(8, 1),
    )(*parts, prepared)
    message = pl.pallas_call(
        functools.partial(correct_kernel, levels, rank),
        out_shape=message_shape(1),
        name="correct",
        **settings(8, 1),
    )(own, other, rest, *grams)
    early = [own] + [swap(own if slot < slots // 2 else other, "rows", 2 * slot) for slot in range(1, slots)]
    first = pl.pallas_call(
        functools.partial(solve_kernel, per_step, width),
        out_shape=floats(rows, columns),
        name="solve",
        **settings(8, 8),
    )(moved, rhs, merged[0])

    coefs = []
    for level in range(1, levels):
        last = level + 1 == levels
        arrived = swap(message, "leaf", 2 ** (level - 1))
        outs = pl.pallas_call(
            functools.partial(level_kernel, levels, level, share),
            out_shape=[floats(share, rank)] + ([] if last else [message_shape(level + 1)]),
            name=f"level{level}",
            **settings(8, 1 if last else 6),
        )(message, arrived, prepared, first if last else arrived)
        coefs.append(outs[0])
        message = outs[-1]
    stack = pl.pallas_call(
        stack_kernel, out_shape=floats(slots, share, rank), name="stack", **settings(8, 0.1),
    )(first, *early)
    second = pl.pallas_call(
        functools.partial(apply_kernel, per_step * width),
        out_shape=floats(rows, columns),
        scratch_shapes=[
            pltpu.VMEM((columns, rank), jnp.float32),
            pltpu.VMEM((2 * rank, columns), jnp.bfloat16),
        ],
        name="apply",
        **settings(8, 1.8),
    )(stack, swap(stack, "rows", 1), first, left_basis)

    pack = pl.pallas_call(
        pack_kernel, out_shape=floats(share, size), name="pack", **settings(8, 0.1),
    )(*coefs)
    pieces = []
    for slot in range(slots):
        piece = swap(pack, "rows", 2 * slot) if slot > 0 else pack
        if slot == slots - 1:
            piece = pl.pallas_call(
                relay_kernel, out_shape=floats(share, size), name="relay", **settings(8, 0.1),
            )(second, piece)
        pieces += [piece, swap(piece, "rows", 1)]
    return pl.pallas_call(
        functools.partial(expand_kernel, levels, per_step * width, count),
        out_specs=pl.BlockSpec(memory_space=pl.ANY),
        out_shape=floats(rows, columns),
        scratch_shapes=[
            pltpu.VMEM((columns, size), jnp.float32),
            pltpu.VMEM((2 * size, columns), jnp.bfloat16),
            pltpu.VMEM((rows, columns), jnp.float32),
            pltpu.SemaphoreType.DMA((nblocks // per_step,)),
        ],
        name="expand",
        **settings(16, 5),
    )(*pieces, second, left_basis)


def solution(mesh):
    return jax.shard_map(
        per_device,
        mesh=mesh,
        in_specs=(
            P(("leaf", "rows"), None),
            P(("leaf", "rows"), None),
            P(("leaf", "rows"), None, None),
            P(None, ("leaf", "rows"), None),
            P(None, ("leaf", "rows"), None),
            P(),
            P(),
        ),
        out_specs=P(("leaf", "rows"), None),
        check_vma=False,
    )
```

```python
import functools

import jax
import jax.numpy as jnp
from jax import lax
from jax.experimental import pallas as pl
from jax.experimental.pallas import tpu as pltpu
from jax.sharding import PartitionSpec as P

HIGHEST = lax.Precision.HIGHEST
MIB = 1 << 20


def dot(a, b, contract, exact=False):
    return lax.dot_general(
        a, b, ((contract[:1], contract[1:]), ((), ())),
        precision=HIGHEST if exact else None, preferred_element_type=jnp.float32,
    )


def halves(value):
    high_part = value.astype(jnp.bfloat16)
    low_part = (value - high_part.astype(jnp.float32)).astype(jnp.bfloat16)
    return high_part, low_part


def swap(value, axis, mask):
    count = lax.axis_size(axis)
    return lax.ppermute(value, axis, [(i, i ^ mask) for i in range(count)])


def blocks_per_step(nblocks, most):
    return max(size for size in range(1, most + 1) if nblocks % size == 0)


def below_pairs(levels, first=0):
    return [(level, below) for level in range(levels) for below in range(first, level)]


def gram_kernel(levels, per_step, width, order_ref, inv_ref, right_ref, left_ref,
                moved_ref, flip_ref, out_ref, order_buf, inv_buf, right_buf, left_buf, gram_ref, order_sem, sems):
    rank = right_ref.shape[2]
    tile = per_step * width
    steps = right_ref.shape[1] // tile
    place = lax.broadcasted_iota(jnp.int32, (width, width), 0)
    order_copy = pltpu.make_async_copy(order_ref, order_buf, order_sem)
    copies = []
    for step in range(steps):
        rows = pl.ds(step * tile, tile)
        blocks = pl.ds(step * per_step, per_step)
        copies.append((
            pltpu.make_async_copy(right_ref.at[:, rows], right_buf.at[:, rows], sems.at[0, step]),
            pltpu.make_async_copy(left_ref.at[:levels - 1, rows], left_buf.at[:, rows], sems.at[1, step]),
            pltpu.make_async_copy(inv_ref.at[blocks], inv_buf.at[blocks], sems.at[2, step]),
        ))
        for index, copy in enumerate(copies[-1]):
            copy.start(priority=(step + (index > 0)) % 2)
        if step == 0:
            order_copy.start()
    gram_ref[...] = jnp.zeros_like(gram_ref)
    for step in range(steps):
        rows = pl.ds(step * tile, tile)
        copies[step][0].wait()
        copies[step][1].wait()
        right = jnp.concatenate([right_buf[l, rows, :] for l in range(levels)], axis=1).T
        flip_ref[:, rows] = right
        left = jnp.concatenate([left_buf[l, rows, :] for l in range(levels - 1)], axis=1)
        gram_ref[...] += dot(right[rank:], left, (1, 0))
        copies[step][2].wait()
        if step == 0:
            order_copy.wait()
        for b in range(per_step):
            block = step * per_step + b
            chosen = (place == order_buf[block:block + 1, :]).astype(jnp.float32).astype(jnp.bfloat16)
            moved_ref[block] = dot(inv_buf[block], chosen, (1, 1)).astype(jnp.bfloat16)
    for spot, (level, below) in enumerate(below_pairs(levels)):
        rows = pl.ds((level - 1) * rank, rank)
        out_ref[:, pl.ds(spot * rank, rank)] = gram_ref[rows, pl.ds(below * rank, rank)]


def weigh_kernel(per_step, width, moved_ref, flip_ref, after_ref, factor_ref):
    kinds = flip_ref.shape[0]

    def body(step, _):
        for b in range(per_step):
            block = step * per_step + b
            lanes = pl.ds(pl.multiple_of(block * width, width), width)
            high_part, low_part = halves(dot(flip_ref[:, lanes], moved_ref[block], (1, 0)))
            factor_ref[:kinds, lanes] = high_part
            factor_ref[kinds:, lanes] = low_part
        return 0

    lax.fori_loop(0, moved_ref.shape[0] // per_step, body, 0)


def solve_kernel(per_step, width, moved_ref, rhs_ref, *refs):
    out_ref = refs[-1]

    def body(step, _):
        for b in range(per_step):
            block = step * per_step + b
            rows = pl.ds(pl.multiple_of(block * width, width), width)
            out_ref[rows, :] = dot(moved_ref[block], rhs_ref[rows, :], (1, 0))
        return 0

    lax.fori_loop(0, moved_ref.shape[0] // per_step, body, 0)


def project_kernel(other, factor_ref, rhs_ref, after_ref, out_ref):
    kinds, part = out_ref.shape
    core = lax.axis_index("rows") % 2
    lanes = pl.ds(pl.multiple_of((1 - core if other else core) * part, part), part)
    total = dot(factor_ref[...], rhs_ref[:, lanes], (1, 0))
    out_ref[...] = total[:kinds] + total[kinds:]


def merge_kernel(keep_ref, got_ref, *refs):
    out_refs, flip_ref = refs[:-1], refs[-1]
    share = out_refs[0].shape[0]
    chip = lax.axis_index("rows") // 2
    flip_ref[...] = (keep_ref[...] + got_ref[...]).T
    for slot, out_ref in enumerate(out_refs):
        out_ref[...] = flip_ref[pl.ds(pl.multiple_of((chip ^ slot) * share, share), share), :]


def add_kernel(mine_ref, got_ref, out_ref):
    out_ref[...] = mine_ref[...] + got_ref[...]


def prepare_kernel(levels, joined_ref, perm_ref, out_ref, joined_buf, sems):
    rank = perm_ref.shape[1]
    leaves = lax.axis_size("leaf")
    leaf = lax.axis_index("leaf")
    copies = []
    for level in range(levels):
        node = 2 * leaves - 2 * leaves // 2 ** level + leaf // 2 ** level
        copies.append(pltpu.make_async_copy(joined_ref.at[node], joined_buf.at[level], sems.at[level]))
        copies[-1].start()
    spot = lax.broadcasted_iota(jnp.int32, (rank, rank), 0)
    for level in range(levels):
        copies[level].wait()
        chosen = (spot == perm_ref[level:level + 1, :]).astype(jnp.float32)
        for side in range(2):
            lanes = pl.ds(side * rank, rank)
            out_ref[level, :, lanes] = dot(joined_buf[level, :, lanes], chosen, (1, 1), True)


def by_side(side, own, other):
    return jnp.where(side == 0, own, other), jnp.where(side == 0, other, own)


def pack_message(message_ref, pieces):
    row = 0
    for piece in pieces:
        message_ref[pl.ds(row, piece.shape[0]), :] = piece
        row += piece.shape[0]


def node_kernel(rank, slots, *refs):
    part_refs = refs[:slots]
    joined_ref, own_ref, other_ref, rest_ref = refs[slots:]
    side = lax.axis_index("rows") // slots
    half = slots // 2
    sums = [sum(ref[...] for ref in part_refs[:half]), sum(ref[...] for ref in part_refs[half:])]
    picked = jnp.concatenate(by_side(side, sums[0][:, :rank], sums[1][:, :rank]), axis=1)
    coef = dot(picked, joined_ref[0], (1, 1), True)
    own_ref[...], other_ref[...] = by_side(side, coef[:, :rank], coef[:, rank:])
    rest_ref[...] = (sums[0] + sums[1])[:, rank:]


def correct_kernel(levels, rank, own_ref, other_ref, rest_ref, mine_ref, theirs_ref, pair_mine_ref,
                   pair_theirs_ref, message_ref):
    grams = [mine_ref[...] + pair_mine_ref[...], theirs_ref[...] + pair_theirs_ref[...]]
    pairs = below_pairs(levels)
    lanes = {pair: slice(spot * rank, (spot + 1) * rank) for spot, pair in enumerate(pairs)}
    joint = jnp.concatenate(
        [jnp.concatenate([gram[:, lanes[level, 0]] for gram in grams], axis=1) for level in range(1, levels)], axis=0)
    rest = rest_ref[...] - dot(jnp.concatenate([own_ref[...], other_ref[...]], axis=1), joint, (1, 1), True)
    pieces = [rest[:, level * rank:(level + 1) * rank] for level in range(levels - 1)]
    for pair in pairs:
        if pair[1] > 0:
            pieces.append(grams[0][:, lanes[pair]] + grams[1][:, lanes[pair]])
    pack_message(message_ref, pieces)


def level_kernel(levels, level, share, sent_ref, got_ref, joined_ref, after_ref, coef_ref, *message_ref):
    rank = sent_ref.shape[1]
    side = lax.axis_index("leaf") // 2 ** (level - 1) % 2
    more = levels - level
    values = []
    for ref in (sent_ref, got_ref):
        values.append([ref[pl.ds(i * share, share), :] for i in range(more)])
    picked = jnp.concatenate(by_side(side, values[0][0], values[1][0]), axis=1)
    coef = dot(picked, joined_ref[level], (1, 1), True)
    sides = by_side(side, coef[:, :rank], coef[:, rank:])
    coef_ref[...] = sides[0]
    if not message_ref:
        return
    pairs = below_pairs(levels, level)
    grams = []
    for ref in (sent_ref, got_ref):
        grams.append({pair: ref[pl.ds(more * share + spot * rank, rank), :] for spot, pair in enumerate(pairs)})
    uppers = list(range(level + 1, levels))
    joint = jnp.concatenate(
        [jnp.concatenate([gram[upper, level] for gram in grams], axis=1) for upper in uppers], axis=0)
    change = dot(jnp.concatenate(sides, axis=1), joint, (1, 1), True)
    pieces = [values[0][upper - level] + values[1][upper - level] - change[:, i * rank:(i + 1) * rank]
              for i, upper in enumerate(uppers)]
    for pair in pairs:
        if pair[1] > level:
            pieces.append(grams[0][pair] + grams[1][pair])
    pack_message(message_ref[0], pieces)


def pack_kernel(*refs):
    refs[-1][...] = jnp.concatenate([ref[...] for ref in refs[:-1]], axis=1)


def stack_kernel(after_ref, *refs):
    for slot, ref in enumerate(refs[:-1]):
        refs[-1][slot] = ref[...]


def relay_kernel(after_ref, ref, out_ref):
    out_ref[...] = ref[...]


def split_factor(pieces, flip_ref, factor_ref):
    share, kinds = pieces[0].shape
    slots = len(pieces) // 2
    me = lax.axis_index("rows")
    for mask, ref in enumerate(pieces):
        owner = me ^ mask
        row = (owner % 2 * slots + owner // 2) * share
        flip_ref[pl.ds(pl.multiple_of(row, share), share), :] = ref[...]
    high_part, low_part = halves(flip_ref[...].T)
    factor_ref[:kinds, :] = high_part
    factor_ref[kinds:, :] = low_part


def apply_kernel(tile, own_ref, pair_ref, first_ref, left_ref, out_ref, flip_ref, factor_ref):
    pieces = [ref.at[slot] for slot in range(own_ref.shape[0]) for ref in (own_ref, pair_ref)]
    split_factor(pieces, flip_ref, factor_ref)
    for row in range(0, out_ref.shape[0], tile):
        rows = pl.ds(row, tile)
        left = jnp.concatenate([left_ref[0, rows, :]] * 2, axis=1)
        out_ref[rows, :] = first_ref[rows, :] - dot(left, factor_ref[...], (1, 0))


def expand_kernel(levels, tile, count, *refs):
    piece_refs = refs[:count]
    first_ref, left_ref, out_ref, flip_ref, factor_ref, out_buf, sems = refs[count:]
    split_factor(piece_refs, flip_ref, factor_ref)
    copies = []
    for step in range(out_buf.shape[0] // tile):
        rows = pl.ds(step * tile, tile)
        left = jnp.concatenate([left_ref[l, rows, :] for l in range(1, levels)] * 2, axis=1)
        out_buf[rows, :] = first_ref[rows, :] - dot(left, factor_ref[...], (1, 0))
        copies.append(pltpu.make_async_copy(out_buf.at[rows], out_ref.at[rows], sems.at[step]))
        copies[-1].start(priority=step % 2)
    for copy in copies:
        copy.wait()


def settings(mib, micros):
    return dict(
        compiler_params=pltpu.CompilerParams(vmem_limit_bytes=mib * MIB),
        cost_estimate=pl.CostEstimate(flops=int(micros * 1.1e9), bytes_accessed=0, transcendentals=0),
    )


def floats(*shape):
    return jax.ShapeDtypeStruct(shape, jnp.float32)


def per_device(rhs, leaf_order, leaf_inv, right_basis, left_basis, rank_perm, joined):
    levels, rows, rank = right_basis.shape
    nblocks, width, _ = leaf_inv.shape
    columns = rhs.shape[1]
    leaves = lax.axis_size("leaf")
    count = lax.axis_size("rows")
    slots = count // 2
    kinds = levels * rank
    size = kinds - rank
    share = columns // count
    gram_lanes = len(below_pairs(levels)) * rank

    per_step = blocks_per_step(nblocks, 3)
    moved, flipped, gram = pl.pallas_call(
        functools.partial(gram_kernel, levels, per_step, width),
        in_specs=[pl.BlockSpec(memory_space=pltpu.HBM)] * 4,
        out_shape=[
            jax.ShapeDtypeStruct((nblocks, width, width), jnp.bfloat16),
            jax.ShapeDtypeStruct((kinds, rows), jnp.bfloat16),
            floats(rank, gram_lanes),
        ],
        scratch_shapes=[
            pltpu.VMEM((nblocks, width), jnp.int32),
            pltpu.VMEM((nblocks, width, width), jnp.bfloat16),
            pltpu.VMEM((levels, rows, rank), jnp.bfloat16),
            pltpu.VMEM((levels - 1, rows, rank), jnp.bfloat16),
            pltpu.VMEM((size, size), jnp.float32),
            pltpu.SemaphoreType.DMA,
            pltpu.SemaphoreType.DMA((3, nblocks // per_step)),
        ],
        name="gram",
        **settings(24, 4),
    )(*(pltpu.with_memory_space_constraint(x, pltpu.HBM) for x in (leaf_order, leaf_inv, right_basis, left_basis)))

    def add(mine, got):
        return pl.pallas_call(
            add_kernel, out_shape=floats(*mine.shape), name="add", **settings(8, 0.1),
        )(mine, got)

    factors = pl.pallas_call(
        functools.partial(weigh_kernel, blocks_per_step(nblocks, 9), width),
        out_shape=jax.ShapeDtypeStruct((2 * kinds, rows), jnp.bfloat16),
        name="weigh",
        **settings(8, 0.3),
    )(moved, flipped, gram)

    def project(other, after):
        return pl.pallas_call(
            functools.partial(project_kernel, other),
            out_shape=floats(kinds, columns // 2),
            name="project_other" if other else "project_own",
            **settings(12, 1 if other else 8),
        )(factors, rhs, after)

    send = project(True, gram)
    got = swap(send, "rows", 1)
    mask = 2
    while mask < slots:
        gram = add(gram, swap(gram, "rows", mask))
        mask *= 2
    keep = project(False, gram)
    merged = pl.pallas_call(
        merge_kernel,
        out_shape=[floats(share, kinds)] * slots,
        scratch_shapes=[pltpu.VMEM((columns // 2, kinds), jnp.float32)],
        name="merge",
        **settings(8, 0.4),
    )(keep, got)
    parts = [merged[0]] + [swap(merged[s], "rows", 2 * s) for s in range(1, slots)]
    gram_other = swap(gram, "rows", slots)
    grams = [gram, gram_other, swap(gram, "rows", 1), swap(gram_other, "rows", 1)]
    prepared = pl.pallas_call(
        functools.partial(prepare_kernel, levels),
        in_specs=[pl.BlockSpec(memory_space=pltpu.HBM), pl.BlockSpec()],
        out_shape=floats(levels, 2 * rank, 2 * rank),
        scratch_shapes=[pltpu.VMEM((levels, 2 * rank, 2 * rank), jnp.float32), pltpu.SemaphoreType.DMA((levels,))],
        name="prepare",
        **settings(8, 2),
    )(pltpu.with_memory_space_constraint(joined, pltpu.HBM), rank_perm)

    def message_shape(level):
        return floats((levels - level) * share + len(below_pairs(levels, level)) * rank, rank)

    own, other, rest = pl.pallas_call(
        functools.partial(node_kernel, rank, slots),
        out_shape=[floats(share, rank)] * 2 + [floats(share, size)],
        name="node",
        **settings(8, 1),
    )(*parts, prepared)
    message = pl.pallas_call(
        functools.partial(correct_kernel, levels, rank),
        out_shape=message_shape(1),
        name="correct",
        **settings(8, 1),
    )(own, other, rest, *grams)
    early = [own] + [swap(own if slot < slots // 2 else other, "rows", 2 * slot) for slot in range(1, slots)]
    first = pl.pallas_call(
        functools.partial(solve_kernel, per_step, width),
        out_shape=floats(rows, columns),
        name="solve",
        **settings(8, 8),
    )(moved, rhs, merged[0])

    coefs = []
    for level in range(1, levels):
        last = level + 1 == levels
        arrived = swap(message, "leaf", 2 ** (level - 1))
        outs = pl.pallas_call(
            functools.partial(level_kernel, levels, level, share),
            out_shape=[floats(share, rank)] + ([] if last else [message_shape(level + 1)]),
            name=f"level{level}",
            **settings(8, 1 if last else 6),
        )(message, arrived, prepared, first if last else arrived)
        coefs.append(outs[0])
        message = outs[-1]
    stack = pl.pallas_call(
        stack_kernel, out_shape=floats(slots, share, rank), name="stack", **settings(8, 0.1),
    )(first, *early)
    second = pl.pallas_call(
        functools.partial(apply_kernel, per_step * width),
        out_shape=floats(rows, columns),
        scratch_shapes=[
            pltpu.VMEM((columns, rank), jnp.float32),
            pltpu.VMEM((2 * rank, columns), jnp.bfloat16),
        ],
        name="apply",
        **settings(8, 1.8),
    )(stack, swap(stack, "rows", 1), first, left_basis)

    pack = pl.pallas_call(
        pack_kernel, out_shape=floats(share, size), name="pack", **settings(8, 0.1),
    )(*coefs)
    pieces = []
    for slot in range(slots):
        piece = swap(pack, "rows", 2 * slot) if slot > 0 else pack
        if slot == slots - 1:
            piece = pl.pallas_call(
                relay_kernel, out_shape=floats(share, size), name="relay", **settings(8, 0.1),
            )(second, piece)
        pieces += [piece, swap(piece, "rows", 1)]
    return pl.pallas_call(
        functools.partial(expand_kernel, levels, per_step * width, count),
        out_specs=pl.BlockSpec(memory_space=pl.ANY),
        out_shape=floats(rows, columns),
        scratch_shapes=[
            pltpu.VMEM((columns, size), jnp.float32),
            pltpu.VMEM((2 * size, columns), jnp.bfloat16),
            pltpu.VMEM((rows, columns), jnp.float32),
            pltpu.SemaphoreType.DMA((nblocks // per_step,)),
        ],
        name="expand",
        **settings(16, 5),
    )(*pieces, second, left_basis)


def solution(mesh):
    return jax.shard_map(
        per_device,
        mesh=mesh,
        in_specs=(
            P(("leaf", "rows"), None),
            P(("leaf", "rows"), None),
            P(("leaf", "rows"), None, None),
            P(None, ("leaf", "rows"), None),
            P(None, ("leaf", "rows"), None),
            P(),
            P(),
        ),
        out_specs=P(("leaf", "rows"), None),
        check_vma=False,
    )
```

```python
import functools

import jax
import jax.numpy as jnp
from jax import lax
from jax.experimental import pallas as pl
from jax.experimental.pallas import tpu as pltpu
from jax.sharding import PartitionSpec as P

HIGHEST = lax.Precision.HIGHEST
MIB = 1 << 20


def dot(a, b, contract, exact=False):
    return lax.dot_general(
        a, b, ((contract[:1], contract[1:]), ((), ())),
        precision=HIGHEST if exact else None, preferred_element_type=jnp.float32,
    )


def halves(value):
    high_part = value.astype(jnp.bfloat16)
    low_part = (value - high_part.astype(jnp.float32)).astype(jnp.bfloat16)
    return high_part, low_part


def swap(value, axis, mask):
    count = lax.axis_size(axis)
    return lax.ppermute(value, axis, [(i, i ^ mask) for i in range(count)])


def blocks_per_step(nblocks, most):
    return max(size for size in range(1, most + 1) if nblocks % size == 0)


def below_pairs(levels, first=0):
    return [(level, below) for level in range(levels) for below in range(first, level)]


def gram_kernel(levels, per_step, width, right_ref, left_ref, flip_ref, out_ref,
                right_buf, left_buf, gram_ref, sems):
    rank = right_ref.shape[2]
    tile = per_step * width
    steps = right_ref.shape[1] // tile

    def copies(step):
        rows = pl.ds(pl.multiple_of(step * tile, tile), tile)
        return (
            pltpu.make_async_copy(right_ref.at[:, rows], right_buf.at[:, rows], sems.at[0, step]),
            pltpu.make_async_copy(left_ref.at[:levels - 1, rows], left_buf.at[:, rows], sems.at[1, step]),
        )

    for step in range(steps):
        for copy in copies(step):
            copy.start()
    gram_ref[...] = jnp.zeros_like(gram_ref)

    def body(step, _):
        for copy in copies(step):
            copy.wait()
        rows = pl.ds(pl.multiple_of(step * tile, tile), tile)
        right = jnp.concatenate([right_buf[l, rows, :] for l in range(levels)], axis=1).T
        flip_ref[:, rows] = right
        left = jnp.concatenate([left_buf[l, rows, :] for l in range(levels - 1)], axis=1)
        gram_ref[...] += dot(right[rank:], left, (1, 0))
        return 0

    lax.fori_loop(0, steps, body, 0)
    for spot, (level, below) in enumerate(below_pairs(levels)):
        rows = pl.ds((level - 1) * rank, rank)
        out_ref[:, pl.ds(spot * rank, rank)] = gram_ref[rows, pl.ds(below * rank, rank)]


def permute_kernel(per_step, width, order_ref, inv_ref, moved_ref):
    place = lax.broadcasted_iota(jnp.int32, (width, width), 0)

    def body(step, _):
        for b in range(per_step):
            block = step * per_step + b
            chosen = (place == order_ref[pl.ds(block, 1), :]).astype(jnp.float32).astype(jnp.bfloat16)
            moved_ref[block] = dot(inv_ref[block], chosen, (1, 1)).astype(jnp.bfloat16)
        return 0

    lax.fori_loop(0, inv_ref.shape[0] // per_step, body, 0)


def weigh_kernel(per_step, width, moved_ref, flip_ref, after_ref, factor_ref):
    kinds = flip_ref.shape[0]

    def body(step, _):
        for b in range(per_step):
            block = step * per_step + b
            lanes = pl.ds(pl.multiple_of(block * width, width), width)
            high_part, low_part = halves(dot(flip_ref[:, lanes], moved_ref[block], (1, 0)))
            factor_ref[:kinds, lanes] = high_part
            factor_ref[kinds:, lanes] = low_part
        return 0

    lax.fori_loop(0, moved_ref.shape[0] // per_step, body, 0)


def solve_kernel(per_step, width, moved_ref, rhs_ref, *refs):
    out_ref = refs[-1]

    def body(step, _):
        for b in range(per_step):
            block = step * per_step + b
            rows = pl.ds(pl.multiple_of(block * width, width), width)
            out_ref[rows, :] = dot(moved_ref[block], rhs_ref[rows, :], (1, 0))
        return 0

    lax.fori_loop(0, moved_ref.shape[0] // per_step, body, 0)


def project_kernel(other, factor_ref, rhs_ref, after_ref, out_ref):
    kinds, part = out_ref.shape
    core = lax.axis_index("rows") % 2
    lanes = pl.ds(pl.multiple_of((1 - core if other else core) * part, part), part)
    total = dot(factor_ref[...], rhs_ref[:, lanes], (1, 0))
    out_ref[...] = total[:kinds] + total[kinds:]


def merge_kernel(keep_ref, got_ref, *refs):
    out_refs, flip_ref = refs[:-1], refs[-1]
    share = out_refs[0].shape[0]
    chip = lax.axis_index("rows") // 2
    flip_ref[...] = (keep_ref[...] + got_ref[...]).T
    for slot, out_ref in enumerate(out_refs):
        out_ref[...] = flip_ref[pl.ds(pl.multiple_of((chip ^ slot) * share, share), share), :]


def add_kernel(mine_ref, got_ref, out_ref):
    out_ref[...] = mine_ref[...] + got_ref[...]


def prepare_kernel(levels, joined_ref, perm_ref, out_ref, joined_buf, sems):
    rank = perm_ref.shape[1]
    leaves = lax.axis_size("leaf")
    leaf = lax.axis_index("leaf")
    copies = []
    for level in range(levels):
        node = 2 * leaves - 2 * leaves // 2 ** level + leaf // 2 ** level
        copies.append(pltpu.make_async_copy(joined_ref.at[node], joined_buf.at[level], sems.at[level]))
        copies[-1].start()
    spot = lax.broadcasted_iota(jnp.int32, (rank, rank), 0)
    for level in range(levels):
        copies[level].wait()
        chosen = (spot == perm_ref[level:level + 1, :]).astype(jnp.float32)
        for side in range(2):
            lanes = pl.ds(side * rank, rank)
            out_ref[level, :, lanes] = dot(joined_buf[level, :, lanes], chosen, (1, 1), True)


def by_side(side, own, other):
    return jnp.where(side == 0, own, other), jnp.where(side == 0, other, own)


def pack_message(message_ref, pieces):
    row = 0
    for piece in pieces:
        message_ref[pl.ds(row, piece.shape[0]), :] = piece
        row += piece.shape[0]


def node_kernel(rank, slots, *refs):
    part_refs = refs[:slots]
    joined_ref, own_ref, other_ref, rest_ref = refs[slots:]
    side = lax.axis_index("rows") // slots
    half = slots // 2
    sums = [sum(ref[...] for ref in part_refs[:half]), sum(ref[...] for ref in part_refs[half:])]
    picked = jnp.concatenate(by_side(side, sums[0][:, :rank], sums[1][:, :rank]), axis=1)
    coef = dot(picked, joined_ref[0], (1, 1), True)
    own_ref[...], other_ref[...] = by_side(side, coef[:, :rank], coef[:, rank:])
    rest_ref[...] = (sums[0] + sums[1])[:, rank:]


def correct_kernel(levels, rank, own_ref, other_ref, rest_ref, mine_ref, theirs_ref, pair_mine_ref,
                   pair_theirs_ref, message_ref):
    grams = [mine_ref[...] + pair_mine_ref[...], theirs_ref[...] + pair_theirs_ref[...]]
    pairs = below_pairs(levels)
    lanes = {pair: slice(spot * rank, (spot + 1) * rank) for spot, pair in enumerate(pairs)}
    joint = jnp.concatenate(
        [jnp.concatenate([gram[:, lanes[level, 0]] for gram in grams], axis=1) for level in range(1, levels)], axis=0)
    rest = rest_ref[...] - dot(jnp.concatenate([own_ref[...], other_ref[...]], axis=1), joint, (1, 1), True)
    pieces = [rest[:, level * rank:(level + 1) * rank] for level in range(levels - 1)]
    for pair in pairs:
        if pair[1] > 0:
            pieces.append(grams[0][:, lanes[pair]] + grams[1][:, lanes[pair]])
    pack_message(message_ref, pieces)


def level_kernel(levels, level, share, sent_ref, got_ref, joined_ref, after_ref, coef_ref, *message_ref):
    rank = sent_ref.shape[1]
    side = lax.axis_index("leaf") // 2 ** (level - 1) % 2
    more = levels - level
    values = []
    for ref in (sent_ref, got_ref):
        values.append([ref[pl.ds(i * share, share), :] for i in range(more)])
    picked = jnp.concatenate(by_side(side, values[0][0], values[1][0]), axis=1)
    coef = dot(picked, joined_ref[level], (1, 1), True)
    sides = by_side(side, coef[:, :rank], coef[:, rank:])
    coef_ref[...] = sides[0]
    if not message_ref:
        return
    pairs = below_pairs(levels, level)
    grams = []
    for ref in (sent_ref, got_ref):
        grams.append({pair: ref[pl.ds(more * share + spot * rank, rank), :] for spot, pair in enumerate(pairs)})
    uppers = list(range(level + 1, levels))
    joint = jnp.concatenate(
        [jnp.concatenate([gram[upper, level] for gram in grams], axis=1) for upper in uppers], axis=0)
    change = dot(jnp.concatenate(sides, axis=1), joint, (1, 1), True)
    pieces = [values[0][upper - level] + values[1][upper - level] - change[:, i * rank:(i + 1) * rank]
              for i, upper in enumerate(uppers)]
    for pair in pairs:
        if pair[1] > level:
            pieces.append(grams[0][pair] + grams[1][pair])
    pack_message(message_ref[0], pieces)


def pack_kernel(*refs):
    refs[-1][...] = jnp.concatenate([ref[...] for ref in refs[:-1]], axis=1)


def stack_kernel(after_ref, *refs):
    for slot, ref in enumerate(refs[:-1]):
        refs[-1][slot] = ref[...]


def relay_kernel(after_ref, ref, out_ref):
    out_ref[...] = ref[...]


def split_factor(pieces, flip_ref, factor_ref):
    share, kinds = pieces[0].shape
    slots = len(pieces) // 2
    me = lax.axis_index("rows")
    for mask, ref in enumerate(pieces):
        owner = me ^ mask
        row = (owner % 2 * slots + owner // 2) * share
        flip_ref[pl.ds(pl.multiple_of(row, share), share), :] = ref[...]
    high_part, low_part = halves(flip_ref[...].T)
    factor_ref[:kinds, :] = high_part
    factor_ref[kinds:, :] = low_part


def apply_kernel(tile, own_ref, pair_ref, first_ref, left_ref, out_ref, flip_ref, factor_ref):
    pieces = [ref.at[slot] for slot in range(own_ref.shape[0]) for ref in (own_ref, pair_ref)]
    split_factor(pieces, flip_ref, factor_ref)
    for row in range(0, out_ref.shape[0], tile):
        rows = pl.ds(row, tile)
        left = jnp.concatenate([left_ref[0, rows, :]] * 2, axis=1)
        out_ref[rows, :] = first_ref[rows, :] - dot(left, factor_ref[...], (1, 0))


def expand_kernel(levels, tile, count, *refs):
    piece_refs = refs[:count]
    first_ref, left_ref, out_ref, flip_ref, factor_ref, out_buf, sems = refs[count:]
    split_factor(piece_refs, flip_ref, factor_ref)
    copies = []
    for step in range(out_buf.shape[0] // tile):
        rows = pl.ds(step * tile, tile)
        left = jnp.concatenate([left_ref[l, rows, :] for l in range(1, levels)] * 2, axis=1)
        out_buf[rows, :] = first_ref[rows, :] - dot(left, factor_ref[...], (1, 0))
        copies.append(pltpu.make_async_copy(out_buf.at[rows], out_ref.at[rows], sems.at[step]))
        copies[-1].start(priority=step % 2)
    for copy in copies:
        copy.wait()


def settings(mib, micros):
    return dict(
        compiler_params=pltpu.CompilerParams(vmem_limit_bytes=mib * MIB),
        cost_estimate=pl.CostEstimate(flops=int(micros * 1.1e9), bytes_accessed=0, transcendentals=0),
    )


def floats(*shape):
    return jax.ShapeDtypeStruct(shape, jnp.float32)


def per_device(rhs, leaf_order, leaf_inv, right_basis, left_basis, rank_perm, joined):
    levels, rows, rank = right_basis.shape
    nblocks, width, _ = leaf_inv.shape
    columns = rhs.shape[1]
    leaves = lax.axis_size("leaf")
    count = lax.axis_size("rows")
    slots = count // 2
    kinds = levels * rank
    size = kinds - rank
    share = columns // count
    gram_lanes = len(below_pairs(levels)) * rank

    per_step = blocks_per_step(nblocks, 3)
    flipped, gram = pl.pallas_call(
        functools.partial(gram_kernel, levels, per_step, width),
        in_specs=[pl.BlockSpec(memory_space=pltpu.HBM)] * 2,
        out_shape=[jax.ShapeDtypeStruct((kinds, rows), jnp.bfloat16), floats(rank, gram_lanes)],
        scratch_shapes=[
            pltpu.VMEM((levels, rows, rank), jnp.bfloat16),
            pltpu.VMEM((levels - 1, rows, rank), jnp.bfloat16),
            pltpu.VMEM((size, size), jnp.float32),
            pltpu.SemaphoreType.DMA((2, nblocks // per_step)),
        ],
        name="gram",
        **settings(24, 3),
    )(pltpu.with_memory_space_constraint(right_basis, pltpu.HBM),
      pltpu.with_memory_space_constraint(left_basis, pltpu.HBM))

    moved = pl.pallas_call(
        functools.partial(permute_kernel, blocks_per_step(nblocks, 9), width),
        out_shape=jax.ShapeDtypeStruct((nblocks, width, width), jnp.bfloat16),
        name="permute",
        **settings(8, 1.5),
    )(leaf_order, leaf_inv)

    def add(mine, got):
        return pl.pallas_call(
            add_kernel, out_shape=floats(*mine.shape), name="add", **settings(8, 0.1),
        )(mine, got)

    factors = pl.pallas_call(
        functools.partial(weigh_kernel, blocks_per_step(nblocks, 9), width),
        out_shape=jax.ShapeDtypeStruct((2 * kinds, rows), jnp.bfloat16),
        name="weigh",
        **settings(8, 2.4),
    )(moved, flipped, gram)

    def project(other, after):
        return pl.pallas_call(
            functools.partial(project_kernel, other),
            out_shape=floats(kinds, columns // 2),
            name="project_other" if other else "project_own",
            **settings(12, 1 if other else 8),
        )(factors, rhs, after)

    send = project(True, gram)
    got = swap(send, "rows", 1)
    mask = 2
    while mask < slots:
        gram = add(gram, swap(gram, "rows", mask))
        mask *= 2
    keep = project(False, gram)
    merged = pl.pallas_call(
        merge_kernel,
        out_shape=[floats(share, kinds)] * slots,
        scratch_shapes=[pltpu.VMEM((columns // 2, kinds), jnp.float32)],
        name="merge",
        **settings(8, 0.4),
    )(keep, got)
    parts = [merged[0]] + [swap(merged[s], "rows", 2 * s) for s in range(1, slots)]
    gram_other = swap(gram, "rows", slots)
    grams = [gram, gram_other, swap(gram, "rows", 1), swap(gram_other, "rows", 1)]
    prepared = pl.pallas_call(
        functools.partial(prepare_kernel, levels),
        in_specs=[pl.BlockSpec(memory_space=pltpu.HBM), pl.BlockSpec()],
        out_shape=floats(levels, 2 * rank, 2 * rank),
        scratch_shapes=[pltpu.VMEM((levels, 2 * rank, 2 * rank), jnp.float32), pltpu.SemaphoreType.DMA((levels,))],
        name="prepare",
        **settings(8, 2),
    )(pltpu.with_memory_space_constraint(joined, pltpu.HBM), rank_perm)

    def message_shape(level):
        return floats((levels - level) * share + len(below_pairs(levels, level)) * rank, rank)

    own, other, rest = pl.pallas_call(
        functools.partial(node_kernel, rank, slots),
        out_shape=[floats(share, rank)] * 2 + [floats(share, size)],
        name="node",
        **settings(8, 1),
    )(*parts, prepared)
    message = pl.pallas_call(
        functools.partial(correct_kernel, levels, rank),
        out_shape=message_shape(1),
        name="correct",
        **settings(8, 1),
    )(own, other, rest, *grams)
    early = [own] + [swap(own if slot < slots // 2 else other, "rows", 2 * slot) for slot in range(1, slots)]
    first = pl.pallas_call(
        functools.partial(solve_kernel, per_step, width),
        out_shape=floats(rows, columns),
        name="solve",
        **settings(8, 8),
    )(moved, rhs, merged[0])

    coefs = []
    for level in range(1, levels):
        last = level + 1 == levels
        arrived = swap(message, "leaf", 2 ** (level - 1))
        outs = pl.pallas_call(
            functools.partial(level_kernel, levels, level, share),
            out_shape=[floats(share, rank)] + ([] if last else [message_shape(level + 1)]),
            name=f"level{level}",
            **settings(8, 1 if last else 6),
        )(message, arrived, prepared, first if last else arrived)
        coefs.append(outs[0])
        message = outs[-1]
    stack = pl.pallas_call(
        stack_kernel, out_shape=floats(slots, share, rank), name="stack", **settings(8, 0.1),
    )(first, *early)
    second = pl.pallas_call(
        functools.partial(apply_kernel, per_step * width),
        out_shape=floats(rows, columns),
        scratch_shapes=[
            pltpu.VMEM((columns, rank), jnp.float32),
            pltpu.VMEM((2 * rank, columns), jnp.bfloat16),
        ],
        name="apply",
        **settings(8, 1.8),
    )(stack, swap(stack, "rows", 1), first, left_basis)

    pack = pl.pallas_call(
        pack_kernel, out_shape=floats(share, size), name="pack", **settings(8, 0.1),
    )(*coefs)
    pieces = []
    for slot in range(slots):
        piece = swap(pack, "rows", 2 * slot) if slot > 0 else pack
        if slot == slots - 1:
            piece = pl.pallas_call(
                relay_kernel, out_shape=floats(share, size), name="relay", **settings(8, 0.1),
            )(second, piece)
        pieces += [piece, swap(piece, "rows", 1)]
    return pl.pallas_call(
        functools.partial(expand_kernel, levels, per_step * width, count),
        out_specs=pl.BlockSpec(memory_space=pl.ANY),
        out_shape=floats(rows, columns),
        scratch_shapes=[
            pltpu.VMEM((columns, size), jnp.float32),
            pltpu.VMEM((2 * size, columns), jnp.bfloat16),
            pltpu.VMEM((rows, columns), jnp.float32),
            pltpu.SemaphoreType.DMA((nblocks // per_step,)),
        ],
        name="expand",
        **settings(16, 5),
    )(*pieces, second, left_basis)


def solution(mesh):
    return jax.shard_map(
        per_device,
        mesh=mesh,
        in_specs=(
            P(("leaf", "rows"), None),
            P(("leaf", "rows"), None),
            P(("leaf", "rows"), None, None),
            P(None, ("leaf", "rows"), None),
            P(None, ("leaf", "rows"), None),
            P(),
            P(),
        ),
        out_specs=P(("leaf", "rows"), None),
        check_vma=False,
    )
```

```python
import functools

import jax
import jax.numpy as jnp
from jax import lax
from jax.experimental import pallas as pl
from jax.experimental.pallas import tpu as pltpu
from jax.sharding import PartitionSpec as P

HIGHEST = lax.Precision.HIGHEST
MIB = 1 << 20


def dot(a, b, contract, exact=False):
    return lax.dot_general(
        a, b, ((contract[:1], contract[1:]), ((), ())),
        precision=HIGHEST if exact else None, preferred_element_type=jnp.float32,
    )


def halves(value):
    high_part = value.astype(jnp.bfloat16)
    low_part = (value - high_part.astype(jnp.float32)).astype(jnp.bfloat16)
    return high_part, low_part


def swap(value, axis, mask):
    count = lax.axis_size(axis)
    return lax.ppermute(value, axis, [(i, i ^ mask) for i in range(count)])


def blocks_per_step(nblocks, most):
    return max(size for size in range(1, most + 1) if nblocks % size == 0)


def below_pairs(levels, first=0):
    return [(level, below) for level in range(levels) for below in range(first, level)]


def gram_kernel(levels, per_step, width, right_ref, left_ref, flip_ref, keep_ref, send_ref,
                right_buf, left_buf, gram_ref, sems):
    rank = right_ref.shape[2]
    half = rank // 2
    tile = per_step * width
    steps = right_ref.shape[1] // tile

    def copies(step):
        rows = pl.ds(pl.multiple_of(step * tile, tile), tile)
        return (
            pltpu.make_async_copy(right_ref.at[:, rows], right_buf.at[:, rows], sems.at[0, step]),
            pltpu.make_async_copy(left_ref.at[:levels - 1, rows], left_buf.at[:, rows], sems.at[1, step]),
        )

    for step in range(steps):
        for copy in copies(step):
            copy.start()
    gram_ref[...] = jnp.zeros_like(gram_ref)

    def body(step, _):
        for copy in copies(step):
            copy.wait()
        rows = pl.ds(pl.multiple_of(step * tile, tile), tile)
        right = jnp.concatenate([right_buf[l, rows, :] for l in range(levels)], axis=1).T
        flip_ref[:, rows] = right
        left = jnp.concatenate([left_buf[l, rows, :] for l in range(levels - 1)], axis=1)
        gram_ref[...] += dot(right[rank:], left, (1, 0))
        return 0

    lax.fori_loop(0, steps, body, 0)
    core = lax.axis_index("rows") % 2
    for spot, (level, below) in enumerate(below_pairs(levels)):
        lanes = pl.ds(spot * rank, rank)
        for ref, side in ((keep_ref, core), (send_ref, 1 - core)):
            rows = pl.ds(pl.multiple_of((level - 1) * rank + side * half, half), half)
            ref[:, lanes] = gram_ref[rows, pl.ds(below * rank, rank)]


def permute_kernel(per_step, width, order_ref, inv_ref, moved_ref):
    place = lax.broadcasted_iota(jnp.int32, (width, width), 0)

    def body(step, _):
        for b in range(per_step):
            block = step * per_step + b
            chosen = (place == order_ref[pl.ds(block, 1), :]).astype(jnp.float32).astype(jnp.bfloat16)
            moved_ref[block] = dot(inv_ref[block], chosen, (1, 1)).astype(jnp.bfloat16)
        return 0

    lax.fori_loop(0, inv_ref.shape[0] // per_step, body, 0)


def weigh_kernel(per_step, width, moved_ref, flip_ref, after_ref, factor_ref):
    kinds = flip_ref.shape[0]

    def body(step, _):
        for b in range(per_step):
            block = step * per_step + b
            lanes = pl.ds(pl.multiple_of(block * width, width), width)
            high_part, low_part = halves(dot(flip_ref[:, lanes], moved_ref[block], (1, 0)))
            factor_ref[:kinds, lanes] = high_part
            factor_ref[kinds:, lanes] = low_part
        return 0

    lax.fori_loop(0, moved_ref.shape[0] // per_step, body, 0)


def solve_kernel(per_step, width, moved_ref, rhs_ref, *refs):
    out_ref = refs[-1]

    def body(step, _):
        for b in range(per_step):
            block = step * per_step + b
            rows = pl.ds(pl.multiple_of(block * width, width), width)
            out_ref[rows, :] = dot(moved_ref[block], rhs_ref[rows, :], (1, 0))
        return 0

    lax.fori_loop(0, moved_ref.shape[0] // per_step, body, 0)


def project_kernel(other, factor_ref, rhs_ref, after_ref, out_ref):
    kinds, part = out_ref.shape
    core = lax.axis_index("rows") % 2
    lanes = pl.ds(pl.multiple_of((1 - core if other else core) * part, part), part)
    total = dot(factor_ref[...], rhs_ref[:, lanes], (1, 0))
    out_ref[...] = total[:kinds] + total[kinds:]


def merge_kernel(keep_ref, got_ref, *refs):
    out_refs, flip_ref = refs[:-1], refs[-1]
    share = out_refs[0].shape[0]
    chip = lax.axis_index("rows") // 2
    flip_ref[...] = (keep_ref[...] + got_ref[...]).T
    for slot, out_ref in enumerate(out_refs):
        out_ref[...] = flip_ref[pl.ds(pl.multiple_of((chip ^ slot) * share, share), share), :]


def add_kernel(mine_ref, got_ref, out_ref):
    out_ref[...] = mine_ref[...] + got_ref[...]


def prepare_kernel(levels, joined_ref, perm_ref, out_ref, joined_buf, sems):
    rank = perm_ref.shape[1]
    leaves = lax.axis_size("leaf")
    leaf = lax.axis_index("leaf")
    copies = []
    for level in range(levels):
        node = 2 * leaves - 2 * leaves // 2 ** level + leaf // 2 ** level
        copies.append(pltpu.make_async_copy(joined_ref.at[node], joined_buf.at[level], sems.at[level]))
        copies[-1].start()
    spot = lax.broadcasted_iota(jnp.int32, (rank, rank), 0)
    for level in range(levels):
        copies[level].wait()
        chosen = (spot == perm_ref[level:level + 1, :]).astype(jnp.float32)
        for side in range(2):
            lanes = pl.ds(side * rank, rank)
            out_ref[level, :, lanes] = dot(joined_buf[level, :, lanes], chosen, (1, 1), True)


def by_side(side, own, other):
    return jnp.where(side == 0, own, other), jnp.where(side == 0, other, own)


def pack_message(message_ref, pieces):
    row = 0
    for piece in pieces:
        message_ref[pl.ds(row, piece.shape[0]), :] = piece
        row += piece.shape[0]


def node_kernel(rank, slots, *refs):
    part_refs = refs[:slots]
    joined_ref, own_ref, other_ref, rest_ref = refs[slots:]
    side = lax.axis_index("rows") // slots
    half = slots // 2
    sums = [sum(ref[...] for ref in part_refs[:half]), sum(ref[...] for ref in part_refs[half:])]
    picked = jnp.concatenate(by_side(side, sums[0][:, :rank], sums[1][:, :rank]), axis=1)
    coef = dot(picked, joined_ref[0], (1, 1), True)
    own_ref[...], other_ref[...] = by_side(side, coef[:, :rank], coef[:, rank:])
    rest_ref[...] = (sums[0] + sums[1])[:, rank:]


def correct_kernel(levels, rank, own_ref, other_ref, rest_ref, mine_ref, theirs_ref, pair_mine_ref,
                   pair_theirs_ref, message_ref):
    core = lax.axis_index("rows") % 2
    grams = [jnp.concatenate(by_side(core, mine_ref[...], pair_mine_ref[...]), axis=0),
             jnp.concatenate(by_side(core, theirs_ref[...], pair_theirs_ref[...]), axis=0)]
    pairs = below_pairs(levels)
    lanes = {pair: slice(spot * rank, (spot + 1) * rank) for spot, pair in enumerate(pairs)}
    joint = jnp.concatenate(
        [jnp.concatenate([gram[:, lanes[level, 0]] for gram in grams], axis=1) for level in range(1, levels)], axis=0)
    rest = rest_ref[...] - dot(jnp.concatenate([own_ref[...], other_ref[...]], axis=1), joint, (1, 1), True)
    pieces = [rest[:, level * rank:(level + 1) * rank] for level in range(levels - 1)]
    for pair in pairs:
        if pair[1] > 0:
            pieces.append(grams[0][:, lanes[pair]] + grams[1][:, lanes[pair]])
    pack_message(message_ref, pieces)


def level_kernel(levels, level, share, sent_ref, got_ref, joined_ref, after_ref, coef_ref, *message_ref):
    rank = sent_ref.shape[1]
    side = lax.axis_index("leaf") // 2 ** (level - 1) % 2
    more = levels - level
    values = []
    for ref in (sent_ref, got_ref):
        values.append([ref[pl.ds(i * share, share), :] for i in range(more)])
    picked = jnp.concatenate(by_side(side, values[0][0], values[1][0]), axis=1)
    coef = dot(picked, joined_ref[level], (1, 1), True)
    sides = by_side(side, coef[:, :rank], coef[:, rank:])
    coef_ref[...] = sides[0]
    if not message_ref:
        return
    pairs = below_pairs(levels, level)
    grams = []
    for ref in (sent_ref, got_ref):
        grams.append({pair: ref[pl.ds(more * share + spot * rank, rank), :] for spot, pair in enumerate(pairs)})
    uppers = list(range(level + 1, levels))
    joint = jnp.concatenate(
        [jnp.concatenate([gram[upper, level] for gram in grams], axis=1) for upper in uppers], axis=0)
    change = dot(jnp.concatenate(sides, axis=1), joint, (1, 1), True)
    pieces = [values[0][upper - level] + values[1][upper - level] - change[:, i * rank:(i + 1) * rank]
              for i, upper in enumerate(uppers)]
    for pair in pairs:
        if pair[1] > level:
            pieces.append(grams[0][pair] + grams[1][pair])
    pack_message(message_ref[0], pieces)


def pack_kernel(*refs):
    refs[-1][...] = jnp.concatenate([ref[...] for ref in refs[:-1]], axis=1)


def stack_kernel(after_ref, *refs):
    for slot, ref in enumerate(refs[:-1]):
        refs[-1][slot] = ref[...]


def relay_kernel(after_ref, ref, out_ref):
    out_ref[...] = ref[...]


def split_factor(pieces, flip_ref, factor_ref):
    share, kinds = pieces[0].shape
    slots = len(pieces) // 2
    me = lax.axis_index("rows")
    for mask, ref in enumerate(pieces):
        owner = me ^ mask
        row = (owner % 2 * slots + owner // 2) * share
        flip_ref[pl.ds(pl.multiple_of(row, share), share), :] = ref[...]
    high_part, low_part = halves(flip_ref[...].T)
    factor_ref[:kinds, :] = high_part
    factor_ref[kinds:, :] = low_part


def apply_kernel(tile, own_ref, pair_ref, first_ref, left_ref, out_ref, flip_ref, factor_ref):
    pieces = [ref.at[slot] for slot in range(own_ref.shape[0]) for ref in (own_ref, pair_ref)]
    split_factor(pieces, flip_ref, factor_ref)
    for row in range(0, out_ref.shape[0], tile):
        rows = pl.ds(row, tile)
        left = jnp.concatenate([left_ref[0, rows, :]] * 2, axis=1)
        out_ref[rows, :] = first_ref[rows, :] - dot(left, factor_ref[...], (1, 0))


def expand_kernel(levels, tile, count, *refs):
    piece_refs = refs[:count]
    first_ref, left_ref, out_ref, flip_ref, factor_ref, out_buf, sems = refs[count:]
    split_factor(piece_refs, flip_ref, factor_ref)
    copies = []
    for step in range(out_buf.shape[0] // tile):
        rows = pl.ds(step * tile, tile)
        left = jnp.concatenate([left_ref[l, rows, :] for l in range(1, levels)] * 2, axis=1)
        out_buf[rows, :] = first_ref[rows, :] - dot(left, factor_ref[...], (1, 0))
        copies.append(pltpu.make_async_copy(out_buf.at[rows], out_ref.at[rows], sems.at[step]))
        copies[-1].start(priority=step % 2)
    for copy in copies:
        copy.wait()


def settings(mib, micros):
    return dict(
        compiler_params=pltpu.CompilerParams(vmem_limit_bytes=mib * MIB),
        cost_estimate=pl.CostEstimate(flops=int(micros * 1.1e9), bytes_accessed=0, transcendentals=0),
    )


def floats(*shape):
    return jax.ShapeDtypeStruct(shape, jnp.float32)


def per_device(rhs, leaf_order, leaf_inv, right_basis, left_basis, rank_perm, joined):
    levels, rows, rank = right_basis.shape
    nblocks, width, _ = leaf_inv.shape
    columns = rhs.shape[1]
    leaves = lax.axis_size("leaf")
    count = lax.axis_size("rows")
    slots = count // 2
    kinds = levels * rank
    size = kinds - rank
    share = columns // count
    gram_lanes = len(below_pairs(levels)) * rank

    per_step = blocks_per_step(nblocks, 3)
    flipped, gram_keep, gram_send = pl.pallas_call(
        functools.partial(gram_kernel, levels, per_step, width),
        in_specs=[pl.BlockSpec(memory_space=pltpu.HBM)] * 2,
        out_shape=[jax.ShapeDtypeStruct((kinds, rows), jnp.bfloat16)] + [floats(rank // 2, gram_lanes)] * 2,
        scratch_shapes=[
            pltpu.VMEM((levels, rows, rank), jnp.bfloat16),
            pltpu.VMEM((levels - 1, rows, rank), jnp.bfloat16),
            pltpu.VMEM((size, size), jnp.float32),
            pltpu.SemaphoreType.DMA((2, nblocks // per_step)),
        ],
        name="gram",
        **settings(24, 3),
    )(pltpu.with_memory_space_constraint(right_basis, pltpu.HBM),
      pltpu.with_memory_space_constraint(left_basis, pltpu.HBM))

    gram_got = swap(gram_send, "rows", 1)
    moved = pl.pallas_call(
        functools.partial(permute_kernel, blocks_per_step(nblocks, 9), width),
        out_shape=jax.ShapeDtypeStruct((nblocks, width, width), jnp.bfloat16),
        name="permute",
        **settings(8, 1.5),
    )(leaf_order, leaf_inv)

    def add(mine, got):
        return pl.pallas_call(
            add_kernel, out_shape=floats(*mine.shape), name="add", **settings(8, 0.1),
        )(mine, got)

    gram = add(gram_keep, gram_got)
    factors = pl.pallas_call(
        functools.partial(weigh_kernel, blocks_per_step(nblocks, 9), width),
        out_shape=jax.ShapeDtypeStruct((2 * kinds, rows), jnp.bfloat16),
        name="weigh",
        **settings(8, 2.4),
    )(moved, flipped, gram)

    def project(other, after):
        return pl.pallas_call(
            functools.partial(project_kernel, other),
            out_shape=floats(kinds, columns // 2),
            name="project_other" if other else "project_own",
            **settings(12, 1 if other else 4),
        )(factors, rhs, after)

    send = project(True, gram)
    got = swap(send, "rows", 1)
    mask = 2
    while mask < slots:
        gram = add(gram, swap(gram, "rows", mask))
        mask *= 2
    keep = project(False, gram)
    merged = pl.pallas_call(
        merge_kernel,
        out_shape=[floats(share, kinds)] * slots,
        scratch_shapes=[pltpu.VMEM((columns // 2, kinds), jnp.float32)],
        name="merge",
        **settings(8, 0.4),
    )(keep, got)
    parts = [merged[0]] + [swap(merged[s], "rows", 2 * s) for s in range(1, slots)]
    gram_other = swap(gram, "rows", slots)
    grams = [gram, gram_other, swap(gram, "rows", 1), swap(gram_other, "rows", 1)]
    prepared = pl.pallas_call(
        functools.partial(prepare_kernel, levels),
        in_specs=[pl.BlockSpec(memory_space=pltpu.HBM), pl.BlockSpec()],
        out_shape=floats(levels, 2 * rank, 2 * rank),
        scratch_shapes=[pltpu.VMEM((levels, 2 * rank, 2 * rank), jnp.float32), pltpu.SemaphoreType.DMA((levels,))],
        name="prepare",
        **settings(8, 2),
    )(pltpu.with_memory_space_constraint(joined, pltpu.HBM), rank_perm)

    def message_shape(level):
        return floats((levels - level) * share + len(below_pairs(levels, level)) * rank, rank)

    own, other, rest = pl.pallas_call(
        functools.partial(node_kernel, rank, slots),
        out_shape=[floats(share, rank)] * 2 + [floats(share, size)],
        name="node",
        **settings(8, 1),
    )(*parts, prepared)
    message = pl.pallas_call(
        functools.partial(correct_kernel, levels, rank),
        out_shape=message_shape(1),
        name="correct",
        **settings(8, 1),
    )(own, other, rest, *grams)
    early = [own] + [swap(own if slot < slots // 2 else other, "rows", 2 * slot) for slot in range(1, slots)]
    first = pl.pallas_call(
        functools.partial(solve_kernel, per_step, width),
        out_shape=floats(rows, columns),
        name="solve",
        **settings(8, 8),
    )(moved, rhs, merged[0])

    coefs = []
    for level in range(1, levels):
        last = level + 1 == levels
        arrived = swap(message, "leaf", 2 ** (level - 1))
        outs = pl.pallas_call(
            functools.partial(level_kernel, levels, level, share),
            out_shape=[floats(share, rank)] + ([] if last else [message_shape(level + 1)]),
            name=f"level{level}",
            **settings(8, 1 if last else 6),
        )(message, arrived, prepared, first if last else arrived)
        coefs.append(outs[0])
        message = outs[-1]
    stack = pl.pallas_call(
        stack_kernel, out_shape=floats(slots, share, rank), name="stack", **settings(8, 0.1),
    )(first, *early)
    second = pl.pallas_call(
        functools.partial(apply_kernel, per_step * width),
        out_shape=floats(rows, columns),
        scratch_shapes=[
            pltpu.VMEM((columns, rank), jnp.float32),
            pltpu.VMEM((2 * rank, columns), jnp.bfloat16),
        ],
        name="apply",
        **settings(8, 1.8),
    )(stack, swap(stack, "rows", 1), first, left_basis)

    pack = pl.pallas_call(
        pack_kernel, out_shape=floats(share, size), name="pack", **settings(8, 0.1),
    )(*coefs)
    pieces = []
    for slot in range(slots):
        piece = swap(pack, "rows", 2 * slot) if slot > 0 else pack
        if slot == slots - 1:
            piece = pl.pallas_call(
                relay_kernel, out_shape=floats(share, size), name="relay", **settings(8, 0.1),
            )(second, piece)
        pieces += [piece, swap(piece, "rows", 1)]
    return pl.pallas_call(
        functools.partial(expand_kernel, levels, per_step * width, count),
        out_specs=pl.BlockSpec(memory_space=pl.ANY),
        out_shape=floats(rows, columns),
        scratch_shapes=[
            pltpu.VMEM((columns, size), jnp.float32),
            pltpu.VMEM((2 * size, columns), jnp.bfloat16),
            pltpu.VMEM((rows, columns), jnp.float32),
            pltpu.SemaphoreType.DMA((nblocks // per_step,)),
        ],
        name="expand",
        **settings(16, 5),
    )(*pieces, second, left_basis)


def solution(mesh):
    return jax.shard_map(
        per_device,
        mesh=mesh,
        in_specs=(
            P(("leaf", "rows"), None),
            P(("leaf", "rows"), None),
            P(("leaf", "rows"), None, None),
            P(None, ("leaf", "rows"), None),
            P(None, ("leaf", "rows"), None),
            P(),
            P(),
        ),
        out_specs=P(("leaf", "rows"), None),
        check_vma=False,
    )
```

```python
import functools

import jax
import jax.numpy as jnp
from jax import lax
from jax.experimental import pallas as pl
from jax.experimental.pallas import tpu as pltpu
from jax.sharding import PartitionSpec as P

HIGHEST = lax.Precision.HIGHEST
MIB = 1 << 20


def dot(a, b, contract, exact=False):
    return lax.dot_general(
        a, b, ((contract[:1], contract[1:]), ((), ())),
        precision=HIGHEST if exact else None, preferred_element_type=jnp.float32,
    )


def halves(value):
    high_part = value.astype(jnp.bfloat16)
    low_part = (value - high_part.astype(jnp.float32)).astype(jnp.bfloat16)
    return high_part, low_part


def swap(value, axis, mask):
    count = lax.axis_size(axis)
    return lax.ppermute(value, axis, [(i, i ^ mask) for i in range(count)])


def blocks_per_step(nblocks, most):
    return max(size for size in range(1, most + 1) if nblocks % size == 0)


def below_pairs(levels, first=0):
    return [(level, below) for level in range(levels) for below in range(first, level)]


def gram_kernel(levels, per_step, width, right_ref, left_ref, flip_ref, keep_ref, send_ref,
                right_buf, left_buf, gram_ref, sems):
    rank = right_ref.shape[2]
    half = rank // 2
    tile = per_step * width
    steps = right_ref.shape[1] // tile

    def copies(step):
        rows = pl.ds(pl.multiple_of(step * tile, tile), tile)
        return (
            pltpu.make_async_copy(right_ref.at[:, rows], right_buf.at[:, rows], sems.at[0, step]),
            pltpu.make_async_copy(left_ref.at[:levels - 1, rows], left_buf.at[:, rows], sems.at[1, step]),
        )

    for step in range(steps):
        for copy in copies(step):
            copy.start()
    gram_ref[...] = jnp.zeros_like(gram_ref)

    def body(step, _):
        for copy in copies(step):
            copy.wait()
        rows = pl.ds(pl.multiple_of(step * tile, tile), tile)
        right = jnp.concatenate([right_buf[l, rows, :] for l in range(levels)], axis=1).T
        flip_ref[:, rows] = right
        left = jnp.concatenate([left_buf[l, rows, :] for l in range(levels - 1)], axis=1)
        gram_ref[...] += dot(right[rank:], left, (1, 0))
        return 0

    lax.fori_loop(0, steps, body, 0)
    core = lax.axis_index("rows") % 2
    for spot, (level, below) in enumerate(below_pairs(levels)):
        lanes = pl.ds(spot * rank, rank)
        for ref, side in ((keep_ref, core), (send_ref, 1 - core)):
            rows = pl.ds(pl.multiple_of((level - 1) * rank + side * half, half), half)
            ref[:, lanes] = gram_ref[rows, pl.ds(below * rank, rank)]


def permute_kernel(per_step, width, order_ref, inv_ref, moved_ref):
    place = lax.broadcasted_iota(jnp.int32, (width, width), 0)

    def body(step, _):
        for b in range(per_step):
            block = step * per_step + b
            chosen = (place == order_ref[pl.ds(block, 1), :]).astype(jnp.float32).astype(jnp.bfloat16)
            moved_ref[block] = dot(inv_ref[block], chosen, (1, 1)).astype(jnp.bfloat16)
        return 0

    lax.fori_loop(0, inv_ref.shape[0] // per_step, body, 0)


def other_lanes(part, other=True):
    core = lax.axis_index("rows") % 2
    return pl.ds(pl.multiple_of((1 - core if other else core) * part, part), part)


def weigh_kernel(per_step, width, moved_ref, flip_ref, after_ref, rhs_ref,
                 factor_ref, rhs_out, out_ref, total_ref, sems):
    kinds, part = out_ref.shape
    tile = per_step * width
    steps = rhs_out.shape[0] // tile
    lanes = other_lanes(part)
    copies = []
    for step in range(steps):
        rows = pl.ds(step * tile, tile)
        copies.append(pltpu.make_async_copy(rhs_ref.at[rows], rhs_out.at[rows], sems.at[step]))
        copies[-1].start(priority=step % 2)

    def weigh(step):
        for block in range(step * per_step, (step + 1) * per_step):
            spot = pl.ds(block * width, width)
            high_part, low_part = halves(dot(flip_ref[:, spot], moved_ref[block], (1, 0)))
            factor_ref[:kinds, spot] = high_part
            factor_ref[kinds:, spot] = low_part

    weigh(0)
    for step in range(steps):
        if step + 1 < steps:
            weigh(step + 1)
        copies[step].wait()
        rows = pl.ds(step * tile, tile)
        term = dot(factor_ref[:, rows], rhs_out[rows, lanes], (1, 0))
        total_ref[...] = term if step == 0 else total_ref[...] + term
    out_ref[...] = total_ref[:kinds] + total_ref[kinds:]


def solve_kernel(per_step, width, moved_ref, rhs_ref, *refs):
    out_ref = refs[-1]

    def body(step, _):
        for b in range(per_step):
            block = step * per_step + b
            rows = pl.ds(pl.multiple_of(block * width, width), width)
            out_ref[rows, :] = dot(moved_ref[block], rhs_ref[rows, :], (1, 0))
        return 0

    lax.fori_loop(0, moved_ref.shape[0] // per_step, body, 0)


def project_kernel(factor_ref, rhs_ref, after_ref, out_ref):
    kinds, part = out_ref.shape
    total = dot(factor_ref[...], rhs_ref[:, other_lanes(part, False)], (1, 0))
    out_ref[...] = total[:kinds] + total[kinds:]


def merge_kernel(keep_ref, got_ref, *refs):
    out_refs, flip_ref = refs[:-1], refs[-1]
    share = out_refs[0].shape[0]
    chip = lax.axis_index("rows") // 2
    flip_ref[...] = (keep_ref[...] + got_ref[...]).T
    for slot, out_ref in enumerate(out_refs):
        out_ref[...] = flip_ref[pl.ds(pl.multiple_of((chip ^ slot) * share, share), share), :]


def add_kernel(mine_ref, got_ref, out_ref):
    out_ref[...] = mine_ref[...] + got_ref[...]


def prepare_kernel(levels, joined_ref, perm_ref, out_ref, joined_buf, sems):
    rank = perm_ref.shape[1]
    leaves = lax.axis_size("leaf")
    leaf = lax.axis_index("leaf")
    copies = []
    for level in range(levels):
        node = 2 * leaves - 2 * leaves // 2 ** level + leaf // 2 ** level
        copies.append(pltpu.make_async_copy(joined_ref.at[node], joined_buf.at[level], sems.at[level]))
        copies[-1].start()
    spot = lax.broadcasted_iota(jnp.int32, (rank, rank), 0)
    for level in range(levels):
        copies[level].wait()
        chosen = (spot == perm_ref[level:level + 1, :]).astype(jnp.float32)
        for side in range(2):
            lanes = pl.ds(side * rank, rank)
            out_ref[level, :, lanes] = dot(joined_buf[level, :, lanes], chosen, (1, 1), True)


def by_side(side, own, other):
    return jnp.where(side == 0, own, other), jnp.where(side == 0, other, own)


def pack_message(message_ref, pieces):
    row = 0
    for piece in pieces:
        message_ref[pl.ds(row, piece.shape[0]), :] = piece
        row += piece.shape[0]


def node_kernel(rank, slots, *refs):
    part_refs = refs[:slots]
    joined_ref, own_ref, other_ref, rest_ref = refs[slots:]
    side = lax.axis_index("rows") // slots
    half = slots // 2
    sums = [sum(ref[...] for ref in part_refs[:half]), sum(ref[...] for ref in part_refs[half:])]
    picked = jnp.concatenate(by_side(side, sums[0][:, :rank], sums[1][:, :rank]), axis=1)
    coef = dot(picked, joined_ref[0], (1, 1), True)
    own_ref[...], other_ref[...] = by_side(side, coef[:, :rank], coef[:, rank:])
    rest_ref[...] = (sums[0] + sums[1])[:, rank:]


def correct_kernel(levels, rank, own_ref, other_ref, rest_ref, mine_ref, theirs_ref, pair_mine_ref,
                   pair_theirs_ref, message_ref):
    core = lax.axis_index("rows") % 2
    grams = [jnp.concatenate(by_side(core, mine_ref[...], pair_mine_ref[...]), axis=0),
             jnp.concatenate(by_side(core, theirs_ref[...], pair_theirs_ref[...]), axis=0)]
    pairs = below_pairs(levels)
    lanes = {pair: slice(spot * rank, (spot + 1) * rank) for spot, pair in enumerate(pairs)}
    joint = jnp.concatenate(
        [jnp.concatenate([gram[:, lanes[level, 0]] for gram in grams], axis=1) for level in range(1, levels)], axis=0)
    rest = rest_ref[...] - dot(jnp.concatenate([own_ref[...], other_ref[...]], axis=1), joint, (1, 1), True)
    pieces = [rest[:, level * rank:(level + 1) * rank] for level in range(levels - 1)]
    for pair in pairs:
        if pair[1] > 0:
            pieces.append(grams[0][:, lanes[pair]] + grams[1][:, lanes[pair]])
    pack_message(message_ref, pieces)


def level_kernel(levels, level, share, sent_ref, got_ref, joined_ref, after_ref, coef_ref, *message_ref):
    rank = sent_ref.shape[1]
    side = lax.axis_index("leaf") // 2 ** (level - 1) % 2
    more = levels - level
    values = []
    for ref in (sent_ref, got_ref):
        values.append([ref[pl.ds(i * share, share), :] for i in range(more)])
    picked = jnp.concatenate(by_side(side, values[0][0], values[1][0]), axis=1)
    coef = dot(picked, joined_ref[level], (1, 1), True)
    sides = by_side(side, coef[:, :rank], coef[:, rank:])
    coef_ref[...] = sides[0]
    if not message_ref:
        return
    pairs = below_pairs(levels, level)
    grams = []
    for ref in (sent_ref, got_ref):
        grams.append({pair: ref[pl.ds(more * share + spot * rank, rank), :] for spot, pair in enumerate(pairs)})
    uppers = list(range(level + 1, levels))
    joint = jnp.concatenate(
        [jnp.concatenate([gram[upper, level] for gram in grams], axis=1) for upper in uppers], axis=0)
    change = dot(jnp.concatenate(sides, axis=1), joint, (1, 1), True)
    pieces = [values[0][upper - level] + values[1][upper - level] - change[:, i * rank:(i + 1) * rank]
              for i, upper in enumerate(uppers)]
    for pair in pairs:
        if pair[1] > level:
            pieces.append(grams[0][pair] + grams[1][pair])
    pack_message(message_ref[0], pieces)


def pack_kernel(*refs):
    refs[-1][...] = jnp.concatenate([ref[...] for ref in refs[:-1]], axis=1)


def stack_kernel(after_ref, *refs):
    for slot, ref in enumerate(refs[:-1]):
        refs[-1][slot] = ref[...]


def relay_kernel(after_ref, ref, out_ref):
    out_ref[...] = ref[...]


def split_factor(pieces, flip_ref, factor_ref):
    share, kinds = pieces[0].shape
    slots = len(pieces) // 2
    me = lax.axis_index("rows")
    for mask, ref in enumerate(pieces):
        owner = me ^ mask
        row = (owner % 2 * slots + owner // 2) * share
        flip_ref[pl.ds(pl.multiple_of(row, share), share), :] = ref[...]
    high_part, low_part = halves(flip_ref[...].T)
    factor_ref[:kinds, :] = high_part
    factor_ref[kinds:, :] = low_part


def apply_kernel(tile, own_ref, pair_ref, first_ref, left_ref, out_ref, flip_ref, factor_ref):
    pieces = [ref.at[slot] for slot in range(own_ref.shape[0]) for ref in (own_ref, pair_ref)]
    split_factor(pieces, flip_ref, factor_ref)
    for row in range(0, out_ref.shape[0], tile):
        rows = pl.ds(row, tile)
        left = jnp.concatenate([left_ref[0, rows, :]] * 2, axis=1)
        out_ref[rows, :] = first_ref[rows, :] - dot(left, factor_ref[...], (1, 0))


def expand_kernel(levels, tile, count, *refs):
    piece_refs = refs[:count]
    first_ref, left_ref, out_ref, flip_ref, factor_ref, out_buf, sems = refs[count:]
    split_factor(piece_refs, flip_ref, factor_ref)
    copies = []
    for step in range(out_buf.shape[0] // tile):
        rows = pl.ds(step * tile, tile)
        left = jnp.concatenate([left_ref[l, rows, :] for l in range(1, levels)] * 2, axis=1)
        out_buf[rows, :] = first_ref[rows, :] - dot(left, factor_ref[...], (1, 0))
        copies.append(pltpu.make_async_copy(out_buf.at[rows], out_ref.at[rows], sems.at[step]))
        copies[-1].start(priority=step % 2)
    for copy in copies:
        copy.wait()


def settings(mib, micros):
    return dict(
        compiler_params=pltpu.CompilerParams(vmem_limit_bytes=mib * MIB),
        cost_estimate=pl.CostEstimate(flops=int(micros * 1.1e9), bytes_accessed=0, transcendentals=0),
    )


def floats(*shape):
    return jax.ShapeDtypeStruct(shape, jnp.float32)


def per_device(rhs, leaf_order, leaf_inv, right_basis, left_basis, rank_perm, joined):
    levels, rows, rank = right_basis.shape
    nblocks, width, _ = leaf_inv.shape
    columns = rhs.shape[1]
    leaves = lax.axis_size("leaf")
    count = lax.axis_size("rows")
    slots = count // 2
    kinds = levels * rank
    size = kinds - rank
    share = columns // count
    gram_lanes = len(below_pairs(levels)) * rank

    per_step = blocks_per_step(nblocks, 3)
    flipped, gram_keep, gram_send = pl.pallas_call(
        functools.partial(gram_kernel, levels, per_step, width),
        in_specs=[pl.BlockSpec(memory_space=pltpu.HBM)] * 2,
        out_shape=[jax.ShapeDtypeStruct((kinds, rows), jnp.bfloat16)] + [floats(rank // 2, gram_lanes)] * 2,
        scratch_shapes=[
            pltpu.VMEM((levels, rows, rank), jnp.bfloat16),
            pltpu.VMEM((levels - 1, rows, rank), jnp.bfloat16),
            pltpu.VMEM((size, size), jnp.float32),
            pltpu.SemaphoreType.DMA((2, nblocks // per_step)),
        ],
        name="gram",
        **settings(24, 3),
    )(pltpu.with_memory_space_constraint(right_basis, pltpu.HBM),
      pltpu.with_memory_space_constraint(left_basis, pltpu.HBM))

    gram_got = swap(gram_send, "rows", 1)
    moved = pl.pallas_call(
        functools.partial(permute_kernel, blocks_per_step(nblocks, 9), width),
        out_shape=jax.ShapeDtypeStruct((nblocks, width, width), jnp.bfloat16),
        name="permute",
        **settings(8, 1.5),
    )(leaf_order, leaf_inv)

    def add(mine, got):
        return pl.pallas_call(
            add_kernel, out_shape=floats(*mine.shape), name="add", **settings(8, 0.1),
        )(mine, got)

    gram = add(gram_keep, gram_got)
    factors, rhs, send = pl.pallas_call(
        functools.partial(weigh_kernel, per_step, width),
        in_specs=[pl.BlockSpec()] * 3 + [pl.BlockSpec(memory_space=pltpu.HBM)],
        out_shape=[
            jax.ShapeDtypeStruct((2 * kinds, rows), jnp.bfloat16),
            jax.ShapeDtypeStruct((rows, columns), jnp.bfloat16),
            floats(kinds, columns // 2),
        ],
        scratch_shapes=[
            pltpu.VMEM((2 * kinds, columns // 2), jnp.float32),
            pltpu.SemaphoreType.DMA((nblocks // per_step,)),
        ],
        name="weigh",
        **settings(12, 2),
    )(moved, flipped, gram, pltpu.with_memory_space_constraint(rhs, pltpu.HBM))
    got = swap(send, "rows", 1)
    mask = 2
    while mask < slots:
        gram = add(gram, swap(gram, "rows", mask))
        mask *= 2
    keep = pl.pallas_call(
        project_kernel, out_shape=floats(kinds, columns // 2), name="project", **settings(12, 4),
    )(factors, rhs, gram)
    merged = pl.pallas_call(
        merge_kernel,
        out_shape=[floats(share, kinds)] * slots,
        scratch_shapes=[pltpu.VMEM((columns // 2, kinds), jnp.float32)],
        name="merge",
        **settings(8, 0.4),
    )(keep, got)
    parts = [merged[0]] + [swap(merged[s], "rows", 2 * s) for s in range(1, slots)]
    gram_other = swap(gram, "rows", slots)
    grams = [gram, gram_other, swap(gram, "rows", 1), swap(gram_other, "rows", 1)]
    prepared = pl.pallas_call(
        functools.partial(prepare_kernel, levels),
        in_specs=[pl.BlockSpec(memory_space=pltpu.HBM), pl.BlockSpec()],
        out_shape=floats(levels, 2 * rank, 2 * rank),
        scratch_shapes=[pltpu.VMEM((levels, 2 * rank, 2 * rank), jnp.float32), pltpu.SemaphoreType.DMA((levels,))],
        name="prepare",
        **settings(8, 2),
    )(pltpu.with_memory_space_constraint(joined, pltpu.HBM), rank_perm)

    def message_shape(level):
        return floats((levels - level) * share + len(below_pairs(levels, level)) * rank, rank)

    own, other, rest = pl.pallas_call(
        functools.partial(node_kernel, rank, slots),
        out_shape=[floats(share, rank)] * 2 + [floats(share, size)],
        name="node",
        **settings(8, 1),
    )(*parts, prepared)
    message = pl.pallas_call(
        functools.partial(correct_kernel, levels, rank),
        out_shape=message_shape(1),
        name="correct",
        **settings(8, 1),
    )(own, other, rest, *grams)
    early = [own] + [swap(own if slot < slots // 2 else other, "rows", 2 * slot) for slot in range(1, slots)]
    first = pl.pallas_call(
        functools.partial(solve_kernel, per_step, width),
        out_shape=floats(rows, columns),
        name="solve",
        **settings(8, 8),
    )(moved, rhs, merged[0])

    coefs = []
    for level in range(1, levels):
        last = level + 1 == levels
        arrived = swap(message, "leaf", 2 ** (level - 1))
        outs = pl.pallas_call(
            functools.partial(level_kernel, levels, level, share),
            out_shape=[floats(share, rank)] + ([] if last else [message_shape(level + 1)]),
            name=f"level{level}",
            **settings(8, 1 if last else 6),
        )(message, arrived, prepared, first if last else arrived)
        coefs.append(outs[0])
        message = outs[-1]
    stack = pl.pallas_call(
        stack_kernel, out_shape=floats(slots, share, rank), name="stack", **settings(8, 0.1),
    )(first, *early)
    second = pl.pallas_call(
        functools.partial(apply_kernel, per_step * width),
        out_shape=floats(rows, columns),
        scratch_shapes=[
            pltpu.VMEM((columns, rank), jnp.float32),
            pltpu.VMEM((2 * rank, columns), jnp.bfloat16),
        ],
        name="apply",
        **settings(8, 1.8),
    )(stack, swap(stack, "rows", 1), first, left_basis)

    pack = pl.pallas_call(
        pack_kernel, out_shape=floats(share, size), name="pack", **settings(8, 0.1),
    )(*coefs)
    pieces = []
    for slot in range(slots):
        piece = swap(pack, "rows", 2 * slot) if slot > 0 else pack
        if slot in (0, slots - 1):
            piece = pl.pallas_call(
                relay_kernel, out_shape=floats(share, size), name="relay", **settings(8, 0.1),
            )(second, piece)
        pieces += [piece, swap(piece, "rows", 1)]
    return pl.pallas_call(
        functools.partial(expand_kernel, levels, per_step * width, count),
        out_specs=pl.BlockSpec(memory_space=pl.ANY),
        out_shape=floats(rows, columns),
        scratch_shapes=[
            pltpu.VMEM((columns, size), jnp.float32),
            pltpu.VMEM((2 * size, columns), jnp.bfloat16),
            pltpu.VMEM((rows, columns), jnp.float32),
            pltpu.SemaphoreType.DMA((nblocks // per_step,)),
        ],
        name="expand",
        **settings(16, 5),
    )(*pieces, second, left_basis)


def solution(mesh):
    return jax.shard_map(
        per_device,
        mesh=mesh,
        in_specs=(
            P(("leaf", "rows"), None),
            P(("leaf", "rows"), None),
            P(("leaf", "rows"), None, None),
            P(None, ("leaf", "rows"), None),
            P(None, ("leaf", "rows"), None),
            P(),
            P(),
        ),
        out_specs=P(("leaf", "rows"), None),
        check_vma=False,
    )
```

```python
import functools

import jax
import jax.numpy as jnp
from jax import lax
from jax.experimental import pallas as pl
from jax.experimental.pallas import tpu as pltpu
from jax.sharding import PartitionSpec as P

HIGHEST = lax.Precision.HIGHEST
MIB = 1 << 20


def dot(a, b, contract, exact=False):
    return lax.dot_general(
        a, b, ((contract[:1], contract[1:]), ((), ())),
        precision=HIGHEST if exact else None, preferred_element_type=jnp.float32,
    )


def halves(value):
    high_part = value.astype(jnp.bfloat16)
    low_part = (value - high_part.astype(jnp.float32)).astype(jnp.bfloat16)
    return high_part, low_part


def swap(value, axis, mask):
    count = lax.axis_size(axis)
    return lax.ppermute(value, axis, [(i, i ^ mask) for i in range(count)])


def blocks_per_step(nblocks, most):
    return max(size for size in range(1, most + 1) if nblocks % size == 0)


def below_pairs(levels, first=0):
    return [(level, below) for level in range(levels) for below in range(first, level)]


def gram_kernel(levels, per_step, width, right_ref, left_ref, flip_ref, keep_ref, send_ref,
                right_buf, left_buf, gram_ref, sems):
    rank = right_ref.shape[2]
    half = rank // 2
    tile = per_step * width
    steps = right_ref.shape[1] // tile

    def copies(step):
        rows = pl.ds(pl.multiple_of(step * tile, tile), tile)
        return (
            pltpu.make_async_copy(right_ref.at[:, rows], right_buf.at[:, rows], sems.at[0, step]),
            pltpu.make_async_copy(left_ref.at[:levels - 1, rows], left_buf.at[:, rows], sems.at[1, step]),
        )

    for step in range(steps):
        for copy in copies(step):
            copy.start()
    gram_ref[...] = jnp.zeros_like(gram_ref)

    def body(step, _):
        for copy in copies(step):
            copy.wait()
        rows = pl.ds(pl.multiple_of(step * tile, tile), tile)
        right = jnp.concatenate([right_buf[l, rows, :] for l in range(levels)], axis=1).T
        flip_ref[:, rows] = right
        left = jnp.concatenate([left_buf[l, rows, :] for l in range(levels - 1)], axis=1)
        gram_ref[...] += dot(right[rank:], left, (1, 0))
        return 0

    lax.fori_loop(0, steps, body, 0)
    core = lax.axis_index("rows") % 2
    for spot, (level, below) in enumerate(below_pairs(levels)):
        lanes = pl.ds(spot * rank, rank)
        for ref, side in ((keep_ref, core), (send_ref, 1 - core)):
            rows = pl.ds(pl.multiple_of((level - 1) * rank + side * half, half), half)
            ref[:, lanes] = gram_ref[rows, pl.ds(below * rank, rank)]


def permute_kernel(per_step, width, order_ref, inv_ref, moved_ref):
    place = lax.broadcasted_iota(jnp.int32, (width, width), 0)

    def body(step, _):
        for b in range(per_step):
            block = step * per_step + b
            chosen = (place == order_ref[pl.ds(block, 1), :]).astype(jnp.float32).astype(jnp.bfloat16)
            moved_ref[block] = dot(inv_ref[block], chosen, (1, 1)).astype(jnp.bfloat16)
        return 0

    lax.fori_loop(0, inv_ref.shape[0] // per_step, body, 0)


def weigh_kernel(per_step, width, moved_ref, flip_ref, after_ref, factor_ref):
    kinds = flip_ref.shape[0]

    def body(step, _):
        for b in range(per_step):
            block = step * per_step + b
            lanes = pl.ds(pl.multiple_of(block * width, width), width)
            high_part, low_part = halves(dot(flip_ref[:, lanes], moved_ref[block], (1, 0)))
            factor_ref[:kinds, lanes] = high_part
            factor_ref[kinds:, lanes] = low_part
        return 0

    lax.fori_loop(0, moved_ref.shape[0] // per_step, body, 0)


def solve_kernel(per_step, width, moved_ref, rhs_ref, *refs):
    out_ref = refs[-1]

    def body(step, _):
        for b in range(per_step):
            block = step * per_step + b
            rows = pl.ds(pl.multiple_of(block * width, width), width)
            out_ref[rows, :] = dot(moved_ref[block], rhs_ref[rows, :], (1, 0))
        return 0

    lax.fori_loop(0, moved_ref.shape[0] // per_step, body, 0)


def project_kernel(other, factor_ref, rhs_ref, after_ref, out_ref):
    kinds, part = out_ref.shape
    core = lax.axis_index("rows") % 2
    lanes = pl.ds(pl.multiple_of((1 - core if other else core) * part, part), part)
    total = dot(factor_ref[...], rhs_ref[:, lanes], (1, 0))
    out_ref[...] = total[:kinds] + total[kinds:]


def merge_kernel(keep_ref, got_ref, *refs):
    out_refs, flip_ref = refs[:-1], refs[-1]
    share = out_refs[0].shape[0]
    chip = lax.axis_index("rows") // 2
    flip_ref[...] = (keep_ref[...] + got_ref[...]).T
    for slot, out_ref in enumerate(out_refs):
        out_ref[...] = flip_ref[pl.ds(pl.multiple_of((chip ^ slot) * share, share), share), :]


def add_kernel(mine_ref, got_ref, out_ref):
    out_ref[...] = mine_ref[...] + got_ref[...]


def prepare_kernel(levels, joined_ref, perm_ref, out_ref, joined_buf, sems):
    rank = perm_ref.shape[1]
    leaves = lax.axis_size("leaf")
    leaf = lax.axis_index("leaf")
    copies = []
    for level in range(levels):
        node = 2 * leaves - 2 * leaves // 2 ** level + leaf // 2 ** level
        copies.append(pltpu.make_async_copy(joined_ref.at[node], joined_buf.at[level], sems.at[level]))
        copies[-1].start()
    spot = lax.broadcasted_iota(jnp.int32, (rank, rank), 0)
    for level in range(levels):
        copies[level].wait()
        chosen = (spot == perm_ref[level:level + 1, :]).astype(jnp.float32)
        for side in range(2):
            lanes = pl.ds(side * rank, rank)
            out_ref[level, :, lanes] = dot(joined_buf[level, :, lanes], chosen, (1, 1), True)


def by_side(side, own, other):
    return jnp.where(side == 0, own, other), jnp.where(side == 0, other, own)


def pack_message(message_ref, pieces):
    row = 0
    for piece in pieces:
        message_ref[pl.ds(row, piece.shape[0]), :] = piece
        row += piece.shape[0]


def node_kernel(rank, slots, *refs):
    part_refs = refs[:slots]
    joined_ref, own_ref, other_ref, rest_ref = refs[slots:]
    side = lax.axis_index("rows") // slots
    half = slots // 2
    sums = [sum(ref[...] for ref in part_refs[:half]), sum(ref[...] for ref in part_refs[half:])]
    picked = jnp.concatenate(by_side(side, sums[0][:, :rank], sums[1][:, :rank]), axis=1)
    coef = dot(picked, joined_ref[0], (1, 1), True)
    own_ref[...], other_ref[...] = by_side(side, coef[:, :rank], coef[:, rank:])
    rest_ref[...] = (sums[0] + sums[1])[:, rank:]


def correct_kernel(levels, rank, own_ref, other_ref, rest_ref, mine_ref, theirs_ref, pair_mine_ref,
                   pair_theirs_ref, message_ref):
    core = lax.axis_index("rows") % 2
    grams = [jnp.concatenate(by_side(core, mine_ref[...], pair_mine_ref[...]), axis=0),
             jnp.concatenate(by_side(core, theirs_ref[...], pair_theirs_ref[...]), axis=0)]
    pairs = below_pairs(levels)
    lanes = {pair: slice(spot * rank, (spot + 1) * rank) for spot, pair in enumerate(pairs)}
    joint = jnp.concatenate(
        [jnp.concatenate([gram[:, lanes[level, 0]] for gram in grams], axis=1) for level in range(1, levels)], axis=0)
    rest = rest_ref[...] - dot(jnp.concatenate([own_ref[...], other_ref[...]], axis=1), joint, (1, 1), True)
    pieces = [rest[:, level * rank:(level + 1) * rank] for level in range(levels - 1)]
    for pair in pairs:
        if pair[1] > 0:
            pieces.append(grams[0][:, lanes[pair]] + grams[1][:, lanes[pair]])
    pack_message(message_ref, pieces)


def level_kernel(levels, level, share, sent_ref, got_ref, joined_ref, after_ref, coef_ref, *message_ref):
    rank = sent_ref.shape[1]
    side = lax.axis_index("leaf") // 2 ** (level - 1) % 2
    more = levels - level
    values = []
    for ref in (sent_ref, got_ref):
        values.append([ref[pl.ds(i * share, share), :] for i in range(more)])
    picked = jnp.concatenate(by_side(side, values[0][0], values[1][0]), axis=1)
    coef = dot(picked, joined_ref[level], (1, 1), True)
    sides = by_side(side, coef[:, :rank], coef[:, rank:])
    coef_ref[...] = sides[0]
    if not message_ref:
        return
    pairs = below_pairs(levels, level)
    grams = []
    for ref in (sent_ref, got_ref):
        grams.append({pair: ref[pl.ds(more * share + spot * rank, rank), :] for spot, pair in enumerate(pairs)})
    uppers = list(range(level + 1, levels))
    joint = jnp.concatenate(
        [jnp.concatenate([gram[upper, level] for gram in grams], axis=1) for upper in uppers], axis=0)
    change = dot(jnp.concatenate(sides, axis=1), joint, (1, 1), True)
    pieces = [values[0][upper - level] + values[1][upper - level] - change[:, i * rank:(i + 1) * rank]
              for i, upper in enumerate(uppers)]
    for pair in pairs:
        if pair[1] > level:
            pieces.append(grams[0][pair] + grams[1][pair])
    pack_message(message_ref[0], pieces)


def pack_kernel(*refs):
    refs[-1][...] = jnp.concatenate([ref[...] for ref in refs[:-1]], axis=1)


def stack_kernel(after_ref, *refs):
    for slot, ref in enumerate(refs[:-1]):
        refs[-1][slot] = ref[...]


def relay_kernel(after_ref, ref, out_ref):
    out_ref[...] = ref[...]


def split_factor(pieces, flip_ref, factor_ref):
    share, kinds = pieces[0].shape
    slots = len(pieces) // 2
    me = lax.axis_index("rows")
    for mask, ref in enumerate(pieces):
        owner = me ^ mask
        row = (owner % 2 * slots + owner // 2) * share
        flip_ref[pl.ds(pl.multiple_of(row, share), share), :] = ref[...]
    high_part, low_part = halves(flip_ref[...].T)
    factor_ref[:kinds, :] = high_part
    factor_ref[kinds:, :] = low_part


def apply_kernel(tile, own_ref, pair_ref, first_ref, left_ref, out_ref, flip_ref, factor_ref):
    pieces = [ref.at[slot] for slot in range(own_ref.shape[0]) for ref in (own_ref, pair_ref)]
    split_factor(pieces, flip_ref, factor_ref)
    for row in range(0, out_ref.shape[0], tile):
        rows = pl.ds(row, tile)
        left = jnp.concatenate([left_ref[0, rows, :]] * 2, axis=1)
        out_ref[rows, :] = first_ref[rows, :] - dot(left, factor_ref[...], (1, 0))


def expand_kernel(levels, tile, count, *refs):
    piece_refs = refs[:count]
    first_ref, left_ref, out_ref, flip_ref, factor_ref, out_buf, sems = refs[count:]
    split_factor(piece_refs, flip_ref, factor_ref)
    copies = []
    for step in range(out_buf.shape[0] // tile):
        rows = pl.ds(step * tile, tile)
        left = jnp.concatenate([left_ref[l, rows, :] for l in range(1, levels)] * 2, axis=1)
        out_buf[rows, :] = first_ref[rows, :] - dot(left, factor_ref[...], (1, 0))
        copies.append(pltpu.make_async_copy(out_buf.at[rows], out_ref.at[rows], sems.at[step]))
        copies[-1].start(priority=step % 2)
    for copy in copies:
        copy.wait()


def settings(mib, micros):
    return dict(
        compiler_params=pltpu.CompilerParams(vmem_limit_bytes=mib * MIB),
        cost_estimate=pl.CostEstimate(flops=int(micros * 1.1e9), bytes_accessed=0, transcendentals=0),
    )


def floats(*shape):
    return jax.ShapeDtypeStruct(shape, jnp.float32)


def per_device(rhs, leaf_order, leaf_inv, right_basis, left_basis, rank_perm, joined):
    levels, rows, rank = right_basis.shape
    nblocks, width, _ = leaf_inv.shape
    columns = rhs.shape[1]
    leaves = lax.axis_size("leaf")
    count = lax.axis_size("rows")
    slots = count // 2
    kinds = levels * rank
    size = kinds - rank
    share = columns // count
    gram_lanes = len(below_pairs(levels)) * rank

    per_step = blocks_per_step(nblocks, 3)
    flipped, gram_keep, gram_send = pl.pallas_call(
        functools.partial(gram_kernel, levels, per_step, width),
        in_specs=[pl.BlockSpec(memory_space=pltpu.HBM)] * 2,
        out_shape=[jax.ShapeDtypeStruct((kinds, rows), jnp.bfloat16)] + [floats(rank // 2, gram_lanes)] * 2,
        scratch_shapes=[
            pltpu.VMEM((levels, rows, rank), jnp.bfloat16),
            pltpu.VMEM((levels - 1, rows, rank), jnp.bfloat16),
            pltpu.VMEM((size, size), jnp.float32),
            pltpu.SemaphoreType.DMA((2, nblocks // per_step)),
        ],
        name="gram",
        **settings(24, 3),
    )(pltpu.with_memory_space_constraint(right_basis, pltpu.HBM),
      pltpu.with_memory_space_constraint(left_basis, pltpu.HBM))

    gram_got = swap(gram_send, "rows", 1)
    moved = pl.pallas_call(
        functools.partial(permute_kernel, blocks_per_step(nblocks, 9), width),
        out_shape=jax.ShapeDtypeStruct((nblocks, width, width), jnp.bfloat16),
        name="permute",
        **settings(8, 1.5),
    )(leaf_order, leaf_inv)

    def add(mine, got):
        return pl.pallas_call(
            add_kernel, out_shape=floats(*mine.shape), name="add", **settings(8, 0.1),
        )(mine, got)

    gram = add(gram_keep, gram_got)
    factors = pl.pallas_call(
        functools.partial(weigh_kernel, blocks_per_step(nblocks, 9), width),
        out_shape=jax.ShapeDtypeStruct((2 * kinds, rows), jnp.bfloat16),
        name="weigh",
        **settings(8, 2.4),
    )(moved, flipped, gram)

    def project(other, after):
        return pl.pallas_call(
            functools.partial(project_kernel, other),
            out_shape=floats(kinds, columns // 2),
            name="project_other" if other else "project_own",
            **settings(12, 1 if other else 4),
        )(factors, rhs, after)

    send = project(True, gram)
    got = swap(send, "rows", 1)
    mask = 2
    while mask < slots:
        gram = add(gram, swap(gram, "rows", mask))
        mask *= 2
    keep = project(False, gram)
    merged = pl.pallas_call(
        merge_kernel,
        out_shape=[floats(share, kinds)] * slots,
        scratch_shapes=[pltpu.VMEM((columns // 2, kinds), jnp.float32)],
        name="merge",
        **settings(8, 0.4),
    )(keep, got)
    parts = [merged[0]] + [swap(merged[s], "rows", 2 * s) for s in range(1, slots)]
    gram_other = swap(gram, "rows", slots)
    grams = [gram, gram_other, swap(gram, "rows", 1), swap(gram_other, "rows", 1)]
    prepared = pl.pallas_call(
        functools.partial(prepare_kernel, levels),
        in_specs=[pl.BlockSpec(memory_space=pltpu.HBM), pl.BlockSpec()],
        out_shape=floats(levels, 2 * rank, 2 * rank),
        scratch_shapes=[pltpu.VMEM((levels, 2 * rank, 2 * rank), jnp.float32), pltpu.SemaphoreType.DMA((levels,))],
        name="prepare",
        **settings(8, 2),
    )(pltpu.with_memory_space_constraint(joined, pltpu.HBM), rank_perm)

    def message_shape(level):
        return floats((levels - level) * share + len(below_pairs(levels, level)) * rank, rank)

    own, other, rest = pl.pallas_call(
        functools.partial(node_kernel, rank, slots),
        out_shape=[floats(share, rank)] * 2 + [floats(share, size)],
        name="node",
        **settings(8, 1),
    )(*parts, prepared)
    message = pl.pallas_call(
        functools.partial(correct_kernel, levels, rank),
        out_shape=message_shape(1),
        name="correct",
        **settings(8, 1),
    )(own, other, rest, *grams)
    early = [own] + [swap(own if slot < slots // 2 else other, "rows", 2 * slot) for slot in range(1, slots)]
    first = pl.pallas_call(
        functools.partial(solve_kernel, per_step, width),
        out_shape=floats(rows, columns),
        name="solve",
        **settings(8, 8),
    )(moved, rhs, merged[0])

    coefs = []
    for level in range(1, levels):
        last = level + 1 == levels
        arrived = swap(message, "leaf", 2 ** (level - 1))
        outs = pl.pallas_call(
            functools.partial(level_kernel, levels, level, share),
            out_shape=[floats(share, rank)] + ([] if last else [message_shape(level + 1)]),
            name=f"level{level}",
            **settings(8, 1 if last else 6),
        )(message, arrived, prepared, first if last else arrived)
        coefs.append(outs[0])
        message = outs[-1]
    stack = pl.pallas_call(
        stack_kernel, out_shape=floats(slots, share, rank), name="stack", **settings(8, 0.1),
    )(first, *early)
    second = pl.pallas_call(
        functools.partial(apply_kernel, per_step * width),
        out_shape=floats(rows, columns),
        scratch_shapes=[
            pltpu.VMEM((columns, rank), jnp.float32),
            pltpu.VMEM((2 * rank, columns), jnp.bfloat16),
        ],
        name="apply",
        **settings(8, 1.8),
    )(stack, swap(stack, "rows", 1), first, left_basis)

    pack = pl.pallas_call(
        pack_kernel, out_shape=floats(share, size), name="pack", **settings(8, 0.1),
    )(*coefs)
    pieces = []
    for slot in range(slots):
        piece = swap(pack, "rows", 2 * slot) if slot > 0 else pack
        if slot in (0, slots - 1):
            piece = pl.pallas_call(
                relay_kernel, out_shape=floats(share, size), name="relay", **settings(8, 0.1),
            )(second, piece)
        pieces += [piece, swap(piece, "rows", 1)]
    return pl.pallas_call(
        functools.partial(expand_kernel, levels, width, count),
        out_specs=pl.BlockSpec(memory_space=pl.ANY),
        out_shape=floats(rows, columns),
        scratch_shapes=[
            pltpu.VMEM((columns, size), jnp.float32),
            pltpu.VMEM((2 * size, columns), jnp.bfloat16),
            pltpu.VMEM((rows, columns), jnp.float32),
            pltpu.SemaphoreType.DMA((nblocks,)),
        ],
        name="expand",
        **settings(16, 5),
    )(*pieces, second, left_basis)


def solution(mesh):
    return jax.shard_map(
        per_device,
        mesh=mesh,
        in_specs=(
            P(("leaf", "rows"), None),
            P(("leaf", "rows"), None),
            P(("leaf", "rows"), None, None),
            P(None, ("leaf", "rows"), None),
            P(None, ("leaf", "rows"), None),
            P(),
            P(),
        ),
        out_specs=P(("leaf", "rows"), None),
        check_vma=False,
    )
```

```python
import functools

import jax
import jax.numpy as jnp
from jax import lax
from jax.experimental import pallas as pl
from jax.experimental.pallas import tpu as pltpu
from jax.sharding import PartitionSpec as P

MIB = 1 << 20


def dot(a, b, contract):
    return lax.dot_general(a, b, ((contract[:1], contract[1:]), ((), ())), preferred_element_type=jnp.float32)


def halves(value):
    high_part = value.astype(jnp.bfloat16)
    low_part = (value - high_part.astype(jnp.float32)).astype(jnp.bfloat16)
    return high_part, low_part


def left_stack(value):
    high_part, low_part = halves(value)
    return jnp.concatenate([high_part, high_part, low_part], axis=1)


def right_stack(value):
    high_part, low_part = halves(value)
    return jnp.concatenate([high_part, low_part, high_part], axis=1)


def swap(value, axis, mask):
    count = lax.axis_size(axis)
    return lax.ppermute(value, axis, [(i, i ^ mask) for i in range(count)])


def blocks_per_step(nblocks, most):
    return max(size for size in range(1, most + 1) if nblocks % size == 0)


def below_pairs(levels, first=0):
    return [(level, below) for level in range(levels) for below in range(first, level)]


def gram_kernel(levels, per_step, width, right_ref, left_ref, flip_ref, keep_ref, send_ref,
                right_buf, left_buf, gram_ref, sems):
    rank = right_ref.shape[2]
    half = rank // 2
    tile = per_step * width
    steps = right_ref.shape[1] // tile

    def copies(step):
        rows = pl.ds(pl.multiple_of(step * tile, tile), tile)
        return (
            pltpu.make_async_copy(right_ref.at[:, rows], right_buf.at[:, rows], sems.at[0, step]),
            pltpu.make_async_copy(left_ref.at[:levels - 1, rows], left_buf.at[:, rows], sems.at[1, step]),
        )

    for step in range(steps):
        for copy in copies(step):
            copy.start()
    gram_ref[...] = jnp.zeros_like(gram_ref)

    def body(step, _):
        for copy in copies(step):
            copy.wait()
        rows = pl.ds(pl.multiple_of(step * tile, tile), tile)
        right = jnp.concatenate([right_buf[l, rows, :] for l in range(levels)], axis=1).T
        flip_ref[:, rows] = right
        left = jnp.concatenate([left_buf[l, rows, :] for l in range(levels - 1)], axis=1)
        gram_ref[...] += dot(right[rank:], left, (1, 0))
        return 0

    lax.fori_loop(0, steps, body, 0)
    core = lax.axis_index("rows") % 2
    for spot, (level, below) in enumerate(below_pairs(levels)):
        lanes = pl.ds(spot * rank, rank)
        for ref, side in ((keep_ref, core), (send_ref, 1 - core)):
            rows = pl.ds(pl.multiple_of((level - 1) * rank + side * half, half), half)
            ref[:, lanes] = gram_ref[rows, pl.ds(below * rank, rank)]


def permute_kernel(per_step, width, order_ref, inv_ref, moved_ref):
    place = lax.broadcasted_iota(jnp.int32, (width, width), 0)

    def body(step, _):
        for b in range(per_step):
            block = step * per_step + b
            chosen = (place == order_ref[pl.ds(block, 1), :]).astype(jnp.float32).astype(jnp.bfloat16)
            moved_ref[block] = dot(inv_ref[block], chosen, (1, 1)).astype(jnp.bfloat16)
        return 0

    lax.fori_loop(0, inv_ref.shape[0] // per_step, body, 0)


def weigh_kernel(per_step, width, moved_ref, flip_ref, after_ref, factor_ref):
    kinds = flip_ref.shape[0]

    def body(step, _):
        for b in range(per_step):
            block = step * per_step + b
            lanes = pl.ds(pl.multiple_of(block * width, width), width)
            high_part, low_part = halves(dot(flip_ref[:, lanes], moved_ref[block], (1, 0)))
            factor_ref[:kinds, lanes] = high_part
            factor_ref[kinds:, lanes] = low_part
        return 0

    lax.fori_loop(0, moved_ref.shape[0] // per_step, body, 0)


def solve_kernel(per_step, width, moved_ref, rhs_ref, *refs):
    out_ref = refs[-1]

    def body(step, _):
        for b in range(per_step):
            block = step * per_step + b
            rows = pl.ds(pl.multiple_of(block * width, width), width)
            out_ref[rows, :] = dot(moved_ref[block], rhs_ref[rows, :], (1, 0))
        return 0

    lax.fori_loop(0, moved_ref.shape[0] // per_step, body, 0)


def project_kernel(other, factor_ref, rhs_ref, after_ref, out_ref):
    kinds, part = out_ref.shape
    core = lax.axis_index("rows") % 2
    lanes = pl.ds(pl.multiple_of((1 - core if other else core) * part, part), part)
    total = dot(factor_ref[...], rhs_ref[:, lanes], (1, 0))
    out_ref[...] = total[:kinds] + total[kinds:]


def merge_kernel(keep_ref, got_ref, *refs):
    out_refs, flip_ref = refs[:-1], refs[-1]
    share = out_refs[0].shape[0]
    chip = lax.axis_index("rows") // 2
    flip_ref[...] = (keep_ref[...] + got_ref[...]).T
    for slot, out_ref in enumerate(out_refs):
        out_ref[...] = flip_ref[pl.ds(pl.multiple_of((chip ^ slot) * share, share), share), :]


def add_kernel(mine_ref, got_ref, out_ref):
    out_ref[...] = mine_ref[...] + got_ref[...]


def prepare_kernel(levels, joined_ref, perm_ref, out_ref, joined_buf, sems):
    rank = perm_ref.shape[1]
    leaves = lax.axis_size("leaf")
    leaf = lax.axis_index("leaf")
    copies = []
    for level in range(levels):
        node = 2 * leaves - 2 * leaves // 2 ** level + leaf // 2 ** level
        copies.append(pltpu.make_async_copy(joined_ref.at[node], joined_buf.at[level], sems.at[level]))
        copies[-1].start()
    spot = lax.broadcasted_iota(jnp.int32, (rank, rank), 0)
    for level in range(levels):
        copies[level].wait()
        chosen = (spot == perm_ref[level:level + 1, :]).astype(jnp.float32).astype(jnp.bfloat16)
        high_part, low_part = halves(joined_buf[level])
        for place, part in enumerate((high_part, low_part, high_part)):
            for side in range(2):
                moved = dot(chosen, part[:, side * rank:(side + 1) * rank], (1, 1)).astype(jnp.bfloat16)
                out_ref[level, pl.ds((2 * place + side) * rank, rank), :] = moved


def by_side(side, own, other):
    return jnp.where(side == 0, own, other), jnp.where(side == 0, other, own)


def pack_message(message_ref, pieces):
    row = 0
    for piece in pieces:
        message_ref[pl.ds(row, piece.shape[0]), :] = piece
        row += piece.shape[0]


def node_kernel(rank, slots, *refs):
    part_refs = refs[:slots]
    joined_ref, own_ref, other_ref, rest_ref = refs[slots:]
    side = lax.axis_index("rows") // slots
    half = slots // 2
    sums = [sum(ref[...] for ref in part_refs[:half]), sum(ref[...] for ref in part_refs[half:])]
    picked = jnp.concatenate(by_side(side, sums[0][:, :rank], sums[1][:, :rank]), axis=1)
    coef = dot(left_stack(picked), joined_ref[0], (1, 0))
    own_ref[...], other_ref[...] = by_side(side, coef[:, :rank], coef[:, rank:])
    rest_ref[...] = (sums[0] + sums[1])[:, rank:]


def correct_kernel(levels, rank, own_ref, other_ref, rest_ref, mine_ref, theirs_ref, pair_mine_ref,
                   pair_theirs_ref, message_ref):
    core = lax.axis_index("rows") % 2
    grams = [jnp.concatenate(by_side(core, mine_ref[...], pair_mine_ref[...]), axis=0),
             jnp.concatenate(by_side(core, theirs_ref[...], pair_theirs_ref[...]), axis=0)]
    pairs = below_pairs(levels)
    lanes = {pair: slice(spot * rank, (spot + 1) * rank) for spot, pair in enumerate(pairs)}
    joint = jnp.concatenate(
        [jnp.concatenate([gram[:, lanes[level, 0]] for gram in grams], axis=1) for level in range(1, levels)], axis=0)
    pair = jnp.concatenate([own_ref[...], other_ref[...]], axis=1)
    rest = rest_ref[...] - dot(left_stack(pair), right_stack(joint), (1, 1))
    pieces = [rest[:, level * rank:(level + 1) * rank] for level in range(levels - 1)]
    for pair in pairs:
        if pair[1] > 0:
            pieces.append(grams[0][:, lanes[pair]] + grams[1][:, lanes[pair]])
    pack_message(message_ref, pieces)


def level_kernel(levels, level, share, sent_ref, got_ref, joined_ref, after_ref, coef_ref, *message_ref):
    rank = sent_ref.shape[1]
    side = lax.axis_index("leaf") // 2 ** (level - 1) % 2
    more = levels - level
    values = []
    for ref in (sent_ref, got_ref):
        values.append([ref[pl.ds(i * share, share), :] for i in range(more)])
    picked = jnp.concatenate(by_side(side, values[0][0], values[1][0]), axis=1)
    coef = dot(left_stack(picked), joined_ref[level], (1, 0))
    sides = by_side(side, coef[:, :rank], coef[:, rank:])
    coef_ref[...] = sides[0]
    if not message_ref:
        return
    pairs = below_pairs(levels, level)
    grams = []
    for ref in (sent_ref, got_ref):
        grams.append({pair: ref[pl.ds(more * share + spot * rank, rank), :] for spot, pair in enumerate(pairs)})
    uppers = list(range(level + 1, levels))
    joint = jnp.concatenate(
        [jnp.concatenate([gram[upper, level] for gram in grams], axis=1) for upper in uppers], axis=0)
    change = dot(left_stack(jnp.concatenate(sides, axis=1)), right_stack(joint), (1, 1))
    pieces = [values[0][upper - level] + values[1][upper - level] - change[:, i * rank:(i + 1) * rank]
              for i, upper in enumerate(uppers)]
    for pair in pairs:
        if pair[1] > level:
            pieces.append(grams[0][pair] + grams[1][pair])
    pack_message(message_ref[0], pieces)


def pack_kernel(*refs):
    refs[-1][...] = jnp.concatenate([ref[...] for ref in refs[:-1]], axis=1)


def stack_kernel(after_ref, *refs):
    for slot, ref in enumerate(refs[:-1]):
        refs[-1][slot] = ref[...]


def relay_kernel(after_ref, ref, out_ref):
    out_ref[...] = ref[...]


def split_factor(pieces, flip_ref, factor_ref):
    share, kinds = pieces[0].shape
    slots = len(pieces) // 2
    me = lax.axis_index("rows")
    for mask, ref in enumerate(pieces):
        owner = me ^ mask
        row = (owner % 2 * slots + owner // 2) * share
        flip_ref[pl.ds(pl.multiple_of(row, share), share), :] = ref[...]
    high_part, low_part = halves(flip_ref[...].T)
    factor_ref[:kinds, :] = high_part
    factor_ref[kinds:, :] = low_part


def apply_kernel(tile, own_ref, pair_ref, first_ref, left_ref, out_ref, flip_ref, factor_ref):
    pieces = [ref.at[slot] for slot in range(own_ref.shape[0]) for ref in (own_ref, pair_ref)]
    split_factor(pieces, flip_ref, factor_ref)
    for row in range(0, out_ref.shape[0], tile):
        rows = pl.ds(row, tile)
        left = jnp.concatenate([left_ref[0, rows, :]] * 2, axis=1)
        out_ref[rows, :] = first_ref[rows, :] - dot(left, factor_ref[...], (1, 0))


def expand_kernel(levels, tile, count, *refs):
    piece_refs = refs[:count]
    first_ref, left_ref, out_ref, flip_ref, factor_ref, out_buf, sems = refs[count:]
    split_factor(piece_refs, flip_ref, factor_ref)
    copies = []
    for step in range(out_buf.shape[0] // tile):
        rows = pl.ds(step * tile, tile)
        left = jnp.concatenate([left_ref[l, rows, :] for l in range(1, levels)] * 2, axis=1)
        out_buf[rows, :] = first_ref[rows, :] - dot(left, factor_ref[...], (1, 0))
        copies.append(pltpu.make_async_copy(out_buf.at[rows], out_ref.at[rows], sems.at[step]))
        copies[-1].start(priority=step % 2)
    for copy in copies:
        copy.wait()


def settings(mib, micros):
    return dict(
        compiler_params=pltpu.CompilerParams(vmem_limit_bytes=mib * MIB),
        cost_estimate=pl.CostEstimate(flops=int(micros * 1.1e9), bytes_accessed=0, transcendentals=0),
    )


def floats(*shape):
    return jax.ShapeDtypeStruct(shape, jnp.float32)


def per_device(rhs, leaf_order, leaf_inv, right_basis, left_basis, rank_perm, joined):
    levels, rows, rank = right_basis.shape
    nblocks, width, _ = leaf_inv.shape
    columns = rhs.shape[1]
    leaves = lax.axis_size("leaf")
    count = lax.axis_size("rows")
    slots = count // 2
    kinds = levels * rank
    size = kinds - rank
    share = columns // count
    gram_lanes = len(below_pairs(levels)) * rank

    per_step = blocks_per_step(nblocks, 3)
    flipped, gram_keep, gram_send = pl.pallas_call(
        functools.partial(gram_kernel, levels, per_step, width),
        in_specs=[pl.BlockSpec(memory_space=pltpu.HBM)] * 2,
        out_shape=[jax.ShapeDtypeStruct((kinds, rows), jnp.bfloat16)] + [floats(rank // 2, gram_lanes)] * 2,
        scratch_shapes=[
            pltpu.VMEM((levels, rows, rank), jnp.bfloat16),
            pltpu.VMEM((levels - 1, rows, rank), jnp.bfloat16),
            pltpu.VMEM((size, size), jnp.float32),
            pltpu.SemaphoreType.DMA((2, nblocks // per_step)),
        ],
        name="gram",
        **settings(24, 3),
    )(pltpu.with_memory_space_constraint(right_basis, pltpu.HBM),
      pltpu.with_memory_space_constraint(left_basis, pltpu.HBM))

    gram_got = swap(gram_send, "rows", 1)
    moved = pl.pallas_call(
        functools.partial(permute_kernel, blocks_per_step(nblocks, 9), width),
        out_shape=jax.ShapeDtypeStruct((nblocks, width, width), jnp.bfloat16),
        name="permute",
        **settings(8, 1.5),
    )(leaf_order, leaf_inv)

    def add(mine, got):
        return pl.pallas_call(
            add_kernel, out_shape=floats(*mine.shape), name="add", **settings(8, 0.1),
        )(mine, got)

    gram = add(gram_keep, gram_got)
    factors = pl.pallas_call(
        functools.partial(weigh_kernel, blocks_per_step(nblocks, 9), width),
        out_shape=jax.ShapeDtypeStruct((2 * kinds, rows), jnp.bfloat16),
        name="weigh",
        **settings(8, 2.4),
    )(moved, flipped, gram)

    def project(other, after):
        return pl.pallas_call(
            functools.partial(project_kernel, other),
            out_shape=floats(kinds, columns // 2),
            name="project_other" if other else "project_own",
            **settings(12, 1 if other else 4),
        )(factors, rhs, after)

    send = project(True, gram)
    got = swap(send, "rows", 1)
    mask = 2
    while mask < slots:
        gram = add(gram, swap(gram, "rows", mask))
        mask *= 2
    keep = project(False, gram)
    merged = pl.pallas_call(
        merge_kernel,
        out_shape=[floats(share, kinds)] * slots,
        scratch_shapes=[pltpu.VMEM((columns // 2, kinds), jnp.float32)],
        name="merge",
        **settings(8, 0.4),
    )(keep, got)
    parts = [merged[0]] + [swap(merged[s], "rows", 2 * s) for s in range(1, slots)]
    gram_other = swap(gram, "rows", slots)
    grams = [gram, gram_other, swap(gram, "rows", 1), swap(gram_other, "rows", 1)]
    prepared = pl.pallas_call(
        functools.partial(prepare_kernel, levels),
        in_specs=[pl.BlockSpec(memory_space=pltpu.HBM), pl.BlockSpec()],
        out_shape=jax.ShapeDtypeStruct((levels, 6 * rank, 2 * rank), jnp.bfloat16),
        scratch_shapes=[pltpu.VMEM((levels, 2 * rank, 2 * rank), jnp.float32), pltpu.SemaphoreType.DMA((levels,))],
        name="prepare",
        **settings(8, 2),
    )(pltpu.with_memory_space_constraint(joined, pltpu.HBM), rank_perm)

    def message_shape(level):
        return floats((levels - level) * share + len(below_pairs(levels, level)) * rank, rank)

    own, other, rest = pl.pallas_call(
        functools.partial(node_kernel, rank, slots),
        out_shape=[floats(share, rank)] * 2 + [floats(share, size)],
        name="node",
        **settings(8, 1),
    )(*parts, prepared)
    message = pl.pallas_call(
        functools.partial(correct_kernel, levels, rank),
        out_shape=message_shape(1),
        name="correct",
        **settings(8, 1),
    )(own, other, rest, *grams)
    early = [own] + [swap(own if slot < slots // 2 else other, "rows", 2 * slot) for slot in range(1, slots)]
    first = pl.pallas_call(
        functools.partial(solve_kernel, per_step, width),
        out_shape=floats(rows, columns),
        name="solve",
        **settings(8, 8),
    )(moved, rhs, merged[0])

    coefs = []
    for level in range(1, levels):
        last = level + 1 == levels
        arrived = swap(message, "leaf", 2 ** (level - 1))
        outs = pl.pallas_call(
            functools.partial(level_kernel, levels, level, share),
            out_shape=[floats(share, rank)] + ([] if last else [message_shape(level + 1)]),
            name=f"level{level}",
            **settings(8, 1 if last else 6),
        )(message, arrived, prepared, first if last else arrived)
        coefs.append(outs[0])
        message = outs[-1]
    stack = pl.pallas_call(
        stack_kernel, out_shape=floats(slots, share, rank), name="stack", **settings(8, 0.1),
    )(first, *early)
    second = pl.pallas_call(
        functools.partial(apply_kernel, per_step * width),
        out_shape=floats(rows, columns),
        scratch_shapes=[
            pltpu.VMEM((columns, rank), jnp.float32),
            pltpu.VMEM((2 * rank, columns), jnp.bfloat16),
        ],
        name="apply",
        **settings(8, 1.8),
    )(stack, swap(stack, "rows", 1), first, left_basis)

    pack = pl.pallas_call(
        pack_kernel, out_shape=floats(share, size), name="pack", **settings(8, 0.1),
    )(*coefs)
    pieces = []
    for slot in range(slots):
        piece = swap(pack, "rows", 2 * slot) if slot > 0 else pack
        if slot in (0, slots - 1):
            piece = pl.pallas_call(
                relay_kernel, out_shape=floats(share, size), name="relay", **settings(8, 0.1),
            )(second, piece)
        pieces += [piece, swap(piece, "rows", 1)]
    return pl.pallas_call(
        functools.partial(expand_kernel, levels, width, count),
        out_specs=pl.BlockSpec(memory_space=pl.ANY),
        out_shape=floats(rows, columns),
        scratch_shapes=[
            pltpu.VMEM((columns, size), jnp.float32),
            pltpu.VMEM((2 * size, columns), jnp.bfloat16),
            pltpu.VMEM((rows, columns), jnp.float32),
            pltpu.SemaphoreType.DMA((nblocks,)),
        ],
        name="expand",
        **settings(16, 5),
    )(*pieces, second, left_basis)


def solution(mesh):
    return jax.shard_map(
        per_device,
        mesh=mesh,
        in_specs=(
            P(("leaf", "rows"), None),
            P(("leaf", "rows"), None),
            P(("leaf", "rows"), None, None),
            P(None, ("leaf", "rows"), None),
            P(None, ("leaf", "rows"), None),
            P(),
            P(),
        ),
        out_specs=P(("leaf", "rows"), None),
        check_vma=False,
    )
```

```python
import functools

import jax
import jax.numpy as jnp
from jax import lax
from jax.experimental import pallas as pl
from jax.experimental.pallas import tpu as pltpu
from jax.sharding import PartitionSpec as P

MIB = 1 << 20


def dot(a, b, contract):
    return lax.dot_general(a, b, ((contract[:1], contract[1:]), ((), ())), preferred_element_type=jnp.float32)


def halves(value):
    high_part = value.astype(jnp.bfloat16)
    low_part = (value - high_part.astype(jnp.float32)).astype(jnp.bfloat16)
    return high_part, low_part


def left_stack(value):
    high_part, low_part = halves(value)
    return jnp.concatenate([high_part, high_part, low_part], axis=1)


def right_stack(value):
    high_part, low_part = halves(value)
    return jnp.concatenate([high_part, low_part, high_part], axis=1)


def swap(value, axis, mask):
    count = lax.axis_size(axis)
    return lax.ppermute(value, axis, [(i, i ^ mask) for i in range(count)])


def blocks_per_step(nblocks, most):
    return max(size for size in range(1, most + 1) if nblocks % size == 0)


def below_pairs(levels, first=0):
    return [(level, below) for level in range(levels) for below in range(first, level)]


def gram_kernel(levels, per_step, width, right_ref, left_ref, flip_ref, keep_ref, send_ref,
                right_buf, left_buf, gram_ref, sems):
    rank = right_ref.shape[2]
    half = rank // 2
    tile = per_step * width
    steps = right_ref.shape[1] // tile

    def copies(step):
        rows = pl.ds(pl.multiple_of(step * tile, tile), tile)
        return (
            pltpu.make_async_copy(right_ref.at[:, rows], right_buf.at[:, rows], sems.at[0, step]),
            pltpu.make_async_copy(left_ref.at[:levels - 1, rows], left_buf.at[:, rows], sems.at[1, step]),
        )

    for step in range(steps):
        for copy in copies(step):
            copy.start()
    gram_ref[...] = jnp.zeros_like(gram_ref)

    def body(step, _):
        for copy in copies(step):
            copy.wait()
        rows = pl.ds(pl.multiple_of(step * tile, tile), tile)
        right = jnp.concatenate([right_buf[l, rows, :] for l in range(levels)], axis=1).T
        flip_ref[:, rows] = right
        left = jnp.concatenate([left_buf[l, rows, :] for l in range(levels - 1)], axis=1)
        gram_ref[...] += dot(right[rank:], left, (1, 0))
        return 0

    lax.fori_loop(0, steps, body, 0)
    core = lax.axis_index("rows") % 2
    for spot, (level, below) in enumerate(below_pairs(levels)):
        lanes = pl.ds(spot * rank, rank)
        for ref, side in ((keep_ref, core), (send_ref, 1 - core)):
            rows = pl.ds(pl.multiple_of((level - 1) * rank + side * half, half), half)
            ref[:, lanes] = gram_ref[rows, pl.ds(below * rank, rank)]


def permute_kernel(per_step, width, order_ref, inv_ref, moved_ref):
    place = lax.broadcasted_iota(jnp.int32, (width, width), 0)

    def body(step, _):
        for b in range(per_step):
            block = step * per_step + b
            chosen = (place == order_ref[pl.ds(block, 1), :]).astype(jnp.float32).astype(jnp.bfloat16)
            moved_ref[block] = dot(inv_ref[block], chosen, (1, 1)).astype(jnp.bfloat16)
        return 0

    lax.fori_loop(0, inv_ref.shape[0] // per_step, body, 0)


def weigh_kernel(per_step, width, moved_ref, flip_ref, after_ref, factor_ref):
    kinds = flip_ref.shape[0]

    def body(step, _):
        for b in range(per_step):
            block = step * per_step + b
            lanes = pl.ds(pl.multiple_of(block * width, width), width)
            high_part, low_part = halves(dot(flip_ref[:, lanes], moved_ref[block], (1, 0)))
            factor_ref[:kinds, lanes] = high_part
            factor_ref[kinds:, lanes] = low_part
        return 0

    lax.fori_loop(0, moved_ref.shape[0] // per_step, body, 0)


def solve_kernel(per_step, width, moved_ref, rhs_ref, *refs):
    out_ref = refs[-1]

    def body(step, _):
        for b in range(per_step):
            block = step * per_step + b
            rows = pl.ds(pl.multiple_of(block * width, width), width)
            out_ref[rows, :] = dot(moved_ref[block], rhs_ref[rows, :], (1, 0))
        return 0

    lax.fori_loop(0, moved_ref.shape[0] // per_step, body, 0)


def project_kernel(other, factor_ref, rhs_ref, after_ref, out_ref):
    kinds, part = out_ref.shape
    core = lax.axis_index("rows") % 2
    lanes = pl.ds(pl.multiple_of((1 - core if other else core) * part, part), part)
    total = dot(factor_ref[...], rhs_ref[:, lanes], (1, 0))
    out_ref[...] = total[:kinds] + total[kinds:]


def merge_kernel(keep_ref, got_ref, *refs):
    out_refs, flip_ref = refs[:-1], refs[-1]
    share = out_refs[0].shape[0]
    chip = lax.axis_index("rows") // 2
    flip_ref[...] = (keep_ref[...] + got_ref[...]).T
    for slot, out_ref in enumerate(out_refs):
        out_ref[...] = flip_ref[pl.ds(pl.multiple_of((chip ^ slot) * share, share), share), :]


def add_kernel(mine_ref, got_ref, out_ref):
    out_ref[...] = mine_ref[...] + got_ref[...]


def prepare_kernel(levels, joined_ref, perm_ref, out_ref, joined_buf, sems):
    rank = perm_ref.shape[1]
    leaves = lax.axis_size("leaf")
    leaf = lax.axis_index("leaf")
    copies = []
    for level in range(levels):
        node = 2 * leaves - 2 * leaves // 2 ** level + leaf // 2 ** level
        copies.append(pltpu.make_async_copy(joined_ref.at[node], joined_buf.at[level], sems.at[level]))
        copies[-1].start()
    spot = lax.broadcasted_iota(jnp.int32, (rank, rank), 0)
    for level in range(levels):
        copies[level].wait()
        chosen = (spot == perm_ref[level:level + 1, :]).astype(jnp.float32).astype(jnp.bfloat16)
        high_part, low_part = halves(joined_buf[level])
        for place, part in enumerate((high_part, low_part, high_part)):
            for side in range(2):
                moved = dot(chosen, part[:, side * rank:(side + 1) * rank], (1, 1)).astype(jnp.bfloat16)
                out_ref[level, pl.ds((2 * place + side) * rank, rank), :] = moved


def by_side(side, own, other):
    return jnp.where(side == 0, own, other), jnp.where(side == 0, other, own)


def pack_message(message_ref, pieces):
    row = 0
    for piece in pieces:
        message_ref[pl.ds(row, piece.shape[0]), :] = piece
        row += piece.shape[0]


def node_kernel(rank, slots, *refs):
    part_refs = refs[:slots]
    joined_ref, own_ref, other_ref, rest_ref = refs[slots:]
    side = lax.axis_index("rows") // slots
    half = slots // 2
    sums = [sum(ref[...] for ref in part_refs[:half]), sum(ref[...] for ref in part_refs[half:])]
    picked = jnp.concatenate(by_side(side, sums[0][:, :rank], sums[1][:, :rank]), axis=1)
    coef = dot(left_stack(picked), joined_ref[0], (1, 0))
    own_ref[...], other_ref[...] = by_side(side, coef[:, :rank], coef[:, rank:])
    rest_ref[...] = (sums[0] + sums[1])[:, rank:]


def correct_kernel(levels, rank, own_ref, other_ref, rest_ref, mine_ref, theirs_ref, pair_mine_ref,
                   pair_theirs_ref, message_ref):
    core = lax.axis_index("rows") % 2
    grams = [jnp.concatenate(by_side(core, mine_ref[...], pair_mine_ref[...]), axis=0),
             jnp.concatenate(by_side(core, theirs_ref[...], pair_theirs_ref[...]), axis=0)]
    pairs = below_pairs(levels)
    lanes = {pair: slice(spot * rank, (spot + 1) * rank) for spot, pair in enumerate(pairs)}
    joint = jnp.concatenate(
        [jnp.concatenate([gram[:, lanes[level, 0]] for gram in grams], axis=1) for level in range(1, levels)], axis=0)
    pair = jnp.concatenate([own_ref[...], other_ref[...]], axis=1)
    rest = rest_ref[...] - dot(left_stack(pair), right_stack(joint), (1, 1))
    pieces = [rest[:, level * rank:(level + 1) * rank] for level in range(levels - 1)]
    for pair in pairs:
        if pair[1] > 0:
            pieces.append(grams[0][:, lanes[pair]] + grams[1][:, lanes[pair]])
    pack_message(message_ref, pieces)


def level_kernel(levels, level, share, sent_ref, got_ref, joined_ref, after_ref, coef_ref, *message_ref):
    rank = sent_ref.shape[1]
    side = lax.axis_index("leaf") // 2 ** (level - 1) % 2
    more = levels - level
    values = []
    for ref in (sent_ref, got_ref):
        values.append([ref[pl.ds(i * share, share), :] for i in range(more)])
    picked = jnp.concatenate(by_side(side, values[0][0], values[1][0]), axis=1)
    coef = dot(left_stack(picked), joined_ref[level], (1, 0))
    sides = by_side(side, coef[:, :rank], coef[:, rank:])
    coef_ref[...] = sides[0]
    if not message_ref:
        return
    pairs = below_pairs(levels, level)
    grams = []
    for ref in (sent_ref, got_ref):
        grams.append({pair: ref[pl.ds(more * share + spot * rank, rank), :] for spot, pair in enumerate(pairs)})
    uppers = list(range(level + 1, levels))
    joint = jnp.concatenate(
        [jnp.concatenate([gram[upper, level] for gram in grams], axis=1) for upper in uppers], axis=0)
    change = dot(left_stack(jnp.concatenate(sides, axis=1)), right_stack(joint), (1, 1))
    pieces = [values[0][upper - level] + values[1][upper - level] - change[:, i * rank:(i + 1) * rank]
              for i, upper in enumerate(uppers)]
    for pair in pairs:
        if pair[1] > level:
            pieces.append(grams[0][pair] + grams[1][pair])
    pack_message(message_ref[0], pieces)


def pack_kernel(*refs):
    refs[-1][...] = jnp.concatenate([ref[...] for ref in refs[:-1]], axis=1)


def stack_kernel(after_ref, *refs):
    for slot, ref in enumerate(refs[:-1]):
        refs[-1][slot] = ref[...]


def relay_kernel(after_ref, ref, out_ref):
    out_ref[...] = ref[...]


def split_factor(pieces, flip_ref, factor_ref):
    share, kinds = pieces[0].shape
    slots = len(pieces) // 2
    me = lax.axis_index("rows")
    for mask, ref in enumerate(pieces):
        owner = me ^ mask
        row = (owner % 2 * slots + owner // 2) * share
        flip_ref[pl.ds(pl.multiple_of(row, share), share), :] = ref[...]
    high_part, low_part = halves(flip_ref[...].T)
    factor_ref[:kinds, :] = high_part
    factor_ref[kinds:, :] = low_part


def apply_kernel(tile, own_ref, pair_ref, first_ref, left_ref, out_ref, flip_ref, factor_ref):
    pieces = [ref.at[slot] for slot in range(own_ref.shape[0]) for ref in (own_ref, pair_ref)]
    split_factor(pieces, flip_ref, factor_ref)
    for row in range(0, out_ref.shape[0], tile):
        rows = pl.ds(row, tile)
        left = jnp.concatenate([left_ref[0, rows, :]] * 2, axis=1)
        out_ref[rows, :] = first_ref[rows, :] - dot(left, factor_ref[...], (1, 0))


def expand_kernel(levels, tile, count, *refs):
    piece_refs = refs[:count]
    first_ref, left_ref, out_ref, flip_ref, factor_ref, out_buf, sems = refs[count:]
    split_factor(piece_refs, flip_ref, factor_ref)
    copies = []
    for step in range(out_buf.shape[0] // tile):
        rows = pl.ds(step * tile, tile)
        left = jnp.concatenate([left_ref[l, rows, :] for l in range(1, levels)] * 2, axis=1)
        out_buf[rows, :] = first_ref[rows, :] - dot(left, factor_ref[...], (1, 0))
        copies.append(pltpu.make_async_copy(out_buf.at[rows], out_ref.at[rows], sems.at[step]))
        copies[-1].start(priority=step % 2)
    for copy in copies:
        copy.wait()


def settings(mib, micros):
    return dict(
        compiler_params=pltpu.CompilerParams(vmem_limit_bytes=mib * MIB),
        cost_estimate=pl.CostEstimate(flops=int(micros * 1.1e9), bytes_accessed=0, transcendentals=0),
    )


def floats(*shape):
    return jax.ShapeDtypeStruct(shape, jnp.float32)


def per_device(rhs, leaf_order, leaf_inv, right_basis, left_basis, rank_perm, joined):
    levels, rows, rank = right_basis.shape
    nblocks, width, _ = leaf_inv.shape
    columns = rhs.shape[1]
    leaves = lax.axis_size("leaf")
    count = lax.axis_size("rows")
    slots = count // 2
    kinds = levels * rank
    size = kinds - rank
    share = columns // count
    gram_lanes = len(below_pairs(levels)) * rank

    per_step = blocks_per_step(nblocks, 3)
    flipped, gram_keep, gram_send = pl.pallas_call(
        functools.partial(gram_kernel, levels, per_step, width),
        in_specs=[pl.BlockSpec(memory_space=pltpu.HBM)] * 2,
        out_shape=[jax.ShapeDtypeStruct((kinds, rows), jnp.bfloat16)] + [floats(rank // 2, gram_lanes)] * 2,
        scratch_shapes=[
            pltpu.VMEM((levels, rows, rank), jnp.bfloat16),
            pltpu.VMEM((levels - 1, rows, rank), jnp.bfloat16),
            pltpu.VMEM((size, size), jnp.float32),
            pltpu.SemaphoreType.DMA((2, nblocks // per_step)),
        ],
        name="gram",
        **settings(24, 3),
    )(pltpu.with_memory_space_constraint(right_basis, pltpu.HBM),
      pltpu.with_memory_space_constraint(left_basis, pltpu.HBM))

    gram_got = swap(gram_send, "rows", 1)
    moved = pl.pallas_call(
        functools.partial(permute_kernel, blocks_per_step(nblocks, 9), width),
        out_shape=jax.ShapeDtypeStruct((nblocks, width, width), jnp.bfloat16),
        name="permute",
        **settings(8, 1.5),
    )(leaf_order, leaf_inv)

    def add(mine, got):
        return pl.pallas_call(
            add_kernel, out_shape=floats(*mine.shape), name="add", **settings(8, 0.1),
        )(mine, got)

    gram = add(gram_keep, gram_got)
    factors = pl.pallas_call(
        functools.partial(weigh_kernel, blocks_per_step(nblocks, 9), width),
        out_shape=jax.ShapeDtypeStruct((2 * kinds, rows), jnp.bfloat16),
        name="weigh",
        **settings(8, 2.4),
    )(moved, flipped, gram)

    def project(other, after):
        return pl.pallas_call(
            functools.partial(project_kernel, other),
            out_shape=floats(kinds, columns // 2),
            name="project_other" if other else "project_own",
            **settings(12, 1 if other else 4),
        )(factors, rhs, after)

    send = project(True, gram)
    got = swap(send, "rows", 1)
    mask = 2
    while mask < slots:
        gram = add(gram, swap(gram, "rows", mask))
        mask *= 2
    keep = project(False, gram)
    merged = pl.pallas_call(
        merge_kernel,
        out_shape=[floats(share, kinds)] * slots,
        scratch_shapes=[pltpu.VMEM((columns // 2, kinds), jnp.float32)],
        name="merge",
        **settings(8, 0.4),
    )(keep, got)
    parts = [merged[0]] + [swap(merged[s], "rows", 2 * s) for s in range(1, slots)]
    gram_other = swap(gram, "rows", slots)
    grams = [gram, gram_other, swap(gram, "rows", 1), swap(gram_other, "rows", 1)]
    prepared = pl.pallas_call(
        functools.partial(prepare_kernel, levels),
        in_specs=[pl.BlockSpec(memory_space=pltpu.HBM), pl.BlockSpec()],
        out_shape=jax.ShapeDtypeStruct((levels, 6 * rank, 2 * rank), jnp.bfloat16),
        scratch_shapes=[pltpu.VMEM((levels, 2 * rank, 2 * rank), jnp.float32), pltpu.SemaphoreType.DMA((levels,))],
        name="prepare",
        **settings(8, 2),
    )(pltpu.with_memory_space_constraint(joined, pltpu.HBM), rank_perm)

    def message_shape(level):
        return floats((levels - level) * share + len(below_pairs(levels, level)) * rank, rank)

    def relay(after, value):
        return pl.pallas_call(
            relay_kernel, out_shape=floats(*value.shape), name="relay", **settings(8, 0.1),
        )(after, value)

    parts[-1] = relay(prepared, parts[-1])
    own, other, rest = pl.pallas_call(
        functools.partial(node_kernel, rank, slots),
        out_shape=[floats(share, rank)] * 2 + [floats(share, size)],
        name="node",
        **settings(8, 1),
    )(*parts, prepared)
    message = pl.pallas_call(
        functools.partial(correct_kernel, levels, rank),
        out_shape=message_shape(1),
        name="correct",
        **settings(8, 1),
    )(own, other, rest, *grams)
    early = [own] + [swap(own if slot < slots // 2 else other, "rows", 2 * slot) for slot in range(1, slots)]
    first = pl.pallas_call(
        functools.partial(solve_kernel, per_step, width),
        out_shape=floats(rows, columns),
        name="solve",
        **settings(8, 8),
    )(moved, rhs, merged[0])

    coefs = []
    for level in range(1, levels):
        last = level + 1 == levels
        arrived = swap(message, "leaf", 2 ** (level - 1))
        outs = pl.pallas_call(
            functools.partial(level_kernel, levels, level, share),
            out_shape=[floats(share, rank)] + ([] if last else [message_shape(level + 1)]),
            name=f"level{level}",
            **settings(8, 1 if last else 6),
        )(message, arrived, prepared, first if last else arrived)
        coefs.append(outs[0])
        message = outs[-1]
    stack = pl.pallas_call(
        stack_kernel, out_shape=floats(slots, share, rank), name="stack", **settings(8, 0.1),
    )(first, *early)
    second = pl.pallas_call(
        functools.partial(apply_kernel, per_step * width),
        out_shape=floats(rows, columns),
        scratch_shapes=[
            pltpu.VMEM((columns, rank), jnp.float32),
            pltpu.VMEM((2 * rank, columns), jnp.bfloat16),
        ],
        name="apply",
        **settings(8, 1.8),
    )(stack, swap(stack, "rows", 1), first, left_basis)

    pack = pl.pallas_call(
        pack_kernel, out_shape=floats(share, size), name="pack", **settings(8, 0.1),
    )(*coefs)
    pieces = []
    for slot in range(slots):
        piece = swap(pack, "rows", 2 * slot) if slot > 0 else pack
        if slot in (0, slots - 1):
            piece = relay(second, piece)
        pieces += [piece, swap(piece, "rows", 1)]
    return pl.pallas_call(
        functools.partial(expand_kernel, levels, width, count),
        out_specs=pl.BlockSpec(memory_space=pl.ANY),
        out_shape=floats(rows, columns),
        scratch_shapes=[
            pltpu.VMEM((columns, size), jnp.float32),
            pltpu.VMEM((2 * size, columns), jnp.bfloat16),
            pltpu.VMEM((rows, columns), jnp.float32),
            pltpu.SemaphoreType.DMA((nblocks,)),
        ],
        name="expand",
        **settings(16, 5),
    )(*pieces, second, left_basis)


def solution(mesh):
    return jax.shard_map(
        per_device,
        mesh=mesh,
        in_specs=(
            P(("leaf", "rows"), None),
            P(("leaf", "rows"), None),
            P(("leaf", "rows"), None, None),
            P(None, ("leaf", "rows"), None),
            P(None, ("leaf", "rows"), None),
            P(),
            P(),
        ),
        out_specs=P(("leaf", "rows"), None),
        check_vma=False,
    )
```

```python
import functools

import jax
import jax.numpy as jnp
from jax import lax
from jax.experimental import pallas as pl
from jax.experimental.pallas import tpu as pltpu
from jax.sharding import PartitionSpec as P

MIB = 1 << 20


def dot(a, b, contract):
    return lax.dot_general(a, b, ((contract[:1], contract[1:]), ((), ())), preferred_element_type=jnp.float32)


def halves(value):
    high_part = value.astype(jnp.bfloat16)
    low_part = (value - high_part.astype(jnp.float32)).astype(jnp.bfloat16)
    return high_part, low_part


def left_stack(value):
    high_part, low_part = halves(value)
    return jnp.concatenate([high_part, high_part, low_part], axis=1)


def right_stack(value):
    high_part, low_part = halves(value)
    return jnp.concatenate([high_part, low_part, high_part], axis=1)


def swap(value, axis, mask):
    count = lax.axis_size(axis)
    return lax.ppermute(value, axis, [(i, i ^ mask) for i in range(count)])


def blocks_per_step(nblocks, most):
    return max(size for size in range(1, most + 1) if nblocks % size == 0)


def below_pairs(levels, first=0):
    return [(level, below) for level in range(levels) for below in range(first, level)]


def gram_kernel(levels, per_step, width, right_ref, left_ref, flip_ref, keep_ref, send_ref,
                right_buf, left_buf, gram_ref, sems):
    rank = right_ref.shape[2]
    half = rank // 2
    tile = per_step * width
    steps = right_ref.shape[1] // tile

    def copies(step):
        rows = pl.ds(pl.multiple_of(step * tile, tile), tile)
        return (
            pltpu.make_async_copy(right_ref.at[:, rows], right_buf.at[:, rows], sems.at[0, step]),
            pltpu.make_async_copy(left_ref.at[:levels - 1, rows], left_buf.at[:, rows], sems.at[1, step]),
        )

    for step in range(steps):
        for copy in copies(step):
            copy.start()
    gram_ref[...] = jnp.zeros_like(gram_ref)

    def body(step, _):
        for copy in copies(step):
            copy.wait()
        rows = pl.ds(pl.multiple_of(step * tile, tile), tile)
        right = jnp.concatenate([right_buf[l, rows, :] for l in range(levels)], axis=1).T
        flip_ref[:, rows] = right
        left = jnp.concatenate([left_buf[l, rows, :] for l in range(levels - 1)], axis=1)
        gram_ref[...] += dot(right[rank:], left, (1, 0))
        return 0

    lax.fori_loop(0, steps, body, 0)
    core = lax.axis_index("rows") % 2
    for spot, (level, below) in enumerate(below_pairs(levels)):
        lanes = pl.ds(spot * rank, rank)
        for ref, side in ((keep_ref, core), (send_ref, 1 - core)):
            rows = pl.ds(pl.multiple_of((level - 1) * rank + side * half, half), half)
            ref[:, lanes] = gram_ref[rows, pl.ds(below * rank, rank)]


def permute_kernel(per_step, width, order_ref, inv_ref, moved_ref):
    place = lax.broadcasted_iota(jnp.int32, (width, width), 0)

    def body(step, _):
        for b in range(per_step):
            block = step * per_step + b
            chosen = (place == order_ref[pl.ds(block, 1), :]).astype(jnp.float32).astype(jnp.bfloat16)
            moved_ref[block] = dot(inv_ref[block], chosen, (1, 1)).astype(jnp.bfloat16)
        return 0

    lax.fori_loop(0, inv_ref.shape[0] // per_step, body, 0)


def weigh_kernel(per_step, width, moved_ref, flip_ref, after_ref, factor_ref):
    kinds = flip_ref.shape[0]

    def body(step, _):
        for b in range(per_step):
            block = step * per_step + b
            lanes = pl.ds(pl.multiple_of(block * width, width), width)
            high_part, low_part = halves(dot(flip_ref[:, lanes], moved_ref[block], (1, 0)))
            factor_ref[:kinds, lanes] = high_part
            factor_ref[kinds:, lanes] = low_part
        return 0

    lax.fori_loop(0, moved_ref.shape[0] // per_step, body, 0)


def solve_kernel(per_step, width, moved_ref, rhs_ref, *refs):
    out_ref = refs[-1]

    def body(step, _):
        for b in range(per_step):
            block = step * per_step + b
            rows = pl.ds(pl.multiple_of(block * width, width), width)
            out_ref[rows, :] = dot(moved_ref[block], rhs_ref[rows, :], (1, 0))
        return 0

    lax.fori_loop(0, moved_ref.shape[0] // per_step, body, 0)


def project_kernel(other, factor_ref, rhs_ref, after_ref, out_ref):
    kinds, part = out_ref.shape
    core = lax.axis_index("rows") % 2
    lanes = pl.ds(pl.multiple_of((1 - core if other else core) * part, part), part)
    total = dot(factor_ref[...], rhs_ref[:, lanes], (1, 0))
    out_ref[...] = total[:kinds] + total[kinds:]


def merge_kernel(keep_ref, got_ref, *refs):
    out_refs, flip_ref = refs[:-1], refs[-1]
    share = out_refs[0].shape[0]
    chip = lax.axis_index("rows") // 2
    flip_ref[...] = (keep_ref[...] + got_ref[...]).T
    for slot, out_ref in enumerate(out_refs):
        out_ref[...] = flip_ref[pl.ds(pl.multiple_of((chip ^ slot) * share, share), share), :]


def add_kernel(mine_ref, got_ref, out_ref):
    out_ref[...] = mine_ref[...] + got_ref[...]


def prepare_kernel(levels, joined_ref, perm_ref, out_ref, joined_buf, sems):
    rank = perm_ref.shape[1]
    leaves = lax.axis_size("leaf")
    leaf = lax.axis_index("leaf")
    copies = []
    for level in range(levels):
        node = 2 * leaves - 2 * leaves // 2 ** level + leaf // 2 ** level
        copies.append(pltpu.make_async_copy(joined_ref.at[node], joined_buf.at[level], sems.at[level]))
        copies[-1].start()
    spot = lax.broadcasted_iota(jnp.int32, (rank, rank), 0)
    for level in range(levels):
        copies[level].wait()
        chosen = (spot == perm_ref[level:level + 1, :]).astype(jnp.float32).astype(jnp.bfloat16)
        high_part, low_part = halves(joined_buf[level])
        for place, part in enumerate((high_part, low_part, high_part)):
            for side in range(2):
                moved = dot(chosen, part[:, side * rank:(side + 1) * rank], (1, 1)).astype(jnp.bfloat16)
                out_ref[level, pl.ds((2 * place + side) * rank, rank), :] = moved


def by_side(side, own, other):
    return jnp.where(side == 0, own, other), jnp.where(side == 0, other, own)


def pack_message(message_ref, pieces):
    row = 0
    for piece in pieces:
        message_ref[pl.ds(row, piece.shape[0]), :] = piece
        row += piece.shape[0]


def node_kernel(rank, slots, *refs):
    part_refs = refs[:slots]
    joined_ref, own_ref, other_ref, rest_ref = refs[slots:]
    side = lax.axis_index("rows") // slots
    half = slots // 2
    sums = [sum(ref[...] for ref in part_refs[:half]), sum(ref[...] for ref in part_refs[half:])]
    picked = jnp.concatenate(by_side(side, sums[0][:, :rank], sums[1][:, :rank]), axis=1)
    coef = dot(left_stack(picked), joined_ref[0], (1, 0))
    own_ref[...], other_ref[...] = by_side(side, coef[:, :rank], coef[:, rank:])
    rest_ref[...] = (sums[0] + sums[1])[:, rank:]


def correct_kernel(levels, rank, own_ref, other_ref, rest_ref, mine_ref, theirs_ref, pair_mine_ref,
                   pair_theirs_ref, message_ref):
    core = lax.axis_index("rows") % 2
    grams = [jnp.concatenate(by_side(core, mine_ref[...], pair_mine_ref[...]), axis=0),
             jnp.concatenate(by_side(core, theirs_ref[...], pair_theirs_ref[...]), axis=0)]
    pairs = below_pairs(levels)
    lanes = {pair: slice(spot * rank, (spot + 1) * rank) for spot, pair in enumerate(pairs)}
    joint = jnp.concatenate(
        [jnp.concatenate([gram[:, lanes[level, 0]] for gram in grams], axis=1) for level in range(1, levels)], axis=0)
    pair = jnp.concatenate([own_ref[...], other_ref[...]], axis=1)
    rest = rest_ref[...] - dot(left_stack(pair), right_stack(joint), (1, 1))
    pieces = [rest[:, level * rank:(level + 1) * rank] for level in range(levels - 1)]
    for pair in pairs:
        if pair[1] > 0:
            pieces.append(grams[0][:, lanes[pair]] + grams[1][:, lanes[pair]])
    pack_message(message_ref, pieces)


def level_kernel(levels, level, share, sent_ref, got_ref, joined_ref, after_ref, coef_ref, *message_ref):
    rank = sent_ref.shape[1]
    side = lax.axis_index("leaf") // 2 ** (level - 1) % 2
    more = levels - level
    values = []
    for ref in (sent_ref, got_ref):
        values.append([ref[pl.ds(i * share, share), :] for i in range(more)])
    picked = jnp.concatenate(by_side(side, values[0][0], values[1][0]), axis=1)
    coef = dot(left_stack(picked), joined_ref[level], (1, 0))
    sides = by_side(side, coef[:, :rank], coef[:, rank:])
    coef_ref[...] = sides[0]
    if not message_ref:
        return
    pairs = below_pairs(levels, level)
    grams = []
    for ref in (sent_ref, got_ref):
        grams.append({pair: ref[pl.ds(more * share + spot * rank, rank), :] for spot, pair in enumerate(pairs)})
    uppers = list(range(level + 1, levels))
    joint = jnp.concatenate(
        [jnp.concatenate([gram[upper, level] for gram in grams], axis=1) for upper in uppers], axis=0)
    change = dot(left_stack(jnp.concatenate(sides, axis=1)), right_stack(joint), (1, 1))
    pieces = [values[0][upper - level] + values[1][upper - level] - change[:, i * rank:(i + 1) * rank]
              for i, upper in enumerate(uppers)]
    for pair in pairs:
        if pair[1] > level:
            pieces.append(grams[0][pair] + grams[1][pair])
    pack_message(message_ref[0], pieces)


def pack_kernel(*refs):
    refs[-1][...] = jnp.concatenate([ref[...] for ref in refs[:-1]], axis=1)


def stack_kernel(after_ref, *refs):
    for slot, ref in enumerate(refs[:-1]):
        refs[-1][slot] = ref[...]


def relay_kernel(after_ref, ref, out_ref):
    out_ref[...] = ref[...]


def split_factor(pieces, flip_ref, factor_ref):
    share, kinds = pieces[0].shape
    slots = len(pieces) // 2
    me = lax.axis_index("rows")
    for mask, ref in enumerate(pieces):
        owner = me ^ mask
        row = (owner % 2 * slots + owner // 2) * share
        flip_ref[pl.ds(pl.multiple_of(row, share), share), :] = ref[...]
    high_part, low_part = halves(flip_ref[...].T)
    factor_ref[:kinds, :] = high_part
    factor_ref[kinds:, :] = low_part


def apply_kernel(tile, own_ref, pair_ref, first_ref, left_ref, out_ref, flip_ref, factor_ref):
    pieces = [ref.at[slot] for slot in range(own_ref.shape[0]) for ref in (own_ref, pair_ref)]
    split_factor(pieces, flip_ref, factor_ref)
    for row in range(0, out_ref.shape[0], tile):
        rows = pl.ds(row, tile)
        left = jnp.concatenate([left_ref[0, rows, :]] * 2, axis=1)
        out_ref[rows, :] = first_ref[rows, :] - dot(left, factor_ref[...], (1, 0))


def half_factor(piece_refs, flip_ref):
    share = piece_refs[0].shape[0]
    chip = lax.axis_index("rows") // 2
    for slot, ref in enumerate(piece_refs):
        flip_ref[pl.ds(pl.multiple_of((chip ^ slot) * share, share), share), :] = ref[...]
    return jnp.concatenate(halves(flip_ref[...].T), axis=0)


def side_lanes(part, other):
    core = lax.axis_index("rows") % 2
    return pl.ds(pl.multiple_of((1 - core if other else core) * part, part), part)


def left_rows(left_ref, rows):
    return jnp.concatenate([left_ref[l, rows, :] for l in range(1, left_ref.shape[0])] * 2, axis=1)


def expand_own_kernel(head, width, slots, *refs):
    first_ref, left_ref, out_ref, factor_ref, flip_ref, out_buf, sems = refs[slots:]
    lanes = side_lanes(out_buf.shape[1], False)
    factor_ref[...] = half_factor(refs[:slots], flip_ref)
    copies = []
    for block in range(head):
        rows = pl.ds(block * width, width)
        out_buf[rows, :] = first_ref[rows, lanes] - dot(left_rows(left_ref, rows), factor_ref[...], (1, 0))
        copies.append(pltpu.make_async_copy(out_buf.at[rows], out_ref.at[rows, lanes], sems.at[block]))
        copies[-1].start(priority=block % 2)
    for copy in copies:
        copy.wait()


def expand_rest_kernel(head, width, slots, *refs):
    own_ref, first_ref, left_ref, _, out_ref, flip_ref, factor_ref, head_buf, out_buf, sems = refs[slots:]
    part = own_ref.shape[1]
    lanes = side_lanes(part, True)
    other = half_factor(refs[:slots], flip_ref)
    factor_ref[:, side_lanes(part, False)] = own_ref[...]
    factor_ref[:, lanes] = other
    copies = []
    for block in range(sems.shape[0]):
        rows = pl.ds(block * width, width)
        left = left_rows(left_ref, rows)
        if block < head:
            head_buf[rows, :] = first_ref[rows, lanes] - dot(left, other, (1, 0))
            copies.append(pltpu.make_async_copy(head_buf.at[rows], out_ref.at[rows, lanes], sems.at[block]))
        else:
            place = pl.ds((block - head) * width, width)
            out_buf[place, :] = first_ref[rows, :] - dot(left, factor_ref[...], (1, 0))
            copies.append(pltpu.make_async_copy(out_buf.at[place], out_ref.at[rows], sems.at[block]))
        copies[-1].start(priority=block % 2)
    for copy in copies:
        copy.wait()


def settings(mib, micros):
    return dict(
        compiler_params=pltpu.CompilerParams(vmem_limit_bytes=mib * MIB),
        cost_estimate=pl.CostEstimate(flops=int(micros * 1.1e9), bytes_accessed=0, transcendentals=0),
    )


def floats(*shape):
    return jax.ShapeDtypeStruct(shape, jnp.float32)


def per_device(rhs, leaf_order, leaf_inv, right_basis, left_basis, rank_perm, joined):
    levels, rows, rank = right_basis.shape
    nblocks, width, _ = leaf_inv.shape
    columns = rhs.shape[1]
    leaves = lax.axis_size("leaf")
    count = lax.axis_size("rows")
    slots = count // 2
    kinds = levels * rank
    size = kinds - rank
    share = columns // count
    gram_lanes = len(below_pairs(levels)) * rank

    per_step = blocks_per_step(nblocks, 3)
    flipped, gram_keep, gram_send = pl.pallas_call(
        functools.partial(gram_kernel, levels, per_step, width),
        in_specs=[pl.BlockSpec(memory_space=pltpu.HBM)] * 2,
        out_shape=[jax.ShapeDtypeStruct((kinds, rows), jnp.bfloat16)] + [floats(rank // 2, gram_lanes)] * 2,
        scratch_shapes=[
            pltpu.VMEM((levels, rows, rank), jnp.bfloat16),
            pltpu.VMEM((levels - 1, rows, rank), jnp.bfloat16),
            pltpu.VMEM((size, size), jnp.float32),
            pltpu.SemaphoreType.DMA((2, nblocks // per_step)),
        ],
        name="gram",
        **settings(24, 3),
    )(pltpu.with_memory_space_constraint(right_basis, pltpu.HBM),
      pltpu.with_memory_space_constraint(left_basis, pltpu.HBM))

    gram_got = swap(gram_send, "rows", 1)
    moved = pl.pallas_call(
        functools.partial(permute_kernel, blocks_per_step(nblocks, 9), width),
        out_shape=jax.ShapeDtypeStruct((nblocks, width, width), jnp.bfloat16),
        name="permute",
        **settings(8, 1.5),
    )(leaf_order, leaf_inv)

    def add(mine, got):
        return pl.pallas_call(
            add_kernel, out_shape=floats(*mine.shape), name="add", **settings(8, 0.1),
        )(mine, got)

    gram = add(gram_keep, gram_got)
    factors = pl.pallas_call(
        functools.partial(weigh_kernel, blocks_per_step(nblocks, 9), width),
        out_shape=jax.ShapeDtypeStruct((2 * kinds, rows), jnp.bfloat16),
        name="weigh",
        **settings(8, 2.4),
    )(moved, flipped, gram)

    def project(other, after):
        return pl.pallas_call(
            functools.partial(project_kernel, other),
            out_shape=floats(kinds, columns // 2),
            name="project_other" if other else "project_own",
            **settings(12, 1 if other else 4),
        )(factors, rhs, after)

    send = project(True, gram)
    got = swap(send, "rows", 1)
    mask = 2
    while mask < slots:
        gram = add(gram, swap(gram, "rows", mask))
        mask *= 2
    keep = project(False, gram)
    merged = pl.pallas_call(
        merge_kernel,
        out_shape=[floats(share, kinds)] * slots,
        scratch_shapes=[pltpu.VMEM((columns // 2, kinds), jnp.float32)],
        name="merge",
        **settings(8, 0.4),
    )(keep, got)
    parts = [merged[0]] + [swap(merged[s], "rows", 2 * s) for s in range(1, slots)]
    gram_other = swap(gram, "rows", slots)
    grams = [gram, gram_other, swap(gram, "rows", 1), swap(gram_other, "rows", 1)]
    prepared = pl.pallas_call(
        functools.partial(prepare_kernel, levels),
        in_specs=[pl.BlockSpec(memory_space=pltpu.HBM), pl.BlockSpec()],
        out_shape=jax.ShapeDtypeStruct((levels, 6 * rank, 2 * rank), jnp.bfloat16),
        scratch_shapes=[pltpu.VMEM((levels, 2 * rank, 2 * rank), jnp.float32), pltpu.SemaphoreType.DMA((levels,))],
        name="prepare",
        **settings(8, 2),
    )(pltpu.with_memory_space_constraint(joined, pltpu.HBM), rank_perm)

    def message_shape(level):
        return floats((levels - level) * share + len(below_pairs(levels, level)) * rank, rank)

    own, other, rest = pl.pallas_call(
        functools.partial(node_kernel, rank, slots),
        out_shape=[floats(share, rank)] * 2 + [floats(share, size)],
        name="node",
        **settings(8, 1),
    )(*parts, prepared)
    message = pl.pallas_call(
        functools.partial(correct_kernel, levels, rank),
        out_shape=message_shape(1),
        name="correct",
        **settings(8, 1),
    )(own, other, rest, *grams)
    early = [own] + [swap(own if slot < slots // 2 else other, "rows", 2 * slot) for slot in range(1, slots)]
    first = pl.pallas_call(
        functools.partial(solve_kernel, per_step, width),
        out_shape=floats(rows, columns),
        name="solve",
        **settings(8, 8),
    )(moved, rhs, merged[0])

    coefs = []
    for level in range(1, levels):
        last = level + 1 == levels
        arrived = swap(message, "leaf", 2 ** (level - 1))
        outs = pl.pallas_call(
            functools.partial(level_kernel, levels, level, share),
            out_shape=[floats(share, rank)] + ([] if last else [message_shape(level + 1)]),
            name=f"level{level}",
            **settings(8, 1 if last else 6),
        )(message, arrived, prepared, first if last else arrived)
        coefs.append(outs[0])
        message = outs[-1]
    stack = pl.pallas_call(
        stack_kernel, out_shape=floats(slots, share, rank), name="stack", **settings(8, 0.1),
    )(first, *early)
    second = pl.pallas_call(
        functools.partial(apply_kernel, per_step * width),
        out_shape=floats(rows, columns),
        scratch_shapes=[
            pltpu.VMEM((columns, rank), jnp.float32),
            pltpu.VMEM((2 * rank, columns), jnp.bfloat16),
        ],
        name="apply",
        **settings(8, 1.8),
    )(stack, swap(stack, "rows", 1), first, left_basis)

    pack = pl.pallas_call(
        pack_kernel, out_shape=floats(share, size), name="pack", **settings(8, 0.1),
    )(*coefs)
    direct, swapped = [], []
    for slot in range(slots):
        piece = swap(pack, "rows", 2 * slot) if slot > 0 else pack
        if slot in (0, slots - 1):
            piece = pl.pallas_call(
                relay_kernel, out_shape=floats(share, size), name="relay", **settings(8, 0.1),
            )(second, piece)
        direct.append(piece)
        swapped.append(swap(piece, "rows", 1))

    head = nblocks // 3
    half = columns // 2
    anywhere = pl.BlockSpec(memory_space=pl.ANY)
    out, factor = pl.pallas_call(
        functools.partial(expand_own_kernel, head, width, slots),
        out_specs=[anywhere, pl.BlockSpec()],
        out_shape=[floats(rows, columns), jax.ShapeDtypeStruct((2 * size, half), jnp.bfloat16)],
        scratch_shapes=[
            pltpu.VMEM((half, size), jnp.float32),
            pltpu.VMEM((head * width, half), jnp.float32),
            pltpu.SemaphoreType.DMA((head,)),
        ],
        name="expand_own",
        **settings(8, 1.2),
    )(*direct, second, left_basis)
    return pl.pallas_call(
        functools.partial(expand_rest_kernel, head, width, slots),
        in_specs=[pl.BlockSpec()] * (slots + 3) + [anywhere],
        out_specs=anywhere,
        out_shape=floats(rows, columns),
        scratch_shapes=[
            pltpu.VMEM((half, size), jnp.float32),
            pltpu.VMEM((2 * size, columns), jnp.bfloat16),
            pltpu.VMEM((head * width, half), jnp.float32),
            pltpu.VMEM((rows - head * width, columns), jnp.float32),
            pltpu.SemaphoreType.DMA((nblocks,)),
        ],
        input_output_aliases={slots + 3: 0},
        name="expand_rest",
        **settings(16, 4),
    )(*swapped, factor, second, left_basis, out)


def solution(mesh):
    return jax.shard_map(
        per_device,
        mesh=mesh,
        in_specs=(
            P(("leaf", "rows"), None),
            P(("leaf", "rows"), None),
            P(("leaf", "rows"), None, None),
            P(None, ("leaf", "rows"), None),
            P(None, ("leaf", "rows"), None),
            P(),
            P(),
        ),
        out_specs=P(("leaf", "rows"), None),
        check_vma=False,
    )
```

```python
import functools

import jax
import jax.numpy as jnp
from jax import lax
from jax.experimental import pallas as pl
from jax.experimental.pallas import tpu as pltpu
from jax.sharding import PartitionSpec as P

MIB = 1 << 20


def dot(a, b, contract):
    return lax.dot_general(a, b, ((contract[:1], contract[1:]), ((), ())), preferred_element_type=jnp.float32)


def halves(value):
    high_part = value.astype(jnp.bfloat16)
    low_part = (value - high_part.astype(jnp.float32)).astype(jnp.bfloat16)
    return high_part, low_part


def left_stack(value):
    high_part, low_part = halves(value)
    return jnp.concatenate([high_part, high_part, low_part], axis=1)


def right_stack(value):
    high_part, low_part = halves(value)
    return jnp.concatenate([high_part, low_part, high_part], axis=1)


def swap(value, axis, mask):
    count = lax.axis_size(axis)
    return lax.ppermute(value, axis, [(i, i ^ mask) for i in range(count)])


def blocks_per_step(nblocks, most):
    return max(size for size in range(1, most + 1) if nblocks % size == 0)


def below_pairs(levels, first=0):
    return [(level, below) for level in range(levels) for below in range(first, level)]


def gram_kernel(levels, per_step, width, right_ref, left_ref, flip_ref, keep_ref, send_ref,
                right_buf, left_buf, gram_ref, sems):
    rank = right_ref.shape[2]
    half = rank // 2
    tile = per_step * width
    steps = right_ref.shape[1] // tile

    def copies(step):
        rows = pl.ds(pl.multiple_of(step * tile, tile), tile)
        return (
            pltpu.make_async_copy(right_ref.at[:, rows], right_buf.at[:, rows], sems.at[0, step]),
            pltpu.make_async_copy(left_ref.at[:levels - 1, rows], left_buf.at[:, rows], sems.at[1, step]),
        )

    for step in range(steps):
        for copy in copies(step):
            copy.start()
    gram_ref[...] = jnp.zeros_like(gram_ref)

    def body(step, _):
        for copy in copies(step):
            copy.wait()
        rows = pl.ds(pl.multiple_of(step * tile, tile), tile)
        right = jnp.concatenate([right_buf[l, rows, :] for l in range(levels)], axis=1).T
        flip_ref[:, rows] = right
        left = jnp.concatenate([left_buf[l, rows, :] for l in range(levels - 1)], axis=1)
        gram_ref[...] += dot(right[rank:], left, (1, 0))
        return 0

    lax.fori_loop(0, steps, body, 0)
    core = lax.axis_index("rows") % 2
    for spot, (level, below) in enumerate(below_pairs(levels)):
        lanes = pl.ds(spot * rank, rank)
        for ref, side in ((keep_ref, core), (send_ref, 1 - core)):
            rows = pl.ds(pl.multiple_of((level - 1) * rank + side * half, half), half)
            ref[:, lanes] = gram_ref[rows, pl.ds(below * rank, rank)]


def permute_kernel(per_step, width, order_ref, inv_ref, moved_ref):
    place = lax.broadcasted_iota(jnp.int32, (width, width), 0)

    def body(step, _):
        for b in range(per_step):
            block = step * per_step + b
            chosen = (place == order_ref[pl.ds(block, 1), :]).astype(jnp.float32).astype(jnp.bfloat16)
            moved_ref[block] = dot(inv_ref[block], chosen, (1, 1)).astype(jnp.bfloat16)
        return 0

    lax.fori_loop(0, inv_ref.shape[0] // per_step, body, 0)


def weigh_kernel(per_step, width, moved_ref, flip_ref, after_ref, factor_ref):
    kinds = flip_ref.shape[0]

    def body(step, _):
        for b in range(per_step):
            block = step * per_step + b
            lanes = pl.ds(pl.multiple_of(block * width, width), width)
            high_part, low_part = halves(dot(flip_ref[:, lanes], moved_ref[block], (1, 0)))
            factor_ref[:kinds, lanes] = high_part
            factor_ref[kinds:, lanes] = low_part
        return 0

    lax.fori_loop(0, moved_ref.shape[0] // per_step, body, 0)


def solve_kernel(per_step, width, moved_ref, rhs_ref, *refs):
    out_ref = refs[-1]

    def body(step, _):
        for b in range(per_step):
            block = step * per_step + b
            rows = pl.ds(pl.multiple_of(block * width, width), width)
            out_ref[rows, :] = dot(moved_ref[block], rhs_ref[rows, :], (1, 0))
        return 0

    lax.fori_loop(0, moved_ref.shape[0] // per_step, body, 0)


def project_kernel(other, factor_ref, rhs_ref, after_ref, out_ref):
    kinds, part = out_ref.shape
    core = lax.axis_index("rows") % 2
    lanes = pl.ds(pl.multiple_of((1 - core if other else core) * part, part), part)
    total = dot(factor_ref[...], rhs_ref[:, lanes], (1, 0))
    out_ref[...] = total[:kinds] + total[kinds:]


def merge_kernel(keep_ref, got_ref, *refs):
    out_refs, flip_ref = refs[:-1], refs[-1]
    share = out_refs[0].shape[0]
    chip = lax.axis_index("rows") // 2
    flip_ref[...] = (keep_ref[...] + got_ref[...]).T
    for slot, out_ref in enumerate(out_refs):
        out_ref[...] = flip_ref[pl.ds(pl.multiple_of((chip ^ slot) * share, share), share), :]


def add_kernel(mine_ref, got_ref, out_ref):
    out_ref[...] = mine_ref[...] + got_ref[...]


def prepare_kernel(levels, joined_ref, perm_ref, after_ref, out_ref, joined_buf, sems):
    rank = perm_ref.shape[1]
    leaves = lax.axis_size("leaf")
    leaf = lax.axis_index("leaf")
    copies = []
    for level in range(levels):
        node = 2 * leaves - 2 * leaves // 2 ** level + leaf // 2 ** level
        copies.append(pltpu.make_async_copy(joined_ref.at[node], joined_buf.at[level], sems.at[level]))
        copies[-1].start()
    spot = lax.broadcasted_iota(jnp.int32, (rank, rank), 0)
    for level in range(levels):
        copies[level].wait()
        chosen = (spot == perm_ref[level:level + 1, :]).astype(jnp.float32).astype(jnp.bfloat16)
        high_part, low_part = halves(joined_buf[level])
        for place, part in enumerate((high_part, low_part)):
            for side in range(2):
                moved = dot(chosen, part[:, side * rank:(side + 1) * rank], (1, 1)).astype(jnp.bfloat16)
                out_ref[level, pl.ds((2 * place + side) * rank, rank), :] = moved
                if place == 0:
                    out_ref[level, pl.ds((4 + side) * rank, rank), :] = moved


def by_side(side, own, other):
    return jnp.where(side == 0, own, other), jnp.where(side == 0, other, own)


def pack_message(message_ref, pieces):
    row = 0
    for piece in pieces:
        message_ref[pl.ds(row, piece.shape[0]), :] = piece
        row += piece.shape[0]


def node_kernel(rank, slots, after_ref, *refs):
    part_refs = refs[:slots]
    joined_ref, own_ref, other_ref, rest_ref = refs[slots:]
    side = lax.axis_index("rows") // slots
    half = slots // 2
    sums = [sum(ref[...] for ref in part_refs[:half]), sum(ref[...] for ref in part_refs[half:])]
    picked = jnp.concatenate(by_side(side, sums[0][:, :rank], sums[1][:, :rank]), axis=1)
    coef = dot(left_stack(picked), joined_ref[0], (1, 0))
    own_ref[...], other_ref[...] = by_side(side, coef[:, :rank], coef[:, rank:])
    rest_ref[...] = (sums[0] + sums[1])[:, rank:]


def correct_kernel(levels, rank, own_ref, other_ref, rest_ref, mine_ref, theirs_ref, pair_mine_ref,
                   pair_theirs_ref, message_ref):
    core = lax.axis_index("rows") % 2
    grams = [jnp.concatenate(by_side(core, mine_ref[...], pair_mine_ref[...]), axis=0),
             jnp.concatenate(by_side(core, theirs_ref[...], pair_theirs_ref[...]), axis=0)]
    pairs = below_pairs(levels)
    lanes = {pair: slice(spot * rank, (spot + 1) * rank) for spot, pair in enumerate(pairs)}
    joint = jnp.concatenate(
        [jnp.concatenate([gram[:, lanes[level, 0]] for gram in grams], axis=1) for level in range(1, levels)], axis=0)
    pair = jnp.concatenate([own_ref[...], other_ref[...]], axis=1)
    rest = rest_ref[...] - dot(left_stack(pair), right_stack(joint), (1, 1))
    pieces = [rest[:, level * rank:(level + 1) * rank] for level in range(levels - 1)]
    for pair in pairs:
        if pair[1] > 0:
            pieces.append(grams[0][:, lanes[pair]] + grams[1][:, lanes[pair]])
    pack_message(message_ref, pieces)


def level_kernel(levels, level, share, sent_ref, got_ref, joined_ref, after_ref, coef_ref, *message_ref):
    rank = sent_ref.shape[1]
    side = lax.axis_index("leaf") // 2 ** (level - 1) % 2
    more = levels - level
    values = []
    for ref in (sent_ref, got_ref):
        values.append([ref[pl.ds(i * share, share), :] for i in range(more)])
    picked = jnp.concatenate(by_side(side, values[0][0], values[1][0]), axis=1)
    coef = dot(left_stack(picked), joined_ref[level], (1, 0))
    sides = by_side(side, coef[:, :rank], coef[:, rank:])
    coef_ref[...] = sides[0]
    if not message_ref:
        return
    pairs = below_pairs(levels, level)
    grams = []
    for ref in (sent_ref, got_ref):
        grams.append({pair: ref[pl.ds(more * share + spot * rank, rank), :] for spot, pair in enumerate(pairs)})
    uppers = list(range(level + 1, levels))
    joint = jnp.concatenate(
        [jnp.concatenate([gram[upper, level] for gram in grams], axis=1) for upper in uppers], axis=0)
    change = dot(left_stack(jnp.concatenate(sides, axis=1)), right_stack(joint), (1, 1))
    pieces = [values[0][upper - level] + values[1][upper - level] - change[:, i * rank:(i + 1) * rank]
              for i, upper in enumerate(uppers)]
    for pair in pairs:
        if pair[1] > level:
            pieces.append(grams[0][pair] + grams[1][pair])
    pack_message(message_ref[0], pieces)


def pack_kernel(*refs):
    refs[-1][...] = jnp.concatenate([ref[...] for ref in refs[:-1]], axis=1)


def stack_kernel(after_ref, *refs):
    for slot, ref in enumerate(refs[:-1]):
        refs[-1][slot] = ref[...]


def join_kernel(after_ref, *refs):
    refs[-1][...] = jnp.concatenate([ref[...] for ref in refs[:-1]], axis=1)


def relay_kernel(after_ref, ref, out_ref):
    out_ref[...] = ref[...]


def split_factor(pieces, flip_ref, factor_ref):
    share, kinds = pieces[0].shape
    slots = len(pieces) // 2
    me = lax.axis_index("rows")
    for mask, ref in enumerate(pieces):
        owner = me ^ mask
        row = (owner % 2 * slots + owner // 2) * share
        flip_ref[pl.ds(pl.multiple_of(row, share), share), :] = ref[...]
    high_part, low_part = halves(flip_ref[...].T)
    factor_ref[:kinds, :] = high_part
    factor_ref[kinds:, :] = low_part


def apply_kernel(tile, own_ref, pair_ref, first_ref, left_ref, after_ref, out_ref, flip_ref, factor_ref):
    pieces = [ref.at[slot] for slot in range(own_ref.shape[0]) for ref in (own_ref, pair_ref)]
    split_factor(pieces, flip_ref, factor_ref)
    for row in range(0, out_ref.shape[0], tile):
        rows = pl.ds(row, tile)
        left = jnp.concatenate([left_ref[0, rows, :]] * 2, axis=1)
        out_ref[rows, :] = first_ref[rows, :] - dot(left, factor_ref[...], (1, 0))


def expand_kernel(levels, tile, count, *refs):
    piece_refs = refs[:count]
    first_ref, left_ref, out_ref, flip_ref, factor_ref, out_buf, sems = refs[count:]
    split_factor(piece_refs, flip_ref, factor_ref)
    copies = []
    for step in range(out_buf.shape[0] // tile):
        rows = pl.ds(step * tile, tile)
        left = jnp.concatenate([left_ref[l, rows, :] for l in range(1, levels)] * 2, axis=1)
        out_buf[rows, :] = first_ref[rows, :] - dot(left, factor_ref[...], (1, 0))
        copies.append(pltpu.make_async_copy(out_buf.at[rows], out_ref.at[rows], sems.at[step]))
        copies[-1].start(priority=step % 2)
    for copy in copies:
        copy.wait()


def settings(mib, micros):
    return dict(
        compiler_params=pltpu.CompilerParams(vmem_limit_bytes=mib * MIB),
        cost_estimate=pl.CostEstimate(flops=int(micros * 1.1e9), bytes_accessed=0, transcendentals=0),
    )


def floats(*shape):
    return jax.ShapeDtypeStruct(shape, jnp.float32)


def per_device(rhs, leaf_order, leaf_inv, right_basis, left_basis, rank_perm, joined):
    levels, rows, rank = right_basis.shape
    nblocks, width, _ = leaf_inv.shape
    columns = rhs.shape[1]
    leaves = lax.axis_size("leaf")
    count = lax.axis_size("rows")
    slots = count // 2
    kinds = levels * rank
    size = kinds - rank
    share = columns // count
    gram_lanes = len(below_pairs(levels)) * rank

    per_step = blocks_per_step(nblocks, 3)
    flipped, gram_keep, gram_send = pl.pallas_call(
        functools.partial(gram_kernel, levels, per_step, width),
        in_specs=[pl.BlockSpec(memory_space=pltpu.HBM)] * 2,
        out_shape=[jax.ShapeDtypeStruct((kinds, rows), jnp.bfloat16)] + [floats(rank // 2, gram_lanes)] * 2,
        scratch_shapes=[
            pltpu.VMEM((levels, rows, rank), jnp.bfloat16),
            pltpu.VMEM((levels - 1, rows, rank), jnp.bfloat16),
            pltpu.VMEM((size, size), jnp.float32),
            pltpu.SemaphoreType.DMA((2, nblocks // per_step)),
        ],
        name="gram",
        **settings(24, 3),
    )(pltpu.with_memory_space_constraint(right_basis, pltpu.HBM),
      pltpu.with_memory_space_constraint(left_basis, pltpu.HBM))

    gram_got = swap(gram_send, "rows", 1)
    moved = pl.pallas_call(
        functools.partial(permute_kernel, blocks_per_step(nblocks, 9), width),
        out_shape=jax.ShapeDtypeStruct((nblocks, width, width), jnp.bfloat16),
        name="permute",
        **settings(8, 1.5),
    )(leaf_order, leaf_inv)

    def add(mine, got):
        return pl.pallas_call(
            add_kernel, out_shape=floats(*mine.shape), name="add", **settings(8, 0.1),
        )(mine, got)

    gram = add(gram_keep, gram_got)
    factors = pl.pallas_call(
        functools.partial(weigh_kernel, blocks_per_step(nblocks, 9), width),
        out_shape=jax.ShapeDtypeStruct((2 * kinds, rows), jnp.bfloat16),
        name="weigh",
        **settings(8, 2.4),
    )(moved, flipped, gram)

    def project(other, after):
        return pl.pallas_call(
            functools.partial(project_kernel, other),
            out_shape=floats(kinds, columns // 2),
            name="project_other" if other else "project_own",
            **settings(12, 1 if other else 4),
        )(factors, rhs, after)

    send = project(True, gram)
    got = swap(send, "rows", 1)
    mask = 2
    while mask < slots:
        gram = add(gram, swap(gram, "rows", mask))
        mask *= 2
    keep = project(False, gram)
    merged = pl.pallas_call(
        merge_kernel,
        out_shape=[floats(share, kinds)] * slots,
        scratch_shapes=[pltpu.VMEM((columns // 2, kinds), jnp.float32)],
        name="merge",
        **settings(8, 0.4),
    )(keep, got)
    parts = [merged[0]] + [swap(merged[s], "rows", 2 * s) for s in range(1, slots)]
    gram_other = swap(gram, "rows", slots)
    prepared = pl.pallas_call(
        functools.partial(prepare_kernel, levels),
        in_specs=[pl.BlockSpec(memory_space=pltpu.HBM), pl.BlockSpec(), pl.BlockSpec()],
        out_shape=jax.ShapeDtypeStruct((levels, 6 * rank, 2 * rank), jnp.bfloat16),
        scratch_shapes=[pltpu.VMEM((levels, 2 * rank, 2 * rank), jnp.float32), pltpu.SemaphoreType.DMA((levels,))],
        name="prepare",
        **settings(8, 2),
    )(pltpu.with_memory_space_constraint(joined, pltpu.HBM), rank_perm, merged[0])

    def message_shape(level):
        return floats((levels - level) * share + len(below_pairs(levels, level)) * rank, rank)

    gram_other = pl.pallas_call(
        relay_kernel, out_shape=floats(*gram.shape), name="relay", **settings(8, 0.1),
    )(prepared, gram_other)
    grams = [gram, gram_other, swap(gram, "rows", 1), swap(gram_other, "rows", 1)]
    first = pl.pallas_call(
        functools.partial(solve_kernel, per_step, width),
        out_shape=floats(rows, columns),
        name="solve",
        **settings(8, 1),
    )(moved, rhs, merged[0])

    own, other, rest = pl.pallas_call(
        functools.partial(node_kernel, rank, slots),
        out_shape=[floats(share, rank)] * 2 + [floats(share, size)],
        name="node",
        **settings(8, 1),
    )(first, *parts, prepared)
    message = pl.pallas_call(
        functools.partial(correct_kernel, levels, rank),
        out_shape=message_shape(1),
        name="correct",
        **settings(8, 1),
    )(own, other, rest, *grams)
    early = [own] + [swap(own if slot < slots // 2 else other, "rows", 2 * slot) for slot in range(1, slots)]
    coefs = []
    for level in range(1, levels):
        last = level + 1 == levels
        arrived = swap(message, "leaf", 2 ** (level - 1))
        outs = pl.pallas_call(
            functools.partial(level_kernel, levels, level, share),
            out_shape=[floats(share, rank)] + ([] if last else [message_shape(level + 1)]),
            name=f"level{level}",
            **settings(8, 1 if last else 6),
        )(message, arrived, prepared, arrived)
        coefs.append(outs[0])
        message = outs[-1]
    packed = coefs[0] if levels == 3 else jnp.concatenate(coefs[:-1], axis=1)
    ahead = swap(packed, "rows", 2 * (slots - 1))
    stack = pl.pallas_call(
        stack_kernel, out_shape=floats(slots, share, rank), name="stack", **settings(8, 0.1),
    )(first, *early)
    second = pl.pallas_call(
        functools.partial(apply_kernel, per_step * width),
        out_shape=floats(rows, columns),
        scratch_shapes=[
            pltpu.VMEM((columns, rank), jnp.float32),
            pltpu.VMEM((2 * rank, columns), jnp.bfloat16),
        ],
        name="apply",
        **settings(8, 1.8),
    )(stack, swap(stack, "rows", 1), first, left_basis, ahead)

    pack = pl.pallas_call(
        pack_kernel, out_shape=floats(share, size), name="pack", **settings(8, 0.1),
    )(*coefs)
    pieces = []
    for slot in range(slots):
        piece = swap(pack, "rows", 2 * slot) if slot > 0 else pack
        if slot == slots - 1:
            tail = swap(coefs[-1], "rows", 2 * slot)
            piece = pl.pallas_call(
                join_kernel, out_shape=floats(share, size), name="join", **settings(8, 0.1),
            )(second, ahead, tail)
        elif slot == 0:
            piece = pl.pallas_call(
                relay_kernel, out_shape=floats(share, size), name="relay", **settings(8, 0.1),
            )(second, piece)
        pieces += [piece, swap(piece, "rows", 1)]
    return pl.pallas_call(
        functools.partial(expand_kernel, levels, width, count),
        out_specs=pl.BlockSpec(memory_space=pl.ANY),
        out_shape=floats(rows, columns),
        scratch_shapes=[
            pltpu.VMEM((columns, size), jnp.float32),
            pltpu.VMEM((2 * size, columns), jnp.bfloat16),
            pltpu.VMEM((rows, columns), jnp.float32),
            pltpu.SemaphoreType.DMA((nblocks,)),
        ],
        name="expand",
        **settings(16, 5),
    )(*pieces, second, left_basis)


def solution(mesh):
    return jax.shard_map(
        per_device,
        mesh=mesh,
        in_specs=(
            P(("leaf", "rows"), None),
            P(("leaf", "rows"), None),
            P(("leaf", "rows"), None, None),
            P(None, ("leaf", "rows"), None),
            P(None, ("leaf", "rows"), None),
            P(),
            P(),
        ),
        out_specs=P(("leaf", "rows"), None),
        check_vma=False,
    )
```

```python
import functools

import jax
import jax.numpy as jnp
from jax import lax
from jax.experimental import pallas as pl
from jax.experimental.pallas import tpu as pltpu
from jax.sharding import PartitionSpec as P

MIB = 1 << 20


def dot(a, b, contract):
    return lax.dot_general(a, b, ((contract[:1], contract[1:]), ((), ())), preferred_element_type=jnp.float32)


def halves(value):
    high_part = value.astype(jnp.bfloat16)
    low_part = (value - high_part.astype(jnp.float32)).astype(jnp.bfloat16)
    return high_part, low_part


def left_stack(value):
    high_part, low_part = halves(value)
    return jnp.concatenate([high_part, high_part, low_part], axis=1)


def right_stack(value):
    high_part, low_part = halves(value)
    return jnp.concatenate([high_part, low_part, high_part], axis=1)


def swap(value, axis, mask):
    count = lax.axis_size(axis)
    return lax.ppermute(value, axis, [(i, i ^ mask) for i in range(count)])


def blocks_per_step(nblocks, most):
    return max(size for size in range(1, most + 1) if nblocks % size == 0)


def below_pairs(levels, first=0):
    return [(level, below) for level in range(levels) for below in range(first, level)]


def gram_kernel(levels, per_step, width, right_ref, left_ref, flip_ref, keep_ref, send_ref,
                right_buf, left_buf, gram_ref, sems):
    rank = right_ref.shape[2]
    half = rank // 2
    tile = per_step * width
    steps = right_ref.shape[1] // tile

    def copies(step):
        rows = pl.ds(pl.multiple_of(step * tile, tile), tile)
        return (
            pltpu.make_async_copy(right_ref.at[:, rows], right_buf.at[:, rows], sems.at[0, step]),
            pltpu.make_async_copy(left_ref.at[:levels - 1, rows], left_buf.at[:, rows], sems.at[1, step]),
        )

    for step in range(steps):
        for copy in copies(step):
            copy.start()
    gram_ref[...] = jnp.zeros_like(gram_ref)

    def body(step, _):
        for copy in copies(step):
            copy.wait()
        rows = pl.ds(pl.multiple_of(step * tile, tile), tile)
        right = jnp.concatenate([right_buf[l, rows, :] for l in range(levels)], axis=1).T
        flip_ref[:, rows] = right
        left = jnp.concatenate([left_buf[l, rows, :] for l in range(levels - 1)], axis=1)
        gram_ref[...] += dot(right[rank:], left, (1, 0))
        return 0

    lax.fori_loop(0, steps, body, 0)
    core = lax.axis_index("rows") % 2
    for spot, (level, below) in enumerate(below_pairs(levels)):
        lanes = pl.ds(spot * rank, rank)
        for ref, side in ((keep_ref, core), (send_ref, 1 - core)):
            rows = pl.ds(pl.multiple_of((level - 1) * rank + side * half, half), half)
            ref[:, lanes] = gram_ref[rows, pl.ds(below * rank, rank)]


def permute_kernel(per_step, width, order_ref, inv_ref, moved_ref):
    place = lax.broadcasted_iota(jnp.int32, (width, width), 0)

    def body(step, _):
        for b in range(per_step):
            block = step * per_step + b
            chosen = (place == order_ref[pl.ds(block, 1), :]).astype(jnp.float32).astype(jnp.bfloat16)
            moved_ref[block] = dot(inv_ref[block], chosen, (1, 1)).astype(jnp.bfloat16)
        return 0

    lax.fori_loop(0, inv_ref.shape[0] // per_step, body, 0)


def weigh_kernel(per_step, width, moved_ref, flip_ref, after_ref, factor_ref):
    kinds = flip_ref.shape[0]

    def body(step, _):
        for b in range(per_step):
            block = step * per_step + b
            lanes = pl.ds(pl.multiple_of(block * width, width), width)
            high_part, low_part = halves(dot(flip_ref[:, lanes], moved_ref[block], (1, 0)))
            factor_ref[:kinds, lanes] = high_part
            factor_ref[kinds:, lanes] = low_part
        return 0

    lax.fori_loop(0, moved_ref.shape[0] // per_step, body, 0)


def solve_kernel(per_step, width, moved_ref, rhs_ref, *refs):
    out_ref = refs[-1]

    def body(step, _):
        for b in range(per_step):
            block = step * per_step + b
            rows = pl.ds(pl.multiple_of(block * width, width), width)
            out_ref[rows, :] = dot(moved_ref[block], rhs_ref[rows, :], (1, 0))
        return 0

    lax.fori_loop(0, moved_ref.shape[0] // per_step, body, 0)


def project_kernel(other, factor_ref, rhs_ref, after_ref, out_ref):
    kinds, part = out_ref.shape
    core = lax.axis_index("rows") % 2
    lanes = pl.ds(pl.multiple_of((1 - core if other else core) * part, part), part)
    total = dot(factor_ref[...], rhs_ref[:, lanes], (1, 0))
    out_ref[...] = total[:kinds] + total[kinds:]


def merge_kernel(keep_ref, got_ref, *refs):
    out_refs, flip_ref = refs[:-1], refs[-1]
    share = out_refs[0].shape[0]
    chip = lax.axis_index("rows") // 2
    flip_ref[...] = (keep_ref[...] + got_ref[...]).T
    for slot, out_ref in enumerate(out_refs):
        out_ref[...] = flip_ref[pl.ds(pl.multiple_of((chip ^ slot) * share, share), share), :]


def add_kernel(mine_ref, got_ref, out_ref):
    out_ref[...] = mine_ref[...] + got_ref[...]


def prepare_kernel(levels, joined_ref, perm_ref, after_ref, out_ref, joined_buf, sems):
    rank = perm_ref.shape[1]
    leaves = lax.axis_size("leaf")
    leaf = lax.axis_index("leaf")
    copies = []
    for level in range(levels):
        node = 2 * leaves - 2 * leaves // 2 ** level + leaf // 2 ** level
        copies.append(pltpu.make_async_copy(joined_ref.at[node], joined_buf.at[level], sems.at[level]))
        copies[-1].start()
    spot = lax.broadcasted_iota(jnp.int32, (rank, rank), 0)
    for level in range(levels):
        copies[level].wait()
        chosen = (spot == perm_ref[level:level + 1, :]).astype(jnp.float32).astype(jnp.bfloat16)
        high_part, low_part = halves(joined_buf[level])
        for place, part in enumerate((high_part, low_part)):
            for side in range(2):
                moved = dot(chosen, part[:, side * rank:(side + 1) * rank], (1, 1)).astype(jnp.bfloat16)
                out_ref[level, pl.ds((2 * place + side) * rank, rank), :] = moved
                if place == 0:
                    out_ref[level, pl.ds((4 + side) * rank, rank), :] = moved


def by_side(side, own, other):
    return jnp.where(side == 0, own, other), jnp.where(side == 0, other, own)


def pack_message(message_ref, pieces):
    row = 0
    for piece in pieces:
        message_ref[pl.ds(row, piece.shape[0]), :] = piece
        row += piece.shape[0]


def node_kernel(rank, slots, after_ref, *refs):
    part_refs = refs[:slots]
    joined_ref, own_ref, other_ref, rest_ref = refs[slots:]
    side = lax.axis_index("rows") // slots
    half = slots // 2
    sums = [sum(ref[...] for ref in part_refs[:half]), sum(ref[...] for ref in part_refs[half:])]
    picked = jnp.concatenate(by_side(side, sums[0][:, :rank], sums[1][:, :rank]), axis=1)
    coef = dot(left_stack(picked), joined_ref[0], (1, 0))
    own_ref[...], other_ref[...] = by_side(side, coef[:, :rank], coef[:, rank:])
    rest_ref[...] = (sums[0] + sums[1])[:, rank:]


def correct_kernel(levels, rank, own_ref, other_ref, rest_ref, mine_ref, theirs_ref, pair_mine_ref,
                   pair_theirs_ref, message_ref):
    core = lax.axis_index("rows") % 2
    grams = [jnp.concatenate(by_side(core, mine_ref[...], pair_mine_ref[...]), axis=0),
             jnp.concatenate(by_side(core, theirs_ref[...], pair_theirs_ref[...]), axis=0)]
    pairs = below_pairs(levels)
    lanes = {pair: slice(spot * rank, (spot + 1) * rank) for spot, pair in enumerate(pairs)}
    joint = jnp.concatenate(
        [jnp.concatenate([gram[:, lanes[level, 0]] for gram in grams], axis=1) for level in range(1, levels)], axis=0)
    pair = jnp.concatenate([own_ref[...], other_ref[...]], axis=1)
    rest = rest_ref[...] - dot(left_stack(pair), right_stack(joint), (1, 1))
    pieces = [rest[:, level * rank:(level + 1) * rank] for level in range(levels - 1)]
    for pair in pairs:
        if pair[1] > 0:
            pieces.append(grams[0][:, lanes[pair]] + grams[1][:, lanes[pair]])
    pack_message(message_ref, pieces)


def level_kernel(levels, level, share, sent_ref, got_ref, joined_ref, after_ref, coef_ref, *message_ref):
    rank = sent_ref.shape[1]
    side = lax.axis_index("leaf") // 2 ** (level - 1) % 2
    more = levels - level
    values = []
    for ref in (sent_ref, got_ref):
        values.append([ref[pl.ds(i * share, share), :] for i in range(more)])
    picked = jnp.concatenate(by_side(side, values[0][0], values[1][0]), axis=1)
    coef = dot(left_stack(picked), joined_ref[level], (1, 0))
    sides = by_side(side, coef[:, :rank], coef[:, rank:])
    coef_ref[...] = sides[0]
    if not message_ref:
        return
    pairs = below_pairs(levels, level)
    grams = []
    for ref in (sent_ref, got_ref):
        grams.append({pair: ref[pl.ds(more * share + spot * rank, rank), :] for spot, pair in enumerate(pairs)})
    uppers = list(range(level + 1, levels))
    joint = jnp.concatenate(
        [jnp.concatenate([gram[upper, level] for gram in grams], axis=1) for upper in uppers], axis=0)
    change = dot(left_stack(jnp.concatenate(sides, axis=1)), right_stack(joint), (1, 1))
    pieces = [values[0][upper - level] + values[1][upper - level] - change[:, i * rank:(i + 1) * rank]
              for i, upper in enumerate(uppers)]
    for pair in pairs:
        if pair[1] > level:
            pieces.append(grams[0][pair] + grams[1][pair])
    pack_message(message_ref[0], pieces)


def pack_kernel(*refs):
    refs[-1][...] = jnp.concatenate([ref[...] for ref in refs[:-1]], axis=1)


def stack_kernel(after_ref, *refs):
    for slot, ref in enumerate(refs[:-1]):
        refs[-1][slot] = ref[...]


def join_kernel(after_ref, *refs):
    refs[-1][...] = jnp.concatenate([ref[...] for ref in refs[:-1]], axis=1)


def relay_kernel(after_ref, ref, out_ref):
    out_ref[...] = ref[...]


def split_factor(pieces, flip_ref, factor_ref):
    share, kinds = pieces[0].shape
    slots = len(pieces) // 2
    me = lax.axis_index("rows")
    for mask, ref in enumerate(pieces):
        owner = me ^ mask
        row = (owner % 2 * slots + owner // 2) * share
        flip_ref[pl.ds(pl.multiple_of(row, share), share), :] = ref[...]
    high_part, low_part = halves(flip_ref[...].T)
    factor_ref[:kinds, :] = high_part
    factor_ref[kinds:, :] = low_part


def apply_kernel(tile, own_ref, pair_ref, first_ref, left_ref, after_ref, out_ref, flip_ref, factor_ref):
    pieces = [ref.at[slot] for slot in range(own_ref.shape[0]) for ref in (own_ref, pair_ref)]
    split_factor(pieces, flip_ref, factor_ref)
    for row in range(0, out_ref.shape[0], tile):
        rows = pl.ds(row, tile)
        left = jnp.concatenate([left_ref[0, rows, :]] * 2, axis=1)
        out_ref[rows, :] = first_ref[rows, :] - dot(left, factor_ref[...], (1, 0))


def expand_kernel(levels, tile, count, *refs):
    piece_refs = refs[:count]
    first_ref, left_ref, out_ref, flip_ref, factor_ref, out_buf, sems = refs[count:]
    split_factor(piece_refs, flip_ref, factor_ref)
    copies = []
    for step in range(out_buf.shape[0] // tile):
        rows = pl.ds(step * tile, tile)
        left = jnp.concatenate([left_ref[l, rows, :] for l in range(1, levels)] * 2, axis=1)
        out_buf[rows, :] = first_ref[rows, :] - dot(left, factor_ref[...], (1, 0))
        copies.append(pltpu.make_async_copy(out_buf.at[rows], out_ref.at[rows], sems.at[step]))
        copies[-1].start(priority=step % 2)
    for copy in copies:
        copy.wait()


def settings(mib, micros):
    return dict(
        compiler_params=pltpu.CompilerParams(vmem_limit_bytes=mib * MIB),
        cost_estimate=pl.CostEstimate(flops=int(micros * 1.1e9), bytes_accessed=0, transcendentals=0),
    )


def floats(*shape):
    return jax.ShapeDtypeStruct(shape, jnp.float32)


def per_device(rhs, leaf_order, leaf_inv, right_basis, left_basis, rank_perm, joined):
    levels, rows, rank = right_basis.shape
    nblocks, width, _ = leaf_inv.shape
    columns = rhs.shape[1]
    leaves = lax.axis_size("leaf")
    count = lax.axis_size("rows")
    slots = count // 2
    kinds = levels * rank
    size = kinds - rank
    share = columns // count
    gram_lanes = len(below_pairs(levels)) * rank

    per_step = blocks_per_step(nblocks, 3)
    flipped, gram_keep, gram_send = pl.pallas_call(
        functools.partial(gram_kernel, levels, per_step, width),
        in_specs=[pl.BlockSpec(memory_space=pltpu.HBM)] * 2,
        out_shape=[jax.ShapeDtypeStruct((kinds, rows), jnp.bfloat16)] + [floats(rank // 2, gram_lanes)] * 2,
        scratch_shapes=[
            pltpu.VMEM((levels, rows, rank), jnp.bfloat16),
            pltpu.VMEM((levels - 1, rows, rank), jnp.bfloat16),
            pltpu.VMEM((size, size), jnp.float32),
            pltpu.SemaphoreType.DMA((2, nblocks // per_step)),
        ],
        name="gram",
        **settings(24, 3),
    )(pltpu.with_memory_space_constraint(right_basis, pltpu.HBM),
      pltpu.with_memory_space_constraint(left_basis, pltpu.HBM))

    gram_got = swap(gram_send, "rows", 1)
    moved = pl.pallas_call(
        functools.partial(permute_kernel, nblocks, width),
        out_shape=jax.ShapeDtypeStruct((nblocks, width, width), jnp.bfloat16),
        name="permute",
        **settings(8, 1.5),
    )(leaf_order, leaf_inv)

    def add(mine, got):
        return pl.pallas_call(
            add_kernel, out_shape=floats(*mine.shape), name="add", **settings(8, 0.1),
        )(mine, got)

    gram = add(gram_keep, gram_got)
    factors = pl.pallas_call(
        functools.partial(weigh_kernel, nblocks, width),
        out_shape=jax.ShapeDtypeStruct((2 * kinds, rows), jnp.bfloat16),
        name="weigh",
        **settings(8, 2.4),
    )(moved, flipped, gram)

    def project(other, after):
        return pl.pallas_call(
            functools.partial(project_kernel, other),
            out_shape=floats(kinds, columns // 2),
            name="project_other" if other else "project_own",
            **settings(12, 1 if other else 4),
        )(factors, rhs, after)

    send = project(True, gram)
    got = swap(send, "rows", 1)
    mask = 2
    while mask < slots:
        gram = add(gram, swap(gram, "rows", mask))
        mask *= 2
    keep = project(False, gram)
    merged = pl.pallas_call(
        merge_kernel,
        out_shape=[floats(share, kinds)] * slots,
        scratch_shapes=[pltpu.VMEM((columns // 2, kinds), jnp.float32)],
        name="merge",
        **settings(8, 0.4),
    )(keep, got)
    parts = [merged[0]] + [swap(merged[s], "rows", 2 * s) for s in range(1, slots)]
    gram_other = swap(gram, "rows", slots)
    prepared = pl.pallas_call(
        functools.partial(prepare_kernel, levels),
        in_specs=[pl.BlockSpec(memory_space=pltpu.HBM), pl.BlockSpec(), pl.BlockSpec()],
        out_shape=jax.ShapeDtypeStruct((levels, 6 * rank, 2 * rank), jnp.bfloat16),
        scratch_shapes=[pltpu.VMEM((levels, 2 * rank, 2 * rank), jnp.float32), pltpu.SemaphoreType.DMA((levels,))],
        name="prepare",
        **settings(8, 0.5),
    )(pltpu.with_memory_space_constraint(joined, pltpu.HBM), rank_perm, merged[0])

    def message_shape(level):
        return floats((levels - level) * share + len(below_pairs(levels, level)) * rank, rank)

    gram_other = pl.pallas_call(
        relay_kernel, out_shape=floats(*gram.shape), name="relay", **settings(8, 0.1),
    )(prepared, gram_other)
    grams = [gram, gram_other, swap(gram, "rows", 1), swap(gram_other, "rows", 1)]
    first = pl.pallas_call(
        functools.partial(solve_kernel, per_step, width),
        out_shape=floats(rows, columns),
        name="solve",
        **settings(8, 0.1),
    )(moved, rhs, merged[0])

    own, other, rest = pl.pallas_call(
        functools.partial(node_kernel, rank, slots),
        out_shape=[floats(share, rank)] * 2 + [floats(share, size)],
        name="node",
        **settings(8, 1),
    )(first, *parts, prepared)
    message = pl.pallas_call(
        functools.partial(correct_kernel, levels, rank),
        out_shape=message_shape(1),
        name="correct",
        **settings(8, 1),
    )(own, other, rest, *grams)
    early = [own] + [swap(own if slot < slots // 2 else other, "rows", 2 * slot) for slot in range(1, slots)]
    coefs = []
    for level in range(1, levels):
        last = level + 1 == levels
        arrived = swap(message, "leaf", 2 ** (level - 1))
        outs = pl.pallas_call(
            functools.partial(level_kernel, levels, level, share),
            out_shape=[floats(share, rank)] + ([] if last else [message_shape(level + 1)]),
            name=f"level{level}",
            **settings(8, 1 if last else 6),
        )(message, arrived, prepared, arrived)
        coefs.append(outs[0])
        message = outs[-1]
    packed = coefs[0] if levels == 3 else jnp.concatenate(coefs[:-1], axis=1)
    ahead = swap(packed, "rows", 2 * (slots - 1))
    stack = pl.pallas_call(
        stack_kernel, out_shape=floats(slots, share, rank), name="stack", **settings(8, 0.1),
    )(first, *early)
    second = pl.pallas_call(
        functools.partial(apply_kernel, per_step * width),
        out_shape=floats(rows, columns),
        scratch_shapes=[
            pltpu.VMEM((columns, rank), jnp.float32),
            pltpu.VMEM((2 * rank, columns), jnp.bfloat16),
        ],
        name="apply",
        **settings(8, 1.8),
    )(stack, swap(stack, "rows", 1), first, left_basis, ahead)

    pack = pl.pallas_call(
        pack_kernel, out_shape=floats(share, size), name="pack", **settings(8, 0.1),
    )(*coefs)
    pieces = []
    for slot in range(slots):
        piece = swap(pack, "rows", 2 * slot) if slot > 0 else pack
        if slot == slots - 1:
            tail = swap(coefs[-1], "rows", 2 * slot)
            piece = pl.pallas_call(
                join_kernel, out_shape=floats(share, size), name="join", **settings(8, 0.1),
            )(second, ahead, tail)
        elif slot == 0:
            piece = pl.pallas_call(
                relay_kernel, out_shape=floats(share, size), name="relay", **settings(8, 0.1),
            )(second, piece)
        pieces += [piece, swap(piece, "rows", 1)]
    return pl.pallas_call(
        functools.partial(expand_kernel, levels, width, count),
        out_specs=pl.BlockSpec(memory_space=pl.ANY),
        out_shape=floats(rows, columns),
        scratch_shapes=[
            pltpu.VMEM((columns, size), jnp.float32),
            pltpu.VMEM((2 * size, columns), jnp.bfloat16),
            pltpu.VMEM((rows, columns), jnp.float32),
            pltpu.SemaphoreType.DMA((nblocks,)),
        ],
        name="expand",
        **settings(16, 5),
    )(*pieces, second, left_basis)


def solution(mesh):
    return jax.shard_map(
        per_device,
        mesh=mesh,
        in_specs=(
            P(("leaf", "rows"), None),
            P(("leaf", "rows"), None),
            P(("leaf", "rows"), None, None),
            P(None, ("leaf", "rows"), None),
            P(None, ("leaf", "rows"), None),
            P(),
            P(),
        ),
        out_specs=P(("leaf", "rows"), None),
        check_vma=False,
    )
```

```python
import functools

import jax
import jax.numpy as jnp
from jax import lax
from jax.experimental import pallas as pl
from jax.experimental.pallas import tpu as pltpu
from jax.sharding import PartitionSpec as P

MIB = 1 << 20


def dot(a, b, contract):
    return lax.dot_general(a, b, ((contract[:1], contract[1:]), ((), ())), preferred_element_type=jnp.float32)


def halves(value):
    high_part = value.astype(jnp.bfloat16)
    low_part = (value - high_part.astype(jnp.float32)).astype(jnp.bfloat16)
    return high_part, low_part


def left_stack(value):
    high_part, low_part = halves(value)
    return jnp.concatenate([high_part, high_part, low_part], axis=1)


def right_stack(value):
    high_part, low_part = halves(value)
    return jnp.concatenate([high_part, low_part, high_part], axis=1)


def swap(value, axis, mask):
    count = lax.axis_size(axis)
    return lax.ppermute(value, axis, [(i, i ^ mask) for i in range(count)])


def blocks_per_step(nblocks, most):
    return max(size for size in range(1, most + 1) if nblocks % size == 0)


def below_pairs(levels, first=0):
    return [(level, below) for level in range(levels) for below in range(first, level)]


def gram_kernel(levels, per_step, width, right_ref, left_ref, flip_ref, keep_ref, send_ref,
                right_buf, left_buf, gram_ref, sems):
    rank = right_ref.shape[2]
    half = rank // 2
    tile = per_step * width
    steps = right_ref.shape[1] // tile

    def copies(step):
        rows = pl.ds(pl.multiple_of(step * tile, tile), tile)
        return (
            pltpu.make_async_copy(right_ref.at[:, rows], right_buf.at[:, rows], sems.at[0, step]),
            pltpu.make_async_copy(left_ref.at[:levels - 1, rows], left_buf.at[:, rows], sems.at[1, step]),
        )

    for step in range(steps):
        for copy in copies(step):
            copy.start()
    gram_ref[...] = jnp.zeros_like(gram_ref)

    def body(step, _):
        for copy in copies(step):
            copy.wait()
        rows = pl.ds(pl.multiple_of(step * tile, tile), tile)
        right = jnp.concatenate([right_buf[l, rows, :] for l in range(levels)], axis=1).T
        flip_ref[:, rows] = right
        left = jnp.concatenate([left_buf[l, rows, :] for l in range(levels - 1)], axis=1)
        gram_ref[...] += dot(right[rank:], left, (1, 0))
        return 0

    lax.fori_loop(0, steps, body, 0)
    core = lax.axis_index("rows") % 2
    for spot, (level, below) in enumerate(below_pairs(levels)):
        lanes = pl.ds(spot * rank, rank)
        for ref, side in ((keep_ref, core), (send_ref, 1 - core)):
            rows = pl.ds(pl.multiple_of((level - 1) * rank + side * half, half), half)
            ref[:, lanes] = gram_ref[rows, pl.ds(below * rank, rank)]


def permute_kernel(per_step, width, order_ref, inv_ref, moved_ref):
    place = lax.broadcasted_iota(jnp.int32, (width, width), 0)

    def body(step, _):
        for b in range(per_step):
            block = step * per_step + b
            chosen = (place == order_ref[pl.ds(block, 1), :]).astype(jnp.float32).astype(jnp.bfloat16)
            moved_ref[block] = dot(inv_ref[block], chosen, (1, 1)).astype(jnp.bfloat16)
        return 0

    lax.fori_loop(0, inv_ref.shape[0] // per_step, body, 0)


def weigh_kernel(per_step, width, moved_ref, flip_ref, after_ref, factor_ref):
    kinds = flip_ref.shape[0]

    def body(step, _):
        for b in range(per_step):
            block = step * per_step + b
            lanes = pl.ds(pl.multiple_of(block * width, width), width)
            high_part, low_part = halves(dot(flip_ref[:, lanes], moved_ref[block], (1, 0)))
            factor_ref[:kinds, lanes] = high_part
            factor_ref[kinds:, lanes] = low_part
        return 0

    lax.fori_loop(0, moved_ref.shape[0] // per_step, body, 0)


def solve_kernel(per_step, width, moved_ref, rhs_ref, *refs):
    out_ref = refs[-1]

    def body(step, _):
        for b in range(per_step):
            block = step * per_step + b
            rows = pl.ds(pl.multiple_of(block * width, width), width)
            out_ref[rows, :] = dot(moved_ref[block], rhs_ref[rows, :], (1, 0))
        return 0

    lax.fori_loop(0, moved_ref.shape[0] // per_step, body, 0)


def project_kernel(other, factor_ref, rhs_ref, after_ref, out_ref):
    kinds, part = out_ref.shape
    core = lax.axis_index("rows") % 2
    lanes = pl.ds(pl.multiple_of((1 - core if other else core) * part, part), part)
    total = dot(factor_ref[...], rhs_ref[:, lanes], (1, 0))
    out_ref[...] = total[:kinds] + total[kinds:]


def merge_kernel(keep_ref, got_ref, *refs):
    out_refs, flip_ref = refs[:-1], refs[-1]
    share = out_refs[0].shape[0]
    chip = lax.axis_index("rows") // 2
    flip_ref[...] = (keep_ref[...] + got_ref[...]).T
    for slot, out_ref in enumerate(out_refs):
        out_ref[...] = flip_ref[pl.ds(pl.multiple_of((chip ^ slot) * share, share), share), :]


def add_kernel(mine_ref, got_ref, out_ref):
    out_ref[...] = mine_ref[...] + got_ref[...]


def prepare_kernel(levels, joined_ref, perm_ref, out_ref, joined_buf, sems):
    rank = perm_ref.shape[1]
    leaves = lax.axis_size("leaf")
    leaf = lax.axis_index("leaf")
    copies = []
    for level in range(levels):
        node = 2 * leaves - 2 * leaves // 2 ** level + leaf // 2 ** level
        copies.append(pltpu.make_async_copy(joined_ref.at[node], joined_buf.at[level], sems.at[level]))
        copies[-1].start()
    spot = lax.broadcasted_iota(jnp.int32, (rank, rank), 0)
    for level in range(levels):
        copies[level].wait()
        chosen = (spot == perm_ref[level:level + 1, :]).astype(jnp.float32).astype(jnp.bfloat16)
        high_part, low_part = halves(joined_buf[level])
        for place, part in enumerate((high_part, low_part, high_part)):
            for side in range(2):
                moved = dot(chosen, part[:, side * rank:(side + 1) * rank], (1, 1)).astype(jnp.bfloat16)
                out_ref[level, pl.ds((2 * place + side) * rank, rank), :] = moved


def by_side(side, own, other):
    return jnp.where(side == 0, own, other), jnp.where(side == 0, other, own)


def pack_message(message_ref, pieces):
    row = 0
    for piece in pieces:
        message_ref[pl.ds(row, piece.shape[0]), :] = piece
        row += piece.shape[0]


def node_kernel(rank, slots, *refs):
    part_refs = refs[:slots]
    joined_ref, own_ref, other_ref, rest_ref = refs[slots:]
    side = lax.axis_index("rows") // slots
    half = slots // 2
    sums = [sum(ref[...] for ref in part_refs[:half]), sum(ref[...] for ref in part_refs[half:])]
    picked = jnp.concatenate(by_side(side, sums[0][:, :rank], sums[1][:, :rank]), axis=1)
    coef = dot(left_stack(picked), joined_ref[0], (1, 0))
    own_ref[...], other_ref[...] = by_side(side, coef[:, :rank], coef[:, rank:])
    rest_ref[...] = (sums[0] + sums[1])[:, rank:]


def correct_kernel(levels, rank, own_ref, other_ref, rest_ref, mine_ref, theirs_ref, pair_mine_ref,
                   pair_theirs_ref, message_ref):
    core = lax.axis_index("rows") % 2
    grams = [jnp.concatenate(by_side(core, mine_ref[...], pair_mine_ref[...]), axis=0),
             jnp.concatenate(by_side(core, theirs_ref[...], pair_theirs_ref[...]), axis=0)]
    pairs = below_pairs(levels)
    lanes = {pair: slice(spot * rank, (spot + 1) * rank) for spot, pair in enumerate(pairs)}
    joint = jnp.concatenate(
        [jnp.concatenate([gram[:, lanes[level, 0]] for gram in grams], axis=1) for level in range(1, levels)], axis=0)
    pair = jnp.concatenate([own_ref[...], other_ref[...]], axis=1)
    rest = rest_ref[...] - dot(left_stack(pair), right_stack(joint), (1, 1))
    pieces = [rest[:, level * rank:(level + 1) * rank] for level in range(levels - 1)]
    for pair in pairs:
        if pair[1] > 0:
            pieces.append(grams[0][:, lanes[pair]] + grams[1][:, lanes[pair]])
    pack_message(message_ref, pieces)


def level_kernel(levels, level, share, sent_ref, got_ref, joined_ref, after_ref, coef_ref, *message_ref):
    rank = sent_ref.shape[1]
    side = lax.axis_index("leaf") // 2 ** (level - 1) % 2
    more = levels - level
    values = []
    for ref in (sent_ref, got_ref):
        values.append([ref[pl.ds(i * share, share), :] for i in range(more)])
    picked = jnp.concatenate(by_side(side, values[0][0], values[1][0]), axis=1)
    coef = dot(left_stack(picked), joined_ref[level], (1, 0))
    sides = by_side(side, coef[:, :rank], coef[:, rank:])
    coef_ref[...] = sides[0]
    if not message_ref:
        return
    pairs = below_pairs(levels, level)
    grams = []
    for ref in (sent_ref, got_ref):
        grams.append({pair: ref[pl.ds(more * share + spot * rank, rank), :] for spot, pair in enumerate(pairs)})
    uppers = list(range(level + 1, levels))
    joint = jnp.concatenate(
        [jnp.concatenate([gram[upper, level] for gram in grams], axis=1) for upper in uppers], axis=0)
    change = dot(left_stack(jnp.concatenate(sides, axis=1)), right_stack(joint), (1, 1))
    pieces = [values[0][upper - level] + values[1][upper - level] - change[:, i * rank:(i + 1) * rank]
              for i, upper in enumerate(uppers)]
    for pair in pairs:
        if pair[1] > level:
            pieces.append(grams[0][pair] + grams[1][pair])
    pack_message(message_ref[0], pieces)


def pack_kernel(*refs):
    refs[-1][...] = jnp.concatenate([ref[...] for ref in refs[:-1]], axis=1)


def stack_kernel(after_ref, *refs):
    for slot, ref in enumerate(refs[:-1]):
        refs[-1][slot] = ref[...]


def relay_kernel(after_ref, ref, out_ref):
    out_ref[...] = ref[...]


def split_factor(pieces, flip_ref, factor_ref):
    share, kinds = pieces[0].shape
    slots = len(pieces) // 2
    me = lax.axis_index("rows")
    for mask, ref in enumerate(pieces):
        owner = me ^ mask
        row = (owner % 2 * slots + owner // 2) * share
        flip_ref[pl.ds(pl.multiple_of(row, share), share), :] = ref[...]
    high_part, low_part = halves(flip_ref[...].T)
    factor_ref[:kinds, :] = high_part
    factor_ref[kinds:, :] = low_part


def apply_kernel(tile, own_ref, pair_ref, first_ref, left_ref, out_ref, flip_ref, factor_ref):
    pieces = [ref.at[slot] for slot in range(own_ref.shape[0]) for ref in (own_ref, pair_ref)]
    split_factor(pieces, flip_ref, factor_ref)
    for row in range(0, out_ref.shape[0], tile):
        rows = pl.ds(row, tile)
        left = jnp.concatenate([left_ref[0, rows, :]] * 2, axis=1)
        out_ref[rows, :] = first_ref[rows, :] - dot(left, factor_ref[...], (1, 0))


def expand_kernel(levels, tile, count, *refs):
    piece_refs = refs[:count]
    first_ref, left_ref, out_ref, flip_ref, factor_ref, out_buf, sems = refs[count:]
    split_factor(piece_refs, flip_ref, factor_ref)
    copies = []
    for step in range(out_buf.shape[0] // tile):
        rows = pl.ds(step * tile, tile)
        left = jnp.concatenate([left_ref[l, rows, :] for l in range(1, levels)] * 2, axis=1)
        out_buf[rows, :] = first_ref[rows, :] - dot(left, factor_ref[...], (1, 0))
        copies.append(pltpu.make_async_copy(out_buf.at[rows], out_ref.at[rows], sems.at[step]))
        copies[-1].start(priority=step % 2)
    for copy in copies:
        copy.wait()


def settings(mib, micros):
    return dict(
        compiler_params=pltpu.CompilerParams(vmem_limit_bytes=mib * MIB),
        cost_estimate=pl.CostEstimate(flops=int(micros * 1.1e9), bytes_accessed=0, transcendentals=0),
    )


def floats(*shape):
    return jax.ShapeDtypeStruct(shape, jnp.float32)


def per_device(rhs, leaf_order, leaf_inv, right_basis, left_basis, rank_perm, joined):
    levels, rows, rank = right_basis.shape
    nblocks, width, _ = leaf_inv.shape
    columns = rhs.shape[1]
    leaves = lax.axis_size("leaf")
    count = lax.axis_size("rows")
    slots = count // 2
    kinds = levels * rank
    size = kinds - rank
    share = columns // count
    gram_lanes = len(below_pairs(levels)) * rank

    per_step = blocks_per_step(nblocks, 3)
    flipped, gram_keep, gram_send = pl.pallas_call(
        functools.partial(gram_kernel, levels, per_step, width),
        in_specs=[pl.BlockSpec(memory_space=pltpu.HBM)] * 2,
        out_shape=[jax.ShapeDtypeStruct((kinds, rows), jnp.bfloat16)] + [floats(rank // 2, gram_lanes)] * 2,
        scratch_shapes=[
            pltpu.VMEM((levels, rows, rank), jnp.bfloat16),
            pltpu.VMEM((levels - 1, rows, rank), jnp.bfloat16),
            pltpu.VMEM((size, size), jnp.float32),
            pltpu.SemaphoreType.DMA((2, nblocks // per_step)),
        ],
        name="gram",
        **settings(24, 3),
    )(pltpu.with_memory_space_constraint(right_basis, pltpu.HBM),
      pltpu.with_memory_space_constraint(left_basis, pltpu.HBM))

    gram_got = swap(gram_send, "rows", 1)
    moved = pl.pallas_call(
        functools.partial(permute_kernel, nblocks, width),
        out_shape=jax.ShapeDtypeStruct((nblocks, width, width), jnp.bfloat16),
        name="permute",
        **settings(8, 1.5),
    )(leaf_order, leaf_inv)

    def add(mine, got):
        return pl.pallas_call(
            add_kernel, out_shape=floats(*mine.shape), name="add", **settings(8, 0.1),
        )(mine, got)

    gram = add(gram_keep, gram_got)
    factors = pl.pallas_call(
        functools.partial(weigh_kernel, nblocks, width),
        out_shape=jax.ShapeDtypeStruct((2 * kinds, rows), jnp.bfloat16),
        name="weigh",
        **settings(8, 2.4),
    )(moved, flipped, gram)

    def project(other, after):
        return pl.pallas_call(
            functools.partial(project_kernel, other),
            out_shape=floats(kinds, columns // 2),
            name="project_other" if other else "project_own",
            **settings(12, 1 if other else 4),
        )(factors, rhs, after)

    send = project(True, gram)
    got = swap(send, "rows", 1)
    mask = 2
    while mask < slots:
        gram = add(gram, swap(gram, "rows", mask))
        mask *= 2
    keep = project(False, gram)
    merged = pl.pallas_call(
        merge_kernel,
        out_shape=[floats(share, kinds)] * slots,
        scratch_shapes=[pltpu.VMEM((columns // 2, kinds), jnp.float32)],
        name="merge",
        **settings(8, 0.4),
    )(keep, got)
    parts = [merged[0]] + [swap(merged[s], "rows", 2 * s) for s in range(1, slots)]
    gram_other = swap(gram, "rows", slots)
    grams = [gram, gram_other, swap(gram, "rows", 1), swap(gram_other, "rows", 1)]
    prepared = pl.pallas_call(
        functools.partial(prepare_kernel, levels),
        in_specs=[pl.BlockSpec(memory_space=pltpu.HBM), pl.BlockSpec()],
        out_shape=jax.ShapeDtypeStruct((levels, 6 * rank, 2 * rank), jnp.bfloat16),
        scratch_shapes=[pltpu.VMEM((levels, 2 * rank, 2 * rank), jnp.float32), pltpu.SemaphoreType.DMA((levels,))],
        name="prepare",
        **settings(8, 2),
    )(pltpu.with_memory_space_constraint(joined, pltpu.HBM), rank_perm)

    def message_shape(level):
        return floats((levels - level) * share + len(below_pairs(levels, level)) * rank, rank)

    own, other, rest = pl.pallas_call(
        functools.partial(node_kernel, rank, slots),
        out_shape=[floats(share, rank)] * 2 + [floats(share, size)],
        name="node",
        **settings(8, 1),
    )(*parts, prepared)
    message = pl.pallas_call(
        functools.partial(correct_kernel, levels, rank),
        out_shape=message_shape(1),
        name="correct",
        **settings(8, 1),
    )(own, other, rest, *grams)
    early = [own] + [swap(own if slot < slots // 2 else other, "rows", 2 * slot) for slot in range(1, slots)]
    first = pl.pallas_call(
        functools.partial(solve_kernel, per_step, width),
        out_shape=floats(rows, columns),
        name="solve",
        **settings(8, 8),
    )(moved, rhs, merged[0])

    coefs = []
    for level in range(1, levels):
        last = level + 1 == levels
        arrived = swap(message, "leaf", 2 ** (level - 1))
        outs = pl.pallas_call(
            functools.partial(level_kernel, levels, level, share),
            out_shape=[floats(share, rank)] + ([] if last else [message_shape(level + 1)]),
            name=f"level{level}",
            **settings(8, 1 if last else 6),
        )(message, arrived, prepared, first if last else arrived)
        coefs.append(outs[0])
        message = outs[-1]
    stack = pl.pallas_call(
        stack_kernel, out_shape=floats(slots, share, rank), name="stack", **settings(8, 0.1),
    )(first, *early)
    second = pl.pallas_call(
        functools.partial(apply_kernel, per_step * width),
        out_shape=floats(rows, columns),
        scratch_shapes=[
            pltpu.VMEM((columns, rank), jnp.float32),
            pltpu.VMEM((2 * rank, columns), jnp.bfloat16),
        ],
        name="apply",
        **settings(8, 1.8),
    )(stack, swap(stack, "rows", 1), first, left_basis)

    pack = pl.pallas_call(
        pack_kernel, out_shape=floats(share, size), name="pack", **settings(8, 0.1),
    )(*coefs)
    pieces = []
    for slot in range(slots):
        piece = swap(pack, "rows", 2 * slot) if slot > 0 else pack
        if slot in (0, slots - 1):
            piece = pl.pallas_call(
                relay_kernel, out_shape=floats(share, size), name="relay", **settings(8, 0.1),
            )(second, piece)
        pieces += [piece, swap(piece, "rows", 1)]
    return pl.pallas_call(
        functools.partial(expand_kernel, levels, width, count),
        out_specs=pl.BlockSpec(memory_space=pl.ANY),
        out_shape=floats(rows, columns),
        scratch_shapes=[
            pltpu.VMEM((columns, size), jnp.float32),
            pltpu.VMEM((2 * size, columns), jnp.bfloat16),
            pltpu.VMEM((rows, columns), jnp.float32),
            pltpu.SemaphoreType.DMA((nblocks,)),
        ],
        name="expand",
        **settings(16, 5),
    )(*pieces, second, left_basis)


def solution(mesh):
    return jax.shard_map(
        per_device,
        mesh=mesh,
        in_specs=(
            P(("leaf", "rows"), None),
            P(("leaf", "rows"), None),
            P(("leaf", "rows"), None, None),
            P(None, ("leaf", "rows"), None),
            P(None, ("leaf", "rows"), None),
            P(),
            P(),
        ),
        out_specs=P(("leaf", "rows"), None),
        check_vma=False,
    )
```

```python
import functools

import jax
import jax.numpy as jnp
from jax import lax
from jax.experimental import pallas as pl
from jax.experimental.pallas import tpu as pltpu
from jax.sharding import PartitionSpec as P

MIB = 1 << 20


def dot(a, b, contract):
    return lax.dot_general(a, b, ((contract[:1], contract[1:]), ((), ())), preferred_element_type=jnp.float32)


def halves(value):
    high_part = value.astype(jnp.bfloat16)
    low_part = (value - high_part.astype(jnp.float32)).astype(jnp.bfloat16)
    return high_part, low_part


def left_stack(value):
    high_part, low_part = halves(value)
    return jnp.concatenate([high_part, high_part, low_part], axis=1)


def right_stack(value):
    high_part, low_part = halves(value)
    return jnp.concatenate([high_part, low_part, high_part], axis=1)


def swap(value, axis, mask):
    count = lax.axis_size(axis)
    return lax.ppermute(value, axis, [(i, i ^ mask) for i in range(count)])


def blocks_per_step(nblocks, most):
    return max(size for size in range(1, most + 1) if nblocks % size == 0)


def below_pairs(levels, first=0):
    return [(level, below) for level in range(levels) for below in range(first, level)]


def gram_kernel(levels, per_step, width, right_ref, left_ref, flip_ref, keep_ref, send_ref,
                right_buf, left_buf, gram_ref, sems):
    rank = right_ref.shape[2]
    half = rank // 2
    tile = per_step * width
    steps = right_ref.shape[1] // tile

    def copies(step):
        rows = pl.ds(pl.multiple_of(step * tile, tile), tile)
        return (
            pltpu.make_async_copy(right_ref.at[:, rows], right_buf.at[:, rows], sems.at[0, step]),
            pltpu.make_async_copy(left_ref.at[:levels - 1, rows], left_buf.at[:, rows], sems.at[1, step]),
        )

    for step in range(steps):
        for copy in copies(step):
            copy.start()
    gram_ref[...] = jnp.zeros_like(gram_ref)

    def body(step, _):
        for copy in copies(step):
            copy.wait()
        rows = pl.ds(pl.multiple_of(step * tile, tile), tile)
        right = jnp.concatenate([right_buf[l, rows, :] for l in range(levels)], axis=1).T
        flip_ref[:, rows] = right
        left = jnp.concatenate([left_buf[l, rows, :] for l in range(levels - 1)], axis=1)
        gram_ref[...] += dot(right[rank:], left, (1, 0))
        return 0

    lax.fori_loop(0, steps, body, 0)
    core = lax.axis_index("rows") % 2
    for spot, (level, below) in enumerate(below_pairs(levels)):
        lanes = pl.ds(spot * rank, rank)
        for ref, side in ((keep_ref, core), (send_ref, 1 - core)):
            rows = pl.ds(pl.multiple_of((level - 1) * rank + side * half, half), half)
            ref[:, lanes] = gram_ref[rows, pl.ds(below * rank, rank)]


def permute_kernel(per_step, width, order_ref, inv_ref, moved_ref):
    place = lax.broadcasted_iota(jnp.int32, (width, width), 0)

    def body(step, _):
        for b in range(per_step):
            block = step * per_step + b
            chosen = (place == order_ref[pl.ds(block, 1), :]).astype(jnp.float32).astype(jnp.bfloat16)
            moved_ref[block] = dot(inv_ref[block], chosen, (1, 1)).astype(jnp.bfloat16)
        return 0

    lax.fori_loop(0, inv_ref.shape[0] // per_step, body, 0)


def weigh_kernel(per_step, width, moved_ref, flip_ref, after_ref, factor_ref):
    kinds = flip_ref.shape[0]

    def body(step, _):
        for b in range(per_step):
            block = step * per_step + b
            lanes = pl.ds(pl.multiple_of(block * width, width), width)
            high_part, low_part = halves(dot(flip_ref[:, lanes], moved_ref[block], (1, 0)))
            factor_ref[:kinds, lanes] = high_part
            factor_ref[kinds:, lanes] = low_part
        return 0

    lax.fori_loop(0, moved_ref.shape[0] // per_step, body, 0)


def solve_kernel(per_step, width, moved_ref, rhs_ref, *refs):
    out_ref = refs[-1]

    def body(step, _):
        for b in range(per_step):
            block = step * per_step + b
            rows = pl.ds(pl.multiple_of(block * width, width), width)
            out_ref[rows, :] = dot(moved_ref[block], rhs_ref[rows, :], (1, 0))
        return 0

    lax.fori_loop(0, moved_ref.shape[0] // per_step, body, 0)


def project_kernel(other, factor_ref, rhs_ref, after_ref, out_ref):
    kinds, part = out_ref.shape
    core = lax.axis_index("rows") % 2
    lanes = pl.ds(pl.multiple_of((1 - core if other else core) * part, part), part)
    total = dot(factor_ref[...], rhs_ref[:, lanes], (1, 0))
    out_ref[...] = total[:kinds] + total[kinds:]


def merge_kernel(keep_ref, got_ref, *refs):
    out_refs, flip_ref = refs[:-1], refs[-1]
    share = out_refs[0].shape[0]
    chip = lax.axis_index("rows") // 2
    flip_ref[...] = (keep_ref[...] + got_ref[...]).T
    for slot, out_ref in enumerate(out_refs):
        out_ref[...] = flip_ref[pl.ds(pl.multiple_of((chip ^ slot) * share, share), share), :]


def add_kernel(mine_ref, got_ref, out_ref):
    out_ref[...] = mine_ref[...] + got_ref[...]


def prepare_kernel(levels, joined_ref, perm_ref, out_ref, joined_buf, sems):
    rank = perm_ref.shape[1]
    leaves = lax.axis_size("leaf")
    leaf = lax.axis_index("leaf")
    copies = []
    for level in range(levels):
        node = 2 * leaves - 2 * leaves // 2 ** level + leaf // 2 ** level
        copies.append(pltpu.make_async_copy(joined_ref.at[node], joined_buf.at[level], sems.at[level]))
        copies[-1].start()
    spot = lax.broadcasted_iota(jnp.int32, (rank, rank), 0)
    for level in range(levels):
        copies[level].wait()
        chosen = (spot == perm_ref[level:level + 1, :]).astype(jnp.float32).astype(jnp.bfloat16)
        high_part, low_part = halves(joined_buf[level])
        for place, part in enumerate((high_part, low_part, high_part)):
            for side in range(2):
                moved = dot(chosen, part[:, side * rank:(side + 1) * rank], (1, 1)).astype(jnp.bfloat16)
                out_ref[level, pl.ds((2 * place + side) * rank, rank), :] = moved


def by_side(side, own, other):
    return jnp.where(side == 0, own, other), jnp.where(side == 0, other, own)


def pack_message(message_ref, pieces):
    row = 0
    for piece in pieces:
        message_ref[pl.ds(row, piece.shape[0]), :] = piece
        row += piece.shape[0]


def node_kernel(rank, slots, *refs):
    part_refs = refs[:slots]
    joined_ref, own_ref, other_ref, rest_ref = refs[slots:]
    side = lax.axis_index("rows") // slots
    half = slots // 2
    sums = [sum(ref[...] for ref in part_refs[:half]), sum(ref[...] for ref in part_refs[half:])]
    picked = jnp.concatenate(by_side(side, sums[0][:, :rank], sums[1][:, :rank]), axis=1)
    coef = dot(left_stack(picked), joined_ref[0], (1, 0))
    own_ref[...], other_ref[...] = by_side(side, coef[:, :rank], coef[:, rank:])
    rest_ref[...] = (sums[0] + sums[1])[:, rank:]


def correct_kernel(levels, rank, own_ref, other_ref, rest_ref, mine_ref, theirs_ref, pair_mine_ref,
                   pair_theirs_ref, message_ref):
    core = lax.axis_index("rows") % 2
    grams = [jnp.concatenate(by_side(core, mine_ref[...], pair_mine_ref[...]), axis=0),
             jnp.concatenate(by_side(core, theirs_ref[...], pair_theirs_ref[...]), axis=0)]
    pairs = below_pairs(levels)
    lanes = {pair: slice(spot * rank, (spot + 1) * rank) for spot, pair in enumerate(pairs)}
    joint = jnp.concatenate(
        [jnp.concatenate([gram[:, lanes[level, 0]] for gram in grams], axis=1) for level in range(1, levels)], axis=0)
    pair = jnp.concatenate([own_ref[...], other_ref[...]], axis=1)
    rest = rest_ref[...] - dot(left_stack(pair), right_stack(joint), (1, 1))
    pieces = [rest[:, level * rank:(level + 1) * rank] for level in range(levels - 1)]
    for pair in pairs:
        if pair[1] > 0:
            pieces.append(grams[0][:, lanes[pair]] + grams[1][:, lanes[pair]])
    pack_message(message_ref, pieces)


def level_kernel(levels, level, share, sent_ref, got_ref, joined_ref, after_ref, coef_ref, *message_ref):
    rank = sent_ref.shape[1]
    side = lax.axis_index("leaf") // 2 ** (level - 1) % 2
    more = levels - level
    values = []
    for ref in (sent_ref, got_ref):
        values.append([ref[pl.ds(i * share, share), :] for i in range(more)])
    picked = jnp.concatenate(by_side(side, values[0][0], values[1][0]), axis=1)
    coef = dot(left_stack(picked), joined_ref[level], (1, 0))
    sides = by_side(side, coef[:, :rank], coef[:, rank:])
    coef_ref[...] = sides[0]
    if not message_ref:
        return
    pairs = below_pairs(levels, level)
    grams = []
    for ref in (sent_ref, got_ref):
        grams.append({pair: ref[pl.ds(more * share + spot * rank, rank), :] for spot, pair in enumerate(pairs)})
    uppers = list(range(level + 1, levels))
    joint = jnp.concatenate(
        [jnp.concatenate([gram[upper, level] for gram in grams], axis=1) for upper in uppers], axis=0)
    change = dot(left_stack(jnp.concatenate(sides, axis=1)), right_stack(joint), (1, 1))
    pieces = [values[0][upper - level] + values[1][upper - level] - change[:, i * rank:(i + 1) * rank]
              for i, upper in enumerate(uppers)]
    for pair in pairs:
        if pair[1] > level:
            pieces.append(grams[0][pair] + grams[1][pair])
    pack_message(message_ref[0], pieces)


def pack_kernel(*refs):
    refs[-1][...] = jnp.concatenate([ref[...] for ref in refs[:-1]], axis=1)


def stack_kernel(after_ref, *refs):
    for slot, ref in enumerate(refs[:-1]):
        refs[-1][slot] = ref[...]


def relay_kernel(after_ref, ref, out_ref):
    out_ref[...] = ref[...]


def split_factor(pieces, flip_ref, factor_ref):
    share, kinds = pieces[0].shape
    slots = len(pieces) // 2
    me = lax.axis_index("rows")
    for mask, ref in enumerate(pieces):
        owner = me ^ mask
        row = (owner % 2 * slots + owner // 2) * share
        flip_ref[pl.ds(pl.multiple_of(row, share), share), :] = ref[...]
    high_part, low_part = halves(flip_ref[...].T)
    factor_ref[:kinds, :] = high_part
    factor_ref[kinds:, :] = low_part


def apply_kernel(tile, own_ref, pair_ref, first_ref, left_ref, out_ref, flip_ref, factor_ref):
    pieces = [ref.at[slot] for slot in range(own_ref.shape[0]) for ref in (own_ref, pair_ref)]
    split_factor(pieces, flip_ref, factor_ref)
    for row in range(0, out_ref.shape[0], tile):
        rows = pl.ds(row, tile)
        left = jnp.concatenate([left_ref[0, rows, :]] * 2, axis=1)
        out_ref[rows, :] = first_ref[rows, :] - dot(left, factor_ref[...], (1, 0))


def expand_kernel(levels, tile, count, *refs):
    piece_refs = refs[:count]
    first_ref, left_ref, out_ref, flip_ref, factor_ref, out_buf, sems = refs[count:]
    split_factor(piece_refs, flip_ref, factor_ref)
    copies = []
    for step in range(out_buf.shape[0] // tile):
        rows = pl.ds(step * tile, tile)
        left = jnp.concatenate([left_ref[l, rows, :] for l in range(1, levels)] * 2, axis=1)
        out_buf[rows, :] = first_ref[rows, :] - dot(left, factor_ref[...], (1, 0))
        copies.append(pltpu.make_async_copy(out_buf.at[rows], out_ref.at[rows], sems.at[step]))
        copies[-1].start(priority=step % 2)
    for copy in copies:
        copy.wait()


def settings(mib, micros):
    return dict(
        compiler_params=pltpu.CompilerParams(vmem_limit_bytes=mib * MIB),
        cost_estimate=pl.CostEstimate(flops=int(micros * 1.1e9), bytes_accessed=0, transcendentals=0),
    )


def floats(*shape):
    return jax.ShapeDtypeStruct(shape, jnp.float32)


def per_device(rhs, leaf_order, leaf_inv, right_basis, left_basis, rank_perm, joined):
    levels, rows, rank = right_basis.shape
    nblocks, width, _ = leaf_inv.shape
    columns = rhs.shape[1]
    leaves = lax.axis_size("leaf")
    count = lax.axis_size("rows")
    slots = count // 2
    kinds = levels * rank
    size = kinds - rank
    share = columns // count
    gram_lanes = len(below_pairs(levels)) * rank

    per_step = blocks_per_step(nblocks, 3)
    chunk = blocks_per_step(nblocks, 2)
    flipped, gram_keep, gram_send = pl.pallas_call(
        functools.partial(gram_kernel, levels, chunk, width),
        in_specs=[pl.BlockSpec(memory_space=pltpu.HBM)] * 2,
        out_shape=[jax.ShapeDtypeStruct((kinds, rows), jnp.bfloat16)] + [floats(rank // 2, gram_lanes)] * 2,
        scratch_shapes=[
            pltpu.VMEM((levels, rows, rank), jnp.bfloat16),
            pltpu.VMEM((levels - 1, rows, rank), jnp.bfloat16),
            pltpu.VMEM((size, size), jnp.float32),
            pltpu.SemaphoreType.DMA((2, nblocks // chunk)),
        ],
        name="gram",
        **settings(24, 3),
    )(pltpu.with_memory_space_constraint(right_basis, pltpu.HBM),
      pltpu.with_memory_space_constraint(left_basis, pltpu.HBM))

    gram_got = swap(gram_send, "rows", 1)
    moved = pl.pallas_call(
        functools.partial(permute_kernel, nblocks, width),
        out_shape=jax.ShapeDtypeStruct((nblocks, width, width), jnp.bfloat16),
        name="permute",
        **settings(8, 1.5),
    )(leaf_order, leaf_inv)

    def add(mine, got):
        return pl.pallas_call(
            add_kernel, out_shape=floats(*mine.shape), name="add", **settings(8, 0.1),
        )(mine, got)

    gram = add(gram_keep, gram_got)
    factors = pl.pallas_call(
        functools.partial(weigh_kernel, nblocks, width),
        out_shape=jax.ShapeDtypeStruct((2 * kinds, rows), jnp.bfloat16),
        name="weigh",
        **settings(8, 2.4),
    )(moved, flipped, gram)

    def project(other, after):
        return pl.pallas_call(
            functools.partial(project_kernel, other),
            out_shape=floats(kinds, columns // 2),
            name="project_other" if other else "project_own",
            **settings(12, 1 if other else 4),
        )(factors, rhs, after)

    send = project(True, gram)
    got = swap(send, "rows", 1)
    mask = 2
    while mask < slots:
        gram = add(gram, swap(gram, "rows", mask))
        mask *= 2
    keep = project(False, gram)
    merged = pl.pallas_call(
        merge_kernel,
        out_shape=[floats(share, kinds)] * slots,
        scratch_shapes=[pltpu.VMEM((columns // 2, kinds), jnp.float32)],
        name="merge",
        **settings(8, 0.4),
    )(keep, got)
    parts = [merged[0]] + [swap(merged[s], "rows", 2 * s) for s in range(1, slots)]
    gram_other = swap(gram, "rows", slots)
    grams = [gram, gram_other, swap(gram, "rows", 1), swap(gram_other, "rows", 1)]
    prepared = pl.pallas_call(
        functools.partial(prepare_kernel, levels),
        in_specs=[pl.BlockSpec(memory_space=pltpu.HBM), pl.BlockSpec()],
        out_shape=jax.ShapeDtypeStruct((levels, 6 * rank, 2 * rank), jnp.bfloat16),
        scratch_shapes=[pltpu.VMEM((levels, 2 * rank, 2 * rank), jnp.float32), pltpu.SemaphoreType.DMA((levels,))],
        name="prepare",
        **settings(8, 2),
    )(pltpu.with_memory_space_constraint(joined, pltpu.HBM), rank_perm)

    def message_shape(level):
        return floats((levels - level) * share + len(below_pairs(levels, level)) * rank, rank)

    own, other, rest = pl.pallas_call(
        functools.partial(node_kernel, rank, slots),
        out_shape=[floats(share, rank)] * 2 + [floats(share, size)],
        name="node",
        **settings(8, 1),
    )(*parts, prepared)
    message = pl.pallas_call(
        functools.partial(correct_kernel, levels, rank),
        out_shape=message_shape(1),
        name="correct",
        **settings(8, 1),
    )(own, other, rest, *grams)
    early = [own] + [swap(own if slot < slots // 2 else other, "rows", 2 * slot) for slot in range(1, slots)]
    first = pl.pallas_call(
        functools.partial(solve_kernel, per_step, width),
        out_shape=floats(rows, columns),
        name="solve",
        **settings(8, 8),
    )(moved, rhs, merged[0])

    coefs = []
    for level in range(1, levels):
        last = level + 1 == levels
        arrived = swap(message, "leaf", 2 ** (level - 1))
        outs = pl.pallas_call(
            functools.partial(level_kernel, levels, level, share),
            out_shape=[floats(share, rank)] + ([] if last else [message_shape(level + 1)]),
            name=f"level{level}",
            **settings(8, 1 if last else 6),
        )(message, arrived, prepared, first if last else arrived)
        coefs.append(outs[0])
        message = outs[-1]
    stack = pl.pallas_call(
        stack_kernel, out_shape=floats(slots, share, rank), name="stack", **settings(8, 0.1),
    )(first, *early)
    second = pl.pallas_call(
        functools.partial(apply_kernel, per_step * width),
        out_shape=floats(rows, columns),
        scratch_shapes=[
            pltpu.VMEM((columns, rank), jnp.float32),
            pltpu.VMEM((2 * rank, columns), jnp.bfloat16),
        ],
        name="apply",
        **settings(8, 1.8),
    )(stack, swap(stack, "rows", 1), first, left_basis)

    pack = pl.pallas_call(
        pack_kernel, out_shape=floats(share, size), name="pack", **settings(8, 0.1),
    )(*coefs)
    pieces = []
    for slot in range(slots):
        piece = swap(pack, "rows", 2 * slot) if slot > 0 else pack
        if slot in (0, slots - 1):
            piece = pl.pallas_call(
                relay_kernel, out_shape=floats(share, size), name="relay", **settings(8, 0.1),
            )(second, piece)
        pieces += [piece, swap(piece, "rows", 1)]
    return pl.pallas_call(
        functools.partial(expand_kernel, levels, width, count),
        out_specs=pl.BlockSpec(memory_space=pl.ANY),
        out_shape=floats(rows, columns),
        scratch_shapes=[
            pltpu.VMEM((columns, size), jnp.float32),
            pltpu.VMEM((2 * size, columns), jnp.bfloat16),
            pltpu.VMEM((rows, columns), jnp.float32),
            pltpu.SemaphoreType.DMA((nblocks,)),
        ],
        name="expand",
        **settings(16, 5),
    )(*pieces, second, left_basis)


def solution(mesh):
    return jax.shard_map(
        per_device,
        mesh=mesh,
        in_specs=(
            P(("leaf", "rows"), None),
            P(("leaf", "rows"), None),
            P(("leaf", "rows"), None, None),
            P(None, ("leaf", "rows"), None),
            P(None, ("leaf", "rows"), None),
            P(),
            P(),
        ),
        out_specs=P(("leaf", "rows"), None),
        check_vma=False,
    )
```
